32 devices in a mesh: groups: 2 (over y), head: 4 (over z), hist: 4 (over x, core).
Axes of the slice: x: 2, y: 2, z: 4, core: 2. Of those that a mesh axis runs over, the one named last changes fastest.
Arguments:
- tokens: bfloat16 [1024, 8192], P('groups', 'hist'), parts along dimension 0, may hold values from -6 to 6
- w_qkvu: bfloat16 [8192, 4, 8192], P('hist', None, 'head'), may hold values from -0.0625 to 0.0625
- k_cache: bfloat16 [4096, 8192], P(('groups', 'hist'), 'head'), parts along dimension 0, may hold values from -6 to 6
- v_cache: bfloat16 [4096, 8192], P(('groups', 'hist'), 'head'), parts along dimension 0
- w_out: bfloat16 [8192, 8192], P('head', 'hist'), may hold values from -0.0625 to 0.0625
- vis_start: int32 [1024], P('groups'), parts along dimension 0, may hold values from 0 to 511, as said below
- vis_end: int32 [1024], P('groups'), parts along dimension 0, may hold values from 1025 to 2048
Outputs:
- layer_out: bfloat16 [1024, 8192], P(('groups', 'head'), 'hist'), parts along dimension 0
The draws below stay inside these ranges and needn't reach their ends.
There are 2 independent parts, one for each index of `groups`. The reference program is written for one: setup_inputs(seed, part) draws one part's arguments, and reference() takes and returns one part's arrays. A program takes and returns all parts, laid end to end along the dimension named above; an argument that names none is the same for every part. Nothing has to cross between parts.
Inputs may be any that keep to these rules, and one draw needn't show every extreme that they name: vis_start and vis_end together leave every candidate 2048 // 4 + 2 or more visible history events.
All inputs are finite; a program needn't handle non-finite values.
Results may differ from the reference program's by a relative error of at most 0.02.
Values may be sent and summed in bfloat16 or wider, within the bound.
No kernel may reach another device: no remote copies, remote signals or barrier semaphores. Data moves between devices by JAX's collectives and lax.ppermute only.
A program may use at most 192 MiB of HBM per device.

```python
import jax
import jax.numpy as jnp
from jax import lax

D = 8192
HEADS = 64
DH = 128
HD = 8192
HIST = 2048
CAND = 512
N_HIST = 4


def spread_ends(base_key, low_draw, high_draw, low_end, high_end):
    pick_key, value_key = jax.random.split(base_key)
    drawn = jax.random.randint(value_key, (CAND,), low_draw, high_draw)
    shuffled = jax.random.permutation(pick_key, CAND)
    places = lax.iota(jnp.int32, CAND)
    drawn = jnp.where(places == shuffled[0], low_end, drawn)
    drawn = jnp.where(places == shuffled[1], high_end, drawn)
    return drawn.astype(jnp.int32)


def draw_vis_start(key, part):
    return spread_ends(jax.random.fold_in(key, 11), 0, HIST // 4, 0, HIST // 4 - 1)


def draw_vis_end(key, part):
    return spread_ends(jax.random.fold_in(key, 23), HIST // 2 + 1, HIST + 1, HIST // 2 + 1, HIST)


def draw_v_cache(key, part):
    base_key, scale_key = jax.random.split(jax.random.fold_in(key, 37), 2)
    columns = lax.iota(jnp.float32, HD) / HD
    column_scale = 0.5 * 10.0 ** columns * jax.random.uniform(scale_key, (HD,), minval=0.7, maxval=1.4)
    entries = jax.random.normal(base_key, (HIST, HD))
    return (entries * column_scale[None, :]).astype(jnp.bfloat16)


def level_of(rng, shape, shards, smallest, top_value):
    level, own = 1.0, jax.random.fold_in(rng, 6)
    for position, blocks in shards:
        draws = jnp.exp(jax.random.uniform(jax.random.fold_in(own, position), (blocks,), jnp.float32, smallest / len(shards), top_value / len(shards)))
        level = level * jnp.repeat(draws, shape[position] // blocks).reshape([-1 if axis == position else 1 for axis in range(len(shape))])
    return level


def normal_values(rng, extent, spread, most, pieces=(), dtype=jnp.bfloat16):
    result = spread * jax.random.normal(rng, extent, jnp.float32)
    if pieces:
        result = result * level_of(rng, extent, pieces, -0.22, 0.18)
    return jnp.clip(result, -most, most).astype(dtype)


def setup_inputs(seed: int = 0, part: int = 0) -> dict:
    splits = jax.random.split(jax.random.key(seed), 8)
    own_keys = jax.random.split(jax.random.fold_in(splits[7], part), 8)
    tokens = normal_values(own_keys[0], (CAND, D), 1.0, 6.0, ((1, 4),))
    w_qkvu = normal_values(splits[1], (D, 4, HD), D ** -0.5, 0.0625, ((0, 4), (2, 4)))
    k_cache = normal_values(own_keys[2], (HIST, HD), 1.0, 6.0, ((0, 4), (1, 4)))
    v_cache = draw_v_cache(jax.random.fold_in(jax.random.fold_in(splits[7], part), 71), part)
    w_out = normal_values(splits[4], (HD, D), HD ** -0.5, 0.0625, ((0, 4), (1, 4)))
    vis_start = draw_vis_start(jax.random.fold_in(jax.random.fold_in(splits[7], part), 71), part)
    vis_end = draw_vis_end(jax.random.fold_in(jax.random.fold_in(splits[7], part), 71), part)
    return dict(tokens=tokens, w_qkvu=w_qkvu, k_cache=k_cache, v_cache=v_cache, w_out=w_out, vis_start=vis_start, vis_end=vis_end)


epsilon = 1e-05

def project_all(tokens, w_qkvu):
    row_block = D // N_HIST
    flat_weight = w_qkvu.reshape(D, 4 * HD)
    running_sum = jnp.zeros((CAND, 4 * HD), jnp.float32)
    for block_index in range(N_HIST):
        lower_row = block_index * row_block
        partial_term = jnp.dot(tokens[:, lower_row:lower_row + row_block], flat_weight[lower_row:lower_row + row_block], preferred_element_type=jnp.float32)
        rounded = lax.optimization_barrier(partial_term.astype(jnp.bfloat16))
        running_sum = running_sum + rounded.astype(jnp.float32)
    return jax.nn.silu(running_sum).astype(jnp.bfloat16).reshape(CAND, 4, HD)

def reference(tokens, w_qkvu, k_cache, v_cache, w_out, vis_start, vis_end):
    projected = project_all(tokens, w_qkvu)
    queries = projected[:, 0].reshape(CAND, HEADS, DH).transpose(1, 0, 2)
    self_keys = projected[:, 1].reshape(CAND, HEADS, DH).transpose(1, 0, 2)
    self_values = projected[:, 2].reshape(CAND, HEADS, DH).transpose(1, 0, 2)
    gate_part = projected[:, 3]
    key_heads = k_cache.reshape(HIST, HEADS, DH).transpose(1, 0, 2)
    value_heads = v_cache.reshape(HIST, HEADS, DH).transpose(1, 0, 2)
    positions = lax.iota(jnp.int32, HIST)
    visible = (positions[None, :] >= vis_start[:, None]) & (positions[None, :] < vis_end[:, None])
    counts = (vis_end - vis_start).astype(jnp.float32)

    def head_output(operands):
        head_query, self_key, self_value, key_head, value_head = operands
        scores = jnp.dot(head_query, key_head.T, preferred_element_type=jnp.float32) * DH ** (-0.5)
        weights = jnp.where(visible, jax.nn.silu(scores), 0.0).astype(jnp.bfloat16)
        history = jnp.dot(weights, value_head, preferred_element_type=jnp.float32)
        own_score = lax.optimization_barrier(jnp.sum(head_query.astype(jnp.float32) * self_key.astype(jnp.float32), axis=1)) * DH ** (-0.5)
        return history / jnp.sqrt(counts)[:, None] + jax.nn.silu(own_score)[:, None] * self_value.astype(jnp.float32)
    per_head = lax.map(head_output, (queries, self_keys, self_values, key_heads, value_heads))
    attended = per_head.transpose(1, 0, 2).reshape(CAND, HD)
    mean_value = lax.optimization_barrier(jnp.sum(attended, axis=1)) / HD
    centered = attended - mean_value[:, None]
    variance = lax.optimization_barrier(jnp.sum(centered * centered, axis=1)) / HD
    normed = centered * lax.rsqrt(variance + epsilon)[:, None]
    gated = (normed * gate_part.astype(jnp.float32)).astype(jnp.bfloat16)
    projected_out = jnp.dot(gated, w_out, preferred_element_type=jnp.float32)
    return (tokens.astype(jnp.float32) + projected_out).astype(jnp.bfloat16)
```

```python
import functools

import jax
import jax.numpy as jnp
from jax import lax
from jax.experimental import pallas as pl
from jax.experimental.pallas import tpu as pltpu
from jax.sharding import PartitionSpec as P

DH = 128
EPSILON = 1e-05
VMEM_LIMIT = 48 * 1024 * 1024

bf16 = jnp.bfloat16
f32 = jnp.float32


def silu(v):
    return 0.5 * v * (1.0 + jnp.tanh(0.5 * v))


def params():
    return pltpu.CompilerParams(vmem_limit_bytes=VMEM_LIMIT)


def project_kernel(t_ref, w_ref, o_ref, wide_ref, rhs_ref):
    depth = w_ref.shape[0]
    wide_ref[...] = w_ref.reshape(depth * 4, DH)[...].astype(f32)
    for i in range(4):
        rhs_ref[:, i * DH:(i + 1) * DH] = wide_ref[pl.ds(i, depth, stride=4), :].astype(bf16)
    res = jnp.dot(t_ref[...], rhs_ref[...], preferred_element_type=f32).astype(bf16)
    owners, _, each, _ = o_ref.shape
    for p in range(owners):
        for i in range(4):
            o_ref[p, i] = res[p * each:(p + 1) * each, i * DH:(i + 1) * DH]


def project(tokens, w, row_chunk, rows, head_first, heads, owners):
    depth = w.shape[0]
    each = rows // owners
    return pl.pallas_call(
        project_kernel,
        grid=(heads,),
        in_specs=[
            pl.BlockSpec((rows, depth), lambda j: (row_chunk, 0)),
            pl.BlockSpec((depth, 4, DH), lambda j: (0, 0, head_first + j)),
        ],
        out_specs=pl.BlockSpec((owners, 4, each, DH), lambda j: (0, 0, 0, j)),
        out_shape=jax.ShapeDtypeStruct((owners, 4, each, heads * DH), bf16),
        scratch_shapes=[pltpu.VMEM((depth * 4, DH), f32), pltpu.VMEM((depth, 4 * DH), bf16)],
        compiler_params=params(),
        cost_estimate=pl.CostEstimate(
            flops=2 * rows * depth * 4 * heads * DH,
            bytes_accessed=depth * 8 * heads * DH + rows * depth * 2,
            transcendentals=0,
        ),
        name="project",
    )(tokens, w)


def attend_kernel(q_ref, k_ref, v_ref, lo_ref, hi_ref, o_ref):
    rows, events = q_ref.shape[0], k_ref.shape[0]
    scores = lax.dot_general(
        q_ref[...], k_ref[...], (((1,), (1,)), ((), ())), preferred_element_type=f32
    ) * DH ** (-0.5)
    at = lax.broadcasted_iota(jnp.int32, (rows, events), 1)
    seen = (at >= lo_ref[...]) & (at < hi_ref[...])
    weights = jnp.where(seen, silu(scores), 0.0).astype(bf16)
    o_ref[...] = jnp.dot(weights, v_ref[...], preferred_element_type=f32).astype(bf16)


def attend(query, k_cache, v_cache, lo, hi, head_first, heads):
    rows, events = query.shape[0], k_cache.shape[0]
    cache = pl.BlockSpec((events, DH), lambda j: (0, head_first + j))
    edge = pl.BlockSpec((rows, 1), lambda j: (0, 0))
    return pl.pallas_call(
        attend_kernel,
        grid=(heads,),
        in_specs=[pl.BlockSpec((rows, DH), lambda j: (0, j)), cache, cache, edge, edge],
        out_specs=pl.BlockSpec((rows, DH), lambda j: (0, j)),
        out_shape=jax.ShapeDtypeStruct((rows, heads * DH), bf16),
        compiler_params=params(),
        cost_estimate=pl.CostEstimate(
            flops=4 * rows * events * heads * DH,
            bytes_accessed=4 * (rows + events) * heads * DH,
            transcendentals=rows * events * heads,
        ),
        name="attend",
    )(query, k_cache, v_cache, lo, hi)


def finish_kernel(chunks, *refs):
    root_ref = refs[0]
    keeps, gots, parts = (refs[1 + k * chunks:1 + (k + 1) * chunks] for k in range(3))
    att_ref, stat_ref = refs[1 + 3 * chunks:]
    rows = root_ref.shape[0]
    root = root_ref[...]
    total = jnp.zeros((rows, 1), f32)
    column = 0
    for keep, got, part in zip(keeps, gots, parts):
        for h in range(keep.shape[1] // DH):
            at = slice(h * DH, (h + 1) * DH)
            summed = keep[:, at].astype(f32) + got[:, at].astype(f32)
            q, k, v = (part[i, :, at].astype(f32) for i in range(3))
            own = silu(jnp.sum(q * k, axis=1, keepdims=True) * DH ** (-0.5))
            value = summed * root + own * v
            att_ref[:, column:column + DH] = value
            total += jnp.sum(value, axis=1, keepdims=True)
            column += DH
    mean = total / column
    spread = jnp.zeros((rows, DH), f32)
    for first in range(0, column, DH):
        away = att_ref[:, first:first + DH] - mean
        spread += away * away
    square = jnp.sum(spread, axis=1, keepdims=True)
    lane = lax.broadcasted_iota(jnp.int32, (rows, DH), 1)
    stat_ref[...] = jnp.where(lane < DH // 2, mean, square)


def finish(root, keeps, gots, parts):
    rows = root.shape[0]
    width = sum(k.shape[1] for k in keeps)
    return pl.pallas_call(
        functools.partial(finish_kernel, len(keeps)),
        out_shape=(
            jax.ShapeDtypeStruct((rows, width), f32),
            jax.ShapeDtypeStruct((rows, DH), f32),
        ),
        compiler_params=params(),
        cost_estimate=pl.CostEstimate(
            flops=20 * rows * width, bytes_accessed=16 * rows * width, transcendentals=0
        ),
        name="finish",
    )(root, *keeps, *gots, *parts)


def gate_kernel(chunks, others, *refs):
    att_ref, stats = refs[0], refs[1:2 + others]
    parts = refs[2 + others:2 + others + chunks]
    out_ref = refs[-1]
    width = att_ref.shape[1]
    means = [s[:, :1] for s in stats]
    mean = sum(means) / len(means)
    square = sum(s[:, DH // 2:DH // 2 + 1] for s in stats)
    square += width * sum((m - mean) * (m - mean) for m in means)
    scale = lax.rsqrt(square / (width * len(means)) + EPSILON)
    column = 0
    for part in parts:
        span = part.shape[2]
        normed = (att_ref[:, column:column + span] - mean) * scale
        out_ref[:, column:column + span] = (normed * part[3].astype(f32)).astype(bf16)
        column += span


def gate_rows(att, stats, parts):
    rows, width = att.shape
    return pl.pallas_call(
        functools.partial(gate_kernel, len(parts), len(stats) - 1),
        out_shape=jax.ShapeDtypeStruct((rows, width), bf16),
        compiler_params=params(),
        cost_estimate=pl.CostEstimate(
            flops=4 * rows * width, bytes_accessed=8 * rows * width, transcendentals=0
        ),
        name="gate",
    )(att, *stats, *parts)


def halving(count):
    return count & (count - 1) == 0


def swap(x, axis, bit):
    count = lax.axis_size(axis)
    return lax.ppermute(x, axis, [(i, i ^ (1 << bit)) for i in range(count)])


def position(axis):
    count, index = lax.axis_size(axis), lax.axis_index(axis)
    if not halving(count):
        return index
    bits = count.bit_length() - 1
    return sum(((index >> b) & 1) << (bits - 1 - b) for b in range(bits))


def scatter(x, axis):
    count, index = lax.axis_size(axis), lax.axis_index(axis)
    if count == 1:
        return x[0], jnp.zeros_like(x[0])
    if not halving(count):
        mine = lax.psum_scatter(x, axis, scatter_dimension=0, tiled=True)[0]
        return mine, jnp.zeros_like(mine)
    bits = count.bit_length() - 1
    for b in range(bits):
        mine, half = (index >> b) & 1, x.shape[0] // 2
        send = lax.dynamic_slice_in_dim(x, (1 - mine) * half, half).astype(bf16)
        keep = lax.dynamic_slice_in_dim(x, mine * half, half)
        got = swap(send, axis, b)
        if b == bits - 1:
            return keep[0], got[0]
        x = keep.astype(f32) + got.astype(f32)


def gather(x, axis):
    count, index = lax.axis_size(axis), lax.axis_index(axis)
    x = x[None]
    if not halving(count):
        return lax.all_gather(x, axis, axis=0, tiled=True)
    for b in reversed(range(count.bit_length() - 1)):
        mine = (index >> b) & 1
        got = swap(x, axis, b)
        x = jnp.where(mine == 0, jnp.concatenate([x, got]), jnp.concatenate([got, x]))
    return x


def all_stats(stat, axis):
    count = lax.axis_size(axis)
    if count > 8:
        every = lax.all_gather(stat, axis)
        return [every[i] for i in range(count)]
    return [stat] + [
        lax.ppermute(stat, axis, [(i, (i + k) % count) for i in range(count)])
        for k in range(1, count)
    ]


def line_scatter(x, axis):
    count, index = lax.axis_size(axis), lax.axis_index(axis)
    if count > 8:
        return lax.psum_scatter(x, axis, scatter_dimension=0, tiled=True)[0].astype(f32)

    def block(at):
        return lax.dynamic_index_in_dim(x, jnp.clip(at, 0, count - 1), 0, False)

    from_left = from_right = None
    for far in range(count - 1, 0, -1):
        right, left = block(index + far), block(index - far)
        if from_left is not None:
            right = (right.astype(f32) + from_left.astype(f32)).astype(bf16)
            left = (left.astype(f32) + from_right.astype(f32)).astype(bf16)
        from_left = lax.ppermute(right, axis, [(i, i + 1) for i in range(count - far)])
        from_right = lax.ppermute(left, axis, [(i, i - 1) for i in range(far, count)])
    total = block(index).astype(f32)
    if from_left is not None:
        total = total + from_left.astype(f32) + from_right.astype(f32)
    return total


def local(tokens, w_qkvu, k_cache, v_cache, w_out, vis_start, vis_end):
    cand, depth = tokens.shape
    owners, zs = lax.axis_size("hist"), lax.axis_size("head")
    width = w_qkvu.shape[2]
    heads = width // DH
    events = k_cache.shape[0]
    place = position("hist")

    row_chunks = 2 if cand % (2 * owners * zs * 16) == 0 else 1
    head_chunks = 2 if heads % 2 == 0 else 1
    rows = cand // row_chunks
    each = rows // owners
    piece = each // zs
    per = heads // head_chunks

    def arrange(x):
        tail = x.shape[1:]
        x = x.reshape((zs, row_chunks, owners, piece) + tail)
        x = jnp.moveaxis(x, (1, 2), (0, 1))
        return x.reshape((cand,) + tail)

    ordered = arrange(tokens)
    first_event = lax.axis_index("hist") * events
    start, end = arrange(vis_start), arrange(vis_end)
    low, high = (start - first_event)[:, None], (end - first_event)[:, None]
    root = lax.rsqrt((end - start).astype(f32))[:, None]

    partials = {
        (r, c): project(ordered, w_qkvu, r, rows, c * per, per, owners)
        for r in range(row_chunks)
        for c in range(head_chunks)
    }
    outs = []
    for r in range(row_chunks):
        span = slice(r * rows, (r + 1) * rows)
        parts, keeps, gots = [], [], []
        for c in range(head_chunks):
            keep, got = scatter(partials[r, c], "hist")
            part = silu(keep.astype(f32) + got.astype(f32)).astype(bf16)
            query = gather(part[0], "hist").reshape(rows, per * DH)
            term = attend(query, k_cache, v_cache, low[span], high[span], c * per, per)
            keep, got = scatter(term.reshape(owners, each, per * DH), "hist")
            parts.append(part)
            keeps.append(keep)
            gots.append(got)
        own_root = lax.dynamic_slice_in_dim(root[span], place * each, each)
        att, stat = finish(own_root, keeps, gots, parts)
        gated = gate_rows(att, all_stats(stat, "head"), parts)
        every = gather(gated, "hist").reshape(rows, width)
        sums = jnp.dot(every, w_out, preferred_element_type=f32).astype(bf16)
        sums = sums.reshape(owners, zs, piece, -1).swapaxes(0, 1)
        outs.append(line_scatter(sums.reshape(zs, each * owners // zs, -1), "head"))
    block = cand // zs
    residual = lax.dynamic_slice_in_dim(tokens, lax.axis_index("head") * block, block)
    return (residual.astype(f32) + jnp.concatenate(outs)).astype(bf16)


def solution(mesh):
    in_specs = (
        P("groups", "hist"),
        P("hist", None, "head"),
        P(("groups", "hist"), "head"),
        P(("groups", "hist"), "head"),
        P("head", "hist"),
        P("groups"),
        P("groups"),
    )
    out_specs = P(("groups", "head"), "hist")
    return jax.shard_map(local, mesh=mesh, in_specs=in_specs, out_specs=out_specs, check_vma=False)
```

```python
import functools

import jax
import jax.numpy as jnp
import numpy as np
from jax import lax
from jax.experimental import pallas as pl
from jax.experimental.pallas import tpu as pltpu
from jax.sharding import PartitionSpec as P

DH = 128
EPSILON = 1e-05
VMEM_LIMIT = 48 * 1024 * 1024

bf16 = jnp.bfloat16
f32 = jnp.float32


def silu(v):
    u = 0.5 * v
    return u + u * jnp.tanh(u)


def params():
    return pltpu.CompilerParams(vmem_limit_bytes=VMEM_LIMIT)


def cost(flops, moved, transcendentals=0):
    return pl.CostEstimate(flops=flops, bytes_accessed=moved, transcendentals=transcendentals)


def project_kernel(t_ref, w_ref, *refs):
    keep_ref, send_ref, wide_ref, rhs_ref = refs[-4:]
    depth = w_ref.shape[0]
    wide_ref[...] = w_ref.reshape(depth * 4, DH)[...].astype(f32)
    for i in range(4):
        rhs_ref[:, i * DH:(i + 1) * DH] = wide_ref[pl.ds(i, depth, stride=4), :].astype(bf16)
    res = jnp.dot(t_ref[...], rhs_ref[...], preferred_element_type=f32).astype(bf16)
    half, _, each, _ = keep_ref.shape
    for p in range(2 * half):
        into = keep_ref if p < half else send_ref
        for i in range(4):
            into[p % half, i] = res[p * each:(p + 1) * each, i * DH:(i + 1) * DH]


def project(tokens, w, head_first, heads, owners, after):
    rows, depth = tokens.shape
    half, each = owners // 2, rows // owners
    shape = jax.ShapeDtypeStruct((half, 4, each, heads * DH), bf16)
    spec = pl.BlockSpec((half, 4, each, DH), lambda j: (0, 0, 0, j))
    return pl.pallas_call(
        project_kernel,
        grid=(heads,),
        in_specs=[
            pl.BlockSpec((rows, depth), lambda j: (0, 0)),
            pl.BlockSpec((depth, 4, DH), lambda j: (0, 0, head_first + j)),
        ] + [pl.BlockSpec(memory_space=pl.ANY)] * len(after),
        out_specs=(spec, spec),
        out_shape=(shape, shape),
        scratch_shapes=[pltpu.VMEM((depth * 4, DH), f32), pltpu.VMEM((depth, 4 * DH), bf16)],
        compiler_params=params(),
        cost_estimate=cost(
            2 * rows * depth * 4 * heads * DH, depth * 8 * heads * DH + rows * depth * 2
        ),
        name="project",
    )(tokens, w, *after)


def activate_kernel(count, *refs):
    total = sum(r[0].astype(f32) for r in refs[:count])
    q_ref, rest_ref = refs[count:]
    part = silu(total).astype(bf16)
    q_ref[...] = part[0]
    rest_ref[...] = part[1:]


def activate(terms):
    _, _, each, width = terms[0].shape
    return pl.pallas_call(
        functools.partial(activate_kernel, len(terms)),
        grid=(1,),
        in_specs=[pl.BlockSpec((1, 4, each, width), lambda j: (0, 0, 0, 0)) for t in terms],
        out_specs=(
            pl.BlockSpec((each, width), lambda j: (0, 0)),
            pl.BlockSpec((3, each, width), lambda j: (0, 0, 0)),
        ),
        out_shape=(
            jax.ShapeDtypeStruct((each, width), bf16),
            jax.ShapeDtypeStruct((3, each, width), bf16),
        ),
        compiler_params=params(),
        cost_estimate=cost(40 * each * width, 32 * each * width),
        name="activate",
    )(*terms)


def attend_kernel(owners, *refs):
    queries = refs[:owners]
    k_ref, v_ref, lo_ref, hi_ref, keep_ref, send_ref, mask_ref = refs[owners:]
    rows, events = mask_ref.shape
    half, each, _ = keep_ref.shape

    @pl.when(pl.program_id(0) == 0)
    def _():
        at = lax.broadcasted_iota(jnp.int32, (rows, events), 1)
        seen = (at >= lo_ref[...]) & (at < hi_ref[...])
        mask_ref[...] = jnp.where(seen, 1.0, 0.0).astype(bf16)

    query = jnp.concatenate([q[...] for q in queries])
    u = lax.dot_general(
        query, k_ref[...], (((1,), (1,)), ((), ())), preferred_element_type=f32
    ) * (0.5 * DH ** (-0.5))
    weights = (u + u * jnp.tanh(u)).astype(bf16) * mask_ref[...]
    term = jnp.dot(weights, v_ref[...], preferred_element_type=f32).astype(bf16)
    for p in range(owners):
        into = keep_ref if p < half else send_ref
        into[p % half] = term[p * each:(p + 1) * each]


def attend(queries, k_cache, v_cache, lo, hi, head_first, heads):
    owners, (each, width) = len(queries), queries[0].shape
    rows, events, half = owners * each, k_cache.shape[0], owners // 2
    cache = pl.BlockSpec((events, DH), lambda j: (0, head_first + j))
    edge = pl.BlockSpec((rows, 1), lambda j: (0, 0))
    shape = jax.ShapeDtypeStruct((half, each, width), bf16)
    spec = pl.BlockSpec((half, each, DH), lambda j: (0, 0, j))
    return pl.pallas_call(
        functools.partial(attend_kernel, owners),
        grid=(heads,),
        in_specs=[pl.BlockSpec((each, DH), lambda j: (0, j))] * owners + [cache, cache, edge, edge],
        out_specs=(spec, spec),
        out_shape=(shape, shape),
        scratch_shapes=[pltpu.VMEM((rows, events), bf16)],
        compiler_params=params(),
        cost_estimate=cost(
            4 * rows * events * width, 4 * (rows + events) * width, rows * events * heads
        ),
        name="attend",
    )(*queries, k_cache, v_cache, lo, hi)


def finish_kernel(chunks, terms, *refs):
    root_ref, att_ref, stat_ref = refs[0], refs[-2], refs[-1]
    rows = root_ref.shape[0]
    root = root_ref[...]
    total = jnp.zeros((rows, 1), f32)
    column = 0
    for c in range(chunks):
        own = refs[1 + c * (terms + 2):1 + (c + 1) * (terms + 2)]
        sums, q_ref, rest_ref = own[:terms], own[terms], own[terms + 1]
        for h in range(q_ref.shape[1] // DH):
            at = slice(h * DH, (h + 1) * DH)
            summed = sum(s[0, :, at].astype(f32) for s in sums)
            product = q_ref[:, at].astype(f32) * rest_ref[0, :, at].astype(f32)
            weight = silu(jnp.sum(product, axis=1, keepdims=True) * DH ** (-0.5))
            value = summed * root + weight * rest_ref[1, :, at].astype(f32)
            att_ref[:, column:column + DH] = value
            total += jnp.sum(value, axis=1, keepdims=True)
            column += DH
    mean = total / column
    spread = jnp.zeros((rows, DH), f32)
    for first in range(0, column, DH):
        away = att_ref[:, first:first + DH] - mean
        spread += away * away
    square = jnp.sum(spread, axis=1, keepdims=True)
    lane = lax.broadcasted_iota(jnp.int32, (rows, DH), 1)
    stat_ref[...] = jnp.where(lane < DH // 2, mean, square)


def finish(root, chunks):
    rows = root.shape[0]
    width = sum(q.shape[1] for _, q, _ in chunks)
    flat, specs = [root], [pl.BlockSpec((rows, 1), lambda j: (0, 0))]
    for sums, q, rest in chunks:
        span = q.shape[1]
        flat += [*sums, q, rest]
        specs += [pl.BlockSpec((1, rows, span), lambda j: (0, 0, 0))] * len(sums)
        specs += [pl.BlockSpec((rows, span), lambda j: (0, 0))]
        specs += [pl.BlockSpec((2, rows, span), lambda j: (0, 0, 0))]
    return pl.pallas_call(
        functools.partial(finish_kernel, len(chunks), len(chunks[0][0])),
        grid=(1,),
        in_specs=specs,
        out_specs=(
            pl.BlockSpec((rows, width), lambda j: (0, 0)),
            pl.BlockSpec((rows, DH), lambda j: (0, 0)),
        ),
        out_shape=(
            jax.ShapeDtypeStruct((rows, width), f32),
            jax.ShapeDtypeStruct((rows, DH), f32),
        ),
        compiler_params=params(),
        cost_estimate=cost(20 * rows * width, 16 * rows * width),
        name="finish",
    )(*flat)


def gate_kernel(count, chunks, order_ref, *refs):
    att_ref, stats, parts, out_ref = refs[0], refs[1:1 + count], refs[1 + count:-1], refs[-1]
    zs, piece, width = att_ref.shape

    def column(first):
        return [s[..., first:first + 1] for s in stats]

    means, squares = column(0), column(DH // 2)
    mean = sum(means) / count
    square = sum(squares) + width * sum((m - mean) * (m - mean) for m in means)
    scale = lax.rsqrt(square / (width * count) + EPSILON)
    first = 0
    for part in parts:
        span = part.shape[-1]
        at = slice(first, first + span)
        normed = (att_ref[..., at] - mean) * scale
        out_ref[0, ..., at] = (normed * part[0].astype(f32)).astype(bf16)
        first += span


def gate_rows(order, att, stats, rests, zs):
    rows, width = att.shape
    piece = rows // zs

    def split(x):
        return x.reshape(x.shape[:-2] + (zs, piece, x.shape[-1]))

    def spec(x):
        return pl.BlockSpec((1,) + x.shape[1:], lambda j, order: (order[j],) + (0,) * (x.ndim - 1))

    att, stats, rests = split(att), [split(s) for s in stats], [split(r) for r in rests]
    return pl.pallas_call(
        functools.partial(gate_kernel, len(stats), len(rests)),
        grid_spec=pltpu.PrefetchScalarGridSpec(
            num_scalar_prefetch=1,
            grid=(zs,),
            in_specs=[spec(att)] + [spec(s) for s in stats] + [
                pl.BlockSpec((1, 1, piece, r.shape[-1]), lambda j, order: (2, order[j], 0, 0))
                for r in rests
            ],
            out_specs=pl.BlockSpec((1, 1, piece, width), lambda j, order: (j, 0, 0, 0)),
        ),
        out_shape=jax.ShapeDtypeStruct((zs, 1, piece, width), bf16),
        compiler_params=params(),
        cost_estimate=cost(4 * rows * width, 8 * rows * width),
        name="gate",
    )(order, att, *stats, *rests).reshape(zs, piece, width)


def close_kernel(at_ref, t_ref, *refs):
    total = t_ref[...].astype(f32)
    for r in refs[:-1]:
        total = total + r[...].astype(f32)
    refs[-1][...] = total.astype(bf16)


def close(place, first, tokens, terms):
    owners, piece, width = terms[0].shape
    term = pl.BlockSpec((1, piece, width), lambda j, at: (j ^ at[0], 0, 0))
    tokens = tokens.reshape(-1, piece, width)
    return pl.pallas_call(
        close_kernel,
        grid_spec=pltpu.PrefetchScalarGridSpec(
            num_scalar_prefetch=1,
            grid=(owners,),
            in_specs=[pl.BlockSpec((1, piece, width), lambda j, at: (at[1] + j, 0, 0))]
            + [term] * len(terms),
            out_specs=pl.BlockSpec((1, piece, width), lambda j, at: (j, 0, 0)),
        ),
        out_shape=jax.ShapeDtypeStruct((owners, piece, width), bf16),
        compiler_params=params(),
        cost_estimate=cost(4 * owners * piece * width, 10 * owners * piece * width),
        name="close",
    )(jnp.stack([place, first]).astype(jnp.int32), tokens, *terms)


def bits_of(axis):
    count = lax.axis_size(axis)
    assert count & (count - 1) == 0
    return count.bit_length() - 1


def place_of(axis):
    index, bits = lax.axis_index(axis), bits_of(axis)
    return sum((((index >> b) & 1) << (bits - 1 - b) for b in range(bits)), jnp.int32(0))


def swap(x, axis, bit):
    return lax.ppermute(
        x, axis, [(i, i ^ (1 << bit)) for i in range(lax.axis_size(axis))]
    )


def scatter(keep, send, axis):
    terms = [keep, swap(send, axis, 0)]
    for b in range(1, bits_of(axis)):
        half = terms[-1].shape[0] // 2
        total = sum(t[half:2 * half].astype(f32) for t in terms)
        send = total.astype(bf16)
        terms.append(swap(send, axis, b))
    return terms, send


def gather(x, axis):
    blocks = [x]
    for b in reversed(range(bits_of(axis))):
        blocks = blocks + [swap(block, axis, b) for block in blocks]
    return blocks


def all_stats(stat, axis):
    count = lax.axis_size(axis)
    if count > 8:
        every = lax.all_gather(stat, axis)
        return [every[i] for i in range(count)]
    return [stat] + [
        lax.ppermute(stat, axis, [(i, (i + k) % count) for i in range(count)])
        for k in range(1, count)
    ]


def far_first(count):
    return np.array(
        [sorted(range(count), key=lambda c: (-abs(c - i), c)) for i in range(count)], np.int32
    )


def line_scatter(blocks, axis):
    count, index = lax.axis_size(axis), lax.axis_index(axis)
    order = far_first(count)

    def pick(step):
        where = {}
        for i in range(count):
            if 0 <= i + step < count:
                where.setdefault(int(np.argmax(order[i] == i + step)), []).append(i)
        slots = sorted(where)
        out = blocks[slots[0]]
        for s in slots[1:]:
            here = functools.reduce(jnp.logical_or, [index == i for i in where[s]])
            out = jnp.where(here, blocks[s], out)
        return out

    from_left = from_right = None
    for far in range(count - 1, 0, -1):
        right, left = pick(far), pick(-far)
        if from_left is not None:
            right = (right.astype(f32) + from_left.astype(f32)).astype(bf16)
            left = (left.astype(f32) + from_right.astype(f32)).astype(bf16)
        from_left = lax.ppermute(right, axis, [(i, i + 1) for i in range(count - far)])
        from_right = lax.ppermute(left, axis, [(i, i - 1) for i in range(far, count)])
    return [blocks[-1]] + [x for x in (from_left, from_right) if x is not None]


def head_chunks(heads):
    if heads % 8:
        return [1] * heads
    unit = heads // 8
    return [unit, 2 * unit, 2 * unit, 2 * unit, unit]


def local(tokens, w_qkvu, k_cache, v_cache, w_out, vis_start, vis_end):
    cand, depth = tokens.shape
    owners, zs = lax.axis_size("hist"), lax.axis_size("head")
    index, place = lax.axis_index("head"), place_of("hist")
    width = w_qkvu.shape[2]
    events = k_cache.shape[0]
    each = cand // owners
    piece = each // zs

    def arrange(x):
        x = x.reshape((zs, owners, piece) + x.shape[1:])
        blocks = [lax.dynamic_index_in_dim(x, p ^ place, 1, False) for p in range(owners)]
        return jnp.stack(blocks).reshape((cand,) + x.shape[3:])

    ordered = arrange(tokens)
    first_event = lax.axis_index("hist") * events
    edges = arrange(jnp.stack([vis_start, vis_end], axis=1))
    start, end = edges[:, :1], edges[:, 1:]
    low, high = start - first_event, end - first_event
    root = lax.rsqrt((end - start)[:each].astype(f32))

    sizes = head_chunks(width // DH)
    firsts = [sum(sizes[:c]) for c in range(len(sizes))]
    summed, sent = [], []
    for c, (first, heads) in enumerate(zip(firsts, sizes)):
        after = [sent[c - 2]] if c >= 2 else []
        keep, send = project(ordered, w_qkvu, first, heads, owners, after)
        terms, last = scatter(keep, send, "hist")
        summed.append(terms)
        sent.append(last)
    chunks = []
    for terms, first, heads in zip(summed, firsts, sizes):
        query, rest = activate(terms)
        keep, send = attend(gather(query, "hist"), k_cache, v_cache, low, high, first, heads)
        sums, _ = scatter(keep, send, "hist")
        chunks.append((sums, query, rest))
    att, stat = finish(root, chunks)
    order = lax.dynamic_index_in_dim(jnp.asarray(far_first(zs)), index, 0, False)
    stats = all_stats(stat, "head")
    gated = gate_rows(order, att, stats, [rest for _, _, rest in chunks], zs)
    pieces = 2 if zs % 2 == 0 and (zs // 2 * piece) % 16 == 0 else 1
    per = zs // pieces
    blocks = []
    for g in range(pieces):
        part = gated[g * per:(g + 1) * per].reshape(per * piece, width)
        rows = jnp.concatenate(gather(part, "hist"))
        sums = jnp.dot(rows, w_out, preferred_element_type=f32).astype(bf16)
        sums = sums.reshape(owners, per, piece, -1)
        blocks += [sums[:, s] for s in range(per)]
    if zs > 8:
        stacked = jnp.stack(blocks)
        back = jnp.argsort(order)
        whole = jnp.take(stacked, back, axis=0)
        terms = [lax.psum_scatter(whole, "head", scatter_dimension=0, tiled=True)[0]]
    else:
        terms = line_scatter(blocks, "head")
    return close(place, index * owners, tokens, terms).reshape(cand // zs, -1)


def solution(mesh):
    in_specs = (
        P("groups", "hist"),
        P("hist", None, "head"),
        P(("groups", "hist"), "head"),
        P(("groups", "hist"), "head"),
        P("head", "hist"),
        P("groups"),
        P("groups"),
    )
    out_specs = P(("groups", "head"), "hist")
    return jax.shard_map(local, mesh=mesh, in_specs=in_specs, out_specs=out_specs, check_vma=False)
```

```python
import functools

import jax
import jax.numpy as jnp
from jax import lax
from jax.experimental import pallas as pl
from jax.experimental.pallas import tpu as pltpu
from jax.sharding import PartitionSpec as P

DH = 128
EPSILON = 1e-05
VMEM_LIMIT = 48 * 1024 * 1024

bf16 = jnp.bfloat16
f32 = jnp.float32


def silu(v):
    u = 0.5 * v
    return u + u * jnp.tanh(u)


def params():
    return pltpu.CompilerParams(vmem_limit_bytes=VMEM_LIMIT)


LIGHT = pl.CostEstimate(flops=1000, bytes_accessed=1000, transcendentals=0)


def project_kernel(parts, owners, at_ref, *refs):
    rows, w_ref = refs[:owners], refs[owners]
    keep_ref, send_ref, lhs_ref = refs[-3 - parts:-parts]
    wides = refs[-parts:]
    zs, chunks, _, piece, _ = rows[0].shape
    depth = w_ref.shape[0] // parts

    @pl.when(pl.program_id(0) == 0)
    def _():
        first = 0
        for r in range(chunks):
            for p in range(owners):
                for z in range(zs):
                    lhs_ref[first:first + piece, :] = rows[p][z, r, 0]
                    first += piece

    flat = w_ref.reshape(depth * parts * 4, DH)
    res = None
    for k, wide in enumerate(wides):
        wide[...] = flat[k * depth * 4:(k + 1) * depth * 4, :].astype(f32)
        rhs = jnp.concatenate(
            [wide[pl.ds(i, depth, stride=4), :].astype(bf16) for i in range(4)], axis=1
        )
        term = jnp.dot(lhs_ref[:, k * depth:(k + 1) * depth], rhs, preferred_element_type=f32)
        res = term if res is None else res + term
    res = res.astype(bf16)
    half, each = keep_ref.shape[1], keep_ref.shape[3]
    for r in range(chunks):
        for p in range(owners):
            into = keep_ref if p < half else send_ref
            first = (r * owners + p) * each
            for i in range(4):
                into[r, p % half, i] = res[first:first + each, i * DH:(i + 1) * DH]


def project(at, tokens, w, head_first, heads, after):
    zs, chunks, owners, piece, depth = tokens.shape
    half, each = owners // 2, zs * piece
    parts = 4 if depth % 512 == 0 else 1
    shape = jax.ShapeDtypeStruct((chunks, half, 4, each, heads * DH), bf16)
    spec = pl.BlockSpec((chunks, half, 4, each, DH), lambda j, at: (0, 0, 0, 0, j))
    return pl.pallas_call(
        functools.partial(project_kernel, parts, owners),
        grid_spec=pltpu.PrefetchScalarGridSpec(
            num_scalar_prefetch=1,
            grid=(heads,),
            in_specs=[
                pl.BlockSpec(
                    (zs, chunks, 1, piece, depth), lambda j, at, p=p: (0, 0, at[0] ^ p, 0, 0)
                )
                for p in range(owners)
            ]
            + [pl.BlockSpec((depth, 4, DH), lambda j, at: (0, 0, head_first + j))]
            + [pl.BlockSpec(memory_space=pl.ANY)] * len(after),
            out_specs=(spec, spec),
            scratch_shapes=[pltpu.VMEM((chunks * owners * each, depth), bf16)]
            + [pltpu.VMEM((depth // parts * 4, DH), f32) for _ in range(parts)],
        ),
        out_shape=(shape, shape),
        compiler_params=params(),
        cost_estimate=LIGHT,
        name="project",
    )(at, *[tokens] * owners, w, *after)


def tie_kernel(*refs):
    pass


def tie(x, *after):
    anywhere = pl.BlockSpec(memory_space=pl.ANY)
    return pl.pallas_call(
        tie_kernel,
        in_specs=[anywhere] * (1 + len(after)),
        out_specs=anywhere,
        out_shape=jax.ShapeDtypeStruct(x.shape, x.dtype),
        input_output_aliases={0: 0},
        cost_estimate=LIGHT,
        name="tie",
    )(x, *after)


def activate_kernel(counts, *refs):
    q_ref, rest_ref = refs[-2:]
    column, at = 0, 0
    for count in counts:
        terms = refs[at:at + count]
        span = terms[0].shape[-1]
        for i in range(4):
            part = silu(sum(t[0, 0, i].astype(f32) for t in terms)).astype(bf16)
            if i == 0:
                q_ref[:, column:column + span] = part
            else:
                rest_ref[i - 1, :, column:column + span] = part
        column += span
        at += count


def activate(r, chunks):
    flat, specs, width = [], [], 0
    for terms in chunks:
        _, _, _, each, span = terms[0][0].shape
        width += span
        for array, offset in terms:
            flat.append(array)
            specs.append(
                pl.BlockSpec((1, 1, 4, each, span), lambda j, at=r - offset: (at, 0, 0, 0, 0))
            )
    return pl.pallas_call(
        functools.partial(activate_kernel, [len(terms) for terms in chunks]),
        grid=(1,),
        in_specs=specs,
        out_specs=(
            pl.BlockSpec((each, width), lambda j: (0, 0)),
            pl.BlockSpec((3, each, width), lambda j: (0, 0, 0)),
        ),
        out_shape=(
            jax.ShapeDtypeStruct((each, width), bf16),
            jax.ShapeDtypeStruct((3, each, width), bf16),
        ),
        compiler_params=params(),
        cost_estimate=LIGHT,
        name="activate",
    )(*flat)


def attend_kernel(owners, at_ref, *refs):
    queries, edges = refs[:owners], refs[owners:2 * owners]
    k_ref, v_ref, keep_ref, send_ref, mask_ref = refs[2 * owners:]
    events = mask_ref.shape[1]
    half, each, _ = keep_ref.shape

    @pl.when(pl.program_id(0) == 0)
    def _():
        zs, _, _, piece, _ = edges[0].shape
        at = lax.broadcasted_iota(jnp.int32, (piece, events), 1)
        for p in range(owners):
            for z in range(zs):
                edge = edges[p][z, 0, 0]
                seen = (at >= edge[:, :1]) & (at < edge[:, 1:])
                first = p * each + z * piece
                mask_ref[first:first + piece, :] = jnp.where(seen, 1.0, 0.0).astype(bf16)

    query = jnp.concatenate([q[...] for q in queries])
    u = lax.dot_general(
        query, k_ref[...], (((1,), (1,)), ((), ())), preferred_element_type=f32
    ) * (0.5 * DH ** (-0.5))
    weights = (u + u * jnp.tanh(u)).astype(bf16) * mask_ref[...]
    term = jnp.dot(weights, v_ref[...], preferred_element_type=f32).astype(bf16)
    for p in range(owners):
        into = keep_ref if p < half else send_ref
        into[p % half] = term[p * each:(p + 1) * each]


def edge_spec(edges, r, p):
    zs, _, _, piece, ends = edges.shape
    return pl.BlockSpec((zs, 1, 1, piece, ends), lambda j, at: (0, r, at[0] ^ p, 0, 0))


def attend(at, r, queries, k_cache, v_cache, edges):
    owners, (each, width) = len(queries), queries[0].shape
    rows, events, half = owners * each, k_cache.shape[0], owners // 2
    cache = pl.BlockSpec((events, DH), lambda j, at: (0, j))
    shape = jax.ShapeDtypeStruct((half, each, width), bf16)
    spec = pl.BlockSpec((half, each, DH), lambda j, at: (0, 0, j))
    return pl.pallas_call(
        functools.partial(attend_kernel, owners),
        grid_spec=pltpu.PrefetchScalarGridSpec(
            num_scalar_prefetch=1,
            grid=(width // DH,),
            in_specs=[pl.BlockSpec((each, DH), lambda j, at: (0, j))] * owners
            + [edge_spec(edges, r, p) for p in range(owners)]
            + [cache, cache],
            out_specs=(spec, spec),
            scratch_shapes=[pltpu.VMEM((rows, events), bf16)],
        ),
        out_shape=(shape, shape),
        compiler_params=params(),
        cost_estimate=LIGHT,
        name="attend",
    )(at, *queries, *[edges] * owners, k_cache, v_cache)


def finish_kernel(terms, at_ref, edge_ref, q_ref, rest_ref, *refs):
    sums, (att_ref, stat_ref) = refs[:terms], refs[terms:]
    rows, width = att_ref.shape
    edge = jnp.concatenate([edge_ref[z, 0, 0] for z in range(edge_ref.shape[0])]).astype(f32)
    root = lax.rsqrt(edge[:, 1:] - edge[:, :1])
    total = jnp.zeros((rows, 1), f32)
    for first in range(0, width, DH):
        at = slice(first, first + DH)
        summed = sum(s[0, 0, :, at].astype(f32) for s in sums)
        product = q_ref[:, at].astype(f32) * rest_ref[0, :, at].astype(f32)
        weight = silu(jnp.sum(product, axis=1, keepdims=True) * DH ** (-0.5))
        value = summed * root + weight * rest_ref[1, :, at].astype(f32)
        att_ref[:, at] = value
        total += jnp.sum(value, axis=1, keepdims=True)
    mean = total / width
    spread = jnp.zeros((rows, DH), f32)
    for first in range(0, width, DH):
        away = att_ref[:, first:first + DH] - mean
        spread += away * away
    square = jnp.sum(spread, axis=1, keepdims=True)
    lane = lax.broadcasted_iota(jnp.int32, (rows, DH), 1)
    stat_ref[...] = jnp.where(lane < DH // 2, mean, square)


def finish(at, r, edges, query, rest, sums):
    rows, width = query.shape
    return pl.pallas_call(
        functools.partial(finish_kernel, len(sums)),
        grid_spec=pltpu.PrefetchScalarGridSpec(
            num_scalar_prefetch=1,
            grid=(1,),
            in_specs=[
                edge_spec(edges, r, 0),
                pl.BlockSpec((rows, width), lambda j, at: (0, 0)),
                pl.BlockSpec((2, rows, width), lambda j, at: (0, 0, 0)),
            ] + [pl.BlockSpec((1, 1, rows, width), lambda j, at: (0, 0, 0, 0))] * len(sums),
            out_specs=(
                pl.BlockSpec((rows, width), lambda j, at: (0, 0)),
                pl.BlockSpec((rows, DH), lambda j, at: (0, 0)),
            ),
        ),
        out_shape=(
            jax.ShapeDtypeStruct((rows, width), f32),
            jax.ShapeDtypeStruct((rows, DH), f32),
        ),
        compiler_params=params(),
        cost_estimate=LIGHT,
        name="finish",
    )(at, edges, query, rest, *sums)


def gate_kernel(count, att_ref, rest_ref, *refs):
    stats, out_ref = refs[:count], refs[-1]
    width = att_ref.shape[1]
    means = [s[:, :1] for s in stats]
    squares = [s[:, DH // 2:DH // 2 + 1] for s in stats]
    mean = sum(means) / count
    square = sum(squares) + width * sum((m - mean) * (m - mean) for m in means)
    scale = lax.rsqrt(square / (width * count) + EPSILON)
    for first in range(0, width, 4 * DH):
        at = slice(first, min(first + 4 * DH, width))
        normed = (att_ref[:, at] - mean) * scale
        out_ref[:, at] = (normed * rest_ref[0, :, at].astype(f32)).astype(bf16)


def gate_rows(att, stats, rest):
    rows, width = att.shape
    return pl.pallas_call(
        functools.partial(gate_kernel, len(stats)),
        grid=(1,),
        in_specs=[
            pl.BlockSpec((rows, width), lambda j: (0, 0)),
            pl.BlockSpec((1, rows, width), lambda j: (2, 0, 0)),
        ] + [pl.BlockSpec((rows, DH), lambda j: (0, 0))] * len(stats),
        out_specs=pl.BlockSpec((rows, width), lambda j: (0, 0)),
        out_shape=jax.ShapeDtypeStruct((rows, width), bf16),
        compiler_params=params(),
        cost_estimate=LIGHT,
        name="gate",
    )(att, rest, *stats)


def output_kernel(owners, zs, index_ref, *refs):
    rows, w_ref, outs, lhs_ref = refs[:owners], refs[owners], refs[owners + 1:-1], refs[-1]
    piece = rows[0].shape[1]

    @pl.when(pl.program_id(0) == 0)
    def _():
        for k in range(zs):
            at = lax.rem(index_ref[0] + k, zs)
            for p in range(owners):
                first = (k * owners + p) * piece
                lhs_ref[first:first + piece, :] = rows[p][at]

    sums = jnp.dot(lhs_ref[...], w_ref[...], preferred_element_type=f32).astype(bf16)
    for k in range(zs):
        for p in range(owners):
            first = (k * owners + p) * piece
            outs[k][p] = sums[first:first + piece]


def output(index, blocks, w_out, zs):
    owners, (each, width) = len(blocks), blocks[0].shape
    piece, columns = each // zs, w_out.shape[1]
    span = 512 if columns % 512 == 0 else columns
    row_spec = pl.BlockSpec((zs, piece, width), lambda j, at: (0, 0, 0))
    return pl.pallas_call(
        functools.partial(output_kernel, owners, zs),
        grid_spec=pltpu.PrefetchScalarGridSpec(
            num_scalar_prefetch=1,
            grid=(columns // span,),
            in_specs=[row_spec] * owners + [pl.BlockSpec((width, span), lambda j, at: (0, j))],
            out_specs=[pl.BlockSpec((owners, piece, span), lambda j, at: (0, 0, j))] * zs,
            scratch_shapes=[pltpu.VMEM((owners * each, width), bf16)],
        ),
        out_shape=[jax.ShapeDtypeStruct((owners, piece, columns), bf16)] * zs,
        compiler_params=params(),
        cost_estimate=LIGHT,
        name="output",
    )(index.reshape(1).astype(jnp.int32), *[b.reshape(zs, piece, width) for b in blocks], w_out)


def close_kernel(counts, at_ref, t_ref, *refs):
    out_ref, first = refs[-1], 0
    for r, count in enumerate(counts):
        terms = refs[first:first + count]
        first += count

        @pl.when(pl.program_id(0) == r)
        def _():
            total = t_ref[...].astype(f32)
            for term in terms:
                total = total + term[...].astype(f32)
            out_ref[...] = total.astype(bf16)


def close(place, first, tokens, chunks):
    owners, piece, width = chunks[0][0].shape
    specs = []
    for r, terms in enumerate(chunks):
        def at_block(i, j, at, r=r):
            return (jnp.where(i == r, j ^ at[0], jnp.where(i < r, at[0], (owners - 1) ^ at[0])), 0, 0)
        specs += [pl.BlockSpec((1, piece, width), at_block)] * len(terms)

    def own(i, j, at):
        return (at[1] + i * owners + j, 0, 0)

    return pl.pallas_call(
        functools.partial(close_kernel, [len(terms) for terms in chunks]),
        grid_spec=pltpu.PrefetchScalarGridSpec(
            num_scalar_prefetch=1,
            grid=(len(chunks), owners),
            in_specs=[pl.BlockSpec((1, piece, width), own)] + specs,
            out_specs=pl.BlockSpec((1, piece, width), lambda i, j, at: (i * owners + j, 0, 0)),
        ),
        out_shape=jax.ShapeDtypeStruct((len(chunks) * owners, piece, width), bf16),
        compiler_params=params(),
        cost_estimate=LIGHT,
        name="close",
    )(
        jnp.stack([place, first]).astype(jnp.int32),
        tokens.reshape(-1, piece, width),
        *[term for terms in chunks for term in terms],
    )


def bits_of(axis):
    count = lax.axis_size(axis)
    assert count & (count - 1) == 0
    return count.bit_length() - 1


def place_of(axis):
    index, bits = lax.axis_index(axis), bits_of(axis)
    return sum((((index >> b) & 1) << (bits - 1 - b) for b in range(bits)), jnp.int32(0))


def swap(x, axis, bit):
    return lax.ppermute(
        x, axis, [(i, i ^ (1 << bit)) for i in range(lax.axis_size(axis))]
    )


def scatter_rest(terms, first, count, axis):
    terms, sent = list(terms), None
    for b in range(1, bits_of(axis)):
        half = terms[-1][0].shape[1] // 2
        total = sum(
            t[first - offset:first - offset + count, half:2 * half].astype(f32)
            for t, offset in terms
        )
        sent = total.astype(bf16)
        terms.append((swap(sent, axis, b), first))
    return terms, sent


def gather(x, axis):
    blocks = [x]
    for b in reversed(range(bits_of(axis))):
        blocks = blocks + [swap(block, axis, b) for block in blocks]
    return blocks


def shifts(blocks, axis):
    count = lax.axis_size(axis)
    return [blocks[0]] + [
        lax.ppermute(blocks[k], axis, [(i, (i + k) % count) for i in range(count)])
        for k in range(1, count)
    ]


def all_stats(stat, axis):
    count = lax.axis_size(axis)
    if count > 8:
        every = lax.all_gather(stat, axis)
        return [every[i] for i in range(count)]
    return shifts([stat] * count, axis)


def head_chunks(heads):
    if heads % 8:
        return [1] * heads
    unit = heads // 8
    return [unit, 2 * unit, 2 * unit, 2 * unit, unit]


def local(tokens, w_qkvu, k_cache, v_cache, w_out, vis_start, vis_end):
    cand, depth = tokens.shape
    owners, zs = lax.axis_size("hist"), lax.axis_size("head")
    index, place = lax.axis_index("head"), place_of("hist")
    width = w_qkvu.shape[2]
    events = k_cache.shape[0]
    chunks = 2 if cand % (2 * owners * zs * 16) == 0 else 1
    piece = cand // (zs * chunks * owners)

    def arrange(x):
        x = x.reshape((zs, chunks, owners, piece) + x.shape[1:])
        if piece % 16 == 0:
            return x
        blocks = [lax.dynamic_index_in_dim(x, p ^ place, 2, False) for p in range(owners)]
        x = jnp.moveaxis(jnp.stack(blocks), 2, 0)
        return x.reshape((1, chunks, owners, zs * piece) + x.shape[4:])

    at = (place if piece % 16 == 0 else jnp.int32(0)).reshape(1)
    ordered = arrange(tokens)
    first_event = lax.axis_index("hist") * events
    edges = arrange(jnp.stack([vis_start - first_event, vis_end - first_event], axis=1))

    sizes = head_chunks(width // DH)
    summed, sent = [[] for _ in range(chunks)], []
    for c, heads in enumerate(sizes):
        after = sent[c - 2] if c >= 2 else []
        keep, send = project(at, ordered, w_qkvu, sum(sizes[:c]), heads, after)
        if c >= 2:
            send = tie(send, summed[0][c - 2][-1][0])
        terms = [(keep, 0), (swap(send, "hist", 0), 0)]
        groups = [(0, chunks)] if c + 1 < len(sizes) else [(r, 1) for r in range(chunks)]
        sent.append([])
        for first, count in groups:
            sums, last = scatter_rest(terms, first, count, "hist")
            for r in range(first, first + count):
                summed[r].append(sums)
            if last is not None:
                sent[-1].append(last)

    results = []
    for r in range(chunks):
        query, rest = activate(r, summed[r])
        keep, send = attend(at, r, gather(query, "hist"), k_cache, v_cache, edges)
        terms = [(keep[None], 0), (swap(send, "hist", 0)[None], 0)]
        sums, _ = scatter_rest(terms, 0, 1, "hist")
        att, stat = finish(at, r, edges, query, rest, [t for t, _ in sums])
        gated = gate_rows(att, all_stats(stat, "head"), rest)
        blocks = gather(gated, "hist")
        if piece % 16 == 0:
            results.append(shifts(output(index, blocks, w_out, zs), "head"))
        else:
            whole = jnp.dot(jnp.concatenate(blocks), w_out, preferred_element_type=f32)
            whole = whole.astype(bf16).reshape(owners, zs, piece, -1).swapaxes(0, 1)
            results.append(
                [lax.psum_scatter(whole, "head", scatter_dimension=0, tiled=True)[0]]
            )
    out = close(place, index * (chunks * owners), tokens, results)
    return out.reshape(cand // zs, -1)


def solution(mesh):
    in_specs = (
        P("groups", "hist"),
        P("hist", None, "head"),
        P(("groups", "hist"), "head"),
        P(("groups", "hist"), "head"),
        P("head", "hist"),
        P("groups"),
        P("groups"),
    )
    out_specs = P(("groups", "head"), "hist")
    return jax.shard_map(local, mesh=mesh, in_specs=in_specs, out_specs=out_specs, check_vma=False)
```

```python
import functools

import jax
import jax.numpy as jnp
from jax import lax
from jax.experimental import pallas as pl
from jax.experimental.pallas import tpu as pltpu
from jax.sharding import PartitionSpec as P

DH = 128
EPSILON = 1e-05
VMEM_LIMIT = 60 * 1024 * 1024

bf16 = jnp.bfloat16
f32 = jnp.float32


def silu(v):
    u = 0.5 * v
    return u + u * jnp.tanh(u)


def params():
    return pltpu.CompilerParams(vmem_limit_bytes=VMEM_LIMIT)


LIGHT = pl.CostEstimate(flops=1000, bytes_accessed=1000, transcendentals=0)


def shuffle(depth):
    row = lax.broadcasted_iota(jnp.int32, (depth, depth), 0)
    column = lax.broadcasted_iota(jnp.int32, (depth, depth), 1)
    slot = column % 8
    return jnp.where(row == column - slot + 2 * (slot % 4) + slot // 4, 1.0, 0.0).astype(bf16)


def split_rows(x):
    x = x.reshape(x.shape[0] // 32, 4, 8, DH)
    slot = lax.broadcasted_iota(jnp.int32, (x.shape[0], 8, DH), 1) % 4
    turned = [x[:, 0]] + [pltpu.roll(x[:, j], j, 1) for j in range(1, 4)]
    outs = []
    for i in range(4):
        out = turned[0]
        for j in range(1, 4):
            out = jnp.where(slot == (i + j) % 4, turned[j], out)
        outs.append(out if i == 0 else pltpu.roll(out, 8 - i, 1))
    return [out.reshape(-1, DH).astype(bf16) for out in outs]


def arrange_kernel(owners, at_ref, *refs):
    rows, out_ref = refs[:owners], refs[owners]
    zs, chunks, _, piece, depth = rows[0].shape
    lhs = jnp.concatenate(
        [rows[p][z, r, 0] for r in range(chunks) for p in range(owners) for z in range(zs)]
    )
    out_ref[...] = jnp.dot(lhs, shuffle(depth), preferred_element_type=f32).astype(bf16)


def arrange_rows(at, tokens):
    zs, chunks, owners, piece, depth = tokens.shape
    rows, span = zs * chunks * owners * piece, 256
    return pl.pallas_call(
        functools.partial(arrange_kernel, owners),
        grid_spec=pltpu.PrefetchScalarGridSpec(
            num_scalar_prefetch=1,
            grid=(depth // span,),
            in_specs=[
                pl.BlockSpec(
                    (zs, chunks, 1, piece, span), lambda j, at, p=p: (0, 0, at[0] ^ p, 0, j)
                )
                for p in range(owners)
            ],
            out_specs=pl.BlockSpec((rows, span), lambda j, at: (0, j)),
        ),
        out_shape=jax.ShapeDtypeStruct((rows, depth), bf16),
        compiler_params=params(),
        cost_estimate=LIGHT,
        name="arrange",
    )(at, *[tokens] * owners)


def project_kernel(parts, t_ref, w_ref, *refs):
    keep_ref, send_ref = refs[-2:]
    chunks, half, _, each, _ = keep_ref.shape
    depth = w_ref.shape[0] // parts
    flat = w_ref.reshape(depth * parts * 4, DH)
    res = None
    for k in range(parts):
        rhs = jnp.concatenate(
            split_rows(flat[k * depth * 4:(k + 1) * depth * 4, :].astype(f32)), axis=1
        )
        term = jnp.dot(t_ref[:, k * depth:(k + 1) * depth], rhs, preferred_element_type=f32)
        res = term if res is None else res + term
    res = res.astype(bf16)
    for r in range(chunks):
        for p in range(2 * half):
            into = keep_ref if p < half else send_ref
            first = (r * 2 * half + p) * each
            for i in range(4):
                into[r, p % half, i] = res[first:first + each, i * DH:(i + 1) * DH]


def project(tokens, w, head_first, heads, chunks, owners, after):
    rows, depth = tokens.shape
    half, each = owners // 2, rows // (chunks * owners)
    parts = 4 if depth % 512 == 0 else 1
    shape = jax.ShapeDtypeStruct((chunks, half, 4, each, heads * DH), bf16)
    spec = pl.BlockSpec((chunks, half, 4, each, DH), lambda j: (0, 0, 0, 0, j))
    return pl.pallas_call(
        functools.partial(project_kernel, parts),
        grid=(heads,),
        in_specs=[
            pl.BlockSpec((rows, depth), lambda j: (0, 0)),
            pl.BlockSpec((depth, 4, DH), lambda j: (0, 0, head_first + j)),
        ] + [pl.BlockSpec(memory_space=pl.ANY)] * len(after),
        out_specs=(spec, spec),
        out_shape=(shape, shape),
        compiler_params=params(),
        cost_estimate=LIGHT,
        name="project",
    )(tokens, w, *after)


def tie_kernel(*refs):
    pass


def tie(x, *after):
    anywhere = pl.BlockSpec(memory_space=pl.ANY)
    return pl.pallas_call(
        tie_kernel,
        in_specs=[anywhere] * (1 + len(after)),
        out_specs=anywhere,
        out_shape=jax.ShapeDtypeStruct(x.shape, x.dtype),
        input_output_aliases={0: 0},
        compiler_params=params(),
        cost_estimate=LIGHT,
        name="tie",
    )(x, *after)


def fold_kernel(*refs):
    refs[-1][...] = sum(r[...].astype(f32) for r in refs[:-1]).astype(bf16)


def fold(terms, first, count):
    half = terms[-1][0].shape[1] // 2
    tail = terms[0][0].shape[2:]
    steps = 2 if tail[-1] % 256 == 0 else 1
    block = (count, half) + tail[:-1] + (tail[-1] // steps,)
    middle = (0,) * (len(tail) - 1)
    return pl.pallas_call(
        fold_kernel,
        grid=(steps,),
        in_specs=[
            pl.BlockSpec(block, lambda j, at=(first - offset) // count: (at, 1) + middle + (j,))
            for _, offset in terms
        ],
        out_specs=pl.BlockSpec(block, lambda j: (0, 0) + middle + (j,)),
        out_shape=jax.ShapeDtypeStruct((count, half) + tail, bf16),
        compiler_params=params(),
        cost_estimate=LIGHT,
        name="fold",
    )(*[t for t, _ in terms])


def activate_kernel(counts, *refs):
    q_ref, rest_ref = refs[-2:]
    column, at = 0, 0
    for count in counts:
        terms = refs[at:at + count]
        span = terms[0].shape[-1]
        for i in range(4):
            part = silu(sum(t[0, 0, i].astype(f32) for t in terms)).astype(bf16)
            if i == 0:
                q_ref[:, column:column + span] = part
            else:
                rest_ref[i - 1, :, column:column + span] = part
        column += span
        at += count


def activate(r, chunks):
    flat, specs, width = [], [], 0
    for terms in chunks:
        _, _, _, each, span = terms[0][0].shape
        width += span
        for array, offset in terms:
            flat.append(array)
            specs.append(
                pl.BlockSpec((1, 1, 4, each, span), lambda j, at=r - offset: (at, 0, 0, 0, 0))
            )
    return pl.pallas_call(
        functools.partial(activate_kernel, [len(terms) for terms in chunks]),
        grid=(1,),
        in_specs=specs,
        out_specs=(
            pl.BlockSpec((each, width), lambda j: (0, 0)),
            pl.BlockSpec((3, each, width), lambda j: (0, 0, 0)),
        ),
        out_shape=(
            jax.ShapeDtypeStruct((each, width), bf16),
            jax.ShapeDtypeStruct((3, each, width), bf16),
        ),
        compiler_params=params(),
        cost_estimate=LIGHT,
        name="activate",
    )(*flat)


def attend_kernel(owners, at_ref, *refs):
    queries, edges = refs[:owners], refs[owners:2 * owners]
    k_ref, v_ref, keep_ref, send_ref, mask_ref = refs[2 * owners:]
    events = mask_ref.shape[1]
    half, each, _ = keep_ref.shape

    @pl.when(pl.program_id(0) == 0)
    def _():
        zs, _, _, piece, _ = edges[0].shape
        at = lax.broadcasted_iota(jnp.int32, (piece, events), 1)
        for p in range(owners):
            for z in range(zs):
                edge = edges[p][z, 0, 0]
                seen = (at >= edge[:, :1]) & (at < edge[:, 1:])
                first = p * each + z * piece
                mask_ref[first:first + piece, :] = jnp.where(seen, 1.0, 0.0).astype(bf16)

    for h in range(k_ref.shape[1] // DH):
        at = slice(h * DH, (h + 1) * DH)
        query = jnp.concatenate([q[:, at] for q in queries])
        u = lax.dot_general(
            query, k_ref[:, at], (((1,), (1,)), ((), ())), preferred_element_type=f32
        ) * (0.5 * DH ** (-0.5))
        weights = (u + u * jnp.tanh(u)).astype(bf16) * mask_ref[...]
        term = jnp.dot(weights, v_ref[:, at], preferred_element_type=f32).astype(bf16)
        for p in range(owners):
            into = keep_ref if p < half else send_ref
            into[p % half, :, at] = term[p * each:(p + 1) * each]


def edge_spec(edges, r, p):
    zs, _, _, piece, ends = edges.shape
    return pl.BlockSpec((zs, 1, 1, piece, ends), lambda j, at: (0, r, at[0] ^ p, 0, 0))


def attend(at, r, queries, k_cache, v_cache, edges):
    owners, (each, width) = len(queries), queries[0].shape
    rows, events, half = owners * each, k_cache.shape[0], owners // 2
    span = 4 * DH if width % (4 * DH) == 0 else DH
    cache = pl.BlockSpec((events, span), lambda j, at: (0, j))
    shape = jax.ShapeDtypeStruct((half, each, width), bf16)
    spec = pl.BlockSpec((half, each, span), lambda j, at: (0, 0, j))
    return pl.pallas_call(
        functools.partial(attend_kernel, owners),
        grid_spec=pltpu.PrefetchScalarGridSpec(
            num_scalar_prefetch=1,
            grid=(width // span,),
            in_specs=[pl.BlockSpec((each, span), lambda j, at: (0, j))] * owners
            + [edge_spec(edges, r, p) for p in range(owners)]
            + [cache, cache],
            out_specs=(spec, spec),
            scratch_shapes=[pltpu.VMEM((rows, events), bf16)],
        ),
        out_shape=(shape, shape),
        compiler_params=params(),
        cost_estimate=LIGHT,
        name="attend",
    )(at, *queries, *[edges] * owners, k_cache, v_cache)


def finish_kernel(terms, at_ref, edge_ref, q_ref, rest_ref, *refs):
    sums, (att_ref, stat_ref) = refs[:terms], refs[terms:]
    rows, width = att_ref.shape
    edge = jnp.concatenate([edge_ref[z, 0, 0] for z in range(edge_ref.shape[0])]).astype(f32)
    root = lax.rsqrt(edge[:, 1:] - edge[:, :1])
    total = jnp.zeros((rows, 1), f32)
    for first in range(0, width, DH):
        at = slice(first, first + DH)
        summed = sum(s[0, 0, :, at].astype(f32) for s in sums)
        product = q_ref[:, at].astype(f32) * rest_ref[0, :, at].astype(f32)
        weight = silu(jnp.sum(product, axis=1, keepdims=True) * DH ** (-0.5))
        value = summed * root + weight * rest_ref[1, :, at].astype(f32)
        att_ref[:, at] = value
        total += jnp.sum(value, axis=1, keepdims=True)
    mean = total / width
    spread = jnp.zeros((rows, DH), f32)
    for first in range(0, width, DH):
        away = att_ref[:, first:first + DH] - mean
        spread += away * away
    square = jnp.sum(spread, axis=1, keepdims=True)
    lane = lax.broadcasted_iota(jnp.int32, (rows, DH), 1)
    stat_ref[...] = jnp.where(lane < DH // 2, mean, square)


def finish(at, r, edges, query, rest, sums):
    rows, width = query.shape
    return pl.pallas_call(
        functools.partial(finish_kernel, len(sums)),
        grid_spec=pltpu.PrefetchScalarGridSpec(
            num_scalar_prefetch=1,
            grid=(1,),
            in_specs=[
                edge_spec(edges, r, 0),
                pl.BlockSpec((rows, width), lambda j, at: (0, 0)),
                pl.BlockSpec((2, rows, width), lambda j, at: (0, 0, 0)),
            ] + [pl.BlockSpec((1, 1, rows, width), lambda j, at: (0, 0, 0, 0))] * len(sums),
            out_specs=(
                pl.BlockSpec((rows, width), lambda j, at: (0, 0)),
                pl.BlockSpec((rows, DH), lambda j, at: (0, 0)),
            ),
        ),
        out_shape=(
            jax.ShapeDtypeStruct((rows, width), f32),
            jax.ShapeDtypeStruct((rows, DH), f32),
        ),
        compiler_params=params(),
        cost_estimate=LIGHT,
        name="finish",
    )(at, edges, query, rest, *sums)


def gate_kernel(count, att_ref, rest_ref, *refs):
    stats, out_ref = refs[:count], refs[-1]
    width = att_ref.shape[1]
    means = [s[:, :1] for s in stats]
    squares = [s[:, DH // 2:DH // 2 + 1] for s in stats]
    mean = sum(means) / count
    square = sum(squares) + width * sum((m - mean) * (m - mean) for m in means)
    scale = lax.rsqrt(square / (width * count) + EPSILON)
    for first in range(0, width, 4 * DH):
        at = slice(first, min(first + 4 * DH, width))
        normed = (att_ref[:, at] - mean) * scale
        out_ref[:, at] = (normed * rest_ref[0, :, at].astype(f32)).astype(bf16)


def gate_rows(att, stats, rest):
    rows, width = att.shape
    return pl.pallas_call(
        functools.partial(gate_kernel, len(stats)),
        grid=(1,),
        in_specs=[
            pl.BlockSpec((rows, width), lambda j: (0, 0)),
            pl.BlockSpec((1, rows, width), lambda j: (2, 0, 0)),
        ] + [pl.BlockSpec((rows, DH), lambda j: (0, 0))] * len(stats),
        out_specs=pl.BlockSpec((rows, width), lambda j: (0, 0)),
        out_shape=jax.ShapeDtypeStruct((rows, width), bf16),
        compiler_params=params(),
        cost_estimate=LIGHT,
        name="gate",
    )(att, rest, *stats)


def output_kernel(owners, zs, index_ref, *refs):
    rows, w_ref, outs, lhs_ref = refs[:owners], refs[owners], refs[owners + 1:-1], refs[-1]
    piece = rows[0].shape[1]

    @pl.when(pl.program_id(0) == 0)
    def _():
        for k in range(zs):
            at = lax.rem(index_ref[0] + k, zs)
            for p in range(owners):
                first = (k * owners + p) * piece
                lhs_ref[first:first + piece, :] = rows[p][at]

    sums = jnp.dot(lhs_ref[...], w_ref[...], preferred_element_type=f32).astype(bf16)
    for k in range(zs):
        for p in range(owners):
            first = (k * owners + p) * piece
            outs[k][p] = sums[first:first + piece]


def output(index, blocks, w_out, zs):
    owners, (each, width) = len(blocks), blocks[0].shape
    piece, columns = each // zs, w_out.shape[1]
    span = 512 if columns % 512 == 0 else columns
    row_spec = pl.BlockSpec((zs, piece, width), lambda j, at: (0, 0, 0))
    return pl.pallas_call(
        functools.partial(output_kernel, owners, zs),
        grid_spec=pltpu.PrefetchScalarGridSpec(
            num_scalar_prefetch=1,
            grid=(columns // span,),
            in_specs=[row_spec] * owners + [pl.BlockSpec((width, span), lambda j, at: (0, j))],
            out_specs=[pl.BlockSpec((owners, piece, span), lambda j, at: (0, 0, j))] * zs,
            scratch_shapes=[pltpu.VMEM((owners * each, width), bf16)],
        ),
        out_shape=[jax.ShapeDtypeStruct((owners, piece, columns), bf16)] * zs,
        compiler_params=params(),
        cost_estimate=LIGHT,
        name="output",
    )(index.reshape(1).astype(jnp.int32), *[b.reshape(zs, piece, width) for b in blocks], w_out)


def close_kernel(counts, at_ref, t_ref, *refs):
    out_ref, first = refs[-1], 0
    owners = refs[0].shape[0]
    for r, count in enumerate(counts):
        terms = refs[first:first + count]
        first += count
        for p in range(owners):
            total = t_ref[r * owners + p].astype(f32)
            for term in terms:
                total = total + term[p ^ at_ref[0]].astype(f32)
            out_ref[r * owners + p] = total.astype(bf16)


def close(place, index, tokens, chunks):
    owners, piece, width = chunks[0][0].shape
    blocks, span = len(chunks) * owners, width // 2
    term = pl.BlockSpec((owners, piece, span), lambda j, at: (0, 0, j))
    return pl.pallas_call(
        functools.partial(close_kernel, [len(terms) for terms in chunks]),
        grid_spec=pltpu.PrefetchScalarGridSpec(
            num_scalar_prefetch=1,
            grid=(2,),
            in_specs=[pl.BlockSpec((blocks, piece, span), lambda j, at: (at[1], 0, j))]
            + [term] * sum(len(terms) for terms in chunks),
            out_specs=pl.BlockSpec((blocks, piece, span), lambda j, at: (0, 0, j)),
        ),
        out_shape=jax.ShapeDtypeStruct((blocks, piece, width), bf16),
        compiler_params=params(),
        cost_estimate=LIGHT,
        name="close",
    )(
        jnp.stack([place, index]).astype(jnp.int32),
        tokens.reshape(-1, piece, width),
        *[term for terms in chunks for term in terms],
    )


def bits_of(axis):
    count = lax.axis_size(axis)
    assert count & (count - 1) == 0
    return count.bit_length() - 1


def place_of(axis):
    index, bits = lax.axis_index(axis), bits_of(axis)
    return sum((((index >> b) & 1) << (bits - 1 - b) for b in range(bits)), jnp.int32(0))


def swap(x, axis, bit):
    return lax.ppermute(
        x, axis, [(i, i ^ (1 << bit)) for i in range(lax.axis_size(axis))]
    )


def scatter_rest(terms, first, count, axis):
    terms, sent = list(terms), None
    for b in range(1, bits_of(axis)):
        sent = fold(terms, first, count)
        terms.append((swap(sent, axis, b), first))
    return terms, sent


def gather(x, axis):
    blocks = [x]
    for b in reversed(range(bits_of(axis))):
        blocks = blocks + [swap(block, axis, b) for block in blocks]
    return blocks


def shifts(blocks, axis):
    count = lax.axis_size(axis)
    return [blocks[0]] + [
        lax.ppermute(blocks[k], axis, [(i, (i + k) % count) for i in range(count)])
        for k in range(1, count)
    ]


def all_stats(stat, axis):
    count = lax.axis_size(axis)
    if count > 8:
        every = lax.all_gather(stat, axis)
        return [every[i] for i in range(count)]
    return shifts([stat] * count, axis)


def head_chunks(heads):
    if heads % 8:
        return [1] * heads
    unit = heads // 8
    return [unit, 2 * unit, 2 * unit, 2 * unit, unit]


def local(tokens, w_qkvu, k_cache, v_cache, w_out, vis_start, vis_end):
    cand, depth = tokens.shape
    owners, zs = lax.axis_size("hist"), lax.axis_size("head")
    index, place = lax.axis_index("head"), place_of("hist")
    width = w_qkvu.shape[2]
    events = k_cache.shape[0]
    chunks = 2 if cand % (2 * owners * zs * 16) == 0 else 1
    piece = cand // (zs * chunks * owners)

    def arrange(x):
        x = x.reshape((zs, chunks, owners, piece) + x.shape[1:])
        if piece % 16 == 0:
            return x
        blocks = [lax.dynamic_index_in_dim(x, p ^ place, 2, False) for p in range(owners)]
        x = jnp.moveaxis(jnp.stack(blocks), 2, 0)
        return x.reshape((1, chunks, owners, zs * piece) + x.shape[4:])

    at = (place if piece % 16 == 0 else jnp.int32(0)).reshape(1)
    ordered = arrange_rows(at, arrange(tokens))
    first_event = lax.axis_index("hist") * events
    edges = arrange(jnp.stack([vis_start - first_event, vis_end - first_event], axis=1))

    sizes = head_chunks(width // DH)
    summed, sent = [[] for _ in range(chunks)], []
    for c, heads in enumerate(sizes):
        after = sent[c - 2] if c >= 2 else [keep] if c else []
        keep, send = project(ordered, w_qkvu, sum(sizes[:c]), heads, chunks, owners, after)
        if c >= 2:
            send = tie(send, summed[0][c - 2][-1][0], *sent[c - 1])
        terms = [(keep, 0), (swap(send, "hist", 0), 0)]
        groups = [(0, chunks)] if c + 1 < len(sizes) else [(r, 1) for r in range(chunks)]
        sent.append([])
        for first, count in groups:
            sums, last = scatter_rest(terms, first, count, "hist")
            for r in range(first, first + count):
                summed[r].append(sums)
            if last is not None:
                sent[-1].append(last)

    results = []
    for r in range(chunks):
        query, rest = activate(r, summed[r])
        keep, send = attend(at, r, gather(query, "hist"), k_cache, v_cache, edges)
        terms = [(keep[None], 0), (swap(send, "hist", 0)[None], 0)]
        sums, _ = scatter_rest(terms, 0, 1, "hist")
        att, stat = finish(at, r, edges, query, rest, [t for t, _ in sums])
        gated = gate_rows(att, all_stats(stat, "head"), rest)
        blocks = gather(gated, "hist")
        if piece % 16 == 0:
            results.append(shifts(output(index, blocks, w_out, zs), "head"))
        else:
            whole = jnp.dot(jnp.concatenate(blocks), w_out, preferred_element_type=f32)
            whole = whole.astype(bf16).reshape(owners, zs, piece, -1).swapaxes(0, 1)
            results.append(
                [lax.psum_scatter(whole, "head", scatter_dimension=0, tiled=True)[0]]
            )
    out = close(place, index, tokens, results)
    return out.reshape(cand // zs, -1)


def solution(mesh):
    in_specs = (
        P("groups", "hist"),
        P("hist", None, "head"),
        P(("groups", "hist"), "head"),
        P(("groups", "hist"), "head"),
        P("head", "hist"),
        P("groups"),
        P("groups"),
    )
    out_specs = P(("groups", "head"), "hist")
    return jax.shard_map(local, mesh=mesh, in_specs=in_specs, out_specs=out_specs, check_vma=False)
```

```python
import functools

import jax
import jax.numpy as jnp
from jax import lax
from jax.experimental import pallas as pl
from jax.experimental.pallas import tpu as pltpu
from jax.sharding import PartitionSpec as P

DH = 128
EPSILON = 1e-05
VMEM_LIMIT = 28 * 1024 * 1024

bf16 = jnp.bfloat16
f32 = jnp.float32


def silu(v):
    u = 0.5 * v
    return u + u * jnp.tanh(u)


def params():
    return pltpu.CompilerParams(vmem_limit_bytes=VMEM_LIMIT)


LIGHT = pl.CostEstimate(flops=1000, bytes_accessed=1000, transcendentals=0)


def anywhere(arrays):
    return [pl.BlockSpec(memory_space=pl.ANY)] * len(arrays)


def project_kernel(parts, owners, after, at_ref, *refs):
    rows, weights = refs[:owners], refs[owners:owners + parts]
    keep_ref, send_ref, lhs_ref = refs[owners + parts + after:][:3]
    wides = refs[-parts:]
    zs, chunks, _, piece, _ = rows[0].shape
    depth = weights[0].shape[0]

    @pl.when(pl.program_id(0) == 0)
    def _():
        first = 0
        for p in range(owners):
            for r in range(chunks):
                for z in range(zs):
                    lhs_ref[first:first + piece, :] = rows[p][z, r, 0]
                    first += piece

    res = None
    for k, wide in enumerate(wides):
        wide[...] = weights[k].reshape(depth * 4, DH)[...].astype(f32)
        rhs = jnp.concatenate(
            [wide[pl.ds(i, depth, stride=4), :].astype(bf16) for i in range(4)], axis=1
        )
        term = jnp.dot(lhs_ref[:, k * depth:(k + 1) * depth], rhs, preferred_element_type=f32)
        res = term if res is None else res + term
    res = res.astype(bf16)
    half, _, each, _ = keep_ref.shape
    for p in range(owners):
        into = keep_ref if p < half else send_ref
        for i in range(4):
            into[p % half, i] = res[p * each:(p + 1) * each, i * DH:(i + 1) * DH]


def project(at, tokens, w, head_first, heads, after):
    zs, chunks, owners, piece, depth = tokens.shape
    half, each = owners // 2, zs * chunks * piece
    parts = 4 if depth % 512 == 0 else 1
    shape = jax.ShapeDtypeStruct((half, 4, each, heads * DH), bf16)
    spec = pl.BlockSpec((half, 4, each, DH), lambda j, at: (0, 0, 0, j))
    return pl.pallas_call(
        functools.partial(project_kernel, parts, owners, len(after)),
        grid_spec=pltpu.PrefetchScalarGridSpec(
            num_scalar_prefetch=1,
            grid=(heads,),
            in_specs=[
                pl.BlockSpec(
                    (zs, chunks, 1, piece, depth), lambda j, at, p=p: (0, 0, at[0] ^ p, 0, 0)
                )
                for p in range(owners)
            ]
            + [
                pl.BlockSpec((depth // parts, 4, DH), lambda j, at, k=k: (k, 0, head_first + j))
                for k in range(parts)
            ]
            + anywhere(after),
            out_specs=(spec, spec),
            scratch_shapes=[pltpu.VMEM((owners * each, depth), bf16)]
            + [pltpu.VMEM((depth // parts * 4, DH), f32) for _ in range(parts)],
        ),
        out_shape=(shape, shape),
        compiler_params=params(),
        cost_estimate=LIGHT,
        name="project",
    )(at, *[tokens] * owners, *[w] * parts, *after)


def tie_kernel(*refs):
    pass


def tie(x, after):
    if not after:
        return x
    return pl.pallas_call(
        tie_kernel,
        in_specs=anywhere([x, *after]),
        out_specs=pl.BlockSpec(memory_space=pl.ANY),
        out_shape=jax.ShapeDtypeStruct(x.shape, x.dtype),
        input_output_aliases={0: 0},
        compiler_params=params(),
        cost_estimate=LIGHT,
        name="tie",
    )(x, *after)


def fold_kernel(*refs):
    refs[-1][...] = sum(r[...].astype(f32) for r in refs[:-1]).astype(bf16)


def fold(terms):
    half, tail = terms[-1].shape[0] // 2, terms[0].shape[1:]
    steps = 2 if tail[-1] % 256 == 0 else 1
    block = (half,) + tail[:-1] + (tail[-1] // steps,)
    middle = (0,) * (len(tail) - 1)
    return pl.pallas_call(
        fold_kernel,
        grid=(steps,),
        in_specs=[pl.BlockSpec(block, lambda j: (1,) + middle + (j,))] * len(terms),
        out_specs=pl.BlockSpec(block, lambda j: (0,) + middle + (j,)),
        out_shape=jax.ShapeDtypeStruct((half,) + tail, bf16),
        compiler_params=params(),
        cost_estimate=LIGHT,
        name="fold",
    )(*terms)


def activate_kernel(count, *refs):
    q_ref, rest_ref = refs[-2:]
    for i in range(4):
        part = silu(sum(t[0, i].astype(f32) for t in refs[:count])).astype(bf16)
        if i == 0:
            q_ref[...] = part
        else:
            rest_ref[i - 1] = part


def activate(terms, after):
    _, _, each, width = terms[0].shape
    return pl.pallas_call(
        functools.partial(activate_kernel, len(terms)),
        grid=(1,),
        in_specs=[pl.BlockSpec((1, 4, each, width), lambda j: (0, 0, 0, 0))] * len(terms)
        + anywhere(after),
        out_specs=(
            pl.BlockSpec((each, width), lambda j: (0, 0)),
            pl.BlockSpec((3, each, width), lambda j: (0, 0, 0)),
        ),
        out_shape=(
            jax.ShapeDtypeStruct((each, width), bf16),
            jax.ShapeDtypeStruct((3, each, width), bf16),
        ),
        compiler_params=params(),
        cost_estimate=LIGHT,
        name="activate",
    )(*terms, *after)


def attend_kernel(owners, at_ref, *refs):
    queries, edges = refs[:owners], refs[owners:2 * owners]
    k_ref, v_ref, keep_ref, send_ref, mask_ref = refs[2 * owners:]
    events = mask_ref.shape[1]
    half, each, _ = keep_ref.shape

    @pl.when(pl.program_id(0) == 0)
    def _():
        zs, chunks, _, piece, _ = edges[0].shape
        at = lax.broadcasted_iota(jnp.int32, (piece, events), 1)
        first = 0
        for p in range(owners):
            for r in range(chunks):
                for z in range(zs):
                    edge = edges[p][z, r, 0]
                    seen = (at >= edge[:, :1]) & (at < edge[:, 1:])
                    mask_ref[first:first + piece, :] = jnp.where(seen, 1.0, 0.0).astype(bf16)
                    first += piece

    for h in range(k_ref.shape[1] // DH):
        at = slice(h * DH, (h + 1) * DH)
        query = jnp.concatenate([q[:, at] for q in queries])
        u = lax.dot_general(
            query, k_ref[:, at], (((1,), (1,)), ((), ())), preferred_element_type=f32
        ) * (0.5 * DH ** (-0.5))
        weights = (u + u * jnp.tanh(u)).astype(bf16) * mask_ref[...]
        term = jnp.dot(weights, v_ref[:, at], preferred_element_type=f32).astype(bf16)
        for p in range(owners):
            into = keep_ref if p < half else send_ref
            into[p % half, :, at] = term[p * each:(p + 1) * each]


def edge_spec(edges, p):
    zs, chunks, _, piece, ends = edges.shape
    return pl.BlockSpec((zs, chunks, 1, piece, ends), lambda j, at: (0, 0, at[0] ^ p, 0, 0))


def attend(at, queries, k_cache, v_cache, edges, head_first):
    owners, (each, width) = len(queries), queries[0].shape
    rows, events, half = owners * each, k_cache.shape[0], owners // 2
    first = head_first * DH
    span = 2 * DH if width % (2 * DH) == 0 and first % (2 * DH) == 0 else DH
    cache = pl.BlockSpec((events, span), lambda j, at: (0, first // span + j))
    shape = jax.ShapeDtypeStruct((half, each, width), bf16)
    spec = pl.BlockSpec((half, each, span), lambda j, at: (0, 0, j))
    return pl.pallas_call(
        functools.partial(attend_kernel, owners),
        grid_spec=pltpu.PrefetchScalarGridSpec(
            num_scalar_prefetch=1,
            grid=(width // span,),
            in_specs=[pl.BlockSpec((each, span), lambda j, at: (0, j))] * owners
            + [edge_spec(edges, p) for p in range(owners)]
            + [cache, cache],
            out_specs=(spec, spec),
            scratch_shapes=[pltpu.VMEM((rows, events), bf16)],
        ),
        out_shape=(shape, shape),
        compiler_params=params(),
        cost_estimate=LIGHT,
        name="attend",
    )(at, *queries, *[edges] * owners, k_cache, v_cache)


def merge(means, squares, widths):
    width = sum(widths)
    mean = sum(m * (w / width) for m, w in zip(means, widths))
    square = sum(squares) + sum(w * (m - mean) * (m - mean) for m, w in zip(means, widths))
    return mean, square


def stat_columns(stats):
    return [s[:, :1] for s in stats], [s[:, DH // 2:DH // 2 + 1] for s in stats]


def finish_kernel(terms, widths, at_ref, edge_ref, q_ref, rest_ref, *refs):
    sums, others, (att_ref, stat_ref) = refs[:terms], refs[terms:-2], refs[-2:]
    rows, width = att_ref.shape
    zs, chunks = edge_ref.shape[:2]
    edge = jnp.concatenate(
        [edge_ref[z, r, 0] for r in range(chunks) for z in range(zs)]
    ).astype(f32)
    root = lax.rsqrt(edge[:, 1:] - edge[:, :1])
    total = jnp.zeros((rows, 1), f32)
    for first in range(0, width, DH):
        at = slice(first, first + DH)
        summed = sum(s[0, :, at].astype(f32) for s in sums)
        product = q_ref[:, at].astype(f32) * rest_ref[0, :, at].astype(f32)
        weight = silu(jnp.sum(product, axis=1, keepdims=True) * DH ** (-0.5))
        value = summed * root + weight * rest_ref[1, :, at].astype(f32)
        att_ref[:, at] = value
        total += jnp.sum(value, axis=1, keepdims=True)
    mean = total / width
    spread = jnp.zeros((rows, DH), f32)
    for first in range(0, width, DH):
        away = att_ref[:, first:first + DH] - mean
        spread += away * away
    square = jnp.sum(spread, axis=1, keepdims=True)
    if others:
        means, squares = stat_columns(others)
        mean, square = merge([mean] + means, [square] + squares, [width] + widths)
    lane = lax.broadcasted_iota(jnp.int32, (rows, DH), 1)
    stat_ref[...] = jnp.where(lane < DH // 2, mean, square)


def finish(at, edges, query, rest, sums, others, widths):
    rows, width = query.shape
    return pl.pallas_call(
        functools.partial(finish_kernel, len(sums), widths),
        grid_spec=pltpu.PrefetchScalarGridSpec(
            num_scalar_prefetch=1,
            grid=(1,),
            in_specs=[
                edge_spec(edges, 0),
                pl.BlockSpec((rows, width), lambda j, at: (0, 0)),
                pl.BlockSpec((2, rows, width), lambda j, at: (0, 0, 0)),
            ]
            + [pl.BlockSpec((1, rows, width), lambda j, at: (0, 0, 0))] * len(sums)
            + [pl.BlockSpec((rows, DH), lambda j, at: (0, 0))] * len(others),
            out_specs=(
                pl.BlockSpec((rows, width), lambda j, at: (0, 0)),
                pl.BlockSpec((rows, DH), lambda j, at: (0, 0)),
            ),
        ),
        out_shape=(
            jax.ShapeDtypeStruct((rows, width), f32),
            jax.ShapeDtypeStruct((rows, DH), f32),
        ),
        compiler_params=params(),
        cost_estimate=LIGHT,
        name="finish",
    )(at, edges, query, rest, *sums, *others)


def gate_kernel(count, parts, *refs):
    stats, atts, rests, outs = (
        refs[:count], refs[count:count + parts],
        refs[count + parts:count + 2 * parts], refs[count + 2 * parts:],
    )
    width = sum(a.shape[1] for a in atts)
    means, squares = stat_columns(stats)
    mean, square = merge(means, squares, [width] * count)
    scale = lax.rsqrt(square / (width * count) + EPSILON)
    rows, column = outs[0].shape[0], 0
    for att, rest in zip(atts, rests):
        span = att.shape[1]
        normed = (att[...] - mean) * scale
        gated = (normed * rest[0].astype(f32)).astype(bf16)
        for r, out in enumerate(outs):
            out[:, column:column + span] = gated[r * rows:(r + 1) * rows]
        column += span


def gate_rows(stats, atts, rests, chunks):
    rows, width = atts[0].shape[0], sum(a.shape[1] for a in atts)
    return pl.pallas_call(
        functools.partial(gate_kernel, len(stats), len(atts)),
        grid=(1,),
        in_specs=[pl.BlockSpec((rows, DH), lambda j: (0, 0))] * len(stats)
        + [pl.BlockSpec((rows, a.shape[1]), lambda j: (0, 0)) for a in atts]
        + [pl.BlockSpec((1, rows, r.shape[2]), lambda j: (2, 0, 0)) for r in rests],
        out_specs=[pl.BlockSpec((rows // chunks, width), lambda j: (0, 0))] * chunks,
        out_shape=[jax.ShapeDtypeStruct((rows // chunks, width), bf16)] * chunks,
        compiler_params=params(),
        cost_estimate=LIGHT,
        name="gate",
    )(*stats, *atts, *rests)


def output_kernel(owners, slots, index_ref, *refs):
    rows, w_ref, (keep_ref, send_ref, lhs_ref) = refs[:owners], refs[owners], refs[-3:]
    piece, half = rows[0].shape[1], len(slots) // 2

    @pl.when(pl.program_id(0) == 0)
    def _():
        first = 0
        for slot in slots:
            for p in range(owners):
                lhs_ref[first:first + piece, :] = rows[p][index_ref[0] ^ slot]
                first += piece

    sums = jnp.dot(lhs_ref[...], w_ref[...], preferred_element_type=f32).astype(bf16)
    for k in range(len(slots)):
        into = keep_ref if k < half else send_ref
        for p in range(owners):
            first = (k * owners + p) * piece
            into[k % half, p] = sums[first:first + piece]


def output(index, blocks, w_out, slots, after):
    owners, (each, width) = len(blocks), blocks[0].shape
    zs = len(slots)
    piece, columns = each // zs, w_out.shape[1]
    span = 512 if columns % 512 == 0 else columns
    row_spec = pl.BlockSpec((zs, piece, width), lambda j, at: (0, 0, 0))
    spec = pl.BlockSpec((zs // 2, owners, piece, span), lambda j, at: (0, 0, 0, j))
    shape = jax.ShapeDtypeStruct((zs // 2, owners, piece, columns), bf16)
    return pl.pallas_call(
        functools.partial(output_kernel, owners, slots),
        grid_spec=pltpu.PrefetchScalarGridSpec(
            num_scalar_prefetch=1,
            grid=(columns // span,),
            in_specs=[row_spec] * owners
            + [pl.BlockSpec((width, span), lambda j, at: (0, j))]
            + anywhere(after),
            out_specs=(spec, spec),
            scratch_shapes=[pltpu.VMEM((owners * each, width), bf16)],
        ),
        out_shape=(shape, shape),
        compiler_params=params(),
        cost_estimate=LIGHT,
        name="output",
    )(
        index.reshape(1).astype(jnp.int32),
        *[b.reshape(zs, piece, width) for b in blocks], w_out, *after,
    )


def close_kernel(counts, at_ref, t_ref, *refs):
    out_ref, first = refs[-1], 0
    owners = refs[0].shape[1]
    for r, count in enumerate(counts):
        terms = refs[first:first + count]
        first += count
        for p in range(owners):
            total = t_ref[r * owners + p].astype(f32)
            for term in terms:
                total = total + term[0, p ^ at_ref[0]].astype(f32)
            out_ref[r * owners + p] = total.astype(bf16)


def close(place, index, tokens, chunks):
    _, owners, piece, width = chunks[0][0].shape
    blocks, span = len(chunks) * owners, width // 2
    term = pl.BlockSpec((1, owners, piece, span), lambda j, at: (0, 0, 0, j))
    return pl.pallas_call(
        functools.partial(close_kernel, [len(terms) for terms in chunks]),
        grid_spec=pltpu.PrefetchScalarGridSpec(
            num_scalar_prefetch=1,
            grid=(2,),
            in_specs=[pl.BlockSpec((blocks, piece, span), lambda j, at: (at[1], 0, j))]
            + [term] * sum(len(terms) for terms in chunks),
            out_specs=pl.BlockSpec((blocks, piece, span), lambda j, at: (0, 0, j)),
        ),
        out_shape=jax.ShapeDtypeStruct((blocks, piece, width), bf16),
        compiler_params=params(),
        cost_estimate=LIGHT,
        name="close",
    )(
        jnp.stack([place, index]).astype(jnp.int32),
        tokens.reshape(-1, piece, width),
        *[term for terms in chunks for term in terms],
    )


def bits_of(axis):
    count = lax.axis_size(axis)
    assert count & (count - 1) == 0
    return count.bit_length() - 1


def reverse(index, bits):
    return sum((((index >> b) & 1) << (bits - 1 - b) for b in range(bits)), 0 * index)


def swap(x, axis, bit):
    return lax.ppermute(
        x, axis, [(i, i ^ (1 << bit)) for i in range(lax.axis_size(axis))]
    )


def scatter(keep, send, axis):
    terms, sent = [keep, swap(send, axis, 0)], send
    for b in range(1, bits_of(axis)):
        sent = fold(terms)
        terms.append(swap(sent, axis, b))
    return terms, sent


def gather(x, axis):
    blocks = [x]
    for b in reversed(range(bits_of(axis))):
        blocks = blocks + [swap(block, axis, b) for block in blocks]
    return blocks


def all_stats(stat, axis):
    count = lax.axis_size(axis)
    if count > 8:
        every = lax.all_gather(stat, axis)
        return [every[i] for i in range(count)]
    return [stat] + [
        lax.ppermute(stat, axis, [(i, (i + k) % count) for i in range(count)])
        for k in range(1, count)
    ]


def head_chunks(heads):
    if heads % 8:
        return [1] * heads
    unit = heads // 8
    return [unit, 2 * unit, 2 * unit, 2 * unit, unit]


def local(tokens, w_qkvu, k_cache, v_cache, w_out, vis_start, vis_end):
    cand, depth = tokens.shape
    owners, zs = lax.axis_size("hist"), lax.axis_size("head")
    index = lax.axis_index("head")
    place = reverse(lax.axis_index("hist"), bits_of("hist"))
    width = w_qkvu.shape[2]
    events = k_cache.shape[0]
    chunks = 2 if cand % (2 * owners * zs * 16) == 0 else 1
    piece = cand // (zs * chunks * owners)

    def arrange(x):
        x = x.reshape((zs, chunks, owners, piece) + x.shape[1:])
        if piece % 16 == 0:
            return x
        blocks = [lax.dynamic_index_in_dim(x, p ^ place, 2, False) for p in range(owners)]
        x = jnp.stack(blocks).swapaxes(1, 2)
        return x.reshape((1, 1, owners, zs * chunks * piece) + x.shape[4:])

    at = (place if piece % 16 == 0 else jnp.int32(0)).reshape(1)
    ordered = arrange(tokens)
    first_event = lax.axis_index("hist") * events
    edges = arrange(jnp.stack([vis_start - first_event, vis_end - first_event], axis=1))

    sizes = head_chunks(width // DH)
    firsts = [sum(sizes[:c]) for c in range(len(sizes))]
    last = len(sizes) - 1
    keeps, sent, parts, terms_of, atts, stats = [], [], [], [], [], []

    def front(c):
        after = keeps[-1:]
        if c >= 2:
            after = after + [sent[c - 2]]
        keep, send = project(at, ordered, w_qkvu, firsts[c], sizes[c], after)
        keeps.append(keep)
        before = [terms_of[c - 1][1]] if c >= 1 else []
        if c >= 2:
            before = before + [terms_of[c - 2][-1]]
        send = tie(send, before)
        terms, out = scatter(keep, send, "hist")
        sent.append(out)
        terms_of.append(terms)

    waits = []

    def middle(c):
        query, rest = activate(terms_of[c], waits[-1:] + (atts[c - 2:c - 1] if c >= 2 else []))
        parts.append((query, rest))
        keep, send = attend(at, gather(query, "hist"), k_cache, v_cache, edges, firsts[c])
        waits.append(keep)
        sums, _ = scatter(keep, send, "hist")
        others = stats if c == last else []
        widths = [s * DH for s in sizes[:c]] if c == last else []
        att, stat = finish(at, edges, query, rest, sums, list(others), widths)
        atts.append(att)
        stats.append(stat)

    for c in range(len(sizes)):
        front(c)
        if c >= 2:
            middle(c - 2)
    for c in range(max(0, len(sizes) - 2), len(sizes)):
        middle(c)

    gated = gate_rows(all_stats(stats[-1], "head"), atts, [rest for _, rest in parts], chunks)
    results, after = [], []
    for rows in gated:
        blocks = gather(rows, "hist")
        if piece % 16 == 0 and zs & (zs - 1) == 0:
            slots = [reverse(k, bits_of("head")) for k in range(zs)]
            keep, send = output(index, blocks, w_out, slots, [])
            send = tie(send, after)
            terms, _ = scatter(keep, send, "head")
            after = [terms[1]]
            results.append(terms)
        else:
            whole = jnp.dot(jnp.concatenate(blocks), w_out, preferred_element_type=f32)
            whole = whole.astype(bf16).reshape(owners, zs, piece, -1).swapaxes(0, 1)
            results.append([lax.psum_scatter(whole, "head", scatter_dimension=0, tiled=True)])
    out = close(place, index, tokens, results)
    return out.reshape(cand // zs, -1)


def solution(mesh):
    in_specs = (
        P("groups", "hist"),
        P("hist", None, "head"),
        P(("groups", "hist"), "head"),
        P(("groups", "hist"), "head"),
        P("head", "hist"),
        P("groups"),
        P("groups"),
    )
    out_specs = P(("groups", "head"), "hist")
    return jax.shard_map(local, mesh=mesh, in_specs=in_specs, out_specs=out_specs, check_vma=False)
```

```python
import functools

import jax
import jax.numpy as jnp
from jax import lax
from jax.experimental import pallas as pl
from jax.experimental.pallas import tpu as pltpu
from jax.sharding import PartitionSpec as P

DH = 128
EPSILON = 1e-05
VMEM_LIMIT = 28 * 1024 * 1024

bf16 = jnp.bfloat16
f32 = jnp.float32


def silu(v):
    u = 0.5 * v
    return u + u * jnp.tanh(u)


def params():
    return pltpu.CompilerParams(vmem_limit_bytes=VMEM_LIMIT)


LIGHT = pl.CostEstimate(flops=1000, bytes_accessed=1000, transcendentals=0)


def far(x):
    return pltpu.with_memory_space_constraint(x, pltpu.HBM)


def anywhere(arrays):
    return [pl.BlockSpec(memory_space=pl.ANY)] * len(arrays)


def project_kernel(parts, owners, after, at_ref, *refs):
    rows, weights = refs[:owners], refs[owners:owners + parts]
    keep_ref, send_ref, lhs_ref = refs[owners + parts + after:][:3]
    wides = refs[-parts:]
    zs, chunks, _, piece, _ = rows[0].shape
    depth = weights[0].shape[0]

    @pl.when(pl.program_id(0) == 0)
    def _():
        first = 0
        for p in range(owners):
            for r in range(chunks):
                for z in range(zs):
                    lhs_ref[first:first + piece, :] = rows[p][z, r, 0]
                    first += piece

    res = None
    for k, wide in enumerate(wides):
        wide[...] = weights[k].reshape(depth * 4, DH)[...].astype(f32)
        rhs = jnp.concatenate(
            [wide[pl.ds(i, depth, stride=4), :].astype(bf16) for i in range(4)], axis=1
        )
        term = jnp.dot(lhs_ref[:, k * depth:(k + 1) * depth], rhs, preferred_element_type=f32)
        res = term if res is None else res + term
    res = res.astype(bf16)
    half, _, each, _ = keep_ref.shape
    for p in range(owners):
        into = keep_ref if p < half else send_ref
        for i in range(4):
            into[p % half, i] = res[p * each:(p + 1) * each, i * DH:(i + 1) * DH]


def project(at, tokens, w, head_first, heads, after):
    zs, chunks, owners, piece, depth = tokens.shape
    half, each = owners // 2, zs * chunks * piece
    parts = 4 if depth % 512 == 0 else 1
    shape = jax.ShapeDtypeStruct((half, 4, each, heads * DH), bf16)
    spec = pl.BlockSpec((half, 4, each, DH), lambda j, at: (0, 0, 0, j))
    return pl.pallas_call(
        functools.partial(project_kernel, parts, owners, len(after)),
        grid_spec=pltpu.PrefetchScalarGridSpec(
            num_scalar_prefetch=1,
            grid=(heads,),
            in_specs=[
                pl.BlockSpec(
                    (zs, chunks, 1, piece, depth), lambda j, at, p=p: (0, 0, at[0] ^ p, 0, 0)
                )
                for p in range(owners)
            ]
            + [
                pl.BlockSpec((depth // parts, 4, DH), lambda j, at, k=k: (k, 0, head_first + j))
                for k in range(parts)
            ]
            + anywhere(after),
            out_specs=(spec, spec),
            scratch_shapes=[pltpu.VMEM((owners * each, depth), bf16)]
            + [pltpu.VMEM((depth // parts * 4, DH), f32) for _ in range(parts)],
        ),
        out_shape=(shape, shape),
        compiler_params=params(),
        cost_estimate=LIGHT,
        name="project",
    )(at, *[far(tokens)] * owners, *[far(w)] * parts, *after)


def tie_kernel(*refs):
    pass


def tie(x, after):
    if not after:
        return x
    return pl.pallas_call(
        tie_kernel,
        in_specs=anywhere([x, *after]),
        out_specs=pl.BlockSpec(memory_space=pl.ANY),
        out_shape=jax.ShapeDtypeStruct(x.shape, x.dtype),
        input_output_aliases={0: 0},
        compiler_params=params(),
        cost_estimate=LIGHT,
        name="tie",
    )(x, *after)


def fold_kernel(*refs):
    refs[-1][...] = sum(r[...].astype(f32) for r in refs[:-1]).astype(bf16)


def fold(terms):
    half, tail = terms[-1].shape[0] // 2, terms[0].shape[1:]
    steps = 2 if tail[-1] % 256 == 0 else 1
    block = (half,) + tail[:-1] + (tail[-1] // steps,)
    middle = (0,) * (len(tail) - 1)
    return pl.pallas_call(
        fold_kernel,
        grid=(steps,),
        in_specs=[pl.BlockSpec(block, lambda j: (1,) + middle + (j,))] * len(terms),
        out_specs=pl.BlockSpec(block, lambda j: (0,) + middle + (j,)),
        out_shape=jax.ShapeDtypeStruct((half,) + tail, bf16),
        compiler_params=params(),
        cost_estimate=LIGHT,
        name="fold",
    )(*terms)


def activate_kernel(count, *refs):
    q_ref, rest_ref = refs[-2:]
    for i in range(4):
        part = silu(sum(t[0, i].astype(f32) for t in refs[:count])).astype(bf16)
        if i == 0:
            q_ref[...] = part
        else:
            rest_ref[i - 1] = part


def activate(terms, after):
    _, _, each, width = terms[0].shape
    return pl.pallas_call(
        functools.partial(activate_kernel, len(terms)),
        grid=(1,),
        in_specs=[pl.BlockSpec((1, 4, each, width), lambda j: (0, 0, 0, 0))] * len(terms)
        + anywhere(after),
        out_specs=(
            pl.BlockSpec((each, width), lambda j: (0, 0)),
            pl.BlockSpec((3, each, width), lambda j: (0, 0, 0)),
        ),
        out_shape=(
            jax.ShapeDtypeStruct((each, width), bf16),
            jax.ShapeDtypeStruct((3, each, width), bf16),
        ),
        compiler_params=params(),
        cost_estimate=LIGHT,
        name="activate",
    )(*terms, *after)


def attend_kernel(owners, at_ref, *refs):
    queries, edges = refs[:owners], refs[owners:2 * owners]
    k_ref, v_ref = refs[2 * owners:2 * owners + 2]
    keep_ref, send_ref, mask_ref = refs[-3:]
    events = mask_ref.shape[1]
    half, each, _ = keep_ref.shape

    @pl.when(pl.program_id(0) == 0)
    def _():
        zs, chunks, _, piece, _ = edges[0].shape
        at = lax.broadcasted_iota(jnp.int32, (piece, events), 1)
        first = 0
        for p in range(owners):
            for r in range(chunks):
                for z in range(zs):
                    edge = edges[p][z, r, 0]
                    seen = (at >= edge[:, :1]) & (at < edge[:, 1:])
                    mask_ref[first:first + piece, :] = jnp.where(seen, 1.0, 0.0).astype(bf16)
                    first += piece

    for h in range(k_ref.shape[1] // DH):
        at = slice(h * DH, (h + 1) * DH)
        query = jnp.concatenate([q[:, at] for q in queries])
        u = lax.dot_general(
            query, k_ref[:, at], (((1,), (1,)), ((), ())), preferred_element_type=f32
        ) * (0.5 * DH ** (-0.5))
        weights = (u + u * jnp.tanh(u)).astype(bf16) * mask_ref[...]
        term = jnp.dot(weights, v_ref[:, at], preferred_element_type=f32).astype(bf16)
        for p in range(owners):
            into = keep_ref if p < half else send_ref
            into[p % half, :, at] = term[p * each:(p + 1) * each]


def edge_spec(edges, p):
    zs, chunks, _, piece, ends = edges.shape
    return pl.BlockSpec((zs, chunks, 1, piece, ends), lambda j, at: (0, 0, at[0] ^ p, 0, 0))


def attend(at, queries, k_cache, v_cache, edges, head_first, after):
    owners, (each, width) = len(queries), queries[0].shape
    rows, events, half = owners * each, k_cache.shape[0], owners // 2
    first = head_first * DH
    span = 2 * DH if width % (2 * DH) == 0 and first % (2 * DH) == 0 else DH
    cache = pl.BlockSpec((events, span), lambda j, at: (0, first // span + j))
    shape = jax.ShapeDtypeStruct((half, each, width), bf16)
    spec = pl.BlockSpec((half, each, span), lambda j, at: (0, 0, j))
    return pl.pallas_call(
        functools.partial(attend_kernel, owners),
        grid_spec=pltpu.PrefetchScalarGridSpec(
            num_scalar_prefetch=1,
            grid=(width // span,),
            in_specs=[pl.BlockSpec((each, span), lambda j, at: (0, j))] * owners
            + [edge_spec(edges, p) for p in range(owners)]
            + [cache, cache]
            + anywhere(after),
            out_specs=(spec, spec),
            scratch_shapes=[pltpu.VMEM((rows, events), bf16)],
        ),
        out_shape=(shape, shape),
        compiler_params=params(),
        cost_estimate=LIGHT,
        name="attend",
    )(at, *queries, *[edges] * owners, far(k_cache), far(v_cache), *after)


def merge(means, squares, widths):
    width = sum(widths)
    mean = sum(m * (w / width) for m, w in zip(means, widths))
    square = sum(squares) + sum(w * (m - mean) * (m - mean) for m, w in zip(means, widths))
    return mean, square


def stat_columns(stats):
    stats = [s[...] for s in stats]
    stats = [s if s.shape[0] > 8 else jnp.concatenate([s] * (DH // 8)).T for s in stats]
    return [s[:, :1] for s in stats], [s[:, 4:5] for s in stats]


def finish_kernel(terms, widths, at_ref, edge_ref, q_ref, rest_ref, *refs):
    sums, others, (att_ref, stat_ref) = refs[:terms], refs[terms:-2], refs[-2:]
    rows, width = att_ref.shape
    zs, chunks = edge_ref.shape[:2]
    edge = jnp.concatenate(
        [edge_ref[z, r, 0] for r in range(chunks) for z in range(zs)]
    ).astype(f32)
    root = lax.rsqrt(edge[:, 1:] - edge[:, :1])
    total = jnp.zeros((rows, 1), f32)
    for first in range(0, width, DH):
        at = slice(first, first + DH)
        summed = sum(s[0, :, at].astype(f32) for s in sums)
        product = q_ref[:, at].astype(f32) * rest_ref[0, :, at].astype(f32)
        weight = silu(jnp.sum(product, axis=1, keepdims=True) * DH ** (-0.5))
        value = summed * root + weight * rest_ref[1, :, at].astype(f32)
        att_ref[:, at] = value
        total += jnp.sum(value, axis=1, keepdims=True)
    mean = total / width
    spread = jnp.zeros((rows, DH), f32)
    for first in range(0, width, DH):
        away = att_ref[:, first:first + DH] - mean
        spread += away * away
    square = jnp.sum(spread, axis=1, keepdims=True)
    if others:
        means, squares = stat_columns(others)
        mean, square = merge([mean] + means, [square] + squares, [width] + widths)
    lane = lax.broadcasted_iota(jnp.int32, (rows, DH), 1)
    stat = jnp.where(lane < 4, mean, square)
    stat_ref[...] = stat if stat_ref.shape == stat.shape else stat.T[:8]


def finish(at, edges, query, rest, sums, others, widths):
    rows, width = query.shape
    stat = (8, rows) if others and rows == DH else (rows, DH)
    return pl.pallas_call(
        functools.partial(finish_kernel, len(sums), widths),
        grid_spec=pltpu.PrefetchScalarGridSpec(
            num_scalar_prefetch=1,
            grid=(1,),
            in_specs=[
                edge_spec(edges, 0),
                pl.BlockSpec((rows, width), lambda j, at: (0, 0)),
                pl.BlockSpec((2, rows, width), lambda j, at: (0, 0, 0)),
            ]
            + [pl.BlockSpec((1, rows, width), lambda j, at: (0, 0, 0))] * len(sums)
            + [pl.BlockSpec((rows, DH), lambda j, at: (0, 0))] * len(others),
            out_specs=(
                pl.BlockSpec((rows, width), lambda j, at: (0, 0)),
                pl.BlockSpec(stat, lambda j, at: (0, 0)),
            ),
        ),
        out_shape=(
            jax.ShapeDtypeStruct((rows, width), f32),
            jax.ShapeDtypeStruct(stat, f32),
        ),
        compiler_params=params(),
        cost_estimate=LIGHT,
        name="finish",
    )(at, edges, query, rest, *sums, *others)


def gate_kernel(count, parts, *refs):
    stats, atts, rests, outs = (
        refs[:count], refs[count:count + parts],
        refs[count + parts:count + 2 * parts], refs[count + 2 * parts:],
    )
    width = sum(a.shape[1] for a in atts)
    means, squares = stat_columns(stats)
    mean, square = merge(means, squares, [width] * count)
    scale = lax.rsqrt(square / (width * count) + EPSILON)
    rows, column = outs[0].shape[0], 0
    for att, rest in zip(atts, rests):
        span = att.shape[1]
        normed = (att[...] - mean) * scale
        gated = (normed * rest[0].astype(f32)).astype(bf16)
        for r, out in enumerate(outs):
            out[:, column:column + span] = gated[r * rows:(r + 1) * rows]
        column += span


def gate_rows(stats, atts, rests, chunks):
    rows, width = atts[0].shape[0], sum(a.shape[1] for a in atts)
    return pl.pallas_call(
        functools.partial(gate_kernel, len(stats), len(atts)),
        grid=(1,),
        in_specs=[pl.BlockSpec(s.shape, lambda j: (0, 0)) for s in stats]
        + [pl.BlockSpec((rows, a.shape[1]), lambda j: (0, 0)) for a in atts]
        + [pl.BlockSpec((1, rows, r.shape[2]), lambda j: (2, 0, 0)) for r in rests],
        out_specs=[pl.BlockSpec((rows // chunks, width), lambda j: (0, 0))] * chunks,
        out_shape=[jax.ShapeDtypeStruct((rows // chunks, width), bf16)] * chunks,
        compiler_params=params(),
        cost_estimate=LIGHT,
        name="gate",
    )(*stats, *atts, *rests)


def output_kernel(owners, slots, index_ref, *refs):
    rows, w_ref, (keep_ref, send_ref, lhs_ref) = refs[:owners], refs[owners], refs[-3:]
    piece, half = rows[0].shape[1], len(slots) // 2

    @pl.when(pl.program_id(0) == 0)
    def _():
        first = 0
        for slot in slots:
            for p in range(owners):
                lhs_ref[first:first + piece, :] = rows[p][index_ref[0] ^ slot]
                first += piece

    sums = jnp.dot(lhs_ref[...], w_ref[...], preferred_element_type=f32).astype(bf16)
    for k in range(len(slots)):
        into = keep_ref if k < half else send_ref
        for p in range(owners):
            first = (k * owners + p) * piece
            into[k % half, p] = sums[first:first + piece]


def output(index, blocks, w_out, slots, column, columns, after):
    owners, (each, width) = len(blocks), blocks[0].shape
    zs = len(slots)
    piece = each // zs
    span = 512 if columns % 512 == 0 else columns
    row_spec = pl.BlockSpec((zs, piece, width), lambda j, at: (0, 0, 0))
    spec = pl.BlockSpec((zs // 2, owners, piece, span), lambda j, at: (0, 0, 0, j))
    shape = jax.ShapeDtypeStruct((zs // 2, owners, piece, columns), bf16)
    return pl.pallas_call(
        functools.partial(output_kernel, owners, slots),
        grid_spec=pltpu.PrefetchScalarGridSpec(
            num_scalar_prefetch=1,
            grid=(columns // span,),
            in_specs=[row_spec] * owners
            + [pl.BlockSpec((width, span), lambda j, at: (0, column // span + j))]
            + anywhere(after),
            out_specs=(spec, spec),
            scratch_shapes=[pltpu.VMEM((owners * each, width), bf16)],
        ),
        out_shape=(shape, shape),
        compiler_params=params(),
        cost_estimate=LIGHT,
        name="output",
    )(
        index.reshape(1).astype(jnp.int32),
        *[b.reshape(zs, piece, width) for b in blocks], far(w_out), *after,
    )


def close_kernel(counts, at_ref, t_ref, *refs):
    out_ref, first = refs[-1], 0
    owners = refs[0].shape[1]
    for r, row in enumerate(counts):
        column = 0
        for count in row:
            terms = refs[first:first + count]
            first += count
            span = terms[0].shape[-1]
            for p in range(owners):
                total = t_ref[r * owners + p, :, column:column + span].astype(f32)
                for term in terms:
                    total = total + term[0, p ^ at_ref[0]].astype(f32)
                out_ref[r * owners + p, :, column:column + span] = total.astype(bf16)
            column += span


def close(place, index, tokens, chunks):
    _, owners, piece, _ = chunks[0][0][0].shape
    blocks, width = len(chunks) * owners, sum(terms[0].shape[-1] for terms in chunks[0])
    flat = [term for row in chunks for terms in row for term in terms]
    return pl.pallas_call(
        functools.partial(close_kernel, [[len(terms) for terms in row] for row in chunks]),
        grid_spec=pltpu.PrefetchScalarGridSpec(
            num_scalar_prefetch=1,
            grid=(1,),
            in_specs=[pl.BlockSpec((blocks, piece, width), lambda j, at: (at[1], 0, 0))]
            + [pl.BlockSpec((1,) + t.shape[1:], lambda j, at: (0, 0, 0, 0)) for t in flat],
            out_specs=pl.BlockSpec((blocks, piece, width), lambda j, at: (0, 0, 0)),
        ),
        out_shape=jax.ShapeDtypeStruct((blocks, piece, width), bf16),
        compiler_params=params(),
        cost_estimate=LIGHT,
        name="close",
    )(
        jnp.stack([place, index]).astype(jnp.int32),
        far(tokens.reshape(-1, piece, width)),
        *flat,
    )


def bits_of(axis):
    count = lax.axis_size(axis)
    assert count & (count - 1) == 0
    return count.bit_length() - 1


def reverse(index, bits):
    return sum((((index >> b) & 1) << (bits - 1 - b) for b in range(bits)), 0 * index)


def swap(x, axis, bit):
    return lax.ppermute(
        x, axis, [(i, i ^ (1 << bit)) for i in range(lax.axis_size(axis))]
    )


def scatter(keep, send, axis):
    terms, sent = [keep, swap(send, axis, 0)], send
    for b in range(1, bits_of(axis)):
        sent = fold(terms)
        terms.append(swap(sent, axis, b))
    return terms, sent


def gather(x, axis):
    blocks = [x]
    for b in reversed(range(bits_of(axis))):
        blocks = blocks + [swap(block, axis, b) for block in blocks]
    return blocks


def all_stats(stat, axis):
    count = lax.axis_size(axis)
    if count > 8:
        every = lax.all_gather(stat, axis)
        return [every[i] for i in range(count)]
    return [stat] + [
        lax.ppermute(stat, axis, [(i, (i + k) % count) for i in range(count)])
        for k in range(1, count)
    ]


def head_chunks(heads):
    if heads % 8:
        return [1] * heads
    unit = heads // 8
    return [unit, 2 * unit, 2 * unit, 3 * unit]


def local(tokens, w_qkvu, k_cache, v_cache, w_out, vis_start, vis_end):
    cand, depth = tokens.shape
    owners, zs = lax.axis_size("hist"), lax.axis_size("head")
    index = lax.axis_index("head")
    place = reverse(lax.axis_index("hist"), bits_of("hist"))
    width = w_qkvu.shape[2]
    events = k_cache.shape[0]
    chunks = 2 if cand % (2 * owners * zs * 16) == 0 else 1
    piece = cand // (zs * chunks * owners)

    def arrange(x):
        x = x.reshape((zs, chunks, owners, piece) + x.shape[1:])
        if piece % 16 == 0:
            return x
        blocks = [lax.dynamic_index_in_dim(x, p ^ place, 2, False) for p in range(owners)]
        x = jnp.stack(blocks).swapaxes(1, 2)
        return x.reshape((1, 1, owners, zs * chunks * piece) + x.shape[4:])

    at = (place if piece % 16 == 0 else jnp.int32(0)).reshape(1)
    ordered = arrange(tokens)
    first_event = lax.axis_index("hist") * events
    edges = arrange(jnp.stack([vis_start - first_event, vis_end - first_event], axis=1))

    sizes = head_chunks(width // DH)
    firsts = [sum(sizes[:c]) for c in range(len(sizes))]
    last = len(sizes) - 1
    keeps, sent, parts, terms_of, atts, stats = [], [], [], [], [], []

    def front(c):
        after = keeps[-1:]
        if c >= 2:
            after = after + [sent[c - 2]]
        if c >= 3:
            after = after + [parts[c - 3][0]]
        keep, send = project(at, ordered, w_qkvu, firsts[c], sizes[c], after)
        keeps.append(keep)
        before = [terms_of[c - 1][1]] if c >= 1 else []
        if c >= 2:
            before = before + [terms_of[c - 2][-1]]
        if c >= 3:
            before = before + queries[c - 3][1:2]
        send = tie(send, before)
        terms, out = scatter(keep, send, "hist")
        sent.append(out)
        terms_of.append(terms)

    waits, queries = [], []

    def middle_first(c):
        after = waits[-1:] + (atts[:-1] if c == last else [])
        parts.append(activate(terms_of[c], after))
        queries.append(gather(parts[c][0], "hist"))

    def middle(c):
        query, rest = parts[c]
        after = atts[-1:] if c == last else []
        keep, send = attend(at, queries[c], k_cache, v_cache, edges, firsts[c], after)
        waits.append(keep)
        sums, _ = scatter(keep, send, "hist")
        others = stats if c == last else []
        widths = [s * DH for s in sizes[:c]] if c == last else []
        att, stat = finish(at, edges, query, rest, sums, list(others), widths)
        atts.append(att)
        stats.append(stat)

    for c in range(len(sizes)):
        front(c)
        if c == 2:
            middle_first(0)
    for c in range(len(sizes)):
        if c == len(parts):
            middle_first(c)
        middle(c)

    gated = gate_rows(all_stats(stats[-1], "head"), atts, [rest for _, rest in parts], chunks)
    columns = w_out.shape[1]
    straight = piece % 16 == 0 and zs & (zs - 1) == 0
    groups = 2 if straight and columns % 1024 == 0 else 1
    results, sends, first_steps, ends = [], [], [], []
    for rows in gated:
        blocks = gather(rows, "hist")
        results.append([])
        for g in range(groups):
            if straight:
                slots = [reverse(k, bits_of("head")) for k in range(zs)]
                span = columns // groups
                keep, send = output(index, blocks, w_out, slots, g * span, span, sends[-1:])
                before = first_steps[-2:-1] + ends[-3:-2]
                send = tie(send, before)
                sends.append(send)
                terms, _ = scatter(keep, send, "head")
                first_steps.append(terms[1])
                ends.append(terms[-1])
            else:
                whole = jnp.dot(jnp.concatenate(blocks), w_out, preferred_element_type=f32)
                whole = whole.astype(bf16).reshape(owners, zs, piece, -1).swapaxes(0, 1)
                terms = [lax.psum_scatter(whole, "head", scatter_dimension=0, tiled=True)]
            results[-1].append(terms)
    out = close(place, index, tokens, results)
    return out.reshape(cand // zs, -1)


def solution(mesh):
    in_specs = (
        P("groups", "hist"),
        P("hist", None, "head"),
        P(("groups", "hist"), "head"),
        P(("groups", "hist"), "head"),
        P("head", "hist"),
        P("groups"),
        P("groups"),
    )
    out_specs = P(("groups", "head"), "hist")
    return jax.shard_map(local, mesh=mesh, in_specs=in_specs, out_specs=out_specs, check_vma=False)
```

```python
import functools

import jax
import jax.numpy as jnp
from jax import lax
from jax.experimental import pallas as pl
from jax.experimental.pallas import tpu as pltpu
from jax.sharding import PartitionSpec as P

DH = 128
EPSILON = 1e-05
VMEM_LIMIT = 28 * 1024 * 1024

bf16 = jnp.bfloat16
f32 = jnp.float32


def silu(v):
    u = 0.5 * v
    return u + u * jnp.tanh(u)


def params():
    return pltpu.CompilerParams(vmem_limit_bytes=VMEM_LIMIT)


LIGHT = pl.CostEstimate(flops=1000, bytes_accessed=1000, transcendentals=0)


def far(x):
    return pltpu.with_memory_space_constraint(x, pltpu.HBM)


def anywhere(arrays):
    return [pl.BlockSpec(memory_space=pl.ANY)] * len(arrays)


def project_kernel(parts, owners, after, at_ref, *refs):
    rows, weights = refs[:owners], refs[owners:owners + parts]
    keep_ref, send_ref, lhs_ref = refs[owners + parts + after:][:3]
    wides = refs[-parts:]
    zs, chunks, _, piece, _ = rows[0].shape
    depth = weights[0].shape[0]

    @pl.when(pl.program_id(0) == 0)
    def _():
        first = 0
        for p in range(owners):
            for r in range(chunks):
                for z in range(zs):
                    lhs_ref[first:first + piece, :] = rows[p][z, r, 0]
                    first += piece

    res = None
    for k, wide in enumerate(wides):
        wide[...] = weights[k].reshape(depth * 4, DH)[...].astype(f32)
        rhs = jnp.concatenate(
            [wide[pl.ds(i, depth, stride=4), :].astype(bf16) for i in range(4)], axis=1
        )
        term = jnp.dot(lhs_ref[:, k * depth:(k + 1) * depth], rhs, preferred_element_type=f32)
        res = term if res is None else res + term
    res = res.astype(bf16)
    half, _, each, _ = keep_ref.shape
    for p in range(owners):
        into = keep_ref if p < half else send_ref
        for i in range(4):
            into[p % half, i] = res[p * each:(p + 1) * each, i * DH:(i + 1) * DH]


def project(at, tokens, w, head_first, heads, after):
    zs, chunks, owners, piece, depth = tokens.shape
    half, each = owners // 2, zs * chunks * piece
    parts = 4 if depth % 512 == 0 else 1
    shape = jax.ShapeDtypeStruct((half, 4, each, heads * DH), bf16)
    spec = pl.BlockSpec((half, 4, each, DH), lambda j, at: (0, 0, 0, j))
    return pl.pallas_call(
        functools.partial(project_kernel, parts, owners, len(after)),
        grid_spec=pltpu.PrefetchScalarGridSpec(
            num_scalar_prefetch=1,
            grid=(heads,),
            in_specs=[
                pl.BlockSpec(
                    (zs, chunks, 1, piece, depth), lambda j, at, p=p: (0, 0, at[0] ^ p, 0, 0)
                )
                for p in range(owners)
            ]
            + [
                pl.BlockSpec((depth // parts, 4, DH), lambda j, at, k=k: (k, 0, head_first + j))
                for k in range(parts)
            ]
            + anywhere(after),
            out_specs=(spec, spec),
            scratch_shapes=[pltpu.VMEM((owners * each, depth), bf16)]
            + [pltpu.VMEM((depth // parts * 4, DH), f32) for _ in range(parts)],
        ),
        out_shape=(shape, shape),
        compiler_params=params(),
        cost_estimate=LIGHT,
        name="project",
    )(at, *[far(tokens)] * owners, *[far(w)] * parts, *after)


def tie_kernel(*refs):
    pass


def tie(x, after):
    if not after:
        return x
    return pl.pallas_call(
        tie_kernel,
        in_specs=anywhere([x, *after]),
        out_specs=pl.BlockSpec(memory_space=pl.ANY),
        out_shape=jax.ShapeDtypeStruct(x.shape, x.dtype),
        input_output_aliases={0: 0},
        compiler_params=params(),
        cost_estimate=LIGHT,
        name="tie",
    )(x, *after)


def fold_kernel(count, *refs):
    refs[-1][...] = sum(r[...].astype(f32) for r in refs[:count]).astype(bf16)


def fold(terms, after=()):
    half, tail = terms[-1].shape[0] // 2, terms[0].shape[1:]
    steps = 2 if tail[-1] % 256 == 0 else 1
    block = (half,) + tail[:-1] + (tail[-1] // steps,)
    middle = (0,) * (len(tail) - 1)
    return pl.pallas_call(
        functools.partial(fold_kernel, len(terms)),
        grid=(steps,),
        in_specs=[pl.BlockSpec(block, lambda j: (1,) + middle + (j,))] * len(terms)
        + anywhere(after),
        out_specs=pl.BlockSpec(block, lambda j: (0,) + middle + (j,)),
        out_shape=jax.ShapeDtypeStruct((half,) + tail, bf16),
        compiler_params=params(),
        cost_estimate=LIGHT,
        name="fold",
    )(*terms, *after)


def activate_kernel(count, *refs):
    q_ref, rest_ref = refs[-2:]
    for i in range(4):
        part = silu(sum(t[0, i].astype(f32) for t in refs[:count])).astype(bf16)
        if i == 0:
            q_ref[...] = part
        else:
            rest_ref[i - 1] = part


def activate(terms, after):
    _, _, each, width = terms[0].shape
    return pl.pallas_call(
        functools.partial(activate_kernel, len(terms)),
        grid=(1,),
        in_specs=[pl.BlockSpec((1, 4, each, width), lambda j: (0, 0, 0, 0))] * len(terms)
        + anywhere(after),
        out_specs=(
            pl.BlockSpec((each, width), lambda j: (0, 0)),
            pl.BlockSpec((3, each, width), lambda j: (0, 0, 0)),
        ),
        out_shape=(
            jax.ShapeDtypeStruct((each, width), bf16),
            jax.ShapeDtypeStruct((3, each, width), bf16),
        ),
        compiler_params=params(),
        cost_estimate=LIGHT,
        name="activate",
    )(*terms, *after)


def attend_kernel(owners, at_ref, *refs):
    queries, edges = refs[:owners], refs[owners:2 * owners]
    k_ref, v_ref = refs[2 * owners:2 * owners + 2]
    keep_ref, send_ref, mask_ref = refs[-3:]
    events = mask_ref.shape[1]
    half, each, _ = keep_ref.shape

    @pl.when(pl.program_id(0) == 0)
    def _():
        zs, chunks, _, piece, _ = edges[0].shape
        at = lax.broadcasted_iota(jnp.int32, (piece, events), 1)
        first = 0
        for p in range(owners):
            for r in range(chunks):
                for z in range(zs):
                    edge = edges[p][z, r, 0]
                    seen = (at >= edge[:, :1]) & (at < edge[:, 1:])
                    mask_ref[first:first + piece, :] = jnp.where(seen, 1.0, 0.0).astype(bf16)
                    first += piece

    for h in range(k_ref.shape[1] // DH):
        at = slice(h * DH, (h + 1) * DH)
        query = jnp.concatenate([q[:, at] for q in queries])
        u = lax.dot_general(
            query, k_ref[:, at], (((1,), (1,)), ((), ())), preferred_element_type=f32
        ) * (0.5 * DH ** (-0.5))
        weights = (u + u * jnp.tanh(u)).astype(bf16) * mask_ref[...]
        term = jnp.dot(weights, v_ref[:, at], preferred_element_type=f32).astype(bf16)
        for p in range(owners):
            into = keep_ref if p < half else send_ref
            into[p % half, :, at] = term[p * each:(p + 1) * each]


def edge_spec(edges, p):
    zs, chunks, _, piece, ends = edges.shape
    return pl.BlockSpec((zs, chunks, 1, piece, ends), lambda j, at: (0, 0, at[0] ^ p, 0, 0))


def attend(at, queries, k_cache, v_cache, edges, head_first, after):
    owners, (each, width) = len(queries), queries[0].shape
    rows, events, half = owners * each, k_cache.shape[0], owners // 2
    first = head_first * DH
    span = 2 * DH if width % (2 * DH) == 0 and first % (2 * DH) == 0 else DH
    cache = pl.BlockSpec((events, span), lambda j, at: (0, first // span + j))
    shape = jax.ShapeDtypeStruct((half, each, width), bf16)
    spec = pl.BlockSpec((half, each, span), lambda j, at: (0, 0, j))
    return pl.pallas_call(
        functools.partial(attend_kernel, owners),
        grid_spec=pltpu.PrefetchScalarGridSpec(
            num_scalar_prefetch=1,
            grid=(width // span,),
            in_specs=[pl.BlockSpec((each, span), lambda j, at: (0, j))] * owners
            + [edge_spec(edges, p) for p in range(owners)]
            + [cache, cache]
            + anywhere(after),
            out_specs=(spec, spec),
            scratch_shapes=[pltpu.VMEM((rows, events), bf16)],
        ),
        out_shape=(shape, shape),
        compiler_params=params(),
        cost_estimate=LIGHT,
        name="attend",
    )(at, *queries, *[edges] * owners, far(k_cache), far(v_cache), *after)


def merge(means, squares, widths):
    width = sum(widths)
    mean = sum(m * (w / width) for m, w in zip(means, widths))
    square = sum(squares) + sum(w * (m - mean) * (m - mean) for m, w in zip(means, widths))
    return mean, square


def stat_columns(stats):
    stats = [s[...] for s in stats]
    stats = [s if s.shape[0] > 8 else jnp.concatenate([s] * (DH // 8)).T for s in stats]
    return [s[:, :1] for s in stats], [s[:, 4:5] for s in stats]


def finish_kernel(terms, widths, at_ref, edge_ref, q_ref, rest_ref, *refs):
    sums, others = refs[:terms], refs[terms:terms + len(widths)]
    att_ref, stat_ref = refs[-2:]
    rows, width = att_ref.shape
    zs, chunks = edge_ref.shape[:2]
    edge = jnp.concatenate(
        [edge_ref[z, r, 0] for r in range(chunks) for z in range(zs)]
    ).astype(f32)
    root = lax.rsqrt(edge[:, 1:] - edge[:, :1])
    total = jnp.zeros((rows, 1), f32)
    for first in range(0, width, DH):
        at = slice(first, first + DH)
        summed = sum(s[0, :, at].astype(f32) for s in sums)
        product = q_ref[:, at].astype(f32) * rest_ref[0, :, at].astype(f32)
        weight = silu(jnp.sum(product, axis=1, keepdims=True) * DH ** (-0.5))
        value = summed * root + weight * rest_ref[1, :, at].astype(f32)
        att_ref[:, at] = value
        total += jnp.sum(value, axis=1, keepdims=True)
    mean = total / width
    spread = jnp.zeros((rows, DH), f32)
    for first in range(0, width, DH):
        away = att_ref[:, first:first + DH] - mean
        spread += away * away
    square = jnp.sum(spread, axis=1, keepdims=True)
    if others:
        means, squares = stat_columns(others)
        mean, square = merge([mean] + means, [square] + squares, [width] + widths)
    lane = lax.broadcasted_iota(jnp.int32, (rows, DH), 1)
    stat = jnp.where(lane < 4, mean, square)
    stat_ref[...] = stat if stat_ref.shape == stat.shape else stat.T[:8]


def finish(at, edges, query, rest, sums, others, widths, after):
    rows, width = query.shape
    stat = (8, rows) if others and rows == DH else (rows, DH)
    return pl.pallas_call(
        functools.partial(finish_kernel, len(sums), widths),
        grid_spec=pltpu.PrefetchScalarGridSpec(
            num_scalar_prefetch=1,
            grid=(1,),
            in_specs=[
                edge_spec(edges, 0),
                pl.BlockSpec((rows, width), lambda j, at: (0, 0)),
                pl.BlockSpec((2, rows, width), lambda j, at: (0, 0, 0)),
            ]
            + [pl.BlockSpec((1, rows, width), lambda j, at: (0, 0, 0))] * len(sums)
            + [pl.BlockSpec((rows, DH), lambda j, at: (0, 0))] * len(others)
            + anywhere(after),
            out_specs=(
                pl.BlockSpec((rows, width), lambda j, at: (0, 0)),
                pl.BlockSpec(stat, lambda j, at: (0, 0)),
            ),
        ),
        out_shape=(
            jax.ShapeDtypeStruct((rows, width), f32),
            jax.ShapeDtypeStruct(stat, f32),
        ),
        compiler_params=params(),
        cost_estimate=LIGHT,
        name="finish",
    )(at, edges, query, rest, *sums, *others, *after)


def gate_kernel(count, parts, *refs):
    stats, atts, rests, outs = (
        refs[:count], refs[count:count + parts],
        refs[count + parts:count + 2 * parts], refs[count + 2 * parts:],
    )
    width = sum(a.shape[1] for a in atts)
    means, squares = stat_columns(stats)
    mean, square = merge(means, squares, [width] * count)
    scale = lax.rsqrt(square / (width * count) + EPSILON)
    rows, column = outs[0].shape[0], 0
    for att, rest in zip(atts, rests):
        span = att.shape[1]
        normed = (att[...] - mean) * scale
        gated = (normed * rest[0].astype(f32)).astype(bf16)
        for r, out in enumerate(outs):
            out[:, column:column + span] = gated[r * rows:(r + 1) * rows]
        column += span


def gate_rows(stats, atts, rests, chunks):
    rows, width = atts[0].shape[0], sum(a.shape[1] for a in atts)
    return pl.pallas_call(
        functools.partial(gate_kernel, len(stats), len(atts)),
        grid=(1,),
        in_specs=[pl.BlockSpec(s.shape, lambda j: (0, 0)) for s in stats]
        + [pl.BlockSpec((rows, a.shape[1]), lambda j: (0, 0)) for a in atts]
        + [pl.BlockSpec((1, rows, r.shape[2]), lambda j: (2, 0, 0)) for r in rests],
        out_specs=[pl.BlockSpec((rows // chunks, width), lambda j: (0, 0))] * chunks,
        out_shape=[jax.ShapeDtypeStruct((rows // chunks, width), bf16)] * chunks,
        compiler_params=params(),
        cost_estimate=LIGHT,
        name="gate",
    )(*stats, *atts, *rests)


def output_kernel(owners, slots, index_ref, *refs):
    rows, w_ref, (keep_ref, send_ref, lhs_ref) = refs[:owners], refs[owners], refs[-3:]
    piece, half = rows[0].shape[1], len(slots) // 2

    @pl.when(pl.program_id(0) == 0)
    def _():
        first = 0
        for slot in slots:
            for p in range(owners):
                lhs_ref[first:first + piece, :] = rows[p][index_ref[0] ^ slot]
                first += piece

    sums = jnp.dot(lhs_ref[...], w_ref[...], preferred_element_type=f32).astype(bf16)
    for k in range(len(slots)):
        into = keep_ref if k < half else send_ref
        for p in range(owners):
            first = (k * owners + p) * piece
            into[k % half, p] = sums[first:first + piece]


def output(index, blocks, w_out, slots, column, columns, after):
    owners, (each, width) = len(blocks), blocks[0].shape
    zs = len(slots)
    piece = each // zs
    span = 512 if columns % 512 == 0 else columns
    row_spec = pl.BlockSpec((zs, piece, width), lambda j, at: (0, 0, 0))
    spec = pl.BlockSpec((zs // 2, owners, piece, span), lambda j, at: (0, 0, 0, j))
    shape = jax.ShapeDtypeStruct((zs // 2, owners, piece, columns), bf16)
    return pl.pallas_call(
        functools.partial(output_kernel, owners, slots),
        grid_spec=pltpu.PrefetchScalarGridSpec(
            num_scalar_prefetch=1,
            grid=(columns // span,),
            in_specs=[row_spec] * owners
            + [pl.BlockSpec((width, span), lambda j, at: (0, column // span + j))]
            + anywhere(after),
            out_specs=(spec, spec),
            scratch_shapes=[pltpu.VMEM((owners * each, width), bf16)],
        ),
        out_shape=(shape, shape),
        compiler_params=params(),
        cost_estimate=LIGHT,
        name="output",
    )(
        index.reshape(1).astype(jnp.int32),
        *[b.reshape(zs, piece, width) for b in blocks], far(w_out), *after,
    )


def close_kernel(counts, at_ref, t_ref, *refs):
    out_ref, first = refs[-1], 0
    owners = refs[0].shape[1]
    for r, row in enumerate(counts):
        column = 0
        for count in row:
            terms = refs[first:first + count]
            first += count
            span = terms[0].shape[-1]
            for p in range(owners):
                total = t_ref[r * owners + p, :, column:column + span].astype(f32)
                for term in terms:
                    total = total + term[0, p ^ at_ref[0]].astype(f32)
                out_ref[r * owners + p, :, column:column + span] = total.astype(bf16)
            column += span


def close(place, index, tokens, chunks):
    _, owners, piece, _ = chunks[0][0][0].shape
    blocks, width = len(chunks) * owners, sum(terms[0].shape[-1] for terms in chunks[0])
    flat = [term for row in chunks for terms in row for term in terms]
    return pl.pallas_call(
        functools.partial(close_kernel, [[len(terms) for terms in row] for row in chunks]),
        grid_spec=pltpu.PrefetchScalarGridSpec(
            num_scalar_prefetch=1,
            grid=(1,),
            in_specs=[pl.BlockSpec((blocks, piece, width), lambda j, at: (at[1], 0, 0))]
            + [pl.BlockSpec((1,) + t.shape[1:], lambda j, at: (0, 0, 0, 0)) for t in flat],
            out_specs=pl.BlockSpec((blocks, piece, width), lambda j, at: (0, 0, 0)),
        ),
        out_shape=jax.ShapeDtypeStruct((blocks, piece, width), bf16),
        compiler_params=params(),
        cost_estimate=LIGHT,
        name="close",
    )(
        jnp.stack([place, index]).astype(jnp.int32),
        far(tokens.reshape(-1, piece, width)),
        *flat,
    )


def bits_of(axis):
    count = lax.axis_size(axis)
    assert count & (count - 1) == 0
    return count.bit_length() - 1


def reverse(index, bits):
    return sum((((index >> b) & 1) << (bits - 1 - b) for b in range(bits)), 0 * index)


def swap(x, axis, bit):
    return lax.ppermute(
        x, axis, [(i, i ^ (1 << bit)) for i in range(lax.axis_size(axis))]
    )


def scatter(keep, got, axis, after=()):
    terms, sent = [keep, got], got
    for b in range(1, bits_of(axis)):
        sent = fold(terms, after)
        terms.append(swap(sent, axis, b))
    return terms, sent


def gather(x, axis):
    blocks = [x]
    for b in reversed(range(bits_of(axis))):
        blocks = blocks + [swap(block, axis, b) for block in blocks]
    return blocks


def all_stats(stat, axis):
    count = lax.axis_size(axis)
    if count > 8:
        every = lax.all_gather(stat, axis)
        return [every[i] for i in range(count)]
    return [stat] + [
        lax.ppermute(stat, axis, [(i, (i + k) % count) for i in range(count)])
        for k in range(1, count)
    ]


def head_chunks(heads):
    if heads % 8:
        return [1] * heads
    unit = heads // 8
    return [unit, 2 * unit, 2 * unit, 2 * unit, unit]


ORDER = [
    "P0", "P1", "F0", "P2", "F1", "A0", "P3", "F2", "P4", "A1", "F3", "T0", "A2", "F4", "T1",
    "A3", "G0", "G1", "T2", "A4", "E0", "E1", "T3", "G2", "T4", "G3", "E2", "G4", "E3", "E4",
]


def local(tokens, w_qkvu, k_cache, v_cache, w_out, vis_start, vis_end):
    cand, depth = tokens.shape
    owners, zs = lax.axis_size("hist"), lax.axis_size("head")
    index = lax.axis_index("head")
    place = reverse(lax.axis_index("hist"), bits_of("hist"))
    width = w_qkvu.shape[2]
    events = k_cache.shape[0]
    chunks = 2 if cand % (2 * owners * zs * 16) == 0 else 1
    piece = cand // (zs * chunks * owners)

    def arrange(x):
        x = x.reshape((zs, chunks, owners, piece) + x.shape[1:])
        if piece % 16 == 0:
            return x
        blocks = [lax.dynamic_index_in_dim(x, p ^ place, 2, False) for p in range(owners)]
        x = jnp.stack(blocks).swapaxes(1, 2)
        return x.reshape((1, 1, owners, zs * chunks * piece) + x.shape[4:])

    at = (place if piece % 16 == 0 else jnp.int32(0)).reshape(1)
    ordered = arrange(tokens)
    first_event = lax.axis_index("hist") * events
    edges = arrange(jnp.stack([vis_start - first_event, vis_end - first_event], axis=1))

    sizes = head_chunks(width // DH)
    firsts = [sum(sizes[:c]) for c in range(len(sizes))]
    last = len(sizes) - 1
    order = ORDER
    if last != 4:
        order = [step + str(c) for step in "PFATGE" for c in range(last + 1)]
    chain, terms, sums, halves, queries, parts, atts, stats = [], {}, {}, {}, {}, {}, {}, {}
    for step, c in [(name[0], int(name[1:])) for name in order]:
        after = chain[-1:]
        if step == "P":
            keep, send = project(at, ordered, w_qkvu, firsts[c], sizes[c], after)
            before = [terms[c - 1][1]] if c >= 1 else []
            before += [terms[c - 2][-1]] if c - 2 in terms and len(terms[c - 2]) > 2 else []
            before += [queries[0][1]] if c == last and 0 in queries else []
            terms[c] = [keep, swap(tie(send, before), "hist", 0)]
            chain.append(keep)
        elif step == "F":
            terms[c], sent = scatter(*terms[c], "hist", after)
            chain.append(sent)
        elif step == "A":
            parts[c] = activate(terms[c], after)
            queries[c] = gather(parts[c][0], "hist")
            chain.append(parts[c][0])
        elif step == "T":
            keep, send = attend(at, queries[c], k_cache, v_cache, edges, firsts[c], after)
            halves[c] = keep, swap(send, "hist", 0)
            chain.append(keep)
        elif step == "G":
            sums[c], sent = scatter(*halves[c], "hist", after)
            chain.append(sent)
        else:
            others = [stats[k] for k in range(last)] if c == last else []
            widths = [size * DH for size in sizes[:last]] if c == last else []
            atts[c], stats[c] = finish(at, edges, *parts[c], sums[c], others, widths, after)
            chain.append(atts[c])

    atts = [atts[c] for c in range(last + 1)]
    rests = [parts[c][1] for c in range(last + 1)]
    gated = gate_rows(all_stats(stats[last], "head"), atts, rests, chunks)
    columns = w_out.shape[1]
    straight = piece % 16 == 0 and zs & (zs - 1) == 0
    groups = 2 if straight and columns % 1024 == 0 else 1
    results, sends, first_steps, ends = [], [], [], []
    for rows in gated:
        blocks = gather(rows, "hist")
        results.append([])
        for g in range(groups):
            if straight:
                slots = [reverse(k, bits_of("head")) for k in range(zs)]
                span = columns // groups
                keep, send = output(index, blocks, w_out, slots, g * span, span, sends[-1:])
                before = first_steps[-2:-1] + ends[-3:-2]
                send = tie(send, before)
                sends.append(send)
                terms, _ = scatter(keep, swap(send, "head", 0), "head")
                first_steps.append(terms[1])
                ends.append(terms[-1])
            else:
                whole = jnp.dot(jnp.concatenate(blocks), w_out, preferred_element_type=f32)
                whole = whole.astype(bf16).reshape(owners, zs, piece, -1).swapaxes(0, 1)
                terms = [lax.psum_scatter(whole, "head", scatter_dimension=0, tiled=True)]
            results[-1].append(terms)
    out = close(place, index, tokens, results)
    return out.reshape(cand // zs, -1)


def solution(mesh):
    in_specs = (
        P("groups", "hist"),
        P("hist", None, "head"),
        P(("groups", "hist"), "head"),
        P(("groups", "hist"), "head"),
        P("head", "hist"),
        P("groups"),
        P("groups"),
    )
    out_specs = P(("groups", "head"), "hist")
    return jax.shard_map(local, mesh=mesh, in_specs=in_specs, out_specs=out_specs, check_vma=False)
```

```python
import functools

import jax
import jax.numpy as jnp
from jax import lax
from jax.experimental import pallas as pl
from jax.experimental.pallas import tpu as pltpu
from jax.sharding import PartitionSpec as P

DH = 128
EPSILON = 1e-05
VMEM_LIMIT = 28 * 1024 * 1024

bf16 = jnp.bfloat16
f32 = jnp.float32


def silu(v):
    u = 0.5 * v
    return u + u * jnp.tanh(u)


def params():
    return pltpu.CompilerParams(vmem_limit_bytes=VMEM_LIMIT)


LIGHT = pl.CostEstimate(flops=1000, bytes_accessed=1000, transcendentals=0)


def far(x):
    return pltpu.with_memory_space_constraint(x, pltpu.HBM)


def anywhere(arrays):
    return [pl.BlockSpec(memory_space=pl.ANY)] * len(arrays)


def project_kernel(parts, owners, after, at_ref, *refs):
    rows, weights = refs[:owners], refs[owners:owners + parts]
    outs, lhs_ref = refs[owners + parts + after:-parts - 1], refs[-parts - 1]
    wides = refs[-parts:]
    zs, chunks, _, piece, _ = rows[0].shape
    depth = weights[0].shape[0]

    @pl.when(pl.program_id(0) == 0)
    def _():
        first = 0
        for p in range(owners):
            for r in range(chunks):
                for z in range(zs):
                    lhs_ref[first:first + piece, :] = rows[p][z, r, 0]
                    first += piece

    res = None
    for k, wide in enumerate(wides):
        wide[...] = weights[k].reshape(depth * 4, DH)[...].astype(f32)
        rhs = jnp.concatenate(
            [wide[pl.ds(i, depth, stride=4), :].astype(bf16) for i in range(4)], axis=1
        )
        term = jnp.dot(lhs_ref[:, k * depth:(k + 1) * depth], rhs, preferred_element_type=f32)
        res = term if res is None else res + term
    res = res.astype(bf16)
    each, first = outs[0].shape[2], 0
    for out in outs:
        for p in range(out.shape[0]):
            for i in range(4):
                out[p, i] = res[first:first + each, i * DH:(i + 1) * DH]
            first += each


def project(at, tokens, w, head_first, heads, after):
    zs, chunks, owners, piece, depth = tokens.shape
    half, each = owners // 2, zs * chunks * piece
    parts = 4 if depth % 512 == 0 else 1
    counts = [half] + ([half // 2] * 2 if half > 1 else [half])
    return pl.pallas_call(
        functools.partial(project_kernel, parts, owners, len(after)),
        grid_spec=pltpu.PrefetchScalarGridSpec(
            num_scalar_prefetch=1,
            grid=(heads,),
            in_specs=[
                pl.BlockSpec(
                    (zs, chunks, 1, piece, depth), lambda j, at, p=p: (0, 0, at[0] ^ p, 0, 0)
                )
                for p in range(owners)
            ]
            + [
                pl.BlockSpec((depth // parts, 4, DH), lambda j, at, k=k: (k, 0, head_first + j))
                for k in range(parts)
            ]
            + anywhere(after),
            out_specs=[
                pl.BlockSpec((n, 4, each, DH), lambda j, at: (0, 0, 0, j)) for n in counts
            ],
            scratch_shapes=[pltpu.VMEM((owners * each, depth), bf16)]
            + [pltpu.VMEM((depth // parts * 4, DH), f32) for _ in range(parts)],
        ),
        out_shape=[jax.ShapeDtypeStruct((n, 4, each, heads * DH), bf16) for n in counts],
        compiler_params=params(),
        cost_estimate=LIGHT,
        name="project",
    )(at, *[far(tokens)] * owners, *[far(w)] * parts, *after)


def tie_kernel(*refs):
    pass


def tie(x, after):
    if not after:
        return x
    return pl.pallas_call(
        tie_kernel,
        in_specs=anywhere([x, *after]),
        out_specs=pl.BlockSpec(memory_space=pl.ANY),
        out_shape=jax.ShapeDtypeStruct(x.shape, x.dtype),
        input_output_aliases={0: 0},
        compiler_params=params(),
        cost_estimate=LIGHT,
        name="tie",
    )(x, *after)


def fold_kernel(count, *refs):
    refs[-1][...] = sum(r[...].astype(f32) for r in refs[:count]).astype(bf16)


def fold(terms, after=()):
    half = terms[0].shape[0] // 2 if len(terms) == 2 else terms[-1].shape[0] // 2
    tail = terms[0].shape[1:]
    steps = 2 if tail[-1] % 256 == 0 else 1
    block = (half,) + tail[:-1] + (tail[-1] // steps,)
    middle = (0,) * (len(tail) - 1)
    firsts = [0 if t.shape[0] == half else 1 for t in terms]
    return pl.pallas_call(
        functools.partial(fold_kernel, len(terms)),
        grid=(steps,),
        in_specs=[pl.BlockSpec(block, lambda j, f=f: (f,) + middle + (j,)) for f in firsts]
        + anywhere(after),
        out_specs=pl.BlockSpec(block, lambda j: (0,) + middle + (j,)),
        out_shape=jax.ShapeDtypeStruct((half,) + tail, bf16),
        compiler_params=params(),
        cost_estimate=LIGHT,
        name="fold",
    )(*terms, *after)


def activate_kernel(counts, *refs):
    q_ref, rest_ref = refs[-2:]
    first, column = 0, 0
    for count in counts:
        terms = refs[first:first + count]
        span = terms[0].shape[-1]
        for i in range(4):
            part = silu(sum(t[0, i].astype(f32) for t in terms)).astype(bf16)
            if i == 0:
                q_ref[:, column:column + span] = part
            else:
                rest_ref[i - 1, :, column:column + span] = part
        first += count
        column += span


def activate(chunks, after):
    each, width = chunks[0][0].shape[2], sum(terms[0].shape[3] for terms in chunks)
    flat = [term for terms in chunks for term in terms]
    return pl.pallas_call(
        functools.partial(activate_kernel, [len(terms) for terms in chunks]),
        grid=(1,),
        in_specs=[pl.BlockSpec((1,) + t.shape[1:], lambda j: (0, 0, 0, 0)) for t in flat]
        + anywhere(after),
        out_specs=(
            pl.BlockSpec((each, width), lambda j: (0, 0)),
            pl.BlockSpec((3, each, width), lambda j: (0, 0, 0)),
        ),
        out_shape=(
            jax.ShapeDtypeStruct((each, width), bf16),
            jax.ShapeDtypeStruct((3, each, width), bf16),
        ),
        compiler_params=params(),
        cost_estimate=LIGHT,
        name="activate",
    )(*flat, *after)


def edge_kernel(base_ref, start_ref, end_ref, out_ref):
    row = lax.broadcasted_iota(jnp.int32, (DH, DH), 0)
    for b in range(start_ref.shape[0]):
        start, end = start_ref[b:b + 1, :], end_ref[b:b + 1, :]
        both = jnp.where(row == 0, start, end) - base_ref[0]
        out_ref[b * DH:(b + 1) * DH, :] = both.astype(f32).T[:, :2].astype(jnp.int32)


def edge_columns(base, start, end):
    count = start.shape[0]
    lines = pl.BlockSpec((count // DH, DH), lambda j, base: (0, 0))
    return pl.pallas_call(
        edge_kernel,
        grid_spec=pltpu.PrefetchScalarGridSpec(
            num_scalar_prefetch=1,
            grid=(1,),
            in_specs=[lines, lines],
            out_specs=pl.BlockSpec((count, 2), lambda j, base: (0, 0)),
        ),
        out_shape=jax.ShapeDtypeStruct((count, 2), jnp.int32),
        compiler_params=params(),
        cost_estimate=LIGHT,
        name="edges",
    )(base.reshape(1), start.reshape(-1, DH), end.reshape(-1, DH))


def attend_kernel(owners, at_ref, *refs):
    queries, edges = refs[:owners], refs[owners:2 * owners]
    k_ref, v_ref = refs[2 * owners:2 * owners + 2]
    keep_ref, send_ref, mask_ref = refs[-3:]
    events = mask_ref.shape[1]
    half, each, _ = keep_ref.shape

    @pl.when(pl.program_id(0) == 0)
    def _():
        zs, chunks, _, piece, _ = edges[0].shape
        at = lax.broadcasted_iota(jnp.int32, (piece, events), 1)
        first = 0
        for p in range(owners):
            for r in range(chunks):
                for z in range(zs):
                    edge = edges[p][z, r, 0]
                    seen = (at >= edge[:, :1]) & (at < edge[:, 1:])
                    mask_ref[first:first + piece, :] = jnp.where(seen, 1.0, 0.0).astype(bf16)
                    first += piece

    for h in range(k_ref.shape[1] // DH):
        at = slice(h * DH, (h + 1) * DH)
        query = jnp.concatenate([q[:, at] for q in queries])
        u = lax.dot_general(
            query, k_ref[:, at], (((1,), (1,)), ((), ())), preferred_element_type=f32
        ) * (0.5 * DH ** (-0.5))
        weights = (u + u * jnp.tanh(u)).astype(bf16) * mask_ref[...]
        term = jnp.dot(weights, v_ref[:, at], preferred_element_type=f32).astype(bf16)
        for p in range(owners):
            into = keep_ref if p < half else send_ref
            into[p % half, :, at] = term[p * each:(p + 1) * each]


def edge_spec(edges, p):
    zs, chunks, _, piece, ends = edges.shape
    return pl.BlockSpec((zs, chunks, 1, piece, ends), lambda j, at: (0, 0, at[0] ^ p, 0, 0))


def attend(at, queries, k_cache, v_cache, edges, head_first, after):
    owners, (each, width) = len(queries), queries[0].shape
    rows, events, half = owners * each, k_cache.shape[0], owners // 2
    first = head_first * DH
    span = max(h for h in range(DH, 4 * DH, DH) if width % h == 0 and first % h == 0)
    cache = pl.BlockSpec((events, span), lambda j, at: (0, first // span + j))
    shape = jax.ShapeDtypeStruct((half, each, width), bf16)
    spec = pl.BlockSpec((half, each, span), lambda j, at: (0, 0, j))
    return pl.pallas_call(
        functools.partial(attend_kernel, owners),
        grid_spec=pltpu.PrefetchScalarGridSpec(
            num_scalar_prefetch=1,
            grid=(width // span,),
            in_specs=[pl.BlockSpec((each, span), lambda j, at: (0, j))] * owners
            + [edge_spec(edges, p) for p in range(owners)]
            + [cache, cache]
            + anywhere(after),
            out_specs=(spec, spec),
            scratch_shapes=[pltpu.VMEM((rows, events), bf16)],
        ),
        out_shape=(shape, shape),
        compiler_params=params(),
        cost_estimate=LIGHT,
        name="attend",
    )(at, *queries, *[edges] * owners, far(k_cache), far(v_cache), *after)


def merge(means, squares, widths):
    width = sum(widths)
    mean = sum(m * (w / width) for m, w in zip(means, widths))
    square = sum(squares) + sum(w * (m - mean) * (m - mean) for m, w in zip(means, widths))
    return mean, square


def stat_columns(stats):
    stats = [s[...] for s in stats]
    stats = [s if s.shape[0] > 8 else jnp.concatenate([s] * (DH // 8)).T for s in stats]
    return [s[:, :1] for s in stats], [s[:, 4:5] for s in stats]


def finish_kernel(terms, widths, at_ref, edge_ref, q_ref, rest_ref, *refs):
    sums, others = refs[:terms], refs[terms:terms + len(widths)]
    att_ref, stat_ref = refs[-2:]
    rows, width = att_ref.shape
    zs, chunks = edge_ref.shape[:2]
    edge = jnp.concatenate(
        [edge_ref[z, r, 0] for r in range(chunks) for z in range(zs)]
    ).astype(f32)
    root = lax.rsqrt(edge[:, 1:] - edge[:, :1])
    total = jnp.zeros((rows, 1), f32)
    for first in range(0, width, DH):
        at = slice(first, first + DH)
        summed = sum(s[0, :, at].astype(f32) for s in sums)
        product = q_ref[:, at].astype(f32) * rest_ref[0, :, at].astype(f32)
        weight = silu(jnp.sum(product, axis=1, keepdims=True) * DH ** (-0.5))
        value = summed * root + weight * rest_ref[1, :, at].astype(f32)
        att_ref[:, at] = value
        total += jnp.sum(value, axis=1, keepdims=True)
    mean = total / width
    spread = jnp.zeros((rows, DH), f32)
    for first in range(0, width, DH):
        away = att_ref[:, first:first + DH] - mean
        spread += away * away
    square = jnp.sum(spread, axis=1, keepdims=True)
    if others:
        means, squares = stat_columns(others)
        mean, square = merge([mean] + means, [square] + squares, [width] + widths)
    lane = lax.broadcasted_iota(jnp.int32, (rows, DH), 1)
    stat = jnp.where(lane < 4, mean, square)
    stat_ref[...] = stat if stat_ref.shape == stat.shape else stat.T[:8]


def finish(at, edges, query, rest, sums, others, widths, after):
    rows, width = query.shape
    stat = (8, rows) if others and rows == DH else (rows, DH)
    return pl.pallas_call(
        functools.partial(finish_kernel, len(sums), widths),
        grid_spec=pltpu.PrefetchScalarGridSpec(
            num_scalar_prefetch=1,
            grid=(1,),
            in_specs=[
                edge_spec(edges, 0),
                pl.BlockSpec((rows, width), lambda j, at: (0, 0)),
                pl.BlockSpec((2, rows, width), lambda j, at: (0, 0, 0)),
            ]
            + [pl.BlockSpec((1, rows, width), lambda j, at: (0, 0, 0))] * len(sums)
            + [pl.BlockSpec((rows, DH), lambda j, at: (0, 0))] * len(others)
            + anywhere(after),
            out_specs=(
                pl.BlockSpec((rows, width), lambda j, at: (0, 0)),
                pl.BlockSpec(stat, lambda j, at: (0, 0)),
            ),
        ),
        out_shape=(
            jax.ShapeDtypeStruct((rows, width), f32),
            jax.ShapeDtypeStruct(stat, f32),
        ),
        compiler_params=params(),
        cost_estimate=LIGHT,
        name="finish",
    )(at, edges, query, rest, *sums, *others, *after)


def gate_kernel(count, parts, *refs):
    stats, atts, rests, outs = (
        refs[:count], refs[count:count + parts],
        refs[count + parts:count + 2 * parts], refs[count + 2 * parts:],
    )
    width = sum(a.shape[1] for a in atts)
    means, squares = stat_columns(stats)
    mean, square = merge(means, squares, [width] * count)
    scale = lax.rsqrt(square / (width * count) + EPSILON)
    rows, column = outs[0].shape[0], 0
    for att, rest in zip(atts, rests):
        span = att.shape[1]
        normed = (att[...] - mean) * scale
        gated = (normed * rest[0].astype(f32)).astype(bf16)
        for r, out in enumerate(outs):
            out[:, column:column + span] = gated[r * rows:(r + 1) * rows]
        column += span


def gate_rows(stats, atts, rests, chunks):
    rows, width = atts[0].shape[0], sum(a.shape[1] for a in atts)
    return pl.pallas_call(
        functools.partial(gate_kernel, len(stats), len(atts)),
        grid=(1,),
        in_specs=[pl.BlockSpec(s.shape, lambda j: (0, 0)) for s in stats]
        + [pl.BlockSpec((rows, a.shape[1]), lambda j: (0, 0)) for a in atts]
        + [pl.BlockSpec((1, rows, r.shape[2]), lambda j: (2, 0, 0)) for r in rests],
        out_specs=[pl.BlockSpec((rows // chunks, width), lambda j: (0, 0))] * chunks,
        out_shape=[jax.ShapeDtypeStruct((rows // chunks, width), bf16)] * chunks,
        compiler_params=params(),
        cost_estimate=LIGHT,
        name="gate",
    )(*stats, *atts, *rests)


def output_kernel(owners, slots, index_ref, *refs):
    rows, w_ref, (keep_ref, send_ref, lhs_ref) = refs[:owners], refs[owners], refs[-3:]
    piece, half = rows[0].shape[1], len(slots) // 2

    @pl.when(pl.program_id(0) == 0)
    def _():
        first = 0
        for slot in slots:
            for p in range(owners):
                lhs_ref[first:first + piece, :] = rows[p][index_ref[0] ^ slot]
                first += piece

    sums = jnp.dot(lhs_ref[...], w_ref[...], preferred_element_type=f32).astype(bf16)
    for k in range(len(slots)):
        into = keep_ref if k < half else send_ref
        for p in range(owners):
            first = (k * owners + p) * piece
            into[k % half, p] = sums[first:first + piece]


def output(index, blocks, w_out, slots, column, columns, after):
    owners, (each, width) = len(blocks), blocks[0].shape
    zs = len(slots)
    piece = each // zs
    span = max(c for c in (512, 256, columns) if columns % c == 0 and column % c == 0)
    row_spec = pl.BlockSpec((zs, piece, width), lambda j, at: (0, 0, 0))
    spec = pl.BlockSpec((zs // 2, owners, piece, span), lambda j, at: (0, 0, 0, j))
    shape = jax.ShapeDtypeStruct((zs // 2, owners, piece, columns), bf16)
    return pl.pallas_call(
        functools.partial(output_kernel, owners, slots),
        grid_spec=pltpu.PrefetchScalarGridSpec(
            num_scalar_prefetch=1,
            grid=(columns // span,),
            in_specs=[row_spec] * owners
            + [pl.BlockSpec((width, span), lambda j, at: (0, column // span + j))]
            + anywhere(after),
            out_specs=(spec, spec),
            scratch_shapes=[pltpu.VMEM((owners * each, width), bf16)],
        ),
        out_shape=(shape, shape),
        compiler_params=params(),
        cost_estimate=LIGHT,
        name="output",
    )(
        index.reshape(1).astype(jnp.int32),
        *[b.reshape(zs, piece, width) for b in blocks], far(w_out), *after,
    )


def close_kernel(counts, at_ref, t_ref, *refs):
    out_ref, first = refs[-1], 0
    owners = refs[0].shape[1]
    for r, row in enumerate(counts):
        column = 0
        for count in row:
            terms = refs[first:first + count]
            first += count
            span = terms[0].shape[-1]
            for p in range(owners):
                total = t_ref[r * owners + p, :, column:column + span].astype(f32)
                for term in terms:
                    total = total + term[0, p ^ at_ref[0]].astype(f32)
                out_ref[r * owners + p, :, column:column + span] = total.astype(bf16)
            column += span


def close(place, index, tokens, chunks):
    _, owners, piece, _ = chunks[0][0][0].shape
    blocks, width = len(chunks) * owners, sum(terms[0].shape[-1] for terms in chunks[0])
    flat = [term for row in chunks for terms in row for term in terms]
    return pl.pallas_call(
        functools.partial(close_kernel, [[len(terms) for terms in row] for row in chunks]),
        grid_spec=pltpu.PrefetchScalarGridSpec(
            num_scalar_prefetch=1,
            grid=(1,),
            in_specs=[pl.BlockSpec((blocks, piece, width), lambda j, at: (at[1], 0, 0))]
            + [pl.BlockSpec((1,) + t.shape[1:], lambda j, at: (0, 0, 0, 0)) for t in flat],
            out_specs=pl.BlockSpec((blocks, piece, width), lambda j, at: (0, 0, 0)),
        ),
        out_shape=jax.ShapeDtypeStruct((blocks, piece, width), bf16),
        compiler_params=params(),
        cost_estimate=LIGHT,
        name="close",
    )(
        jnp.stack([place, index]).astype(jnp.int32),
        far(tokens.reshape(-1, piece, width)),
        *flat,
    )


def bits_of(axis):
    count = lax.axis_size(axis)
    assert count & (count - 1) == 0
    return count.bit_length() - 1


def reverse(index, bits):
    return sum((((index >> b) & 1) << (bits - 1 - b) for b in range(bits)), 0 * index)


def swap(x, axis, bit):
    return lax.ppermute(
        x, axis, [(i, i ^ (1 << bit)) for i in range(lax.axis_size(axis))]
    )


def scatter(keep, gots, axis, after=()):
    terms, sent = [keep, gots[0]], gots[-1]
    for b in range(1, bits_of(axis)):
        sent = fold([keep, gots[-1]] if b == 1 else terms, after)
        terms.append(swap(sent, axis, b))
    return terms, sent


def gather(x, axis, after=()):
    blocks = [x]
    for b in reversed(range(bits_of(axis))):
        blocks = blocks + [swap(block, axis, b) for block in blocks]
        if len(blocks) == 2:
            blocks[1] = tie(blocks[1], after)
    return blocks


def all_stats(stat, axis):
    count = lax.axis_size(axis)
    if count > 8:
        every = lax.all_gather(stat, axis)
        return [every[i] for i in range(count)]
    return [stat] + [
        lax.ppermute(stat, axis, [(i, (i + k) % count) for i in range(count)])
        for k in range(1, count)
    ]


def head_chunks(heads):
    if heads % 8:
        return [1] * heads
    unit = heads // 8
    return [unit, 2 * unit, 2 * unit, 2 * unit, unit]


GROUPS = [[0, 1], [2], [3], [4]]
ORDER = [
    "P0", "P1", "F0", "P2", "F1", "P3", "F2", "A0", "F3", "P4", "A1", "F4", "T0", "G0", "A2",
    "T1", "A3", "G1", "E0", "T2", "G2", "T3", "E1", "G3", "E2", "E3",
]


def local(tokens, w_qkvu, k_cache, v_cache, w_out, vis_start, vis_end):
    cand, depth = tokens.shape
    owners, zs = lax.axis_size("hist"), lax.axis_size("head")
    index = lax.axis_index("head")
    place = reverse(lax.axis_index("hist"), bits_of("hist"))
    width = w_qkvu.shape[2]
    events = k_cache.shape[0]
    chunks = 2 if cand % (2 * owners * zs * 16) == 0 else 1
    piece = cand // (zs * chunks * owners)

    def arrange(x):
        x = x.reshape((zs, chunks, owners, piece) + x.shape[1:])
        if piece % 16 == 0:
            return x
        blocks = [lax.dynamic_index_in_dim(x, p ^ place, 2, False) for p in range(owners)]
        x = jnp.stack(blocks).swapaxes(1, 2)
        return x.reshape((1, 1, owners, zs * chunks * piece) + x.shape[4:])

    at = (place if piece % 16 == 0 else jnp.int32(0)).reshape(1)
    ordered = arrange(tokens)
    first_event = lax.axis_index("hist") * events
    edges = arrange(edge_columns(first_event, vis_start, vis_end))

    sizes = head_chunks(width // DH)
    firsts = [sum(sizes[:c]) for c in range(len(sizes))]
    groups, order = GROUPS, ORDER
    if len(sizes) != 5:
        groups = [[c] for c in range(len(sizes))]
        order = [step + str(c) for step in "PFATGE" for c in range(len(sizes))]
    last = len(groups) - 1
    heads = [sum(sizes[c] for c in group) for group in groups]
    chain, keeps, firsts_got, terms, sums = [], {}, {}, {}, {}
    halves, queries, parts, atts, stats = {}, {}, {}, {}, {}
    for step, c in [(name[0], int(name[1:])) for name in order]:
        after = chain[-1:]
        if step == "P":
            keep, *sends = project(at, ordered, w_qkvu, firsts[c], sizes[c], after)
            before = firsts_got[c - 1] if c >= 1 else []
            before = before + [terms[0][-1]] if c == 2 and 0 in terms else before
            firsts_got[c] = [swap(tie(send, before), "hist", 0) for send in reversed(sends)][::-1]
            keeps[c] = keep
            chain.append(keep)
        elif step == "F":
            terms[c], sent = scatter(keeps[c], firsts_got[c], "hist", after)
            chain.append(sent)
        elif step == "A":
            parts[c] = activate([terms[k] for k in groups[c]], after)
            queries[c] = gather(parts[c][0], "hist")
            chain.append(parts[c][0])
        elif step == "T":
            first = firsts[groups[c][0]]
            keep, send = attend(at, queries[c], k_cache, v_cache, edges, first, after)
            halves[c] = keep, [swap(send, "hist", 0)]
            chain.append(keep)
        elif step == "G":
            sums[c], sent = scatter(*halves[c], "hist", after)
            chain.append(sent)
        else:
            others = [stats[k] for k in range(last)] if c == last else []
            widths = [size * DH for size in heads[:last]] if c == last else []
            atts[c], stats[c] = finish(at, edges, *parts[c], sums[c], others, widths, after)
            chain.append(atts[c])

    atts = [atts[c] for c in range(last + 1)]
    rests = [parts[c][1] for c in range(last + 1)]
    gated = gate_rows(all_stats(stats[last], "head"), atts, rests, chunks)
    columns = w_out.shape[1]
    straight = piece % 16 == 0 and zs & (zs - 1) == 0
    results, sends, first_steps, ends = [], [], [], []
    for r, rows in enumerate(gated):
        results.append([])
        if not straight:
            blocks = gather(rows, "hist")
            whole = jnp.dot(jnp.concatenate(blocks), w_out, preferred_element_type=f32)
            whole = whole.astype(bf16).reshape(owners, zs, piece, -1).swapaxes(0, 1)
            whole = lax.psum_scatter(whole, "head", scatter_dimension=0, tiled=True)
            results[-1].append([whole])
            continue
        blocks = gather(rows, "hist", sends[-1:] + first_steps[:1])
        slots = [reverse(k, bits_of("head")) for k in range(zs)]
        unit = columns // 8
        spans = [columns]
        if unit % (2 * DH) == 0:
            spans = [4 * unit, 4 * unit] if r == 0 else [5 * unit, 3 * unit]
        for g, span in enumerate(spans):
            first = sum(spans[:g])
            keep, send = output(index, blocks, w_out, slots, first, span, sends[-1:])
            send = tie(send, first_steps[-2:-1] + ends[-3:-2])
            sends.append(send)
            terms, _ = scatter(keep, [swap(send, "head", 0)], "head")
            first_steps.append(terms[1])
            ends.append(terms[-1])
            results[-1].append(terms)
    out = close(place, index, tokens, results)
    return out.reshape(cand // zs, -1)


def solution(mesh):
    in_specs = (
        P("groups", "hist"),
        P("hist", None, "head"),
        P(("groups", "hist"), "head"),
        P(("groups", "hist"), "head"),
        P("head", "hist"),
        P("groups"),
        P("groups"),
    )
    out_specs = P(("groups", "head"), "hist")
    return jax.shard_map(local, mesh=mesh, in_specs=in_specs, out_specs=out_specs, check_vma=False)
```

```python
import functools

import jax
import jax.numpy as jnp
from jax import lax
from jax.experimental import pallas as pl
from jax.experimental.pallas import tpu as pltpu
from jax.sharding import PartitionSpec as P

DH = 128
EPSILON = 1e-05
VMEM_LIMIT = 28 * 1024 * 1024

bf16 = jnp.bfloat16
f32 = jnp.float32


def silu(v):
    u = 0.5 * v
    return u + u * jnp.tanh(u)


def params():
    return pltpu.CompilerParams(vmem_limit_bytes=VMEM_LIMIT)


LIGHT = pl.CostEstimate(flops=1000, bytes_accessed=1000, transcendentals=0)


def far(x):
    return pltpu.with_memory_space_constraint(x, pltpu.HBM)


def anywhere(arrays):
    return [pl.BlockSpec(memory_space=pl.ANY)] * len(arrays)


def project_kernel(parts, owners, after, at_ref, *refs):
    rows, weights = refs[:owners], refs[owners:owners + parts]
    outs, lhs_ref = refs[owners + parts + after:-parts - 1], refs[-parts - 1]
    wides = refs[-parts:]
    zs, chunks, _, piece, _ = rows[0].shape
    depth = weights[0].shape[0]

    @pl.when(pl.program_id(0) == 0)
    def _():
        first = 0
        for p in range(owners):
            for r in range(chunks):
                for z in range(zs):
                    lhs_ref[first:first + piece, :] = rows[p][z, r, 0]
                    first += piece

    res = None
    for k, wide in enumerate(wides):
        wide[...] = weights[k].reshape(depth * 4, DH)[...].astype(f32)
        rhs = jnp.concatenate(
            [wide[pl.ds(i, depth, stride=4), :].astype(bf16) for i in range(4)], axis=1
        )
        term = jnp.dot(lhs_ref[:, k * depth:(k + 1) * depth], rhs, preferred_element_type=f32)
        res = term if res is None else res + term
    res = res.astype(bf16)
    each, first = outs[0].shape[2], 0
    for out in outs:
        for p in range(out.shape[0]):
            for i in range(4):
                out[p, i] = res[first:first + each, i * DH:(i + 1) * DH]
            first += each


def parts_of(owners):
    half = owners // 2
    return [half, half // 2, half // 2] if half > 1 else [half, half]


def project(at, tokens, w, head_first, heads, after):
    zs, chunks, owners, piece, depth = tokens.shape
    each, counts = zs * chunks * piece, parts_of(owners)
    parts = 4 if depth % 512 == 0 else 1
    return pl.pallas_call(
        functools.partial(project_kernel, parts, owners, len(after)),
        grid_spec=pltpu.PrefetchScalarGridSpec(
            num_scalar_prefetch=1,
            grid=(heads,),
            in_specs=[
                pl.BlockSpec(
                    (zs, chunks, 1, piece, depth), lambda j, at, p=p: (0, 0, at[0] ^ p, 0, 0)
                )
                for p in range(owners)
            ]
            + [
                pl.BlockSpec((depth // parts, 4, DH), lambda j, at, k=k: (k, 0, head_first + j))
                for k in range(parts)
            ]
            + anywhere(after),
            out_specs=[
                pl.BlockSpec((n, 4, each, DH), lambda j, at: (0, 0, 0, j)) for n in counts
            ],
            scratch_shapes=[pltpu.VMEM((owners * each, depth), bf16)]
            + [pltpu.VMEM((depth // parts * 4, DH), f32) for _ in range(parts)],
        ),
        out_shape=[jax.ShapeDtypeStruct((n, 4, each, heads * DH), bf16) for n in counts],
        compiler_params=params(),
        cost_estimate=LIGHT,
        name="project",
    )(at, *[far(tokens)] * owners, *[far(w)] * parts, *after)


def tie_kernel(*refs):
    pass


def tie(x, after):
    if not after:
        return x
    return pl.pallas_call(
        tie_kernel,
        in_specs=anywhere([x, *after]),
        out_specs=pl.BlockSpec(memory_space=pl.ANY),
        out_shape=jax.ShapeDtypeStruct(x.shape, x.dtype),
        input_output_aliases={0: 0},
        compiler_params=params(),
        cost_estimate=LIGHT,
        name="tie",
    )(x, *after)


def fold_kernel(count, *refs):
    refs[-1][...] = sum(r[...].astype(f32) for r in refs[:count]).astype(bf16)


def fold(terms, after=()):
    half = terms[0].shape[0] // 2 if len(terms) == 2 else terms[-1].shape[0] // 2
    tail = terms[0].shape[1:]
    steps = 2 if tail[-1] % 256 == 0 else 1
    block = (half,) + tail[:-1] + (tail[-1] // steps,)
    middle = (0,) * (len(tail) - 1)
    firsts = [0 if t.shape[0] == half else 1 for t in terms]
    return pl.pallas_call(
        functools.partial(fold_kernel, len(terms)),
        grid=(steps,),
        in_specs=[pl.BlockSpec(block, lambda j, f=f: (f,) + middle + (j,)) for f in firsts]
        + anywhere(after),
        out_specs=pl.BlockSpec(block, lambda j: (0,) + middle + (j,)),
        out_shape=jax.ShapeDtypeStruct((half,) + tail, bf16),
        compiler_params=params(),
        cost_estimate=LIGHT,
        name="fold",
    )(*terms, *after)


def activate_kernel(counts, *refs):
    q_ref, rest_ref = refs[-2:]
    first, column = 0, 0
    for count in counts:
        terms = refs[first:first + count]
        span = terms[0].shape[-1]
        for i in range(4):
            part = silu(sum(t[0, i].astype(f32) for t in terms)).astype(bf16)
            if i == 0:
                q_ref[:, column:column + span] = part
            else:
                rest_ref[i - 1, :, column:column + span] = part
        first += count
        column += span


def activate(chunks, after):
    each, width = chunks[0][0].shape[2], sum(terms[0].shape[3] for terms in chunks)
    flat = [term for terms in chunks for term in terms]
    return pl.pallas_call(
        functools.partial(activate_kernel, [len(terms) for terms in chunks]),
        grid=(1,),
        in_specs=[pl.BlockSpec((1,) + t.shape[1:], lambda j: (0, 0, 0, 0)) for t in flat]
        + anywhere(after),
        out_specs=(
            pl.BlockSpec((each, width), lambda j: (0, 0)),
            pl.BlockSpec((3, each, width), lambda j: (0, 0, 0)),
        ),
        out_shape=(
            jax.ShapeDtypeStruct((each, width), bf16),
            jax.ShapeDtypeStruct((3, each, width), bf16),
        ),
        compiler_params=params(),
        cost_estimate=LIGHT,
        name="activate",
    )(*flat, *after)


def edge_kernel(base_ref, start_ref, end_ref, out_ref):
    row = lax.broadcasted_iota(jnp.int32, (DH, DH), 0)
    for b in range(start_ref.shape[0]):
        start, end = start_ref[b:b + 1, :], end_ref[b:b + 1, :]
        both = jnp.where(row == 0, start, end) - base_ref[0]
        out_ref[b * DH:(b + 1) * DH, :] = both.astype(f32).T[:, :2].astype(jnp.int32)


def edge_columns(base, start, end):
    count = start.shape[0]
    lines = pl.BlockSpec((count // DH, DH), lambda j, base: (0, 0))
    return pl.pallas_call(
        edge_kernel,
        grid_spec=pltpu.PrefetchScalarGridSpec(
            num_scalar_prefetch=1,
            grid=(1,),
            in_specs=[lines, lines],
            out_specs=pl.BlockSpec((count, 2), lambda j, base: (0, 0)),
        ),
        out_shape=jax.ShapeDtypeStruct((count, 2), jnp.int32),
        compiler_params=params(),
        cost_estimate=LIGHT,
        name="edges",
    )(base.reshape(1), start.reshape(-1, DH), end.reshape(-1, DH))


def attend_kernel(owners, sends, at_ref, *refs):
    queries, edges = refs[:owners], refs[owners:2 * owners]
    k_ref, v_ref = refs[2 * owners:2 * owners + 2]
    outs, mask_ref = refs[-1 - sends:-1], refs[-1]
    events = mask_ref.shape[1]
    each = outs[0].shape[1]

    @pl.when(pl.program_id(0) == 0)
    def _():
        zs, chunks, _, piece, _ = edges[0].shape
        at = lax.broadcasted_iota(jnp.int32, (piece, events), 1)
        first = 0
        for p in range(owners):
            for r in range(chunks):
                for z in range(zs):
                    edge = edges[p][z, r, 0]
                    seen = (at >= edge[:, :1]) & (at < edge[:, 1:])
                    mask_ref[first:first + piece, :] = jnp.where(seen, 1.0, 0.0).astype(bf16)
                    first += piece

    for h in range(k_ref.shape[1] // DH):
        at = slice(h * DH, (h + 1) * DH)
        query = jnp.concatenate([q[:, at] for q in queries])
        u = lax.dot_general(
            query, k_ref[:, at], (((1,), (1,)), ((), ())), preferred_element_type=f32
        ) * (0.5 * DH ** (-0.5))
        weights = (u + u * jnp.tanh(u)).astype(bf16) * mask_ref[...]
        term = jnp.dot(weights, v_ref[:, at], preferred_element_type=f32).astype(bf16)
        first = 0
        for out in outs:
            for p in range(out.shape[0]):
                out[p, :, at] = term[first:first + each]
                first += each


def edge_spec(edges, p):
    zs, chunks, _, piece, ends = edges.shape
    return pl.BlockSpec((zs, chunks, 1, piece, ends), lambda j, at: (0, 0, at[0] ^ p, 0, 0))


def attend(at, queries, k_cache, v_cache, edges, head_first, after):
    owners, (each, width) = len(queries), queries[0].shape
    rows, events, counts = owners * each, k_cache.shape[0], parts_of(owners)
    first = head_first * DH
    span = max(h for h in range(DH, 4 * DH, DH) if width % h == 0 and first % h == 0)
    cache = pl.BlockSpec((events, span), lambda j, at: (0, first // span + j))
    return pl.pallas_call(
        functools.partial(attend_kernel, owners, len(counts)),
        grid_spec=pltpu.PrefetchScalarGridSpec(
            num_scalar_prefetch=1,
            grid=(width // span,),
            in_specs=[pl.BlockSpec((each, span), lambda j, at: (0, j))] * owners
            + [edge_spec(edges, p) for p in range(owners)]
            + [cache, cache]
            + anywhere(after),
            out_specs=[pl.BlockSpec((n, each, span), lambda j, at: (0, 0, j)) for n in counts],
            scratch_shapes=[pltpu.VMEM((rows, events), bf16)],
        ),
        out_shape=[jax.ShapeDtypeStruct((n, each, width), bf16) for n in counts],
        compiler_params=params(),
        cost_estimate=LIGHT,
        name="attend",
    )(at, *queries, *[edges] * owners, far(k_cache), far(v_cache), *after)


def merge(means, squares, widths):
    width = sum(widths)
    mean = sum(m * (w / width) for m, w in zip(means, widths))
    square = sum(squares) + sum(w * (m - mean) * (m - mean) for m, w in zip(means, widths))
    return mean, square


def stat_columns(stats):
    stats = [s[...] for s in stats]
    stats = [s if s.shape[0] > 8 else jnp.concatenate([s] * (DH // 8)).T for s in stats]
    return [s[:, :1] for s in stats], [s[:, 4:5] for s in stats]


def finish_kernel(terms, widths, at_ref, edge_ref, q_ref, rest_ref, *refs):
    sums, others = refs[:terms], refs[terms:terms + len(widths)]
    att_ref, stat_ref = refs[-2:]
    rows, width = att_ref.shape
    zs, chunks = edge_ref.shape[:2]
    edge = jnp.concatenate(
        [edge_ref[z, r, 0] for r in range(chunks) for z in range(zs)]
    ).astype(f32)
    root = lax.rsqrt(edge[:, 1:] - edge[:, :1])
    total = jnp.zeros((rows, 1), f32)
    for first in range(0, width, DH):
        at = slice(first, first + DH)
        summed = sum(s[0, :, at].astype(f32) for s in sums)
        product = q_ref[:, at].astype(f32) * rest_ref[0, :, at].astype(f32)
        weight = silu(jnp.sum(product, axis=1, keepdims=True) * DH ** (-0.5))
        value = summed * root + weight * rest_ref[1, :, at].astype(f32)
        att_ref[:, at] = value
        total += jnp.sum(value, axis=1, keepdims=True)
    mean = total / width
    spread = jnp.zeros((rows, DH), f32)
    for first in range(0, width, DH):
        away = att_ref[:, first:first + DH] - mean
        spread += away * away
    square = jnp.sum(spread, axis=1, keepdims=True)
    if others:
        means, squares = stat_columns(others)
        mean, square = merge([mean] + means, [square] + squares, [width] + widths)
    lane = lax.broadcasted_iota(jnp.int32, (rows, DH), 1)
    stat = jnp.where(lane < 4, mean, square)
    stat_ref[...] = stat if stat_ref.shape == stat.shape else stat.T[:8]


def finish(at, edges, query, rest, sums, others, widths, after):
    rows, width = query.shape
    stat = (8, rows) if others and rows == DH else (rows, DH)
    return pl.pallas_call(
        functools.partial(finish_kernel, len(sums), widths),
        grid_spec=pltpu.PrefetchScalarGridSpec(
            num_scalar_prefetch=1,
            grid=(1,),
            in_specs=[
                edge_spec(edges, 0),
                pl.BlockSpec((rows, width), lambda j, at: (0, 0)),
                pl.BlockSpec((2, rows, width), lambda j, at: (0, 0, 0)),
            ]
            + [pl.BlockSpec((1, rows, width), lambda j, at: (0, 0, 0))] * len(sums)
            + [pl.BlockSpec((rows, DH), lambda j, at: (0, 0))] * len(others)
            + anywhere(after),
            out_specs=(
                pl.BlockSpec((rows, width), lambda j, at: (0, 0)),
                pl.BlockSpec(stat, lambda j, at: (0, 0)),
            ),
        ),
        out_shape=(
            jax.ShapeDtypeStruct((rows, width), f32),
            jax.ShapeDtypeStruct(stat, f32),
        ),
        compiler_params=params(),
        cost_estimate=LIGHT,
        name="finish",
    )(at, edges, query, rest, *sums, *others, *after)


def gate_kernel(count, parts, *refs):
    stats, atts, rests, outs = (
        refs[:count], refs[count:count + parts],
        refs[count + parts:count + 2 * parts], refs[count + 2 * parts:],
    )
    width = sum(a.shape[1] for a in atts)
    means, squares = stat_columns(stats)
    mean, square = merge(means, squares, [width] * count)
    scale = lax.rsqrt(square / (width * count) + EPSILON)
    rows, column = outs[0].shape[0], 0
    for att, rest in zip(atts, rests):
        span = att.shape[1]
        normed = (att[...] - mean) * scale
        gated = (normed * rest[0].astype(f32)).astype(bf16)
        for r, out in enumerate(outs):
            out[:, column:column + span] = gated[r * rows:(r + 1) * rows]
        column += span


def gate_rows(stats, atts, rests, chunks):
    rows, width = atts[0].shape[0], sum(a.shape[1] for a in atts)
    return pl.pallas_call(
        functools.partial(gate_kernel, len(stats), len(atts)),
        grid=(1,),
        in_specs=[pl.BlockSpec(s.shape, lambda j: (0, 0)) for s in stats]
        + [pl.BlockSpec((rows, a.shape[1]), lambda j: (0, 0)) for a in atts]
        + [pl.BlockSpec((1, rows, r.shape[2]), lambda j: (2, 0, 0)) for r in rests],
        out_specs=[pl.BlockSpec((rows // chunks, width), lambda j: (0, 0))] * chunks,
        out_shape=[jax.ShapeDtypeStruct((rows // chunks, width), bf16)] * chunks,
        compiler_params=params(),
        cost_estimate=LIGHT,
        name="gate",
    )(*stats, *atts, *rests)


def output_kernel(owners, after, order_ref, *refs):
    rows, w_ref, outs, lhs_ref = refs[:owners], refs[owners], refs[owners + 1 + after:-1], refs[-1]
    piece = rows[0].shape[1]

    @pl.when(pl.program_id(0) == 0)
    def _():
        first = 0
        for k in range(rows[0].shape[0]):
            for p in range(owners):
                lhs_ref[first:first + piece, :] = rows[p][order_ref[k]]
                first += piece

    sums = jnp.dot(lhs_ref[...], w_ref[...], preferred_element_type=f32).astype(bf16)
    first = 0
    for out in outs:
        for k in range(out.shape[0]):
            for p in range(owners):
                out[k, p] = sums[first:first + piece]
                first += piece


def output(order, counts, blocks, w_out, column, columns, after):
    owners, (each, width), zs = len(blocks), blocks[0].shape, sum(counts)
    piece = each // zs
    span = max(c for c in (512, 256, columns) if columns % c == 0 and column % c == 0)
    row_spec = pl.BlockSpec((zs, piece, width), lambda j, at: (0, 0, 0))
    return pl.pallas_call(
        functools.partial(output_kernel, owners, len(after)),
        grid_spec=pltpu.PrefetchScalarGridSpec(
            num_scalar_prefetch=1,
            grid=(columns // span,),
            in_specs=[row_spec] * owners
            + [pl.BlockSpec((width, span), lambda j, at: (0, column // span + j))]
            + anywhere(after),
            out_specs=[
                pl.BlockSpec((n, owners, piece, span), lambda j, at: (0, 0, 0, j)) for n in counts
            ],
            scratch_shapes=[pltpu.VMEM((owners * each, width), bf16)],
        ),
        out_shape=[jax.ShapeDtypeStruct((n, owners, piece, columns), bf16) for n in counts],
        compiler_params=params(),
        cost_estimate=LIGHT,
        name="output",
    )(order, *[b.reshape(zs, piece, width) for b in blocks], far(w_out), *after)


def close_kernel(counts, at_ref, t_ref, *refs):
    out_ref, first = refs[-1], 0
    owners = refs[0].shape[1]
    for r, row in enumerate(counts):
        column = 0
        for count in row:
            terms = refs[first:first + count]
            first += count
            span = terms[0].shape[-1]
            for p in range(owners):
                total = t_ref[r * owners + p, :, column:column + span].astype(f32)
                for term in terms:
                    total = total + term[0, p ^ at_ref[0]].astype(f32)
                out_ref[r * owners + p, :, column:column + span] = total.astype(bf16)
            column += span


def close(place, index, tokens, chunks):
    _, owners, piece, _ = chunks[0][0][0].shape
    blocks, width = len(chunks) * owners, sum(terms[0].shape[-1] for terms in chunks[0])
    flat = [term for row in chunks for terms in row for term in terms]
    return pl.pallas_call(
        functools.partial(close_kernel, [[len(terms) for terms in row] for row in chunks]),
        grid_spec=pltpu.PrefetchScalarGridSpec(
            num_scalar_prefetch=1,
            grid=(1,),
            in_specs=[pl.BlockSpec((blocks, piece, width), lambda j, at: (at[1], 0, 0))]
            + [pl.BlockSpec((1,) + t.shape[1:], lambda j, at: (0, 0, 0, 0)) for t in flat],
            out_specs=pl.BlockSpec((blocks, piece, width), lambda j, at: (0, 0, 0)),
        ),
        out_shape=jax.ShapeDtypeStruct((blocks, piece, width), bf16),
        compiler_params=params(),
        cost_estimate=LIGHT,
        name="close",
    )(
        jnp.stack([place, index]).astype(jnp.int32),
        far(tokens.reshape(-1, piece, width)),
        *flat,
    )


def bits_of(axis):
    count = lax.axis_size(axis)
    assert count & (count - 1) == 0
    return count.bit_length() - 1


def reverse(index, bits):
    return sum((((index >> b) & 1) << (bits - 1 - b) for b in range(bits)), 0 * index)


def swap(x, axis, bit):
    return lax.ppermute(
        x, axis, [(i, i ^ (1 << bit)) for i in range(lax.axis_size(axis))]
    )


def scatter(keep, gots, axis, after=()):
    terms, sent = [keep, gots[0]], gots[-1]
    for b in range(1, bits_of(axis)):
        sent = fold([keep, gots[-1]] if b == 1 else terms, after)
        terms.append(swap(sent, axis, b))
    return terms, sent


def gather(x, axis, after=()):
    blocks = [x]
    for b in reversed(range(bits_of(axis))):
        blocks = blocks + [swap(block, axis, b) for block in blocks]
        if len(blocks) == 2:
            blocks[1] = tie(blocks[1], after)
    return blocks


def shift(x, axis, k):
    count = lax.axis_size(axis)
    return lax.ppermute(x, axis, [(i, (i + k) % count) for i in range(count)])


def all_stats(stat, axis):
    count = lax.axis_size(axis)
    if count > 8:
        every = lax.all_gather(stat, axis)
        return [every[i] for i in range(count)]
    return [stat] + [shift(stat, axis, k) for k in range(1, count)]


def head_chunks(heads):
    if heads % 8:
        return [1] * heads
    unit = heads // 8
    return [unit, 2 * unit, 2 * unit, 2 * unit, unit]


GROUPS = [[0, 1], [2], [3], [4]]
ORDER = [
    "P0", "P1", "F0", "P2", "F1", "P3", "F2", "A0", "F3", "P4", "A1", "F4", "T0", "G0", "A2",
    "T1", "A3", "G1", "E0", "T2", "G2", "T3", "E1", "G3", "E2", "E3",
]


def local(tokens, w_qkvu, k_cache, v_cache, w_out, vis_start, vis_end):
    cand, depth = tokens.shape
    owners, zs = lax.axis_size("hist"), lax.axis_size("head")
    index = lax.axis_index("head")
    place = reverse(lax.axis_index("hist"), bits_of("hist"))
    width = w_qkvu.shape[2]
    events = k_cache.shape[0]
    chunks = 2 if cand % (2 * owners * zs * 16) == 0 else 1
    piece = cand // (zs * chunks * owners)

    def arrange(x):
        x = x.reshape((zs, chunks, owners, piece) + x.shape[1:])
        if piece % 16 == 0:
            return x
        blocks = [lax.dynamic_index_in_dim(x, p ^ place, 2, False) for p in range(owners)]
        x = jnp.stack(blocks).swapaxes(1, 2)
        return x.reshape((1, 1, owners, zs * chunks * piece) + x.shape[4:])

    at = (place if piece % 16 == 0 else jnp.int32(0)).reshape(1)
    ordered = arrange(tokens)
    first_event = lax.axis_index("hist") * events
    edges = arrange(edge_columns(first_event, vis_start, vis_end))

    sizes = head_chunks(width // DH)
    firsts = [sum(sizes[:c]) for c in range(len(sizes))]
    groups, order = GROUPS, ORDER
    if len(sizes) != 5:
        groups = [[c] for c in range(len(sizes))]
        order = [step + str(c) for step in "PFATGE" for c in range(len(sizes))]
    last = len(groups) - 1
    heads = [sum(sizes[c] for c in group) for group in groups]
    chain, keeps, firsts_got, terms, sums = [], {}, {}, {}, {}
    halves, queries, parts, atts, stats = {}, {}, {}, {}, {}
    for step, c in [(name[0], int(name[1:])) for name in order]:
        after = chain[-1:]
        if step == "P":
            keep, *sends = project(at, ordered, w_qkvu, firsts[c], sizes[c], after)
            before = firsts_got[c - 1] if c >= 1 else []
            before = before + [terms[0][-1]] if c == 2 and 0 in terms else before
            firsts_got[c] = [swap(tie(send, before), "hist", 0) for send in reversed(sends)][::-1]
            keeps[c] = keep
            chain.append(keep)
        elif step == "F":
            terms[c], sent = scatter(keeps[c], firsts_got[c], "hist", after)
            chain.append(sent)
        elif step == "A":
            parts[c] = activate([terms[k] for k in groups[c]], after)
            queries[c] = gather(parts[c][0], "hist")
            chain.append(parts[c][0])
        elif step == "T":
            first = firsts[groups[c][0]]
            keep, *sends = attend(at, queries[c], k_cache, v_cache, edges, first, after)
            halves[c] = keep, [swap(send, "hist", 0) for send in sends]
            chain.append(keep)
        elif step == "G":
            sums[c], sent = scatter(*halves[c], "hist", after)
            chain.append(sent)
        else:
            others = [stats[k] for k in range(last)] if c == last else []
            widths = [size * DH for size in heads[:last]] if c == last else []
            atts[c], stats[c] = finish(at, edges, *parts[c], sums[c], others, widths, after)
            chain.append(atts[c])

    atts = [atts[c] for c in range(last + 1)]
    rests = [parts[c][1] for c in range(last + 1)]
    gated = gate_rows(all_stats(stats[last], "head"), atts, rests, chunks)
    columns = w_out.shape[1]
    straight = piece % 16 == 0 and zs & (zs - 1) == 0
    steps = jnp.arange(zs, dtype=jnp.int32)
    shifted = (index + steps) % zs
    halved = index ^ reverse(steps, bits_of("head")) if straight else shifted
    results, last_sent, before = [], [], {}
    for r, rows in enumerate(gated):
        results.append([])
        if not straight:
            blocks = gather(rows, "hist")
            whole = jnp.dot(jnp.concatenate(blocks), w_out, preferred_element_type=f32)
            whole = whole.astype(bf16).reshape(owners, zs, piece, -1).swapaxes(0, 1)
            whole = lax.psum_scatter(whole, "head", scatter_dimension=0, tiled=True)
            results[-1].append([whole])
            continue
        blocks = gather(rows, "hist", before.get(r, []))
        spans = [columns // 2] * 2 if columns % 1024 == 0 else [columns]
        for g, span in enumerate(spans):
            direct = len(spans) == 1 or g == r
            order = shifted if direct else halved
            counts = [1] * zs if direct else [zs // 2] * 2
            own, *others = output(order, counts, blocks, w_out, g * span, span, last_sent)
            others = [tie(x, before.get((r, g), [])) for x in others]
            last_sent = others[-1:]
            if direct:
                arrived = [shift(x, "head", k + 1) for k, x in enumerate(others)]
                terms = [own] + arrived
                if r == 0:
                    before[1] = arrived[zs // 2 - 1:zs // 2]
                    before[1, 0] = arrived
            else:
                arrived = swap(others[0], "head", 0)
                terms, _ = scatter(own, [arrived], "head")
                if r == 0:
                    before[1, 0] = before.get((1, 0), []) + [arrived]
                    before[1, 1] = [terms[-1]]
            results[-1].append(terms)
    out = close(place, index, tokens, results)
    return out.reshape(cand // zs, -1)


def solution(mesh):
    in_specs = (
        P("groups", "hist"),
        P("hist", None, "head"),
        P(("groups", "hist"), "head"),
        P(("groups", "hist"), "head"),
        P("head", "hist"),
        P("groups"),
        P("groups"),
    )
    out_specs = P(("groups", "head"), "hist")
    return jax.shard_map(local, mesh=mesh, in_specs=in_specs, out_specs=out_specs, check_vma=False)
```

```python
import functools

import jax
import jax.numpy as jnp
from jax import lax
from jax.experimental import pallas as pl
from jax.experimental.pallas import tpu as pltpu
from jax.sharding import PartitionSpec as P

DH = 128
EPSILON = 1e-05
VMEM_LIMIT = 28 * 1024 * 1024

bf16 = jnp.bfloat16
f32 = jnp.float32


def silu(v):
    u = 0.5 * v
    return u + u * jnp.tanh(u)


def params():
    return pltpu.CompilerParams(vmem_limit_bytes=VMEM_LIMIT)


LIGHT = pl.CostEstimate(flops=1000, bytes_accessed=1000, transcendentals=0)
STEP = pl.CostEstimate(flops=1000, bytes_accessed=4_000_000, transcendentals=0)


def far(x):
    return pltpu.with_memory_space_constraint(x, pltpu.HBM)


def anywhere(arrays):
    return [pl.BlockSpec(memory_space=pl.ANY)] * len(arrays)


def project_kernel(parts, owners, after, at_ref, *refs):
    rows, weights = refs[:owners], refs[owners:owners + parts]
    outs, lhs_ref = refs[owners + parts + after:-parts - 1], refs[-parts - 1]
    wides = refs[-parts:]
    zs, chunks, _, piece, _ = rows[0].shape
    depth = weights[0].shape[0]

    @pl.when(pl.program_id(0) == 0)
    def _():
        first = 0
        for p in range(owners):
            for r in range(chunks):
                for z in range(zs):
                    lhs_ref[first:first + piece, :] = rows[p][z, r, 0]
                    first += piece

    res = None
    for k, wide in enumerate(wides):
        wide[...] = weights[k].reshape(depth * 4, DH)[...].astype(f32)
        rhs = jnp.concatenate(
            [wide[pl.ds(i, depth, stride=4), :].astype(bf16) for i in range(4)], axis=1
        )
        term = jnp.dot(lhs_ref[:, k * depth:(k + 1) * depth], rhs, preferred_element_type=f32)
        res = term if res is None else res + term
    res = res.astype(bf16)
    each, first = outs[0].shape[2], 0
    for out in outs:
        for p in range(out.shape[0]):
            for i in range(4):
                out[p, i] = res[first:first + each, i * DH:(i + 1) * DH]
            first += each


def parts_of(owners):
    half = owners // 2
    return [half, half // 2, half // 2] if half > 1 else [half, half]


def project(at, tokens, w, head_first, heads, after):
    zs, chunks, owners, piece, depth = tokens.shape
    each, counts = zs * chunks * piece, parts_of(owners)
    parts = 4 if depth % 512 == 0 else 1
    return pl.pallas_call(
        functools.partial(project_kernel, parts, owners, len(after)),
        grid_spec=pltpu.PrefetchScalarGridSpec(
            num_scalar_prefetch=1,
            grid=(heads,),
            in_specs=[
                pl.BlockSpec(
                    (zs, chunks, 1, piece, depth), lambda j, at, p=p: (0, 0, at[0] ^ p, 0, 0)
                )
                for p in range(owners)
            ]
            + [
                pl.BlockSpec((depth // parts, 4, DH), lambda j, at, k=k: (k, 0, head_first + j))
                for k in range(parts)
            ]
            + anywhere(after),
            out_specs=[
                pl.BlockSpec((n, 4, each, DH), lambda j, at: (0, 0, 0, j)) for n in counts
            ],
            scratch_shapes=[pltpu.VMEM((owners * each, depth), bf16)]
            + [pltpu.VMEM((depth // parts * 4, DH), f32) for _ in range(parts)],
        ),
        out_shape=[jax.ShapeDtypeStruct((n, 4, each, heads * DH), bf16) for n in counts],
        compiler_params=params(),
        cost_estimate=LIGHT,
        name="project",
    )(at, *[far(tokens)] * owners, *[far(w)] * parts, *after)


def tie_kernel(*refs):
    pass


def tie(x, after):
    if not after:
        return x
    return pl.pallas_call(
        tie_kernel,
        in_specs=anywhere([x, *after]),
        out_specs=pl.BlockSpec(memory_space=pl.ANY),
        out_shape=jax.ShapeDtypeStruct(x.shape, x.dtype),
        input_output_aliases={0: 0},
        compiler_params=params(),
        cost_estimate=LIGHT,
        name="tie",
    )(x, *after)


def fold_kernel(count, *refs):
    refs[-1][...] = sum(r[...].astype(f32) for r in refs[:count]).astype(bf16)


def fold(terms, after=(), told=LIGHT):
    half = terms[0].shape[0] // 2 if len(terms) == 2 else terms[-1].shape[0] // 2
    tail = terms[0].shape[1:]
    steps = 2 if tail[-1] % 256 == 0 else 1
    block = (half,) + tail[:-1] + (tail[-1] // steps,)
    middle = (0,) * (len(tail) - 1)
    firsts = [0 if t.shape[0] == half else 1 for t in terms]
    return pl.pallas_call(
        functools.partial(fold_kernel, len(terms)),
        grid=(steps,),
        in_specs=[pl.BlockSpec(block, lambda j, f=f: (f,) + middle + (j,)) for f in firsts]
        + anywhere(after),
        out_specs=pl.BlockSpec(block, lambda j: (0,) + middle + (j,)),
        out_shape=jax.ShapeDtypeStruct((half,) + tail, bf16),
        compiler_params=params(),
        cost_estimate=told,
        name="fold",
    )(*terms, *after)


def activate_kernel(counts, *refs):
    q_ref, rest_ref = refs[-2:]
    first, column = 0, 0
    for count in counts:
        terms = refs[first:first + count]
        span = terms[0].shape[-1]
        for i in range(4):
            part = silu(sum(t[0, i].astype(f32) for t in terms)).astype(bf16)
            if i == 0:
                q_ref[:, column:column + span] = part
            else:
                rest_ref[i - 1, :, column:column + span] = part
        first += count
        column += span


def activate(chunks, after):
    each, width = chunks[0][0].shape[2], sum(terms[0].shape[3] for terms in chunks)
    flat = [term for terms in chunks for term in terms]
    return pl.pallas_call(
        functools.partial(activate_kernel, [len(terms) for terms in chunks]),
        grid=(1,),
        in_specs=[pl.BlockSpec((1,) + t.shape[1:], lambda j: (0, 0, 0, 0)) for t in flat]
        + anywhere(after),
        out_specs=(
            pl.BlockSpec((each, width), lambda j: (0, 0)),
            pl.BlockSpec((3, each, width), lambda j: (0, 0, 0)),
        ),
        out_shape=(
            jax.ShapeDtypeStruct((each, width), bf16),
            jax.ShapeDtypeStruct((3, each, width), bf16),
        ),
        compiler_params=params(),
        cost_estimate=LIGHT,
        name="activate",
    )(*flat, *after)


def edge_kernel(base_ref, start_ref, end_ref, out_ref):
    row = lax.broadcasted_iota(jnp.int32, (DH, DH), 0)
    for b in range(start_ref.shape[0]):
        start, end = start_ref[b:b + 1, :], end_ref[b:b + 1, :]
        both = jnp.where(row == 0, start, end) - base_ref[0]
        out_ref[b * DH:(b + 1) * DH, :] = both.astype(f32).T[:, :2].astype(jnp.int32)


def edge_columns(base, start, end):
    count = start.shape[0]
    lines = pl.BlockSpec((count // DH, DH), lambda j, base: (0, 0))
    return pl.pallas_call(
        edge_kernel,
        grid_spec=pltpu.PrefetchScalarGridSpec(
            num_scalar_prefetch=1,
            grid=(1,),
            in_specs=[lines, lines],
            out_specs=pl.BlockSpec((count, 2), lambda j, base: (0, 0)),
        ),
        out_shape=jax.ShapeDtypeStruct((count, 2), jnp.int32),
        compiler_params=params(),
        cost_estimate=LIGHT,
        name="edges",
    )(base.reshape(1), start.reshape(-1, DH), end.reshape(-1, DH))


def attend_kernel(owners, sends, at_ref, *refs):
    queries, edges = refs[:owners], refs[owners:2 * owners]
    k_ref, v_ref = refs[2 * owners:2 * owners + 2]
    outs, mask_ref = refs[-1 - sends:-1], refs[-1]
    events = mask_ref.shape[1]
    each = outs[0].shape[1]

    @pl.when(pl.program_id(0) == 0)
    def _():
        zs, chunks, _, piece, _ = edges[0].shape
        at = lax.broadcasted_iota(jnp.int32, (piece, events), 1)
        first = 0
        for p in range(owners):
            for r in range(chunks):
                for z in range(zs):
                    edge = edges[p][z, r, 0]
                    seen = (at >= edge[:, :1]) & (at < edge[:, 1:])
                    mask_ref[first:first + piece, :] = jnp.where(seen, 1.0, 0.0).astype(bf16)
                    first += piece

    for h in range(k_ref.shape[1] // DH):
        at = slice(h * DH, (h + 1) * DH)
        query = jnp.concatenate([q[:, at] for q in queries])
        u = lax.dot_general(
            query, k_ref[:, at], (((1,), (1,)), ((), ())), preferred_element_type=f32
        ) * (0.5 * DH ** (-0.5))
        weights = (u + u * jnp.tanh(u)).astype(bf16) * mask_ref[...]
        term = jnp.dot(weights, v_ref[:, at], preferred_element_type=f32).astype(bf16)
        first = 0
        for out in outs:
            for p in range(out.shape[0]):
                out[p, :, at] = term[first:first + each]
                first += each


def edge_spec(edges, p):
    zs, chunks, _, piece, ends = edges.shape
    return pl.BlockSpec((zs, chunks, 1, piece, ends), lambda j, at: (0, 0, at[0] ^ p, 0, 0))


def attend(at, queries, k_cache, v_cache, edges, head_first, after):
    owners, (each, width) = len(queries), queries[0].shape
    rows, events, counts = owners * each, k_cache.shape[0], parts_of(owners)
    first = head_first * DH
    span = max(h for h in range(DH, 4 * DH, DH) if width % h == 0 and first % h == 0)
    cache = pl.BlockSpec((events, span), lambda j, at: (0, first // span + j))
    return pl.pallas_call(
        functools.partial(attend_kernel, owners, len(counts)),
        grid_spec=pltpu.PrefetchScalarGridSpec(
            num_scalar_prefetch=1,
            grid=(width // span,),
            in_specs=[pl.BlockSpec((each, span), lambda j, at: (0, j))] * owners
            + [edge_spec(edges, p) for p in range(owners)]
            + [cache, cache]
            + anywhere(after),
            out_specs=[pl.BlockSpec((n, each, span), lambda j, at: (0, 0, j)) for n in counts],
            scratch_shapes=[pltpu.VMEM((rows, events), bf16)],
        ),
        out_shape=[jax.ShapeDtypeStruct((n, each, width), bf16) for n in counts],
        compiler_params=params(),
        cost_estimate=LIGHT,
        name="attend",
    )(at, *queries, *[edges] * owners, far(k_cache), far(v_cache), *after)


def merge(means, squares, widths):
    width = sum(widths)
    mean = sum(m * (w / width) for m, w in zip(means, widths))
    square = sum(squares) + sum(w * (m - mean) * (m - mean) for m, w in zip(means, widths))
    return mean, square


def stat_columns(stats):
    stats = [s[...] for s in stats]
    stats = [s if s.shape[0] > 8 else jnp.concatenate([s] * (DH // 8)).T for s in stats]
    return [s[:, :1] for s in stats], [s[:, 4:5] for s in stats]


def finish_kernel(terms, widths, at_ref, edge_ref, q_ref, rest_ref, *refs):
    sums, others = refs[:terms], refs[terms:terms + len(widths)]
    att_ref, stat_ref = refs[-2:]
    rows, width = att_ref.shape
    zs, chunks = edge_ref.shape[:2]
    edge = jnp.concatenate(
        [edge_ref[z, r, 0] for r in range(chunks) for z in range(zs)]
    ).astype(f32)
    root = lax.rsqrt(edge[:, 1:] - edge[:, :1])
    total = jnp.zeros((rows, 1), f32)
    for first in range(0, width, DH):
        at = slice(first, first + DH)
        summed = sum(s[0, :, at].astype(f32) for s in sums)
        product = q_ref[:, at].astype(f32) * rest_ref[0, :, at].astype(f32)
        weight = silu(jnp.sum(product, axis=1, keepdims=True) * DH ** (-0.5))
        value = summed * root + weight * rest_ref[1, :, at].astype(f32)
        att_ref[:, at] = value
        total += jnp.sum(value, axis=1, keepdims=True)
    mean = total / width
    spread = jnp.zeros((rows, DH), f32)
    for first in range(0, width, DH):
        away = att_ref[:, first:first + DH] - mean
        spread += away * away
    square = jnp.sum(spread, axis=1, keepdims=True)
    if others:
        means, squares = stat_columns(others)
        mean, square = merge([mean] + means, [square] + squares, [width] + widths)
    lane = lax.broadcasted_iota(jnp.int32, (rows, DH), 1)
    stat = jnp.where(lane < 4, mean, square)
    stat_ref[...] = stat if stat_ref.shape == stat.shape else stat.T[:8]


def finish(at, edges, query, rest, sums, others, widths, after):
    rows, width = query.shape
    stat = (8, rows) if others and rows == DH else (rows, DH)
    return pl.pallas_call(
        functools.partial(finish_kernel, len(sums), widths),
        grid_spec=pltpu.PrefetchScalarGridSpec(
            num_scalar_prefetch=1,
            grid=(1,),
            in_specs=[
                edge_spec(edges, 0),
                pl.BlockSpec((rows, width), lambda j, at: (0, 0)),
                pl.BlockSpec((2, rows, width), lambda j, at: (0, 0, 0)),
            ]
            + [pl.BlockSpec((1, rows, width), lambda j, at: (0, 0, 0))] * len(sums)
            + [pl.BlockSpec((rows, DH), lambda j, at: (0, 0))] * len(others)
            + anywhere(after),
            out_specs=(
                pl.BlockSpec((rows, width), lambda j, at: (0, 0)),
                pl.BlockSpec(stat, lambda j, at: (0, 0)),
            ),
        ),
        out_shape=(
            jax.ShapeDtypeStruct((rows, width), f32),
            jax.ShapeDtypeStruct(stat, f32),
        ),
        compiler_params=params(),
        cost_estimate=LIGHT,
        name="finish",
    )(at, edges, query, rest, *sums, *others, *after)


def gate_kernel(count, parts, *refs):
    stats, atts, rests, outs = (
        refs[:count], refs[count:count + parts],
        refs[count + parts:count + 2 * parts], refs[count + 2 * parts:],
    )
    width = sum(a.shape[1] for a in atts)
    means, squares = stat_columns(stats)
    mean, square = merge(means, squares, [width] * count)
    scale = lax.rsqrt(square / (width * count) + EPSILON)
    rows, column = outs[0].shape[0], 0
    for att, rest in zip(atts, rests):
        span = att.shape[1]
        normed = (att[...] - mean) * scale
        gated = (normed * rest[0].astype(f32)).astype(bf16)
        for r, out in enumerate(outs):
            out[:, column:column + span] = gated[r * rows:(r + 1) * rows]
        column += span


def gate_rows(stats, atts, rests, chunks):
    rows, width = atts[0].shape[0], sum(a.shape[1] for a in atts)
    return pl.pallas_call(
        functools.partial(gate_kernel, len(stats), len(atts)),
        grid=(1,),
        in_specs=[pl.BlockSpec(s.shape, lambda j: (0, 0)) for s in stats]
        + [pl.BlockSpec((rows, a.shape[1]), lambda j: (0, 0)) for a in atts]
        + [pl.BlockSpec((1, rows, r.shape[2]), lambda j: (2, 0, 0)) for r in rests],
        out_specs=[pl.BlockSpec((rows // chunks, width), lambda j: (0, 0))] * chunks,
        out_shape=[jax.ShapeDtypeStruct((rows // chunks, width), bf16)] * chunks,
        compiler_params=params(),
        cost_estimate=LIGHT,
        name="gate",
    )(*stats, *atts, *rests)


def output_kernel(owners, after, order_ref, *refs):
    rows, w_ref, outs, lhs_ref = refs[:owners], refs[owners], refs[owners + 1 + after:-1], refs[-1]
    piece = rows[0].shape[1]

    @pl.when(pl.program_id(0) == 0)
    def _():
        first = 0
        for k in range(rows[0].shape[0]):
            for p in range(owners):
                lhs_ref[first:first + piece, :] = rows[p][order_ref[k]]
                first += piece

    sums = jnp.dot(lhs_ref[...], w_ref[...], preferred_element_type=f32).astype(bf16)
    first = 0
    for out in outs:
        for k in range(out.shape[0]):
            for p in range(owners):
                out[k, p] = sums[first:first + piece]
                first += piece


def output(order, counts, blocks, w_out, column, columns, after):
    owners, (each, width), zs = len(blocks), blocks[0].shape, sum(counts)
    piece = each // zs
    span = max(c for c in (512, 256, columns) if columns % c == 0 and column % c == 0)
    row_spec = pl.BlockSpec((zs, piece, width), lambda j, at: (0, 0, 0))
    return pl.pallas_call(
        functools.partial(output_kernel, owners, len(after)),
        grid_spec=pltpu.PrefetchScalarGridSpec(
            num_scalar_prefetch=1,
            grid=(columns // span,),
            in_specs=[row_spec] * owners
            + [pl.BlockSpec((width, span), lambda j, at: (0, column // span + j))]
            + anywhere(after),
            out_specs=[
                pl.BlockSpec((n, owners, piece, span), lambda j, at: (0, 0, 0, j)) for n in counts
            ],
            scratch_shapes=[pltpu.VMEM((owners * each, width), bf16)],
        ),
        out_shape=[jax.ShapeDtypeStruct((n, owners, piece, columns), bf16) for n in counts],
        compiler_params=params(),
        cost_estimate=LIGHT,
        name="output",
    )(order, *[b.reshape(zs, piece, width) for b in blocks], far(w_out), *after)


def close_kernel(count, at_ref, t_ref, *refs):
    out_ref, mark_ref = refs[-2:]
    mark_ref[...] = jnp.zeros_like(mark_ref)
    for p in range(out_ref.shape[0]):
        total = t_ref[p].astype(f32)
        for term in refs[:count]:
            total = total + term[0, p ^ at_ref[0]].astype(f32)
        out_ref[p] = total.astype(bf16)


def close(place, index, tokens, chunks, r, g, terms, out, after):
    _, owners, piece, span = terms[0].shape
    at = jnp.stack([place, index * chunks + r]).astype(jnp.int32)
    into = [] if out is None else [out]
    return pl.pallas_call(
        functools.partial(close_kernel, len(terms)),
        grid_spec=pltpu.PrefetchScalarGridSpec(
            num_scalar_prefetch=1,
            grid=(1,),
            in_specs=[pl.BlockSpec((owners, piece, span), lambda j, at: (at[1], 0, g))]
            + [pl.BlockSpec((1,) + t.shape[1:], lambda j, at: (0, 0, 0, 0)) for t in terms]
            + anywhere(into) + anywhere(after),
            out_specs=(
                pl.BlockSpec((owners, piece, span), lambda j, at: (r, 0, g)),
                pl.BlockSpec((8, DH), lambda j, at: (0, 0)),
            ),
        ),
        out_shape=(
            jax.ShapeDtypeStruct((chunks * owners, piece, tokens.shape[1]), bf16),
            jax.ShapeDtypeStruct((8, DH), f32),
        ),
        input_output_aliases={} if out is None else {2 + len(terms): 0},
        compiler_params=params(),
        cost_estimate=STEP,
        name="close",
    )(at, far(tokens.reshape(-1, piece, tokens.shape[1])), *terms, *into, *after)


def bits_of(axis):
    count = lax.axis_size(axis)
    assert count & (count - 1) == 0
    return count.bit_length() - 1


def reverse(index, bits):
    return sum((((index >> b) & 1) << (bits - 1 - b) for b in range(bits)), 0 * index)


def swap(x, axis, bit):
    return lax.ppermute(
        x, axis, [(i, i ^ (1 << bit)) for i in range(lax.axis_size(axis))]
    )


def scatter(keep, gots, axis, after=(), told=LIGHT):
    terms, sent = [keep, gots[0]], gots[-1]
    for b in range(1, bits_of(axis)):
        sent = fold([keep, gots[-1]] if b == 1 else terms, after, told)
        terms.append(swap(sent, axis, b))
    return terms, sent


def gather(x, axis, after=()):
    blocks = [x]
    for b in reversed(range(bits_of(axis))):
        blocks = blocks + [swap(block, axis, b) for block in blocks]
        if len(blocks) == 2:
            blocks[1] = tie(blocks[1], after)
    return blocks


def shift(x, axis, k):
    count = lax.axis_size(axis)
    return lax.ppermute(x, axis, [(i, (i + k) % count) for i in range(count)])


def all_stats(stat, axis):
    count = lax.axis_size(axis)
    if count > 8:
        every = lax.all_gather(stat, axis)
        return [every[i] for i in range(count)]
    return [stat] + [shift(stat, axis, k) for k in range(1, count)]


def head_chunks(heads):
    if heads % 8:
        return [1] * heads
    unit = heads // 8
    return [unit, 2 * unit, 2 * unit, 2 * unit, unit]


GROUPS = [[0, 1], [2], [3], [4]]
ORDER = [
    "P0", "P1", "F0", "P2", "F1", "P3", "F2", "A0", "F3", "P4", "A1", "F4", "T0", "G0", "A2",
    "T1", "A3", "G1", "E0", "T2", "G2", "T3", "E1", "G3", "E2", "E3",
]


def local(tokens, w_qkvu, k_cache, v_cache, w_out, vis_start, vis_end):
    cand, depth = tokens.shape
    owners, zs = lax.axis_size("hist"), lax.axis_size("head")
    index = lax.axis_index("head")
    place = reverse(lax.axis_index("hist"), bits_of("hist"))
    width = w_qkvu.shape[2]
    events = k_cache.shape[0]
    chunks = 2 if cand % (2 * owners * zs * 16) == 0 else 1
    piece = cand // (zs * chunks * owners)

    def arrange(x):
        x = x.reshape((zs, chunks, owners, piece) + x.shape[1:])
        if piece % 16 == 0:
            return x
        blocks = [lax.dynamic_index_in_dim(x, p ^ place, 2, False) for p in range(owners)]
        x = jnp.stack(blocks).swapaxes(1, 2)
        return x.reshape((1, 1, owners, zs * chunks * piece) + x.shape[4:])

    at = (place if piece % 16 == 0 else jnp.int32(0)).reshape(1)
    ordered = arrange(tokens)
    first_event = lax.axis_index("hist") * events
    edges = arrange(edge_columns(first_event, vis_start, vis_end))

    sizes = head_chunks(width // DH)
    firsts = [sum(sizes[:c]) for c in range(len(sizes))]
    groups, order = GROUPS, ORDER
    if len(sizes) != 5:
        groups = [[c] for c in range(len(sizes))]
        order = [step + str(c) for step in "PFATGE" for c in range(len(sizes))]
    last = len(groups) - 1
    heads = [sum(sizes[c] for c in group) for group in groups]
    chain, keeps, firsts_got, terms, sums = [], {}, {}, {}, {}
    halves, queries, parts, atts, stats = {}, {}, {}, {}, {}
    for step, c in [(name[0], int(name[1:])) for name in order]:
        after = chain[-1:]
        if step == "P":
            keep, *sends = project(at, ordered, w_qkvu, firsts[c], sizes[c], after)
            before = firsts_got[c - 1] if c >= 1 else []
            before = before + [terms[0][-1]] if c == 2 and 0 in terms else before
            firsts_got[c] = [swap(tie(send, before), "hist", 0) for send in reversed(sends)][::-1]
            keeps[c] = keep
            chain.append(keep)
        elif step == "F":
            terms[c], sent = scatter(keeps[c], firsts_got[c], "hist", after)
            chain.append(sent)
        elif step == "A":
            parts[c] = activate([terms[k] for k in groups[c]], after)
            queries[c] = gather(parts[c][0], "hist")
            chain.append(parts[c][0])
        elif step == "T":
            first = firsts[groups[c][0]]
            keep, *sends = attend(at, queries[c], k_cache, v_cache, edges, first, after)
            halves[c] = keep, [swap(send, "hist", 0) for send in sends]
            chain.append(keep)
        elif step == "G":
            sums[c], sent = scatter(*halves[c], "hist", after)
            chain.append(sent)
        else:
            others = [stats[k] for k in range(last)] if c == last else []
            widths = [size * DH for size in heads[:last]] if c == last else []
            atts[c], stats[c] = finish(at, edges, *parts[c], sums[c], others, widths, after)
            chain.append(atts[c])

    atts = [atts[c] for c in range(last + 1)]
    rests = [parts[c][1] for c in range(last + 1)]
    gated = gate_rows(all_stats(stats[last], "head"), atts, rests, chunks)
    columns = w_out.shape[1]
    straight = piece % 16 == 0 and zs & (zs - 1) == 0
    out, last_out = None, []
    if not straight:
        for r, rows in enumerate(gated):
            whole = jnp.concatenate(gather(rows, "hist"))
            whole = jnp.dot(whole, w_out, preferred_element_type=f32).astype(bf16)
            whole = whole.reshape(owners, zs, piece, -1).swapaxes(0, 1)
            whole = lax.psum_scatter(whole, "head", scatter_dimension=0, tiled=True)
            out, _ = close(place, index, tokens, chunks, r, 0, [whole], out, [])
        return out.reshape(cand // zs, -1)
    halved = index ^ reverse(jnp.arange(zs, dtype=jnp.int32), bits_of("head"))
    groups = 2 if columns % 1024 == 0 else 1
    span = columns // groups
    pieces, first_out, counts = [], [], [zs // 2] * 2 if zs > 1 else [1]
    for r, rows in enumerate(gated):
        blocks = gather(rows, "hist", first_out)
        for g in range(groups):
            own, *others = output(halved, counts, blocks, w_out, g * span, span, last_out)
            pieces.append((r, g, own, [swap(x, "head", 0) for x in others]))
            last_out, first_out = [own], first_out or [own]
    closing, chain = [], last_out
    for r, g, own, arrived in pieces:
        terms, sent = scatter(own, arrived, "head", chain, STEP) if arrived else ([own], own)
        chain = [sent]
        closing.append((r, g, terms))
        if len(closing) > 1:
            out, mark = close(place, index, tokens, chunks, *closing.pop(0), out, chain)
            chain = [mark]
    for last_piece in closing:
        out, _ = close(place, index, tokens, chunks, *last_piece, out, [])
    return out.reshape(cand // zs, -1)


def solution(mesh):
    in_specs = (
        P("groups", "hist"),
        P("hist", None, "head"),
        P(("groups", "hist"), "head"),
        P(("groups", "hist"), "head"),
        P("head", "hist"),
        P("groups"),
        P("groups"),
    )
    out_specs = P(("groups", "head"), "hist")
    return jax.shard_map(local, mesh=mesh, in_specs=in_specs, out_specs=out_specs, check_vma=False)
```

```python
import functools

import jax
import jax.numpy as jnp
from jax import lax
from jax.experimental import pallas as pl
from jax.experimental.pallas import tpu as pltpu
from jax.sharding import PartitionSpec as P

DH = 128
EPSILON = 1e-05
VMEM_LIMIT = 28 * 1024 * 1024

bf16 = jnp.bfloat16
f32 = jnp.float32


def silu(v):
    u = 0.5 * v
    return u + u * jnp.tanh(u)


def params():
    return pltpu.CompilerParams(vmem_limit_bytes=VMEM_LIMIT)


LIGHT = pl.CostEstimate(flops=1000, bytes_accessed=1000, transcendentals=0)


def far(x):
    return pltpu.with_memory_space_constraint(x, pltpu.HBM)


def anywhere(arrays):
    return [pl.BlockSpec(memory_space=pl.ANY)] * len(arrays)


def project_kernel(parts, owners, after, at_ref, *refs):
    rows, weights = refs[:owners], refs[owners:owners + parts]
    outs, lhs_ref = refs[owners + parts + after:-parts - 1], refs[-parts - 1]
    wides = refs[-parts:]
    zs, chunks, _, piece, _ = rows[0].shape
    depth = weights[0].shape[0]

    @pl.when(pl.program_id(0) == 0)
    def _():
        first = 0
        for p in range(owners):
            for r in range(chunks):
                for z in range(zs):
                    lhs_ref[first:first + piece, :] = rows[p][z, r, 0]
                    first += piece

    res = None
    for k, wide in enumerate(wides):
        wide[...] = weights[k].reshape(depth * 4, DH)[...].astype(f32)
        rhs = jnp.concatenate(
            [wide[pl.ds(i, depth, stride=4), :].astype(bf16) for i in range(4)], axis=1
        )
        term = jnp.dot(lhs_ref[:, k * depth:(k + 1) * depth], rhs, preferred_element_type=f32)
        res = term if res is None else res + term
    res = res.astype(bf16)
    each, first = outs[0].shape[2], 0
    for out in outs:
        for p in range(out.shape[0]):
            for i in range(4):
                out[p, i] = res[first:first + each, i * DH:(i + 1) * DH]
            first += each


def parts_of(owners):
    half = owners // 2
    return [half, half // 2, half // 2] if half > 1 else [half, half]


def project(at, tokens, w, head_first, heads, after):
    zs, chunks, owners, piece, depth = tokens.shape
    each, counts = zs * chunks * piece, parts_of(owners)
    parts = 4 if depth % 512 == 0 else 1
    return pl.pallas_call(
        functools.partial(project_kernel, parts, owners, len(after)),
        grid_spec=pltpu.PrefetchScalarGridSpec(
            num_scalar_prefetch=1,
            grid=(heads,),
            in_specs=[
                pl.BlockSpec(
                    (zs, chunks, 1, piece, depth), lambda j, at, p=p: (0, 0, at[0] ^ p, 0, 0)
                )
                for p in range(owners)
            ]
            + [
                pl.BlockSpec((depth // parts, 4, DH), lambda j, at, k=k: (k, 0, head_first + j))
                for k in range(parts)
            ]
            + anywhere(after),
            out_specs=[
                pl.BlockSpec((n, 4, each, DH), lambda j, at: (0, 0, 0, j)) for n in counts
            ],
            scratch_shapes=[pltpu.VMEM((owners * each, depth), bf16)]
            + [pltpu.VMEM((depth // parts * 4, DH), f32) for _ in range(parts)],
        ),
        out_shape=[jax.ShapeDtypeStruct((n, 4, each, heads * DH), bf16) for n in counts],
        compiler_params=params(),
        cost_estimate=LIGHT,
        name="project",
    )(at, *[far(tokens)] * owners, *[far(w)] * parts, *after)


def tie_kernel(*refs):
    pass


def tie(x, after):
    if not after:
        return x
    return pl.pallas_call(
        tie_kernel,
        in_specs=anywhere([x, *after]),
        out_specs=pl.BlockSpec(memory_space=pl.ANY),
        out_shape=jax.ShapeDtypeStruct(x.shape, x.dtype),
        input_output_aliases={0: 0},
        compiler_params=params(),
        cost_estimate=LIGHT,
        name="tie",
    )(x, *after)


def fold_kernel(count, *refs):
    refs[-1][...] = sum(r[...].astype(f32) for r in refs[:count]).astype(bf16)


def fold(terms, after=()):
    half = terms[0].shape[0] // 2 if len(terms) == 2 else terms[-1].shape[0] // 2
    tail = terms[0].shape[1:]
    steps = 2 if tail[-1] % 256 == 0 else 1
    block = (half,) + tail[:-1] + (tail[-1] // steps,)
    middle = (0,) * (len(tail) - 1)
    firsts = [0 if t.shape[0] == half else 1 for t in terms]
    return pl.pallas_call(
        functools.partial(fold_kernel, len(terms)),
        grid=(steps,),
        in_specs=[pl.BlockSpec(block, lambda j, f=f: (f,) + middle + (j,)) for f in firsts]
        + anywhere(after),
        out_specs=pl.BlockSpec(block, lambda j: (0,) + middle + (j,)),
        out_shape=jax.ShapeDtypeStruct((half,) + tail, bf16),
        compiler_params=params(),
        cost_estimate=LIGHT,
        name="fold",
    )(*terms, *after)


def activate_kernel(counts, *refs):
    q_ref, rest_ref = refs[-2:]
    first, column = 0, 0
    for count in counts:
        terms = refs[first:first + count]
        span = terms[0].shape[-1]
        for i in range(4):
            part = silu(sum(t[0, i].astype(f32) for t in terms)).astype(bf16)
            if i == 0:
                q_ref[:, column:column + span] = part
            else:
                rest_ref[i - 1, :, column:column + span] = part
        first += count
        column += span


def activate(chunks, after):
    each, width = chunks[0][0].shape[2], sum(terms[0].shape[3] for terms in chunks)
    flat = [term for terms in chunks for term in terms]
    return pl.pallas_call(
        functools.partial(activate_kernel, [len(terms) for terms in chunks]),
        grid=(1,),
        in_specs=[pl.BlockSpec((1,) + t.shape[1:], lambda j: (0, 0, 0, 0)) for t in flat]
        + anywhere(after),
        out_specs=(
            pl.BlockSpec((each, width), lambda j: (0, 0)),
            pl.BlockSpec((3, each, width), lambda j: (0, 0, 0)),
        ),
        out_shape=(
            jax.ShapeDtypeStruct((each, width), bf16),
            jax.ShapeDtypeStruct((3, each, width), bf16),
        ),
        compiler_params=params(),
        cost_estimate=LIGHT,
        name="activate",
    )(*flat, *after)


def edge_kernel(base_ref, start_ref, end_ref, out_ref):
    row = lax.broadcasted_iota(jnp.int32, (DH, DH), 0)
    for b in range(start_ref.shape[0]):
        start, end = start_ref[b:b + 1, :], end_ref[b:b + 1, :]
        both = jnp.where(row == 0, start, end) - base_ref[0]
        out_ref[b * DH:(b + 1) * DH, :] = both.astype(f32).T[:, :2].astype(jnp.int32)


def edge_columns(base, start, end):
    count = start.shape[0]
    lines = pl.BlockSpec((count // DH, DH), lambda j, base: (0, 0))
    return pl.pallas_call(
        edge_kernel,
        grid_spec=pltpu.PrefetchScalarGridSpec(
            num_scalar_prefetch=1,
            grid=(1,),
            in_specs=[lines, lines],
            out_specs=pl.BlockSpec((count, 2), lambda j, base: (0, 0)),
        ),
        out_shape=jax.ShapeDtypeStruct((count, 2), jnp.int32),
        compiler_params=params(),
        cost_estimate=LIGHT,
        name="edges",
    )(base.reshape(1), start.reshape(-1, DH), end.reshape(-1, DH))


def attend_kernel(owners, sends, at_ref, *refs):
    queries, edges = refs[:owners], refs[owners:2 * owners]
    k_ref, v_ref = refs[2 * owners:2 * owners + 2]
    outs, mask_ref = refs[-1 - sends:-1], refs[-1]
    events = mask_ref.shape[1]
    each = outs[0].shape[1]

    @pl.when(pl.program_id(0) == 0)
    def _():
        zs, chunks, _, piece, _ = edges[0].shape
        at = lax.broadcasted_iota(jnp.int32, (piece, events), 1)
        first = 0
        for p in range(owners):
            for r in range(chunks):
                for z in range(zs):
                    edge = edges[p][z, r, 0]
                    seen = (at >= edge[:, :1]) & (at < edge[:, 1:])
                    mask_ref[first:first + piece, :] = jnp.where(seen, 1.0, 0.0).astype(bf16)
                    first += piece

    for h in range(k_ref.shape[1] // DH):
        at = slice(h * DH, (h + 1) * DH)
        query = jnp.concatenate([q[:, at] for q in queries])
        u = lax.dot_general(
            query, k_ref[:, at], (((1,), (1,)), ((), ())), preferred_element_type=f32
        ) * (0.5 * DH ** (-0.5))
        weights = (u + u * jnp.tanh(u)).astype(bf16) * mask_ref[...]
        term = jnp.dot(weights, v_ref[:, at], preferred_element_type=f32).astype(bf16)
        first = 0
        for out in outs:
            for p in range(out.shape[0]):
                out[p, :, at] = term[first:first + each]
                first += each


def edge_spec(edges, p):
    zs, chunks, _, piece, ends = edges.shape
    return pl.BlockSpec((zs, chunks, 1, piece, ends), lambda j, at: (0, 0, at[0] ^ p, 0, 0))


def attend(at, queries, k_cache, v_cache, edges, head_first, after):
    owners, (each, width) = len(queries), queries[0].shape
    rows, events, counts = owners * each, k_cache.shape[0], parts_of(owners)
    first = head_first * DH
    span = max(h for h in range(DH, 4 * DH, DH) if width % h == 0 and first % h == 0)
    cache = pl.BlockSpec((events, span), lambda j, at: (0, first // span + j))
    return pl.pallas_call(
        functools.partial(attend_kernel, owners, len(counts)),
        grid_spec=pltpu.PrefetchScalarGridSpec(
            num_scalar_prefetch=1,
            grid=(width // span,),
            in_specs=[pl.BlockSpec((each, span), lambda j, at: (0, j))] * owners
            + [edge_spec(edges, p) for p in range(owners)]
            + [cache, cache]
            + anywhere(after),
            out_specs=[pl.BlockSpec((n, each, span), lambda j, at: (0, 0, j)) for n in counts],
            scratch_shapes=[pltpu.VMEM((rows, events), bf16)],
        ),
        out_shape=[jax.ShapeDtypeStruct((n, each, width), bf16) for n in counts],
        compiler_params=params(),
        cost_estimate=LIGHT,
        name="attend",
    )(at, *queries, *[edges] * owners, far(k_cache), far(v_cache), *after)


def merge(means, squares, widths):
    width = sum(widths)
    mean = sum(m * (w / width) for m, w in zip(means, widths))
    square = sum(squares) + sum(w * (m - mean) * (m - mean) for m, w in zip(means, widths))
    return mean, square


def stat_columns(stats):
    stats = [s[...] for s in stats]
    stats = [s if s.shape[0] > 8 else jnp.concatenate([s] * (DH // 8)).T for s in stats]
    return [s[:, :1] for s in stats], [s[:, 4:5] for s in stats]


def finish_kernel(terms, widths, at_ref, edge_ref, q_ref, rest_ref, *refs):
    sums, others = refs[:terms], refs[terms:terms + len(widths)]
    att_ref, stat_ref = refs[-2:]
    rows, width = att_ref.shape
    zs, chunks = edge_ref.shape[:2]
    edge = jnp.concatenate(
        [edge_ref[z, r, 0] for r in range(chunks) for z in range(zs)]
    ).astype(f32)
    root = lax.rsqrt(edge[:, 1:] - edge[:, :1])
    total = jnp.zeros((rows, 1), f32)
    for first in range(0, width, DH):
        at = slice(first, first + DH)
        summed = sum(s[0, :, at].astype(f32) for s in sums)
        product = q_ref[:, at].astype(f32) * rest_ref[0, :, at].astype(f32)
        weight = silu(jnp.sum(product, axis=1, keepdims=True) * DH ** (-0.5))
        value = summed * root + weight * rest_ref[1, :, at].astype(f32)
        att_ref[:, at] = value
        total += jnp.sum(value, axis=1, keepdims=True)
    mean = total / width
    spread = jnp.zeros((rows, DH), f32)
    for first in range(0, width, DH):
        away = att_ref[:, first:first + DH] - mean
        spread += away * away
    square = jnp.sum(spread, axis=1, keepdims=True)
    if others:
        means, squares = stat_columns(others)
        mean, square = merge([mean] + means, [square] + squares, [width] + widths)
    lane = lax.broadcasted_iota(jnp.int32, (rows, DH), 1)
    stat = jnp.where(lane < 4, mean, square)
    stat_ref[...] = stat if stat_ref.shape == stat.shape else stat.T[:8]


def finish(at, edges, query, rest, sums, others, widths, after):
    rows, width = query.shape
    stat = (8, rows) if others and rows == DH else (rows, DH)
    return pl.pallas_call(
        functools.partial(finish_kernel, len(sums), widths),
        grid_spec=pltpu.PrefetchScalarGridSpec(
            num_scalar_prefetch=1,
            grid=(1,),
            in_specs=[
                edge_spec(edges, 0),
                pl.BlockSpec((rows, width), lambda j, at: (0, 0)),
                pl.BlockSpec((2, rows, width), lambda j, at: (0, 0, 0)),
            ]
            + [pl.BlockSpec((1, rows, width), lambda j, at: (0, 0, 0))] * len(sums)
            + [pl.BlockSpec((rows, DH), lambda j, at: (0, 0))] * len(others)
            + anywhere(after),
            out_specs=(
                pl.BlockSpec((rows, width), lambda j, at: (0, 0)),
                pl.BlockSpec(stat, lambda j, at: (0, 0)),
            ),
        ),
        out_shape=(
            jax.ShapeDtypeStruct((rows, width), f32),
            jax.ShapeDtypeStruct(stat, f32),
        ),
        compiler_params=params(),
        cost_estimate=LIGHT,
        name="finish",
    )(at, edges, query, rest, *sums, *others, *after)


def gate_kernel(count, parts, *refs):
    stats, atts, rests, outs = (
        refs[:count], refs[count:count + parts],
        refs[count + parts:count + 2 * parts], refs[count + 2 * parts:],
    )
    width = sum(a.shape[1] for a in atts)
    means, squares = stat_columns(stats)
    mean, square = merge(means, squares, [width] * count)
    scale = lax.rsqrt(square / (width * count) + EPSILON)
    rows, column = outs[0].shape[0], 0
    for att, rest in zip(atts, rests):
        span = att.shape[1]
        normed = (att[...] - mean) * scale
        gated = (normed * rest[0].astype(f32)).astype(bf16)
        for r, out in enumerate(outs):
            out[:, column:column + span] = gated[r * rows:(r + 1) * rows]
        column += span


def gate_rows(stats, atts, rests, chunks):
    rows, width = atts[0].shape[0], sum(a.shape[1] for a in atts)
    return pl.pallas_call(
        functools.partial(gate_kernel, len(stats), len(atts)),
        grid=(1,),
        in_specs=[pl.BlockSpec(s.shape, lambda j: (0, 0)) for s in stats]
        + [pl.BlockSpec((rows, a.shape[1]), lambda j: (0, 0)) for a in atts]
        + [pl.BlockSpec((1, rows, r.shape[2]), lambda j: (2, 0, 0)) for r in rests],
        out_specs=[pl.BlockSpec((rows // chunks, width), lambda j: (0, 0))] * chunks,
        out_shape=[jax.ShapeDtypeStruct((rows // chunks, width), bf16)] * chunks,
        compiler_params=params(),
        cost_estimate=LIGHT,
        name="gate",
    )(*stats, *atts, *rests)


def output_kernel(owners, after, order_ref, *refs):
    rows, w_ref, outs, lhs_ref = refs[:owners], refs[owners], refs[owners + 1 + after:-1], refs[-1]
    piece = rows[0].shape[1]

    @pl.when(pl.program_id(0) == 0)
    def _():
        first = 0
        for k in range(rows[0].shape[0]):
            for p in range(owners):
                lhs_ref[first:first + piece, :] = rows[p][order_ref[k]]
                first += piece

    sums = jnp.dot(lhs_ref[...], w_ref[...], preferred_element_type=f32).astype(bf16)
    first = 0
    for out in outs:
        for k in range(out.shape[0]):
            for p in range(owners):
                out[k, p] = sums[first:first + piece]
                first += piece


def output(order, counts, blocks, w_out, column, columns, after):
    owners, (each, width), zs = len(blocks), blocks[0].shape, sum(counts)
    piece = each // zs
    span = max(c for c in (512, 256, columns) if columns % c == 0 and column % c == 0)
    row_spec = pl.BlockSpec((zs, piece, width), lambda j, at: (0, 0, 0))
    return pl.pallas_call(
        functools.partial(output_kernel, owners, len(after)),
        grid_spec=pltpu.PrefetchScalarGridSpec(
            num_scalar_prefetch=1,
            grid=(columns // span,),
            in_specs=[row_spec] * owners
            + [pl.BlockSpec((width, span), lambda j, at: (0, column // span + j))]
            + anywhere(after),
            out_specs=[
                pl.BlockSpec((n, owners, piece, span), lambda j, at: (0, 0, 0, j)) for n in counts
            ],
            scratch_shapes=[pltpu.VMEM((owners * each, width), bf16)],
        ),
        out_shape=[jax.ShapeDtypeStruct((n, owners, piece, columns), bf16) for n in counts],
        compiler_params=params(),
        cost_estimate=LIGHT,
        name="output",
    )(order, *[b.reshape(zs, piece, width) for b in blocks], far(w_out), *after)


def close_kernel(counts, at_ref, t_ref, *refs):
    out_ref, mark_ref = refs[-2:]
    mark_ref[...] = jnp.zeros_like(mark_ref)
    first, column = 0, 0
    for count in counts:
        terms = refs[first:first + count]
        span = terms[0].shape[-1]
        at = slice(column, column + span)
        for p in range(out_ref.shape[0]):
            total = t_ref[p, :, at].astype(f32)
            for term in terms:
                total = total + term[0, p ^ at_ref[0]].astype(f32)
            out_ref[p, :, at] = total.astype(bf16)
        first += count
        column += span


def close(place, index, tokens, chunks, r, groups, out, after):
    _, owners, piece, _ = groups[0][0].shape
    width = tokens.shape[1]
    at = jnp.stack([place, index * chunks + r]).astype(jnp.int32)
    flat = [term for terms in groups for term in terms]
    into = [] if out is None else [out]
    return pl.pallas_call(
        functools.partial(close_kernel, [len(terms) for terms in groups]),
        grid_spec=pltpu.PrefetchScalarGridSpec(
            num_scalar_prefetch=1,
            grid=(1,),
            in_specs=[pl.BlockSpec((owners, piece, width), lambda j, at: (at[1], 0, 0))]
            + [pl.BlockSpec((1,) + t.shape[1:], lambda j, at: (0, 0, 0, 0)) for t in flat]
            + anywhere(into) + anywhere(after),
            out_specs=(
                pl.BlockSpec((owners, piece, width), lambda j, at: (r, 0, 0)),
                pl.BlockSpec((8, DH), lambda j, at: (0, 0)),
            ),
        ),
        out_shape=(
            jax.ShapeDtypeStruct((chunks * owners, piece, width), bf16),
            jax.ShapeDtypeStruct((8, DH), f32),
        ),
        input_output_aliases={} if out is None else {2 + len(flat): 0},
        compiler_params=params(),
        cost_estimate=LIGHT,
        name="close",
    )(at, far(tokens.reshape(-1, piece, width)), *flat, *into, *after)


def bits_of(axis):
    count = lax.axis_size(axis)
    assert count & (count - 1) == 0
    return count.bit_length() - 1


def reverse(index, bits):
    return sum((((index >> b) & 1) << (bits - 1 - b) for b in range(bits)), 0 * index)


def swap(x, axis, bit):
    return lax.ppermute(
        x, axis, [(i, i ^ (1 << bit)) for i in range(lax.axis_size(axis))]
    )


def scatter(keep, gots, axis, after=()):
    terms, sent = [keep, gots[0]], gots[-1]
    for b in range(1, bits_of(axis)):
        sent = fold([keep, gots[-1]] if b == 1 else terms, after)
        terms.append(swap(sent, axis, b))
    return terms, sent


def gather(x, axis, after=()):
    blocks = [x]
    for b in reversed(range(bits_of(axis))):
        blocks = blocks + [swap(block, axis, b) for block in blocks]
        if len(blocks) == 2:
            blocks[1] = tie(blocks[1], after)
    return blocks


def shift(x, axis, k):
    count = lax.axis_size(axis)
    return lax.ppermute(x, axis, [(i, (i + k) % count) for i in range(count)])


def all_stats(stat, axis):
    count = lax.axis_size(axis)
    if count > 8:
        every = lax.all_gather(stat, axis)
        return [every[i] for i in range(count)]
    return [stat] + [shift(stat, axis, k) for k in range(1, count)]


def head_chunks(heads):
    if heads % 8:
        return [1] * heads
    unit = heads // 8
    return [unit, 2 * unit, 2 * unit, 2 * unit, unit]


GROUPS = [[0, 1], [2], [3], [4]]
ORDER = [
    "P0", "P1", "F0", "P2", "F1", "P3", "F2", "A0", "F3", "P4", "A1", "F4", "T0", "G0", "A2",
    "T1", "A3", "G1", "E0", "T2", "G2", "T3", "E1", "G3", "E2", "E3",
]


def local(tokens, w_qkvu, k_cache, v_cache, w_out, vis_start, vis_end):
    cand, depth = tokens.shape
    owners, zs = lax.axis_size("hist"), lax.axis_size("head")
    index = lax.axis_index("head")
    place = reverse(lax.axis_index("hist"), bits_of("hist"))
    width = w_qkvu.shape[2]
    events = k_cache.shape[0]
    chunks = 2 if cand % (2 * owners * zs * 16) == 0 else 1
    piece = cand // (zs * chunks * owners)

    def arrange(x):
        x = x.reshape((zs, chunks, owners, piece) + x.shape[1:])
        if piece % 16 == 0:
            return x
        blocks = [lax.dynamic_index_in_dim(x, p ^ place, 2, False) for p in range(owners)]
        x = jnp.stack(blocks).swapaxes(1, 2)
        return x.reshape((1, 1, owners, zs * chunks * piece) + x.shape[4:])

    at = (place if piece % 16 == 0 else jnp.int32(0)).reshape(1)
    ordered = arrange(tokens)
    first_event = lax.axis_index("hist") * events
    edges = arrange(edge_columns(first_event, vis_start, vis_end))

    sizes = head_chunks(width // DH)
    firsts = [sum(sizes[:c]) for c in range(len(sizes))]
    groups, order = GROUPS, ORDER
    if len(sizes) != 5:
        groups = [[c] for c in range(len(sizes))]
        order = [step + str(c) for step in "PFATGE" for c in range(len(sizes))]
    last = len(groups) - 1
    heads = [sum(sizes[c] for c in group) for group in groups]
    chain, keeps, firsts_got, terms, sums = [], {}, {}, {}, {}
    halves, queries, parts, atts, stats = {}, {}, {}, {}, {}
    for step, c in [(name[0], int(name[1:])) for name in order]:
        after = chain[-1:]
        if step == "P":
            keep, *sends = project(at, ordered, w_qkvu, firsts[c], sizes[c], after)
            before = firsts_got[c - 1] if c >= 1 else []
            before = before + [terms[0][-1]] if c == 2 and 0 in terms else before
            firsts_got[c] = [swap(tie(send, before), "hist", 0) for send in reversed(sends)][::-1]
            keeps[c] = keep
            chain.append(keep)
        elif step == "F":
            terms[c], sent = scatter(keeps[c], firsts_got[c], "hist", after)
            chain.append(sent)
        elif step == "A":
            parts[c] = activate([terms[k] for k in groups[c]], after)
            queries[c] = gather(parts[c][0], "hist")
            chain.append(parts[c][0])
        elif step == "T":
            first = firsts[groups[c][0]]
            keep, *sends = attend(at, queries[c], k_cache, v_cache, edges, first, after)
            halves[c] = keep, [swap(send, "hist", 0) for send in sends]
            chain.append(keep)
        elif step == "G":
            sums[c], sent = scatter(*halves[c], "hist", after)
            chain.append(sent)
        else:
            others = [stats[k] for k in range(last)] if c == last else []
            widths = [size * DH for size in heads[:last]] if c == last else []
            atts[c], stats[c] = finish(at, edges, *parts[c], sums[c], others, widths, after)
            chain.append(atts[c])

    atts = [atts[c] for c in range(last + 1)]
    rests = [parts[c][1] for c in range(last + 1)]
    gated = gate_rows(all_stats(stats[last], "head"), atts, rests, chunks)
    columns = w_out.shape[1]
    straight = piece % 16 == 0 and zs & (zs - 1) == 0
    out = None
    if not straight:
        for r, rows in enumerate(gated):
            whole = jnp.concatenate(gather(rows, "hist"))
            whole = jnp.dot(whole, w_out, preferred_element_type=f32).astype(bf16)
            whole = whole.reshape(owners, zs, piece, -1).swapaxes(0, 1)
            whole = lax.psum_scatter(whole, "head", scatter_dimension=0, tiled=True)
            out, _ = close(place, index, tokens, chunks, r, [[whole]], out, [])
        return out.reshape(cand // zs, -1)
    halved = index ^ reverse(jnp.arange(zs, dtype=jnp.int32), bits_of("head"))
    spans = [columns // 2] * 2 if columns % 1024 == 0 else [columns]
    counts = [zs // 2] * 2 if zs > 1 else [1]
    pieces = [(r, sum(spans[:g]), span) for r in range(chunks) for g, span in enumerate(spans)]
    chain, made, groups, blocks = [], [], [[] for _ in range(chunks)], {}

    def sum_next():
        r, own, arrived = made.pop(0)
        terms, sent = scatter(own, arrived, "head", chain) if arrived else ([own], own)
        groups[r].append(terms)
        return [sent]

    first_out = []
    for r, column, span in pieces:
        if r not in blocks:
            blocks[r] = gather(gated[r], "hist", first_out)
        own, *others = output(halved, counts, blocks[r], w_out, column, span, chain)
        made.append((r, own, [swap(x, "head", 0) for x in others]))
        chain, first_out = [own], first_out or [own]
    while len(made) > 1:
        chain = sum_next()
    for r in range(chunks):
        if r == chunks - 1:
            sum_next()
        out, mark = close(place, index, tokens, chunks, r, groups[r], out, chain)
        chain = [mark]
    return out.reshape(cand // zs, -1)


def solution(mesh):
    in_specs = (
        P("groups", "hist"),
        P("hist", None, "head"),
        P(("groups", "hist"), "head"),
        P(("groups", "hist"), "head"),
        P("head", "hist"),
        P("groups"),
        P("groups"),
    )
    out_specs = P(("groups", "head"), "hist")
    return jax.shard_map(local, mesh=mesh, in_specs=in_specs, out_specs=out_specs, check_vma=False)
```

```python
import functools

import jax
import jax.numpy as jnp
from jax import lax
from jax.experimental import pallas as pl
from jax.experimental.pallas import tpu as pltpu
from jax.sharding import PartitionSpec as P

DH = 128
EPSILON = 1e-05
VMEM_LIMIT = 28 * 1024 * 1024

bf16 = jnp.bfloat16
f32 = jnp.float32


def silu(v):
    u = 0.5 * v
    return u + u * jnp.tanh(u)


def params():
    return pltpu.CompilerParams(vmem_limit_bytes=VMEM_LIMIT)


LIGHT = pl.CostEstimate(flops=1000, bytes_accessed=1000, transcendentals=0)
STEP = pl.CostEstimate(flops=1000, bytes_accessed=4_000_000, transcendentals=0)


def far(x):
    return pltpu.with_memory_space_constraint(x, pltpu.HBM)


def anywhere(arrays):
    return [pl.BlockSpec(memory_space=pl.ANY)] * len(arrays)


def project_kernel(parts, owners, after, at_ref, *refs):
    rows, weights = refs[:owners], refs[owners:owners + parts]
    outs, lhs_ref = refs[owners + parts + after:-parts - 1], refs[-parts - 1]
    wides = refs[-parts:]
    zs, chunks, _, piece, _ = rows[0].shape
    depth = weights[0].shape[0]

    @pl.when(pl.program_id(0) == 0)
    def _():
        first = 0
        for p in range(owners):
            for r in range(chunks):
                for z in range(zs):
                    lhs_ref[first:first + piece, :] = rows[p][z, r, 0]
                    first += piece

    res = None
    for k, wide in enumerate(wides):
        wide[...] = weights[k].reshape(depth * 4, DH)[...].astype(f32)
        rhs = jnp.concatenate(
            [wide[pl.ds(i, depth, stride=4), :].astype(bf16) for i in range(4)], axis=1
        )
        term = jnp.dot(lhs_ref[:, k * depth:(k + 1) * depth], rhs, preferred_element_type=f32)
        res = term if res is None else res + term
    res = res.astype(bf16)
    each, first = outs[0].shape[2], 0
    for out in outs:
        for p in range(out.shape[0]):
            for i in range(4):
                out[p, i] = res[first:first + each, i * DH:(i + 1) * DH]
            first += each


def parts_of(owners):
    half = owners // 2
    return [half, half // 2, half // 2] if half > 1 else [half, half]


def project(at, tokens, w, head_first, heads, after):
    zs, chunks, owners, piece, depth = tokens.shape
    each, counts = zs * chunks * piece, parts_of(owners)
    parts = 4 if depth % 512 == 0 else 1
    return pl.pallas_call(
        functools.partial(project_kernel, parts, owners, len(after)),
        grid_spec=pltpu.PrefetchScalarGridSpec(
            num_scalar_prefetch=1,
            grid=(heads,),
            in_specs=[
                pl.BlockSpec(
                    (zs, chunks, 1, piece, depth), lambda j, at, p=p: (0, 0, at[0] ^ p, 0, 0)
                )
                for p in range(owners)
            ]
            + [
                pl.BlockSpec((depth // parts, 4, DH), lambda j, at, k=k: (k, 0, head_first + j))
                for k in range(parts)
            ]
            + anywhere(after),
            out_specs=[
                pl.BlockSpec((n, 4, each, DH), lambda j, at: (0, 0, 0, j)) for n in counts
            ],
            scratch_shapes=[pltpu.VMEM((owners * each, depth), bf16)]
            + [pltpu.VMEM((depth // parts * 4, DH), f32) for _ in range(parts)],
        ),
        out_shape=[jax.ShapeDtypeStruct((n, 4, each, heads * DH), bf16) for n in counts],
        compiler_params=params(),
        cost_estimate=LIGHT,
        name="project",
    )(at, *[far(tokens)] * owners, *[far(w)] * parts, *after)


def tie_kernel(*refs):
    pass


def tie(x, after):
    if not after:
        return x
    return pl.pallas_call(
        tie_kernel,
        in_specs=anywhere([x, *after]),
        out_specs=pl.BlockSpec(memory_space=pl.ANY),
        out_shape=jax.ShapeDtypeStruct(x.shape, x.dtype),
        input_output_aliases={0: 0},
        compiler_params=params(),
        cost_estimate=LIGHT,
        name="tie",
    )(x, *after)


def fold_kernel(count, *refs):
    refs[-1][...] = sum(r[...].astype(f32) for r in refs[:count]).astype(bf16)


def fold(terms, after=(), told=LIGHT):
    half = terms[0].shape[0] // 2 if len(terms) == 2 else terms[-1].shape[0] // 2
    tail = terms[0].shape[1:]
    steps = 2 if tail[-1] % 256 == 0 else 1
    block = (half,) + tail[:-1] + (tail[-1] // steps,)
    middle = (0,) * (len(tail) - 1)
    firsts = [0 if t.shape[0] == half else 1 for t in terms]
    return pl.pallas_call(
        functools.partial(fold_kernel, len(terms)),
        grid=(steps,),
        in_specs=[pl.BlockSpec(block, lambda j, f=f: (f,) + middle + (j,)) for f in firsts]
        + anywhere(after),
        out_specs=pl.BlockSpec(block, lambda j: (0,) + middle + (j,)),
        out_shape=jax.ShapeDtypeStruct((half,) + tail, bf16),
        compiler_params=params(),
        cost_estimate=told,
        name="fold",
    )(*terms, *after)


def activate_kernel(counts, *refs):
    q_ref, rest_ref = refs[-2:]
    first, column = 0, 0
    for count in counts:
        terms = refs[first:first + count]
        span = terms[0].shape[-1]
        for i in range(4):
            part = silu(sum(t[0, i].astype(f32) for t in terms)).astype(bf16)
            if i == 0:
                q_ref[:, column:column + span] = part
            else:
                rest_ref[i - 1, :, column:column + span] = part
        first += count
        column += span


def activate(chunks, after):
    each, width = chunks[0][0].shape[2], sum(terms[0].shape[3] for terms in chunks)
    flat = [term for terms in chunks for term in terms]
    return pl.pallas_call(
        functools.partial(activate_kernel, [len(terms) for terms in chunks]),
        grid=(1,),
        in_specs=[pl.BlockSpec((1,) + t.shape[1:], lambda j: (0, 0, 0, 0)) for t in flat]
        + anywhere(after),
        out_specs=(
            pl.BlockSpec((each, width), lambda j: (0, 0)),
            pl.BlockSpec((3, each, width), lambda j: (0, 0, 0)),
        ),
        out_shape=(
            jax.ShapeDtypeStruct((each, width), bf16),
            jax.ShapeDtypeStruct((3, each, width), bf16),
        ),
        compiler_params=params(),
        cost_estimate=LIGHT,
        name="activate",
    )(*flat, *after)


def edge_kernel(base_ref, start_ref, end_ref, out_ref):
    row = lax.broadcasted_iota(jnp.int32, (DH, DH), 0)
    for b in range(start_ref.shape[0]):
        start, end = start_ref[b:b + 1, :], end_ref[b:b + 1, :]
        both = jnp.where(row == 0, start, end) - base_ref[0]
        out_ref[b * DH:(b + 1) * DH, :] = both.astype(f32).T[:, :2].astype(jnp.int32)


def edge_columns(base, start, end):
    count = start.shape[0]
    lines = pl.BlockSpec((count // DH, DH), lambda j, base: (0, 0))
    return pl.pallas_call(
        edge_kernel,
        grid_spec=pltpu.PrefetchScalarGridSpec(
            num_scalar_prefetch=1,
            grid=(1,),
            in_specs=[lines, lines],
            out_specs=pl.BlockSpec((count, 2), lambda j, base: (0, 0)),
        ),
        out_shape=jax.ShapeDtypeStruct((count, 2), jnp.int32),
        compiler_params=params(),
        cost_estimate=LIGHT,
        name="edges",
    )(base.reshape(1), start.reshape(-1, DH), end.reshape(-1, DH))


def attend_kernel(owners, sends, at_ref, *refs):
    queries, edges = refs[:owners], refs[owners:2 * owners]
    k_ref, v_ref = refs[2 * owners:2 * owners + 2]
    outs, mask_ref = refs[-1 - sends:-1], refs[-1]
    events = mask_ref.shape[1]
    each = outs[0].shape[1]

    @pl.when(pl.program_id(0) == 0)
    def _():
        zs, chunks, _, piece, _ = edges[0].shape
        at = lax.broadcasted_iota(jnp.int32, (piece, events), 1)
        first = 0
        for p in range(owners):
            for r in range(chunks):
                for z in range(zs):
                    edge = edges[p][z, r, 0]
                    seen = (at >= edge[:, :1]) & (at < edge[:, 1:])
                    mask_ref[first:first + piece, :] = jnp.where(seen, 1.0, 0.0).astype(bf16)
                    first += piece

    for h in range(k_ref.shape[1] // DH):
        at = slice(h * DH, (h + 1) * DH)
        query = jnp.concatenate([q[:, at] for q in queries])
        u = lax.dot_general(
            query, k_ref[:, at], (((1,), (1,)), ((), ())), preferred_element_type=f32
        ) * (0.5 * DH ** (-0.5))
        weights = (u + u * jnp.tanh(u)).astype(bf16) * mask_ref[...]
        term = jnp.dot(weights, v_ref[:, at], preferred_element_type=f32).astype(bf16)
        first = 0
        for out in outs:
            for p in range(out.shape[0]):
                out[p, :, at] = term[first:first + each]
                first += each


def edge_spec(edges, p):
    zs, chunks, _, piece, ends = edges.shape
    return pl.BlockSpec((zs, chunks, 1, piece, ends), lambda j, at: (0, 0, at[0] ^ p, 0, 0))


def attend(at, queries, k_cache, v_cache, edges, head_first, after):
    owners, (each, width) = len(queries), queries[0].shape
    rows, events, counts = owners * each, k_cache.shape[0], parts_of(owners)
    first = head_first * DH
    span = max(h for h in range(DH, 4 * DH, DH) if width % h == 0 and first % h == 0)
    cache = pl.BlockSpec((events, span), lambda j, at: (0, first // span + j))
    return pl.pallas_call(
        functools.partial(attend_kernel, owners, len(counts)),
        grid_spec=pltpu.PrefetchScalarGridSpec(
            num_scalar_prefetch=1,
            grid=(width // span,),
            in_specs=[pl.BlockSpec((each, span), lambda j, at: (0, j))] * owners
            + [edge_spec(edges, p) for p in range(owners)]
            + [cache, cache]
            + anywhere(after),
            out_specs=[pl.BlockSpec((n, each, span), lambda j, at: (0, 0, j)) for n in counts],
            scratch_shapes=[pltpu.VMEM((rows, events), bf16)],
        ),
        out_shape=[jax.ShapeDtypeStruct((n, each, width), bf16) for n in counts],
        compiler_params=params(),
        cost_estimate=LIGHT,
        name="attend",
    )(at, *queries, *[edges] * owners, far(k_cache), far(v_cache), *after)


def merge(means, squares, widths):
    width = sum(widths)
    mean = sum(m * (w / width) for m, w in zip(means, widths))
    square = sum(squares) + sum(w * (m - mean) * (m - mean) for m, w in zip(means, widths))
    return mean, square


def stat_columns(stats):
    stats = [s[...] for s in stats]
    stats = [s if s.shape[0] > 8 else jnp.concatenate([s] * (DH // 8)).T for s in stats]
    return [s[:, :1] for s in stats], [s[:, 4:5] for s in stats]


def finish_kernel(terms, widths, at_ref, edge_ref, q_ref, rest_ref, *refs):
    sums, others = refs[:terms], refs[terms:terms + len(widths)]
    att_ref, stat_ref = refs[-2:]
    rows, width = att_ref.shape
    zs, chunks = edge_ref.shape[:2]
    edge = jnp.concatenate(
        [edge_ref[z, r, 0] for r in range(chunks) for z in range(zs)]
    ).astype(f32)
    root = lax.rsqrt(edge[:, 1:] - edge[:, :1])
    total = jnp.zeros((rows, 1), f32)
    for first in range(0, width, DH):
        at = slice(first, first + DH)
        summed = sum(s[0, :, at].astype(f32) for s in sums)
        product = q_ref[:, at].astype(f32) * rest_ref[0, :, at].astype(f32)
        weight = silu(jnp.sum(product, axis=1, keepdims=True) * DH ** (-0.5))
        value = summed * root + weight * rest_ref[1, :, at].astype(f32)
        att_ref[:, at] = value
        total += jnp.sum(value, axis=1, keepdims=True)
    mean = total / width
    spread = jnp.zeros((rows, DH), f32)
    for first in range(0, width, DH):
        away = att_ref[:, first:first + DH] - mean
        spread += away * away
    square = jnp.sum(spread, axis=1, keepdims=True)
    if others:
        means, squares = stat_columns(others)
        mean, square = merge([mean] + means, [square] + squares, [width] + widths)
    lane = lax.broadcasted_iota(jnp.int32, (rows, DH), 1)
    stat = jnp.where(lane < 4, mean, square)
    stat_ref[...] = stat if stat_ref.shape == stat.shape else stat.T[:8]


def finish(at, edges, query, rest, sums, others, widths, after):
    rows, width = query.shape
    stat = (8, rows) if others and rows == DH else (rows, DH)
    return pl.pallas_call(
        functools.partial(finish_kernel, len(sums), widths),
        grid_spec=pltpu.PrefetchScalarGridSpec(
            num_scalar_prefetch=1,
            grid=(1,),
            in_specs=[
                edge_spec(edges, 0),
                pl.BlockSpec((rows, width), lambda j, at: (0, 0)),
                pl.BlockSpec((2, rows, width), lambda j, at: (0, 0, 0)),
            ]
            + [pl.BlockSpec((1, rows, width), lambda j, at: (0, 0, 0))] * len(sums)
            + [pl.BlockSpec((rows, DH), lambda j, at: (0, 0))] * len(others)
            + anywhere(after),
            out_specs=(
                pl.BlockSpec((rows, width), lambda j, at: (0, 0)),
                pl.BlockSpec(stat, lambda j, at: (0, 0)),
            ),
        ),
        out_shape=(
            jax.ShapeDtypeStruct((rows, width), f32),
            jax.ShapeDtypeStruct(stat, f32),
        ),
        compiler_params=params(),
        cost_estimate=LIGHT,
        name="finish",
    )(at, edges, query, rest, *sums, *others, *after)


def merge_kernel(width, *refs):
    (m, n), (s, t) = (
        [r[:4] if r.shape[0] == 8 else r[:, :4] for r in refs[:2]],
        [r[4:] if r.shape[0] == 8 else r[:, 4:8] for r in refs[:2]],
    )
    mean, square = merge([m, n], [s, t], [width] * 2)
    if refs[2].shape[0] == 8:
        refs[2][:4], refs[2][4:] = mean, square
    else:
        lane = lax.broadcasted_iota(jnp.int32, refs[2].shape, 1)
        refs[2][...] = jnp.where(lane < 4, mean[:, :1], square[:, :1])


def merge_stats(stats, width):
    return pl.pallas_call(
        functools.partial(merge_kernel, width),
        out_shape=jax.ShapeDtypeStruct(stats[0].shape, f32),
        compiler_params=params(),
        cost_estimate=LIGHT,
        name="merge",
    )(*stats)


def gate_kernel(count, parts, width, *refs):
    stats, atts, rests, outs = (
        refs[:count], refs[count:count + parts],
        refs[count + parts:count + 2 * parts], refs[count + 2 * parts:],
    )
    means, squares = stat_columns(stats)
    mean, square = merge(means, squares, [width] * count)
    scale = lax.rsqrt(square / (width * count) + EPSILON)
    rows, column = outs[0].shape[0], 0
    for att, rest in zip(atts, rests):
        span = att.shape[1]
        normed = (att[...] - mean) * scale
        gated = (normed * rest[0].astype(f32)).astype(bf16)
        for r, out in enumerate(outs):
            out[:, column:column + span] = gated[r * rows:(r + 1) * rows]
        column += span


def gate_rows(stats, stat_width, atts, rests, chunks):
    rows, width = atts[0].shape[0], sum(a.shape[1] for a in atts)
    return pl.pallas_call(
        functools.partial(gate_kernel, len(stats), len(atts), stat_width),
        grid=(1,),
        in_specs=[pl.BlockSpec(s.shape, lambda j: (0, 0)) for s in stats]
        + [pl.BlockSpec((rows, a.shape[1]), lambda j: (0, 0)) for a in atts]
        + [pl.BlockSpec((1, rows, r.shape[2]), lambda j: (2, 0, 0)) for r in rests],
        out_specs=[pl.BlockSpec((rows // chunks, width), lambda j: (0, 0))] * chunks,
        out_shape=[jax.ShapeDtypeStruct((rows // chunks, width), bf16)] * chunks,
        compiler_params=params(),
        cost_estimate=LIGHT,
        name="gate",
    )(*stats, *atts, *rests)


def output_kernel(owners, slots, after, index_ref, *refs):
    rows, w_ref, outs, lhs_ref = refs[:owners], refs[owners], refs[owners + 1 + after:-1], refs[-1]
    piece = rows[0].shape[1]

    @pl.when(pl.program_id(0) == 0)
    def _():
        first = 0
        for slot in slots:
            for p in range(owners):
                lhs_ref[first:first + piece, :] = rows[p][index_ref[0] ^ slot]
                first += piece

    sums = jnp.dot(lhs_ref[...], w_ref[...], preferred_element_type=f32).astype(bf16)
    first = 0
    for out in outs:
        for k in range(out.shape[0]):
            for p in range(owners):
                out[k, p] = sums[first:first + piece]
                first += piece


def output(index, slots, counts, blocks, w_out, column, columns, after):
    owners, (each, width), zs = len(blocks), blocks[0].shape, sum(counts)
    piece = each // zs
    span = max(c for c in (512, 256, columns) if columns % c == 0 and column % c == 0)
    row_spec = pl.BlockSpec((zs, piece, width), lambda j, at: (0, 0, 0))
    return pl.pallas_call(
        functools.partial(output_kernel, owners, slots, len(after)),
        grid_spec=pltpu.PrefetchScalarGridSpec(
            num_scalar_prefetch=1,
            grid=(columns // span,),
            in_specs=[row_spec] * owners
            + [pl.BlockSpec((width, span), lambda j, at: (0, column // span + j))]
            + anywhere(after),
            out_specs=[
                pl.BlockSpec((n, owners, piece, span), lambda j, at: (0, 0, 0, j)) for n in counts
            ],
            scratch_shapes=[pltpu.VMEM((owners * each, width), bf16)],
        ),
        out_shape=[jax.ShapeDtypeStruct((n, owners, piece, columns), bf16) for n in counts],
        compiler_params=params(),
        cost_estimate=LIGHT,
        name="output",
    )(
        index.reshape(1).astype(jnp.int32),
        *[b.reshape(zs, piece, width) for b in blocks], far(w_out), *after,
    )


def close_kernel(count, at_ref, t_ref, *refs):
    out_ref, mark_ref = refs[-2:]
    mark_ref[...] = jnp.zeros_like(mark_ref)
    for p in range(out_ref.shape[0]):
        total = t_ref[p].astype(f32)
        for term in refs[:count]:
            total = total + term[0, p ^ at_ref[0]].astype(f32)
        out_ref[p] = total.astype(bf16)


def close(place, index, tokens, chunks, r, g, terms, out, after):
    _, owners, piece, span = terms[0].shape
    at = jnp.stack([place, index * chunks + r]).astype(jnp.int32)
    into = [] if out is None else [out]
    return pl.pallas_call(
        functools.partial(close_kernel, len(terms)),
        grid_spec=pltpu.PrefetchScalarGridSpec(
            num_scalar_prefetch=1,
            grid=(1,),
            in_specs=[pl.BlockSpec((owners, piece, span), lambda j, at: (at[1], 0, g))]
            + [pl.BlockSpec((1,) + t.shape[1:], lambda j, at: (0, 0, 0, 0)) for t in terms]
            + anywhere(into) + anywhere(after),
            out_specs=(
                pl.BlockSpec((owners, piece, span), lambda j, at: (r, 0, g)),
                pl.BlockSpec((8, DH), lambda j, at: (0, 0)),
            ),
        ),
        out_shape=(
            jax.ShapeDtypeStruct((chunks * owners, piece, tokens.shape[1]), bf16),
            jax.ShapeDtypeStruct((8, DH), f32),
        ),
        input_output_aliases={} if out is None else {2 + len(terms): 0},
        compiler_params=params(),
        cost_estimate=STEP,
        name="close",
    )(at, far(tokens.reshape(-1, piece, tokens.shape[1])), *terms, *into, *after)


def bits_of(axis):
    count = lax.axis_size(axis)
    assert count & (count - 1) == 0
    return count.bit_length() - 1


def reverse(index, bits):
    return sum((((index >> b) & 1) << (bits - 1 - b) for b in range(bits)), 0 * index)


def swap(x, axis, bit):
    return lax.ppermute(
        x, axis, [(i, i ^ (1 << bit)) for i in range(lax.axis_size(axis))]
    )


def scatter(keep, gots, axis, after=(), told=LIGHT):
    terms, sent = [keep, gots[0]], gots[-1]
    for b in range(1, bits_of(axis)):
        sent = fold([keep, gots[-1]] if b == 1 else terms, after, told)
        terms.append(swap(sent, axis, b))
    return terms, sent


def gather(x, axis, after=()):
    blocks = [x]
    for b in reversed(range(bits_of(axis))):
        blocks = blocks + [swap(block, axis, b) for block in blocks]
        if len(blocks) == 2:
            blocks[1] = tie(blocks[1], after)
    return blocks


def all_stats(stat, width, axis):
    count = lax.axis_size(axis)
    if count > 8 or count & (count - 1):
        every = lax.all_gather(stat, axis)
        return [every[i] for i in range(count)], width
    stats = [stat]
    for b in range(bits_of(axis)):
        if b:
            width, stats = 2 * width, [merge_stats(stats, width)]
        stats.append(swap(stats[0], axis, b))
    return stats, width


def head_chunks(heads):
    if heads % 8:
        return [1] * heads
    unit = heads // 8
    return [unit, 2 * unit, 2 * unit, 2 * unit, unit]


GROUPS = [[0, 1], [2], [3], [4]]
ORDER = [
    "P0", "P1", "F0", "P2", "F1", "P3", "F2", "A0", "F3", "P4", "A1", "F4", "T0", "G0", "A2",
    "T1", "A3", "G1", "T2", "E0", "G2", "T3", "G3", "E1", "E2", "E3",
]


def local(tokens, w_qkvu, k_cache, v_cache, w_out, vis_start, vis_end):
    cand, depth = tokens.shape
    owners, zs = lax.axis_size("hist"), lax.axis_size("head")
    index = lax.axis_index("head")
    place = reverse(lax.axis_index("hist"), bits_of("hist"))
    width = w_qkvu.shape[2]
    events = k_cache.shape[0]
    chunks = 2 if cand % (2 * owners * zs * 16) == 0 else 1
    piece = cand // (zs * chunks * owners)

    def arrange(x):
        x = x.reshape((zs, chunks, owners, piece) + x.shape[1:])
        if piece % 16 == 0:
            return x
        blocks = [lax.dynamic_index_in_dim(x, p ^ place, 2, False) for p in range(owners)]
        x = jnp.stack(blocks).swapaxes(1, 2)
        return x.reshape((1, 1, owners, zs * chunks * piece) + x.shape[4:])

    at = (place if piece % 16 == 0 else jnp.int32(0)).reshape(1)
    ordered = arrange(tokens)
    first_event = lax.axis_index("hist") * events
    edges = arrange(edge_columns(first_event, vis_start, vis_end))

    sizes = head_chunks(width // DH)
    firsts = [sum(sizes[:c]) for c in range(len(sizes))]
    groups, order = GROUPS, ORDER
    if len(sizes) != 5:
        groups = [[c] for c in range(len(sizes))]
        order = [step + str(c) for step in "PFATGE" for c in range(len(sizes))]
    last = len(groups) - 1
    heads = [sum(sizes[c] for c in group) for group in groups]
    chain, keeps, firsts_got, terms, sums = [], {}, {}, {}, {}
    halves, queries, parts, atts, stats = {}, {}, {}, {}, {}
    for step, c in [(name[0], int(name[1:])) for name in order]:
        after = chain[-1:]
        if step == "P":
            keep, *sends = project(at, ordered, w_qkvu, firsts[c], sizes[c], after)
            before = firsts_got[c - 1] if c >= 1 else []
            before = before + [terms[0][-1]] if c == 2 and 0 in terms else before
            firsts_got[c] = [swap(tie(send, before), "hist", 0) for send in reversed(sends)][::-1]
            keeps[c] = keep
            chain.append(keep)
        elif step == "F":
            terms[c], sent = scatter(keeps[c], firsts_got[c], "hist", after)
            chain.append(sent)
        elif step == "A":
            parts[c] = activate([terms[k] for k in groups[c]], after)
            queries[c] = gather(parts[c][0], "hist")
            chain.append(parts[c][0])
        elif step == "T":
            first = firsts[groups[c][0]]
            keep, *sends = attend(at, queries[c], k_cache, v_cache, edges, first, after)
            halves[c] = keep, [swap(send, "hist", 0) for send in sends]
            chain.append(keep)
        elif step == "G":
            sums[c], sent = scatter(*halves[c], "hist", after)
            chain.append(sent)
        else:
            others = [stats[k] for k in range(last)] if c == last else []
            widths = [size * DH for size in heads[:last]] if c == last else []
            atts[c], stats[c] = finish(at, edges, *parts[c], sums[c], others, widths, after)
            chain.append(atts[c])

    atts = [atts[c] for c in range(last + 1)]
    rests = [parts[c][1] for c in range(last + 1)]
    every, stat_width = all_stats(stats[last], width, "head")
    gated = gate_rows(every, stat_width, atts, rests, chunks)
    columns = w_out.shape[1]
    straight = piece % 16 == 0 and zs & (zs - 1) == 0
    out, last_out = None, []
    if not straight:
        for r, rows in enumerate(gated):
            whole = jnp.concatenate(gather(rows, "hist"))
            whole = jnp.dot(whole, w_out, preferred_element_type=f32).astype(bf16)
            whole = whole.reshape(owners, zs, piece, -1).swapaxes(0, 1)
            whole = lax.psum_scatter(whole, "head", scatter_dimension=0, tiled=True)
            out, _ = close(place, index, tokens, chunks, r, 0, [whole], out, [])
        return out.reshape(cand // zs, -1)
    slots = [reverse(k, bits_of("head")) for k in range(zs)]
    groups = 2 if columns % 1024 == 0 else 1
    span = columns // groups
    pieces, first_out, counts = [], [], [zs // 2] * 2 if zs > 1 else [1]
    for r, rows in enumerate(gated):
        blocks = gather(rows, "hist", first_out)
        for g in range(groups):
            own, *others = output(
                index, slots, counts, blocks, w_out, g * span, span, last_out
            )
            pieces.append((r, g, own, [swap(x, "head", 0) for x in others]))
            last_out, first_out = [own], first_out or [own]
    closing, chain = [], last_out
    for r, g, own, arrived in pieces:
        terms, sent = scatter(own, arrived, "head", chain, STEP) if arrived else ([own], own)
        chain = [sent]
        closing.append((r, g, terms))
        if len(closing) > 1:
            out, mark = close(place, index, tokens, chunks, *closing.pop(0), out, chain)
            chain = [mark]
    for last_piece in closing:
        out, _ = close(place, index, tokens, chunks, *last_piece, out, [])
    return out.reshape(cand // zs, -1)


def solution(mesh):
    in_specs = (
        P("groups", "hist"),
        P("hist", None, "head"),
        P(("groups", "hist"), "head"),
        P(("groups", "hist"), "head"),
        P("head", "hist"),
        P("groups"),
        P("groups"),
    )
    out_specs = P(("groups", "head"), "hist")
    return jax.shard_map(local, mesh=mesh, in_specs=in_specs, out_specs=out_specs, check_vma=False)
```

```python
import functools

import jax
import jax.numpy as jnp
from jax import lax
from jax.experimental import pallas as pl
from jax.experimental.pallas import tpu as pltpu
from jax.sharding import PartitionSpec as P

DH = 128
EPSILON = 1e-05
VMEM_LIMIT = 28 * 1024 * 1024

bf16 = jnp.bfloat16
f32 = jnp.float32


def silu(v):
    u = 0.5 * v
    return u + u * jnp.tanh(u)


def params():
    return pltpu.CompilerParams(vmem_limit_bytes=VMEM_LIMIT)


LIGHT = pl.CostEstimate(flops=1000, bytes_accessed=1000, transcendentals=0)


def far(x):
    return pltpu.with_memory_space_constraint(x, pltpu.HBM)


def anywhere(arrays):
    return [pl.BlockSpec(memory_space=pl.ANY)] * len(arrays)


def project_kernel(parts, owners, after, at_ref, *refs):
    rows, weights = refs[:owners], refs[owners:owners + parts]
    outs, lhs_ref = refs[owners + parts + after:-parts - 1], refs[-parts - 1]
    wides = refs[-parts:]
    zs, chunks, _, piece, _ = rows[0].shape
    depth = weights[0].shape[0]

    @pl.when(pl.program_id(0) == 0)
    def _():
        first = 0
        for p in range(owners):
            for r in range(chunks):
                for z in range(zs):
                    lhs_ref[first:first + piece, :] = rows[p][z, r, 0]
                    first += piece

    res = None
    for k, wide in enumerate(wides):
        wide[...] = weights[k].reshape(depth * 4, DH)[...].astype(f32)
        rhs = jnp.concatenate(
            [wide[pl.ds(i, depth, stride=4), :].astype(bf16) for i in range(4)], axis=1
        )
        term = jnp.dot(lhs_ref[:, k * depth:(k + 1) * depth], rhs, preferred_element_type=f32)
        res = term if res is None else res + term
    res = res.astype(bf16)
    each, first = outs[0].shape[2], 0
    for out in outs:
        for p in range(out.shape[0]):
            for i in range(4):
                out[p, i] = res[first:first + each, i * DH:(i + 1) * DH]
            first += each


def parts_of(owners):
    half = owners // 2
    return [half, half // 2, half // 2] if half > 1 else [half, half]


def project(at, tokens, w, head_first, heads, after):
    zs, chunks, owners, piece, depth = tokens.shape
    each, counts = zs * chunks * piece, parts_of(owners)
    parts = 4 if depth % 512 == 0 else 1
    return pl.pallas_call(
        functools.partial(project_kernel, parts, owners, len(after)),
        grid_spec=pltpu.PrefetchScalarGridSpec(
            num_scalar_prefetch=1,
            grid=(heads,),
            in_specs=[
                pl.BlockSpec(
                    (zs, chunks, 1, piece, depth), lambda j, at, p=p: (0, 0, at[0] ^ p, 0, 0)
                )
                for p in range(owners)
            ]
            + [
                pl.BlockSpec((depth // parts, 4, DH), lambda j, at, k=k: (k, 0, head_first + j))
                for k in range(parts)
            ]
            + anywhere(after),
            out_specs=[
                pl.BlockSpec((n, 4, each, DH), lambda j, at: (0, 0, 0, j)) for n in counts
            ],
            scratch_shapes=[pltpu.VMEM((owners * each, depth), bf16)]
            + [pltpu.VMEM((depth // parts * 4, DH), f32) for _ in range(parts)],
        ),
        out_shape=[jax.ShapeDtypeStruct((n, 4, each, heads * DH), bf16) for n in counts],
        compiler_params=params(),
        cost_estimate=LIGHT,
        name="project",
    )(at, *[far(tokens)] * owners, *[far(w)] * parts, *after)


def tie_kernel(*refs):
    pass


def tie(x, after):
    if not after:
        return x
    return pl.pallas_call(
        tie_kernel,
        in_specs=anywhere([x, *after]),
        out_specs=pl.BlockSpec(memory_space=pl.ANY),
        out_shape=jax.ShapeDtypeStruct(x.shape, x.dtype),
        input_output_aliases={0: 0},
        compiler_params=params(),
        cost_estimate=LIGHT,
        name="tie",
    )(x, *after)


def fold_kernel(count, *refs):
    refs[-1][...] = sum(r[...].astype(f32) for r in refs[:count]).astype(bf16)


def fold(terms, after=()):
    half = terms[0].shape[0] // 2 if len(terms) == 2 else terms[-1].shape[0] // 2
    tail = terms[0].shape[1:]
    steps = 2 if tail[-1] % 256 == 0 else 1
    block = (half,) + tail[:-1] + (tail[-1] // steps,)
    middle = (0,) * (len(tail) - 1)
    firsts = [0 if t.shape[0] == half else 1 for t in terms]
    return pl.pallas_call(
        functools.partial(fold_kernel, len(terms)),
        grid=(steps,),
        in_specs=[pl.BlockSpec(block, lambda j, f=f: (f,) + middle + (j,)) for f in firsts]
        + anywhere(after),
        out_specs=pl.BlockSpec(block, lambda j: (0,) + middle + (j,)),
        out_shape=jax.ShapeDtypeStruct((half,) + tail, bf16),
        compiler_params=params(),
        cost_estimate=LIGHT,
        name="fold",
    )(*terms, *after)


def activate_kernel(counts, *refs):
    q_ref, rest_ref = refs[-2:]
    first, column = 0, 0
    for count in counts:
        terms = refs[first:first + count]
        span = terms[0].shape[-1]
        for i in range(4):
            part = silu(sum(t[0, i].astype(f32) for t in terms)).astype(bf16)
            if i == 0:
                q_ref[:, column:column + span] = part
            else:
                rest_ref[i - 1, :, column:column + span] = part
        first += count
        column += span


def activate(chunks, after):
    each, width = chunks[0][0].shape[2], sum(terms[0].shape[3] for terms in chunks)
    flat = [term for terms in chunks for term in terms]
    return pl.pallas_call(
        functools.partial(activate_kernel, [len(terms) for terms in chunks]),
        grid=(1,),
        in_specs=[pl.BlockSpec((1,) + t.shape[1:], lambda j: (0, 0, 0, 0)) for t in flat]
        + anywhere(after),
        out_specs=(
            pl.BlockSpec((each, width), lambda j: (0, 0)),
            pl.BlockSpec((3, each, width), lambda j: (0, 0, 0)),
        ),
        out_shape=(
            jax.ShapeDtypeStruct((each, width), bf16),
            jax.ShapeDtypeStruct((3, each, width), bf16),
        ),
        compiler_params=params(),
        cost_estimate=LIGHT,
        name="activate",
    )(*flat, *after)


def edge_kernel(base_ref, start_ref, end_ref, out_ref):
    row = lax.broadcasted_iota(jnp.int32, (DH, DH), 0)
    for b in range(start_ref.shape[0]):
        start, end = start_ref[b:b + 1, :], end_ref[b:b + 1, :]
        both = jnp.where(row == 0, start, end) - base_ref[0]
        out_ref[b * DH:(b + 1) * DH, :] = both.astype(f32).T[:, :2].astype(jnp.int32)


def edge_columns(base, start, end):
    count = start.shape[0]
    lines = pl.BlockSpec((count // DH, DH), lambda j, base: (0, 0))
    return pl.pallas_call(
        edge_kernel,
        grid_spec=pltpu.PrefetchScalarGridSpec(
            num_scalar_prefetch=1,
            grid=(1,),
            in_specs=[lines, lines],
            out_specs=pl.BlockSpec((count, 2), lambda j, base: (0, 0)),
        ),
        out_shape=jax.ShapeDtypeStruct((count, 2), jnp.int32),
        compiler_params=params(),
        cost_estimate=LIGHT,
        name="edges",
    )(base.reshape(1), start.reshape(-1, DH), end.reshape(-1, DH))


def attend_kernel(owners, sends, at_ref, *refs):
    queries, edges = refs[:owners], refs[owners:2 * owners]
    k_ref, v_ref = refs[2 * owners:2 * owners + 2]
    outs, mask_ref = refs[-1 - sends:-1], refs[-1]
    events = mask_ref.shape[1]
    each = outs[0].shape[1]

    @pl.when(pl.program_id(0) == 0)
    def _():
        zs, chunks, _, piece, _ = edges[0].shape
        at = lax.broadcasted_iota(jnp.int32, (piece, events), 1)
        first = 0
        for p in range(owners):
            for r in range(chunks):
                for z in range(zs):
                    edge = edges[p][z, r, 0]
                    seen = (at >= edge[:, :1]) & (at < edge[:, 1:])
                    mask_ref[first:first + piece, :] = jnp.where(seen, 1.0, 0.0).astype(bf16)
                    first += piece

    for h in range(k_ref.shape[1] // DH):
        at = slice(h * DH, (h + 1) * DH)
        query = jnp.concatenate([q[:, at] for q in queries])
        u = lax.dot_general(
            query, k_ref[:, at], (((1,), (1,)), ((), ())), preferred_element_type=f32
        ) * (0.5 * DH ** (-0.5))
        weights = (u + u * jnp.tanh(u)).astype(bf16) * mask_ref[...]
        term = jnp.dot(weights, v_ref[:, at], preferred_element_type=f32).astype(bf16)
        first = 0
        for out in outs:
            for p in range(out.shape[0]):
                out[p, :, at] = term[first:first + each]
                first += each


def edge_spec(edges, p):
    zs, chunks, _, piece, ends = edges.shape
    return pl.BlockSpec((zs, chunks, 1, piece, ends), lambda j, at: (0, 0, at[0] ^ p, 0, 0))


def attend(at, queries, k_cache, v_cache, edges, head_first, after):
    owners, (each, width) = len(queries), queries[0].shape
    rows, events, counts = owners * each, k_cache.shape[0], parts_of(owners)
    first = head_first * DH
    span = max(h for h in range(DH, 4 * DH, DH) if width % h == 0 and first % h == 0)
    cache = pl.BlockSpec((events, span), lambda j, at: (0, first // span + j))
    return pl.pallas_call(
        functools.partial(attend_kernel, owners, len(counts)),
        grid_spec=pltpu.PrefetchScalarGridSpec(
            num_scalar_prefetch=1,
            grid=(width // span,),
            in_specs=[pl.BlockSpec((each, span), lambda j, at: (0, j))] * owners
            + [edge_spec(edges, p) for p in range(owners)]
            + [cache, cache]
            + anywhere(after),
            out_specs=[pl.BlockSpec((n, each, span), lambda j, at: (0, 0, j)) for n in counts],
            scratch_shapes=[pltpu.VMEM((rows, events), bf16)],
        ),
        out_shape=[jax.ShapeDtypeStruct((n, each, width), bf16) for n in counts],
        compiler_params=params(),
        cost_estimate=LIGHT,
        name="attend",
    )(at, *queries, *[edges] * owners, far(k_cache), far(v_cache), *after)


def merge(means, squares, widths):
    width = sum(widths)
    mean = sum(m * (w / width) for m, w in zip(means, widths))
    square = sum(squares) + sum(w * (m - mean) * (m - mean) for m, w in zip(means, widths))
    return mean, square


def stat_columns(stats):
    stats = [s[...] for s in stats]
    stats = [s if s.shape[0] > 8 else jnp.concatenate([s] * (DH // 8)).T for s in stats]
    return [s[:, :1] for s in stats], [s[:, 4:5] for s in stats]


def finish_kernel(terms, widths, at_ref, edge_ref, q_ref, rest_ref, *refs):
    sums, others = refs[:terms], refs[terms:terms + len(widths)]
    att_ref, stat_ref = refs[-2:]
    rows, width = att_ref.shape
    zs, chunks = edge_ref.shape[:2]
    edge = jnp.concatenate(
        [edge_ref[z, r, 0] for r in range(chunks) for z in range(zs)]
    ).astype(f32)
    root = lax.rsqrt(edge[:, 1:] - edge[:, :1])
    total = jnp.zeros((rows, 1), f32)
    for first in range(0, width, DH):
        at = slice(first, first + DH)
        summed = sum(s[0, :, at].astype(f32) for s in sums)
        product = q_ref[:, at].astype(f32) * rest_ref[0, :, at].astype(f32)
        weight = silu(jnp.sum(product, axis=1, keepdims=True) * DH ** (-0.5))
        value = summed * root + weight * rest_ref[1, :, at].astype(f32)
        att_ref[:, at] = value
        total += jnp.sum(value, axis=1, keepdims=True)
    mean = total / width
    spread = jnp.zeros((rows, DH), f32)
    for first in range(0, width, DH):
        away = att_ref[:, first:first + DH] - mean
        spread += away * away
    square = jnp.sum(spread, axis=1, keepdims=True)
    if others:
        means, squares = stat_columns(others)
        mean, square = merge([mean] + means, [square] + squares, [width] + widths)
    lane = lax.broadcasted_iota(jnp.int32, (rows, DH), 1)
    stat = jnp.where(lane < 4, mean, square)
    stat_ref[...] = stat if stat_ref.shape == stat.shape else stat.T[:8]


def finish(at, edges, query, rest, sums, others, widths, after):
    rows, width = query.shape
    stat = (8, rows) if others and rows == DH else (rows, DH)
    return pl.pallas_call(
        functools.partial(finish_kernel, len(sums), widths),
        grid_spec=pltpu.PrefetchScalarGridSpec(
            num_scalar_prefetch=1,
            grid=(1,),
            in_specs=[
                edge_spec(edges, 0),
                pl.BlockSpec((rows, width), lambda j, at: (0, 0)),
                pl.BlockSpec((2, rows, width), lambda j, at: (0, 0, 0)),
            ]
            + [pl.BlockSpec((1, rows, width), lambda j, at: (0, 0, 0))] * len(sums)
            + [pl.BlockSpec((rows, DH), lambda j, at: (0, 0))] * len(others)
            + anywhere(after),
            out_specs=(
                pl.BlockSpec((rows, width), lambda j, at: (0, 0)),
                pl.BlockSpec(stat, lambda j, at: (0, 0)),
            ),
        ),
        out_shape=(
            jax.ShapeDtypeStruct((rows, width), f32),
            jax.ShapeDtypeStruct(stat, f32),
        ),
        compiler_params=params(),
        cost_estimate=LIGHT,
        name="finish",
    )(at, edges, query, rest, *sums, *others, *after)


def merge_kernel(width, *refs):
    (m, n), (s, t) = (
        [r[:4] if r.shape[0] == 8 else r[:, :4] for r in refs[:2]],
        [r[4:] if r.shape[0] == 8 else r[:, 4:8] for r in refs[:2]],
    )
    mean, square = merge([m, n], [s, t], [width] * 2)
    if refs[2].shape[0] == 8:
        refs[2][:4], refs[2][4:] = mean, square
    else:
        lane = lax.broadcasted_iota(jnp.int32, refs[2].shape, 1)
        refs[2][...] = jnp.where(lane < 4, mean[:, :1], square[:, :1])


def merge_stats(stats, width):
    return pl.pallas_call(
        functools.partial(merge_kernel, width),
        out_shape=jax.ShapeDtypeStruct(stats[0].shape, f32),
        compiler_params=params(),
        cost_estimate=LIGHT,
        name="merge",
    )(*stats)


def gate_kernel(count, parts, width, *refs):
    stats, atts, rests, outs = (
        refs[:count], refs[count:count + parts],
        refs[count + parts:count + 2 * parts], refs[count + 2 * parts:],
    )
    means, squares = stat_columns(stats)
    mean, square = merge(means, squares, [width] * count)
    scale = lax.rsqrt(square / (width * count) + EPSILON)
    rows, column = outs[0].shape[0], 0
    for att, rest in zip(atts, rests):
        span = att.shape[1]
        normed = (att[...] - mean) * scale
        gated = (normed * rest[0].astype(f32)).astype(bf16)
        for r, out in enumerate(outs):
            out[:, column:column + span] = gated[r * rows:(r + 1) * rows]
        column += span
    for out in outs:
        if out.shape[1] > column:
            out[:, column:] = jnp.zeros((rows, out.shape[1] - column), bf16)


def gate_rows(stats, stat_width, atts, rests, chunks):
    rows, width = atts[0].shape[0], sum(a.shape[1] for a in atts)
    widths = [width + DH * min(r, 1) for r in range(chunks)]
    return pl.pallas_call(
        functools.partial(gate_kernel, len(stats), len(atts), stat_width),
        grid=(1,),
        in_specs=[pl.BlockSpec(s.shape, lambda j: (0, 0)) for s in stats]
        + [pl.BlockSpec((rows, a.shape[1]), lambda j: (0, 0)) for a in atts]
        + [pl.BlockSpec((1, rows, r.shape[2]), lambda j: (2, 0, 0)) for r in rests],
        out_specs=[pl.BlockSpec((rows // chunks, w), lambda j: (0, 0)) for w in widths],
        out_shape=[jax.ShapeDtypeStruct((rows // chunks, w), bf16) for w in widths],
        compiler_params=params(),
        cost_estimate=LIGHT,
        name="gate",
    )(*stats, *atts, *rests)


def output_kernel(owners, slots, after, index_ref, *refs):
    rows, w_ref, outs, lhs_ref = refs[:owners], refs[owners], refs[owners + 1 + after:-1], refs[-1]
    piece = rows[0].shape[1]

    @pl.when(pl.program_id(0) == 0)
    def _():
        first = 0
        for slot in slots:
            for p in range(owners):
                lhs_ref[first:first + piece, :] = rows[p][index_ref[0] ^ slot]
                first += piece

    sums = jnp.dot(lhs_ref[...], w_ref[...], preferred_element_type=f32).astype(bf16)
    first = 0
    for out in outs:
        for k in range(out.shape[0]):
            for p in range(owners):
                out[k, p] = sums[first:first + piece]
                first += piece


def output(index, slots, counts, blocks, w_out, column, columns, after):
    owners, each, zs = len(blocks), blocks[0].shape[0], sum(counts)
    width, piece = w_out.shape[0], each // zs
    span = max(c for c in (512, 256, columns) if columns % c == 0 and column % c == 0)
    row_spec = pl.BlockSpec((zs, piece, width), lambda j, at: (0, 0, 0))
    return pl.pallas_call(
        functools.partial(output_kernel, owners, slots, len(after)),
        grid_spec=pltpu.PrefetchScalarGridSpec(
            num_scalar_prefetch=1,
            grid=(columns // span,),
            in_specs=[row_spec] * owners
            + [pl.BlockSpec((width, span), lambda j, at: (0, column // span + j))]
            + anywhere(after),
            out_specs=[
                pl.BlockSpec((n, owners, piece, span), lambda j, at: (0, 0, 0, j)) for n in counts
            ],
            scratch_shapes=[pltpu.VMEM((owners * each, width), bf16)],
        ),
        out_shape=[jax.ShapeDtypeStruct((n, owners, piece, columns), bf16) for n in counts],
        compiler_params=params(),
        cost_estimate=LIGHT,
        name="output",
    )(
        index.reshape(1).astype(jnp.int32),
        *[b.reshape(zs, piece, b.shape[1]) for b in blocks], far(w_out), *after,
    )


def close_kernel(count, at_ref, t_ref, *refs):
    out_ref, mark_ref = refs[-2:]
    mark_ref[...] = jnp.zeros_like(mark_ref)
    for p in range(out_ref.shape[0]):
        total = t_ref[p].astype(f32)
        for term in refs[:count]:
            total = total + term[0, p ^ at_ref[0]].astype(f32)
        out_ref[p] = total.astype(bf16)


def close(place, index, tokens, chunks, r, g, terms, out, after):
    _, owners, piece, span = terms[0].shape
    at = jnp.stack([place, index * chunks + r]).astype(jnp.int32)
    into = [] if out is None else [out]
    return pl.pallas_call(
        functools.partial(close_kernel, len(terms)),
        grid_spec=pltpu.PrefetchScalarGridSpec(
            num_scalar_prefetch=1,
            grid=(1,),
            in_specs=[pl.BlockSpec((owners, piece, span), lambda j, at: (at[1], 0, g))]
            + [pl.BlockSpec((1,) + t.shape[1:], lambda j, at: (0, 0, 0, 0)) for t in terms]
            + anywhere(into) + anywhere(after),
            out_specs=(
                pl.BlockSpec((owners, piece, span), lambda j, at: (r, 0, g)),
                pl.BlockSpec((8, DH), lambda j, at: (0, 0)),
            ),
        ),
        out_shape=(
            jax.ShapeDtypeStruct((chunks * owners, piece, tokens.shape[1]), bf16),
            jax.ShapeDtypeStruct((8, DH), f32),
        ),
        input_output_aliases={} if out is None else {2 + len(terms): 0},
        compiler_params=params(),
        cost_estimate=LIGHT,
        name="close",
    )(at, far(tokens.reshape(-1, piece, tokens.shape[1])), *terms, *into, *after)


def bits_of(axis):
    count = lax.axis_size(axis)
    assert count & (count - 1) == 0
    return count.bit_length() - 1


def reverse(index, bits):
    return sum((((index >> b) & 1) << (bits - 1 - b) for b in range(bits)), 0 * index)


def swap(x, axis, bit):
    return lax.ppermute(
        x, axis, [(i, i ^ (1 << bit)) for i in range(lax.axis_size(axis))]
    )


def scatter(keep, gots, axis, after=()):
    terms, sent = [keep, gots[0]], gots[-1]
    for b in range(1, bits_of(axis)):
        sent = fold([keep, gots[-1]] if b == 1 else terms, after)
        terms.append(swap(sent, axis, b))
    return terms, sent


def gather(x, axis, after=()):
    blocks = [x]
    for b in reversed(range(bits_of(axis))):
        blocks = blocks + [swap(block, axis, b) for block in blocks]
        if len(blocks) == 2:
            blocks[1] = tie(blocks[1], after)
    return blocks


def all_stats(stat, width, axis):
    count = lax.axis_size(axis)
    if count > 8 or count & (count - 1):
        every = lax.all_gather(stat, axis)
        return [every[i] for i in range(count)], width
    stats = [stat]
    for b in range(bits_of(axis)):
        if b:
            width, stats = 2 * width, [merge_stats(stats, width)]
        stats.append(swap(stats[0], axis, b))
    return stats, width


def head_chunks(heads):
    if heads % 8:
        return [1] * heads
    unit = heads // 8
    return [unit, 2 * unit, 2 * unit, 2 * unit, unit]


GROUPS = [[0, 1], [2], [3], [4]]
ORDER = [
    "P0", "P1", "F0", "P2", "F1", "P3", "F2", "A0", "F3", "P4", "A1", "F4", "T0", "G0", "A2",
    "T1", "A3", "G1", "T2", "E0", "G2", "T3", "G3", "E1", "E2", "E3",
]


def local(tokens, w_qkvu, k_cache, v_cache, w_out, vis_start, vis_end):
    cand, depth = tokens.shape
    owners, zs = lax.axis_size("hist"), lax.axis_size("head")
    index = lax.axis_index("head")
    place = reverse(lax.axis_index("hist"), bits_of("hist"))
    width = w_qkvu.shape[2]
    events = k_cache.shape[0]
    chunks = 2 if cand % (2 * owners * zs * 16) == 0 else 1
    piece = cand // (zs * chunks * owners)

    def arrange(x):
        x = x.reshape((zs, chunks, owners, piece) + x.shape[1:])
        if piece % 16 == 0:
            return x
        blocks = [lax.dynamic_index_in_dim(x, p ^ place, 2, False) for p in range(owners)]
        x = jnp.stack(blocks).swapaxes(1, 2)
        return x.reshape((1, 1, owners, zs * chunks * piece) + x.shape[4:])

    at = (place if piece % 16 == 0 else jnp.int32(0)).reshape(1)
    ordered = arrange(tokens)
    first_event = lax.axis_index("hist") * events
    edges = arrange(edge_columns(first_event, vis_start, vis_end))

    sizes = head_chunks(width // DH)
    firsts = [sum(sizes[:c]) for c in range(len(sizes))]
    groups, order = GROUPS, ORDER
    if len(sizes) != 5:
        groups = [[c] for c in range(len(sizes))]
        order = [step + str(c) for step in "PFATGE" for c in range(len(sizes))]
    last = len(groups) - 1
    heads = [sum(sizes[c] for c in group) for group in groups]
    chain, keeps, firsts_got, terms, sums = [], {}, {}, {}, {}
    halves, queries, parts, atts, stats = {}, {}, {}, {}, {}
    for step, c in [(name[0], int(name[1:])) for name in order]:
        after = chain[-1:]
        if step == "P":
            keep, *sends = project(at, ordered, w_qkvu, firsts[c], sizes[c], after)
            before = firsts_got[c - 1] if c >= 1 else []
            before = before + [terms[0][-1]] if c == 2 and 0 in terms else before
            firsts_got[c] = [swap(tie(send, before), "hist", 0) for send in reversed(sends)][::-1]
            keeps[c] = keep
            chain.append(keep)
        elif step == "F":
            terms[c], sent = scatter(keeps[c], firsts_got[c], "hist", after)
            chain.append(sent)
        elif step == "A":
            parts[c] = activate([terms[k] for k in groups[c]], after)
            queries[c] = gather(parts[c][0], "hist")
            chain.append(parts[c][0])
        elif step == "T":
            first = firsts[groups[c][0]]
            keep, *sends = attend(at, queries[c], k_cache, v_cache, edges, first, after)
            halves[c] = keep, [swap(send, "hist", 0) for send in sends]
            chain.append(keep)
        elif step == "G":
            sums[c], sent = scatter(*halves[c], "hist", after)
            chain.append(sent)
        else:
            others = [stats[k] for k in range(last)] if c == last else []
            widths = [size * DH for size in heads[:last]] if c == last else []
            atts[c], stats[c] = finish(at, edges, *parts[c], sums[c], others, widths, after)
            chain.append(atts[c])

    atts = [atts[c] for c in range(last + 1)]
    rests = [parts[c][1] for c in range(last + 1)]
    every, stat_width = all_stats(stats[last], width, "head")
    gated = gate_rows(every, stat_width, atts, rests, chunks)
    columns = w_out.shape[1]
    straight = piece % 16 == 0 and zs & (zs - 1) == 0
    out, last_out = None, []
    if not straight:
        for r, rows in enumerate(gated):
            whole = jnp.concatenate(gather(rows, "hist"))[:, :width]
            whole = jnp.dot(whole, w_out, preferred_element_type=f32).astype(bf16)
            whole = whole.reshape(owners, zs, piece, -1).swapaxes(0, 1)
            whole = lax.psum_scatter(whole, "head", scatter_dimension=0, tiled=True)
            out, _ = close(place, index, tokens, chunks, r, 0, [whole], out, [])
        return out.reshape(cand // zs, -1)
    slots = [reverse(k, bits_of("head")) for k in range(zs)]
    groups = 2 if columns % 1024 == 0 else 1
    span = columns // groups
    pieces, first_out, counts = [], [], [zs // 2] * 2 if zs > 1 else [1]
    for r, rows in enumerate(gated):
        blocks = gather(rows, "hist", first_out)
        for g in range(groups):
            own, *others = output(
                index, slots, counts, blocks, w_out, g * span, span, last_out
            )
            before = pieces[-2][3] if len(pieces) > 1 else []
            pieces.append((r, g, own, [swap(tie(x, before), "head", 0) for x in others]))
            last_out, first_out = [own], first_out or [own]
    closing, chain = [], last_out
    for r, g, own, arrived in pieces:
        terms, sent = scatter(own, arrived, "head", chain) if arrived else ([own], own)
        chain = [sent]
        closing.append((r, g, terms))
        if len(closing) > 2:
            out, mark = close(place, index, tokens, chunks, *closing.pop(0), out, chain)
            chain = [mark]
    for last_piece in closing:
        out, mark = close(place, index, tokens, chunks, *last_piece, out, chain)
        chain = [mark]
    return out.reshape(cand // zs, -1)


def solution(mesh):
    in_specs = (
        P("groups", "hist"),
        P("hist", None, "head"),
        P(("groups", "hist"), "head"),
        P(("groups", "hist"), "head"),
        P("head", "hist"),
        P("groups"),
        P("groups"),
    )
    out_specs = P(("groups", "head"), "hist")
    return jax.shard_map(local, mesh=mesh, in_specs=in_specs, out_specs=out_specs, check_vma=False)
```

```python
import functools

import jax
import jax.numpy as jnp
from jax import lax
from jax.experimental import pallas as pl
from jax.experimental.pallas import tpu as pltpu
from jax.sharding import PartitionSpec as P

DH = 128
EPSILON = 1e-05
VMEM_LIMIT = 28 * 1024 * 1024

bf16 = jnp.bfloat16
f32 = jnp.float32


def silu(v):
    u = 0.5 * v
    return u + u * jnp.tanh(u)


def params():
    return pltpu.CompilerParams(vmem_limit_bytes=VMEM_LIMIT)


LIGHT = pl.CostEstimate(flops=1000, bytes_accessed=1000, transcendentals=0)


def far(x):
    return pltpu.with_memory_space_constraint(x, pltpu.HBM)


def anywhere(arrays):
    return [pl.BlockSpec(memory_space=pl.ANY)] * len(arrays)


def project_kernel(parts, owners, after, at_ref, *refs):
    rows, weights = refs[:owners], refs[owners:owners + parts]
    outs, lhs_ref = refs[owners + parts + after:-parts - 1], refs[-parts - 1]
    wides = refs[-parts:]
    zs, chunks, _, piece, _ = rows[0].shape
    depth = weights[0].shape[0]

    @pl.when(pl.program_id(0) == 0)
    def _():
        first = 0
        for p in range(owners):
            for r in range(chunks):
                for z in range(zs):
                    lhs_ref[first:first + piece, :] = rows[p][z, r, 0]
                    first += piece

    res = None
    for k, wide in enumerate(wides):
        wide[...] = weights[k].reshape(depth * 4, DH)[...].astype(f32)
        rhs = jnp.concatenate(
            [wide[pl.ds(i, depth, stride=4), :].astype(bf16) for i in range(4)], axis=1
        )
        term = jnp.dot(lhs_ref[:, k * depth:(k + 1) * depth], rhs, preferred_element_type=f32)
        res = term if res is None else res + term
    res = res.astype(bf16)
    each, first = outs[0].shape[2], 0
    for out in outs:
        for p in range(out.shape[0]):
            for i in range(4):
                out[p, i] = res[first:first + each, i * DH:(i + 1) * DH]
            first += each


def parts_of(owners):
    half = owners // 2
    return [half, half // 2, half // 2] if half > 1 else [half, half]


def project(at, tokens, w, head_first, heads, after):
    zs, chunks, owners, piece, depth = tokens.shape
    each, counts = zs * chunks * piece, parts_of(owners)
    parts = 4 if depth % 512 == 0 else 1
    return pl.pallas_call(
        functools.partial(project_kernel, parts, owners, len(after)),
        grid_spec=pltpu.PrefetchScalarGridSpec(
            num_scalar_prefetch=1,
            grid=(heads,),
            in_specs=[
                pl.BlockSpec(
                    (zs, chunks, 1, piece, depth), lambda j, at, p=p: (0, 0, at[0] ^ p, 0, 0)
                )
                for p in range(owners)
            ]
            + [
                pl.BlockSpec((depth // parts, 4, DH), lambda j, at, k=k: (k, 0, head_first + j))
                for k in range(parts)
            ]
            + anywhere(after),
            out_specs=[
                pl.BlockSpec((n, 4, each, DH), lambda j, at: (0, 0, 0, j)) for n in counts
            ],
            scratch_shapes=[pltpu.VMEM((owners * each, depth), bf16)]
            + [pltpu.VMEM((depth // parts * 4, DH), f32) for _ in range(parts)],
        ),
        out_shape=[jax.ShapeDtypeStruct((n, 4, each, heads * DH), bf16) for n in counts],
        compiler_params=params(),
        cost_estimate=LIGHT,
        name="project",
    )(at, *[far(tokens)] * owners, *[far(w)] * parts, *after)


def tie_kernel(*refs):
    pass


def tie(x, after):
    if not after:
        return x
    return pl.pallas_call(
        tie_kernel,
        in_specs=anywhere([x, *after]),
        out_specs=pl.BlockSpec(memory_space=pl.ANY),
        out_shape=jax.ShapeDtypeStruct(x.shape, x.dtype),
        input_output_aliases={0: 0},
        compiler_params=params(),
        cost_estimate=LIGHT,
        name="tie",
    )(x, *after)


def fold_kernel(count, *refs):
    refs[-1][...] = sum(r[...].astype(f32) for r in refs[:count]).astype(bf16)


def fold(terms, after=()):
    half = terms[0].shape[0] // 2 if len(terms) == 2 else terms[-1].shape[0] // 2
    tail = terms[0].shape[1:]
    steps = 2 if tail[-1] % 256 == 0 else 1
    block = (half,) + tail[:-1] + (tail[-1] // steps,)
    middle = (0,) * (len(tail) - 1)
    firsts = [0 if t.shape[0] == half else 1 for t in terms]
    return pl.pallas_call(
        functools.partial(fold_kernel, len(terms)),
        grid=(steps,),
        in_specs=[pl.BlockSpec(block, lambda j, f=f: (f,) + middle + (j,)) for f in firsts]
        + anywhere(after),
        out_specs=pl.BlockSpec(block, lambda j: (0,) + middle + (j,)),
        out_shape=jax.ShapeDtypeStruct((half,) + tail, bf16),
        compiler_params=params(),
        cost_estimate=LIGHT,
        name="fold",
    )(*terms, *after)


def activate_kernel(counts, *refs):
    q_ref, rest_ref = refs[-2:]
    first, column = 0, 0
    for count in counts:
        terms = refs[first:first + count]
        span = terms[0].shape[-1]
        for i in range(4):
            part = silu(sum(t[0, i].astype(f32) for t in terms)).astype(bf16)
            if i == 0:
                q_ref[:, column:column + span] = part
            else:
                rest_ref[i - 1, :, column:column + span] = part
        first += count
        column += span


def activate(chunks, after):
    each, width = chunks[0][0].shape[2], sum(terms[0].shape[3] for terms in chunks)
    flat = [term for terms in chunks for term in terms]
    return pl.pallas_call(
        functools.partial(activate_kernel, [len(terms) for terms in chunks]),
        grid=(1,),
        in_specs=[pl.BlockSpec((1,) + t.shape[1:], lambda j: (0, 0, 0, 0)) for t in flat]
        + anywhere(after),
        out_specs=(
            pl.BlockSpec((each, width), lambda j: (0, 0)),
            pl.BlockSpec((3, each, width), lambda j: (0, 0, 0)),
        ),
        out_shape=(
            jax.ShapeDtypeStruct((each, width), bf16),
            jax.ShapeDtypeStruct((3, each, width), bf16),
        ),
        compiler_params=params(),
        cost_estimate=LIGHT,
        name="activate",
    )(*flat, *after)


def edge_kernel(base_ref, start_ref, end_ref, out_ref):
    row = lax.broadcasted_iota(jnp.int32, (DH, DH), 0)
    for b in range(start_ref.shape[0]):
        start, end = start_ref[b:b + 1, :], end_ref[b:b + 1, :]
        both = jnp.where(row == 0, start, end) - base_ref[0]
        out_ref[b * DH:(b + 1) * DH, :] = both.astype(f32).T[:, :2].astype(jnp.int32)


def edge_columns(base, start, end):
    count = start.shape[0]
    lines = pl.BlockSpec((count // DH, DH), lambda j, base: (0, 0))
    return pl.pallas_call(
        edge_kernel,
        grid_spec=pltpu.PrefetchScalarGridSpec(
            num_scalar_prefetch=1,
            grid=(1,),
            in_specs=[lines, lines],
            out_specs=pl.BlockSpec((count, 2), lambda j, base: (0, 0)),
        ),
        out_shape=jax.ShapeDtypeStruct((count, 2), jnp.int32),
        compiler_params=params(),
        cost_estimate=LIGHT,
        name="edges",
    )(base.reshape(1), start.reshape(-1, DH), end.reshape(-1, DH))


def attend_kernel(owners, sends, at_ref, *refs):
    queries, edges = refs[:owners], refs[owners:2 * owners]
    k_ref, v_ref = refs[2 * owners:2 * owners + 2]
    outs, mask_ref = refs[-1 - sends:-1], refs[-1]
    events = mask_ref.shape[1]
    each = outs[0].shape[1]

    @pl.when(pl.program_id(0) == 0)
    def _():
        zs, chunks, _, piece, _ = edges[0].shape
        at = lax.broadcasted_iota(jnp.int32, (piece, events), 1)
        first = 0
        for p in range(owners):
            for r in range(chunks):
                for z in range(zs):
                    edge = edges[p][z, r, 0]
                    seen = (at >= edge[:, :1]) & (at < edge[:, 1:])
                    mask_ref[first:first + piece, :] = jnp.where(seen, 1.0, 0.0).astype(bf16)
                    first += piece

    for h in range(k_ref.shape[1] // DH):
        at = slice(h * DH, (h + 1) * DH)
        query = jnp.concatenate([q[:, at] for q in queries])
        u = lax.dot_general(
            query, k_ref[:, at], (((1,), (1,)), ((), ())), preferred_element_type=f32
        ) * (0.5 * DH ** (-0.5))
        weights = (u + u * jnp.tanh(u)).astype(bf16) * mask_ref[...]
        term = jnp.dot(weights, v_ref[:, at], preferred_element_type=f32).astype(bf16)
        first = 0
        for out in outs:
            for p in range(out.shape[0]):
                out[p, :, at] = term[first:first + each]
                first += each


def edge_spec(edges, p):
    zs, chunks, _, piece, ends = edges.shape
    return pl.BlockSpec((zs, chunks, 1, piece, ends), lambda j, at: (0, 0, at[0] ^ p, 0, 0))


def attend(at, queries, k_cache, v_cache, edges, head_first, after):
    owners, (each, width) = len(queries), queries[0].shape
    rows, events, counts = owners * each, k_cache.shape[0], parts_of(owners)
    first = head_first * DH
    span = max(h for h in range(DH, 4 * DH, DH) if width % h == 0 and first % h == 0)
    cache = pl.BlockSpec((events, span), lambda j, at: (0, first // span + j))
    return pl.pallas_call(
        functools.partial(attend_kernel, owners, len(counts)),
        grid_spec=pltpu.PrefetchScalarGridSpec(
            num_scalar_prefetch=1,
            grid=(width // span,),
            in_specs=[pl.BlockSpec((each, span), lambda j, at: (0, j))] * owners
            + [edge_spec(edges, p) for p in range(owners)]
            + [cache, cache]
            + anywhere(after),
            out_specs=[pl.BlockSpec((n, each, span), lambda j, at: (0, 0, j)) for n in counts],
            scratch_shapes=[pltpu.VMEM((rows, events), bf16)],
        ),
        out_shape=[jax.ShapeDtypeStruct((n, each, width), bf16) for n in counts],
        compiler_params=params(),
        cost_estimate=LIGHT,
        name="attend",
    )(at, *queries, *[edges] * owners, far(k_cache), far(v_cache), *after)


def merge(means, squares, widths):
    width = sum(widths)
    mean = sum(m * (w / width) for m, w in zip(means, widths))
    square = sum(squares) + sum(w * (m - mean) * (m - mean) for m, w in zip(means, widths))
    return mean, square


def stat_columns(stats):
    stats = [s[...] for s in stats]
    stats = [s if s.shape[0] > 8 else jnp.concatenate([s] * (DH // 8)).T for s in stats]
    return [s[:, :1] for s in stats], [s[:, 4:5] for s in stats]


def finish_kernel(terms, widths, at_ref, edge_ref, q_ref, rest_ref, *refs):
    sums, others = refs[:terms], refs[terms:terms + len(widths)]
    att_ref, stat_ref = refs[-2:]
    rows, width = att_ref.shape
    zs, chunks = edge_ref.shape[:2]
    edge = jnp.concatenate(
        [edge_ref[z, r, 0] for r in range(chunks) for z in range(zs)]
    ).astype(f32)
    root = lax.rsqrt(edge[:, 1:] - edge[:, :1])
    total = jnp.zeros((rows, 1), f32)
    for first in range(0, width, DH):
        at = slice(first, first + DH)
        summed = sum(s[0, :, at].astype(f32) for s in sums)
        product = q_ref[:, at].astype(f32) * rest_ref[0, :, at].astype(f32)
        weight = silu(jnp.sum(product, axis=1, keepdims=True) * DH ** (-0.5))
        value = summed * root + weight * rest_ref[1, :, at].astype(f32)
        att_ref[:, at] = value
        total += jnp.sum(value, axis=1, keepdims=True)
    mean = total / width
    spread = jnp.zeros((rows, DH), f32)
    for first in range(0, width, DH):
        away = att_ref[:, first:first + DH] - mean
        spread += away * away
    square = jnp.sum(spread, axis=1, keepdims=True)
    if others:
        means, squares = stat_columns(others)
        mean, square = merge([mean] + means, [square] + squares, [width] + widths)
    lane = lax.broadcasted_iota(jnp.int32, (rows, DH), 1)
    stat = jnp.where(lane < 4, mean, square)
    stat_ref[...] = stat if stat_ref.shape == stat.shape else stat.T[:8]


def finish(at, edges, query, rest, sums, others, widths, after):
    rows, width = query.shape
    stat = (8, rows) if others and rows == DH else (rows, DH)
    return pl.pallas_call(
        functools.partial(finish_kernel, len(sums), widths),
        grid_spec=pltpu.PrefetchScalarGridSpec(
            num_scalar_prefetch=1,
            grid=(1,),
            in_specs=[
                edge_spec(edges, 0),
                pl.BlockSpec((rows, width), lambda j, at: (0, 0)),
                pl.BlockSpec((2, rows, width), lambda j, at: (0, 0, 0)),
            ]
            + [pl.BlockSpec((1, rows, width), lambda j, at: (0, 0, 0))] * len(sums)
            + [pl.BlockSpec((rows, DH), lambda j, at: (0, 0))] * len(others)
            + anywhere(after),
            out_specs=(
                pl.BlockSpec((rows, width), lambda j, at: (0, 0)),
                pl.BlockSpec(stat, lambda j, at: (0, 0)),
            ),
        ),
        out_shape=(
            jax.ShapeDtypeStruct((rows, width), f32),
            jax.ShapeDtypeStruct(stat, f32),
        ),
        compiler_params=params(),
        cost_estimate=LIGHT,
        name="finish",
    )(at, edges, query, rest, *sums, *others, *after)


def merge_kernel(width, *refs):
    (m, n), (s, t) = (
        [r[:4] if r.shape[0] == 8 else r[:, :4] for r in refs[:2]],
        [r[4:] if r.shape[0] == 8 else r[:, 4:8] for r in refs[:2]],
    )
    mean, square = merge([m, n], [s, t], [width] * 2)
    if refs[2].shape[0] == 8:
        refs[2][:4], refs[2][4:] = mean, square
    else:
        lane = lax.broadcasted_iota(jnp.int32, refs[2].shape, 1)
        refs[2][...] = jnp.where(lane < 4, mean[:, :1], square[:, :1])


def merge_stats(stats, width):
    return pl.pallas_call(
        functools.partial(merge_kernel, width),
        out_shape=jax.ShapeDtypeStruct(stats[0].shape, f32),
        compiler_params=params(),
        cost_estimate=LIGHT,
        name="merge",
    )(*stats)


def gate_kernel(count, parts, width, *refs):
    stats, atts, rests, outs = (
        refs[:count], refs[count:count + parts],
        refs[count + parts:count + 2 * parts], refs[count + 2 * parts:],
    )
    means, squares = stat_columns(stats)
    mean, square = merge(means, squares, [width] * count)
    scale = lax.rsqrt(square / (width * count) + EPSILON)
    rows, column = outs[0].shape[0], 0
    for att, rest in zip(atts, rests):
        span = att.shape[1]
        normed = (att[...] - mean) * scale
        gated = (normed * rest[0].astype(f32)).astype(bf16)
        for r, out in enumerate(outs):
            out[:, column:column + span] = gated[r * rows:(r + 1) * rows]
        column += span
    for out in outs:
        if out.shape[1] > column:
            out[:, column:] = jnp.zeros((rows, out.shape[1] - column), bf16)


def gate_rows(stats, stat_width, atts, rests, chunks):
    rows, width = atts[0].shape[0], sum(a.shape[1] for a in atts)
    widths = [width + DH * min(r, 1) for r in range(chunks)]
    return pl.pallas_call(
        functools.partial(gate_kernel, len(stats), len(atts), stat_width),
        grid=(1,),
        in_specs=[pl.BlockSpec(s.shape, lambda j: (0, 0)) for s in stats]
        + [pl.BlockSpec((rows, a.shape[1]), lambda j: (0, 0)) for a in atts]
        + [pl.BlockSpec((1, rows, r.shape[2]), lambda j: (2, 0, 0)) for r in rests],
        out_specs=[pl.BlockSpec((rows // chunks, w), lambda j: (0, 0)) for w in widths],
        out_shape=[jax.ShapeDtypeStruct((rows // chunks, w), bf16) for w in widths],
        compiler_params=params(),
        cost_estimate=LIGHT,
        name="gate",
    )(*stats, *atts, *rests)


def output_kernel(owners, slots, after, index_ref, *refs):
    rows, w_ref, outs, lhs_ref = refs[:owners], refs[owners], refs[owners + 1 + after:-1], refs[-1]
    piece = rows[0].shape[1]

    @pl.when(pl.program_id(0) == 0)
    def _():
        first = 0
        for slot in slots:
            for p in range(owners):
                lhs_ref[first:first + piece, :] = rows[p][index_ref[0] ^ slot]
                first += piece

    sums = jnp.dot(lhs_ref[...], w_ref[...], preferred_element_type=f32).astype(bf16)
    first = 0
    for out in outs:
        for k in range(out.shape[0]):
            for p in range(owners):
                out[k, p] = sums[first:first + piece]
                first += piece


def output(index, slots, counts, blocks, w_out, column, columns, after):
    owners, each, zs = len(blocks), blocks[0].shape[0], sum(counts)
    width, piece = w_out.shape[0], each // zs
    span = max(c for c in (512, 256, columns) if columns % c == 0 and column % c == 0)
    row_spec = pl.BlockSpec((zs, piece, width), lambda j, at: (0, 0, 0))
    return pl.pallas_call(
        functools.partial(output_kernel, owners, slots, len(after)),
        grid_spec=pltpu.PrefetchScalarGridSpec(
            num_scalar_prefetch=1,
            grid=(columns // span,),
            in_specs=[row_spec] * owners
            + [pl.BlockSpec((width, span), lambda j, at: (0, column // span + j))]
            + anywhere(after),
            out_specs=[
                pl.BlockSpec((n, owners, piece, span), lambda j, at: (0, 0, 0, j)) for n in counts
            ],
            scratch_shapes=[pltpu.VMEM((owners * each, width), bf16)],
        ),
        out_shape=[jax.ShapeDtypeStruct((n, owners, piece, columns), bf16) for n in counts],
        compiler_params=params(),
        cost_estimate=LIGHT,
        name="output",
    )(
        index.reshape(1).astype(jnp.int32),
        *[b.reshape(zs, piece, b.shape[1]) for b in blocks], far(w_out), *after,
    )


def close_kernel(count, at_ref, t_ref, *refs):
    out_ref, mark_ref = refs[-2:]
    mark_ref[...] = jnp.zeros_like(mark_ref)
    for p in range(out_ref.shape[0]):
        total = t_ref[p].astype(f32)
        for term in refs[:count]:
            total = total + term[0, p ^ at_ref[0]].astype(f32)
        out_ref[p] = total.astype(bf16)


def close(place, index, tokens, chunks, r, g, terms, out, after):
    _, owners, piece, span = terms[0].shape
    at = jnp.stack([place, index * chunks + r]).astype(jnp.int32)
    into = [] if out is None else [out]
    return pl.pallas_call(
        functools.partial(close_kernel, len(terms)),
        grid_spec=pltpu.PrefetchScalarGridSpec(
            num_scalar_prefetch=1,
            grid=(1,),
            in_specs=[pl.BlockSpec((owners, piece, span), lambda j, at: (at[1], 0, g))]
            + [pl.BlockSpec((1,) + t.shape[1:], lambda j, at: (0, 0, 0, 0)) for t in terms]
            + anywhere(into) + anywhere(after),
            out_specs=(
                pl.BlockSpec((owners, piece, span), lambda j, at: (r, 0, g)),
                pl.BlockSpec((8, DH), lambda j, at: (0, 0)),
            ),
        ),
        out_shape=(
            jax.ShapeDtypeStruct((chunks * owners, piece, tokens.shape[1]), bf16),
            jax.ShapeDtypeStruct((8, DH), f32),
        ),
        input_output_aliases={} if out is None else {2 + len(terms): 0},
        compiler_params=params(),
        cost_estimate=LIGHT,
        name="close",
    )(at, far(tokens.reshape(-1, piece, tokens.shape[1])), *terms, *into, *after)


def bits_of(axis):
    count = lax.axis_size(axis)
    assert count & (count - 1) == 0
    return count.bit_length() - 1


def reverse(index, bits):
    return sum((((index >> b) & 1) << (bits - 1 - b) for b in range(bits)), 0 * index)


def swap(x, axis, bit):
    return lax.ppermute(
        x, axis, [(i, i ^ (1 << bit)) for i in range(lax.axis_size(axis))]
    )


def scatter(keep, gots, axis, after=()):
    terms, sent = [keep, gots[0]], gots[-1]
    for b in range(1, bits_of(axis)):
        sent = fold([keep, gots[-1]] if b == 1 else terms, after)
        terms.append(swap(sent, axis, b))
    return terms, sent


def gather(x, axis, after=()):
    blocks = [x]
    for b in reversed(range(bits_of(axis))):
        blocks = blocks + [swap(block, axis, b) for block in blocks]
        if len(blocks) == 2:
            blocks[1] = tie(blocks[1], after)
    return blocks


def all_stats(stat, width, axis):
    count = lax.axis_size(axis)
    if count > 8 or count & (count - 1):
        every = lax.all_gather(stat, axis)
        return [every[i] for i in range(count)], width
    stats = [stat]
    for b in range(bits_of(axis)):
        if b:
            width, stats = 2 * width, [merge_stats(stats, width)]
        stats.append(swap(stats[0], axis, b))
    return stats, width


def head_chunks(heads):
    if heads % 8:
        return [1] * heads
    unit = heads // 8
    return [unit, 2 * unit, 2 * unit, 2 * unit, unit]


GROUPS = [[0, 1], [2], [3], [4]]
ORDER = [
    "P0", "P1", "F0", "P2", "F1", "P3", "F2", "A0", "F3", "P4", "A1", "F4", "T0", "G0", "A2",
    "T1", "A3", "G1", "T2", "E0", "G2", "T3", "G3", "E1", "E2", "E3",
]


def local(tokens, w_qkvu, k_cache, v_cache, w_out, vis_start, vis_end):
    cand, depth = tokens.shape
    owners, zs = lax.axis_size("hist"), lax.axis_size("head")
    index = lax.axis_index("head")
    place = reverse(lax.axis_index("hist"), bits_of("hist"))
    width = w_qkvu.shape[2]
    events = k_cache.shape[0]
    chunks = 2 if cand % (2 * owners * zs * 16) == 0 else 1
    piece = cand // (zs * chunks * owners)

    def arrange(x):
        x = x.reshape((zs, chunks, owners, piece) + x.shape[1:])
        if piece % 16 == 0:
            return x
        blocks = [lax.dynamic_index_in_dim(x, p ^ place, 2, False) for p in range(owners)]
        x = jnp.stack(blocks).swapaxes(1, 2)
        return x.reshape((1, 1, owners, zs * chunks * piece) + x.shape[4:])

    at = (place if piece % 16 == 0 else jnp.int32(0)).reshape(1)
    ordered = arrange(tokens)
    first_event = lax.axis_index("hist") * events
    edges = arrange(edge_columns(first_event, vis_start, vis_end))

    sizes = head_chunks(width // DH)
    firsts = [sum(sizes[:c]) for c in range(len(sizes))]
    groups, order = GROUPS, ORDER
    if len(sizes) != 5:
        groups = [[c] for c in range(len(sizes))]
        order = [step + str(c) for step in "PFATGE" for c in range(len(sizes))]
    last = len(groups) - 1
    heads = [sum(sizes[c] for c in group) for group in groups]
    chain, keeps, firsts_got, terms, sums = [], {}, {}, {}, {}
    halves, queries, parts, atts, stats = {}, {}, {}, {}, {}
    for step, c in [(name[0], int(name[1:])) for name in order]:
        after = chain[-1:]
        if step == "P":
            keep, *sends = project(at, ordered, w_qkvu, firsts[c], sizes[c], after)
            before = firsts_got[c - 1] if c >= 1 else []
            before = before + [terms[0][-1]] if c == 2 and 0 in terms else before
            firsts_got[c] = [swap(tie(send, before), "hist", 0) for send in reversed(sends)][::-1]
            keeps[c] = keep
            chain.append(keep)
        elif step == "F":
            terms[c], sent = scatter(keeps[c], firsts_got[c], "hist", after)
            chain.append(sent)
        elif step == "A":
            parts[c] = activate([terms[k] for k in groups[c]], after)
            queries[c] = gather(parts[c][0], "hist")
            chain.append(parts[c][0])
        elif step == "T":
            first = firsts[groups[c][0]]
            keep, *sends = attend(at, queries[c], k_cache, v_cache, edges, first, after)
            halves[c] = keep, [swap(send, "hist", 0) for send in sends]
            chain.append(keep)
        elif step == "G":
            sums[c], sent = scatter(*halves[c], "hist", after)
            chain.append(sent)
        else:
            others = [stats[k] for k in range(last)] if c == last else []
            widths = [size * DH for size in heads[:last]] if c == last else []
            atts[c], stats[c] = finish(at, edges, *parts[c], sums[c], others, widths, after)
            chain.append(atts[c])

    atts = [atts[c] for c in range(last + 1)]
    rests = [parts[c][1] for c in range(last + 1)]
    every, stat_width = all_stats(stats[last], width, "head")
    gated = gate_rows(every, stat_width, atts, rests, chunks)
    columns = w_out.shape[1]
    straight = piece % 16 == 0 and zs & (zs - 1) == 0
    out = None
    if not straight:
        for r, rows in enumerate(gated):
            whole = jnp.concatenate(gather(rows, "hist"))[:, :width]
            whole = jnp.dot(whole, w_out, preferred_element_type=f32).astype(bf16)
            whole = whole.reshape(owners, zs, piece, -1).swapaxes(0, 1)
            whole = lax.psum_scatter(whole, "head", scatter_dimension=0, tiled=True)
            out, _ = close(place, index, tokens, chunks, r, 0, [whole], out, [])
        return out.reshape(cand // zs, -1)
    slots = [reverse(k, bits_of("head")) for k in range(zs)]
    groups = 2 if columns % 1024 == 0 else 1
    span = columns // groups
    counts = [zs // 2] * 2 if zs > 1 else [1]
    plan = [(r, g) for r in range(chunks) for g in range(groups)]
    chain, first_out, blocks, made, folded = [], [], {}, [], []

    def fold_next():
        own, arrived = made[len(folded)]
        terms, sent = scatter(own, arrived, "head", chain) if arrived else ([own], own)
        folded.append(terms)
        return [sent]

    for n, (r, g) in enumerate(plan):
        if r not in blocks:
            blocks[r] = gather(gated[r], "hist", first_out)
        own, *others = output(index, slots, counts, blocks[r], w_out, g * span, span, chain)
        before = made[n - 2][1] if n > 1 else []
        before = before + [folded[0][-1]] if folded else before
        made.append((own, [swap(tie(x, before), "head", 0) for x in others]))
        chain, first_out = [own], first_out or [own]
        if n == 2:
            chain = fold_next()
    closed = 0
    while closed < len(plan):
        if len(folded) < len(plan):
            chain = fold_next()
        if len(folded) > closed + 2 or len(folded) == len(plan):
            r, g = plan[closed]
            out, mark = close(place, index, tokens, chunks, r, g, folded[closed], out, chain)
            chain, closed = [mark], closed + 1
    return out.reshape(cand // zs, -1)


def solution(mesh):
    in_specs = (
        P("groups", "hist"),
        P("hist", None, "head"),
        P(("groups", "hist"), "head"),
        P(("groups", "hist"), "head"),
        P("head", "hist"),
        P("groups"),
        P("groups"),
    )
    out_specs = P(("groups", "head"), "hist")
    return jax.shard_map(local, mesh=mesh, in_specs=in_specs, out_specs=out_specs, check_vma=False)
```

```python
import functools

import jax
import jax.numpy as jnp
from jax import lax
from jax.experimental import pallas as pl
from jax.experimental.pallas import tpu as pltpu
from jax.sharding import PartitionSpec as P

DH = 128
EPSILON = 1e-05
VMEM_LIMIT = 28 * 1024 * 1024

bf16 = jnp.bfloat16
f32 = jnp.float32


def silu(v):
    u = 0.5 * v
    return u + u * jnp.tanh(u)


def params():
    return pltpu.CompilerParams(vmem_limit_bytes=VMEM_LIMIT)


LIGHT = pl.CostEstimate(flops=1000, bytes_accessed=1000, transcendentals=0)


def far(x):
    return pltpu.with_memory_space_constraint(x, pltpu.HBM)


def anywhere(arrays):
    return [pl.BlockSpec(memory_space=pl.ANY)] * len(arrays)


def project_kernel(parts, owners, after, at_ref, *refs):
    rows, weights = refs[:owners], refs[owners:owners + parts]
    outs, lhs_ref = refs[owners + parts + after:-parts - 1], refs[-parts - 1]
    wides = refs[-parts:]
    zs, chunks, _, piece, _ = rows[0].shape
    depth = weights[0].shape[0]

    @pl.when(pl.program_id(0) == 0)
    def _():
        first = 0
        for p in range(owners):
            for r in range(chunks):
                for z in range(zs):
                    lhs_ref[first:first + piece, :] = rows[p][z, r, 0]
                    first += piece

    res = None
    for k, wide in enumerate(wides):
        wide[...] = weights[k].reshape(depth * 4, DH)[...].astype(f32)
        rhs = jnp.concatenate(
            [wide[pl.ds(i, depth, stride=4), :].astype(bf16) for i in range(4)], axis=1
        )
        term = jnp.dot(lhs_ref[:, k * depth:(k + 1) * depth], rhs, preferred_element_type=f32)
        res = term if res is None else res + term
    res = res.astype(bf16)
    each, first = outs[0].shape[2], 0
    for out in outs:
        for p in range(out.shape[0]):
            for i in range(4):
                out[p, i] = res[first:first + each, i * DH:(i + 1) * DH]
            first += each


def parts_of(owners):
    half = owners // 2
    return [half, half // 2, half // 2] if half > 1 else [half, half]


def project(at, tokens, w, head_first, heads, after):
    zs, chunks, owners, piece, depth = tokens.shape
    each, counts = zs * chunks * piece, parts_of(owners)
    parts = 4 if depth % 512 == 0 else 1
    return pl.pallas_call(
        functools.partial(project_kernel, parts, owners, len(after)),
        grid_spec=pltpu.PrefetchScalarGridSpec(
            num_scalar_prefetch=1,
            grid=(heads,),
            in_specs=[
                pl.BlockSpec(
                    (zs, chunks, 1, piece, depth), lambda j, at, p=p: (0, 0, at[0] ^ p, 0, 0)
                )
                for p in range(owners)
            ]
            + [
                pl.BlockSpec((depth // parts, 4, DH), lambda j, at, k=k: (k, 0, head_first + j))
                for k in range(parts)
            ]
            + anywhere(after),
            out_specs=[
                pl.BlockSpec((n, 4, each, DH), lambda j, at: (0, 0, 0, j)) for n in counts
            ],
            scratch_shapes=[pltpu.VMEM((owners * each, depth), bf16)]
            + [pltpu.VMEM((depth // parts * 4, DH), f32) for _ in range(parts)],
        ),
        out_shape=[jax.ShapeDtypeStruct((n, 4, each, heads * DH), bf16) for n in counts],
        compiler_params=params(),
        cost_estimate=LIGHT,
        name="project",
    )(at, *[far(tokens)] * owners, *[far(w)] * parts, *after)


def tie_kernel(*refs):
    pass


def tie(x, after):
    if not after:
        return x
    return pl.pallas_call(
        tie_kernel,
        in_specs=anywhere([x, *after]),
        out_specs=pl.BlockSpec(memory_space=pl.ANY),
        out_shape=jax.ShapeDtypeStruct(x.shape, x.dtype),
        input_output_aliases={0: 0},
        compiler_params=params(),
        cost_estimate=LIGHT,
        name="tie",
    )(x, *after)


def fold_kernel(count, *refs):
    refs[-1][...] = sum(r[...].astype(f32) for r in refs[:count]).astype(bf16)


def fold(terms, after=()):
    half = terms[0].shape[0] // 2 if len(terms) == 2 else terms[-1].shape[0] // 2
    tail = terms[0].shape[1:]
    steps = 2 if tail[-1] % 256 == 0 else 1
    block = (half,) + tail[:-1] + (tail[-1] // steps,)
    middle = (0,) * (len(tail) - 1)
    firsts = [0 if t.shape[0] == half else 1 for t in terms]
    return pl.pallas_call(
        functools.partial(fold_kernel, len(terms)),
        grid=(steps,),
        in_specs=[pl.BlockSpec(block, lambda j, f=f: (f,) + middle + (j,)) for f in firsts]
        + anywhere(after),
        out_specs=pl.BlockSpec(block, lambda j: (0,) + middle + (j,)),
        out_shape=jax.ShapeDtypeStruct((half,) + tail, bf16),
        compiler_params=params(),
        cost_estimate=LIGHT,
        name="fold",
    )(*terms, *after)


def activate_kernel(counts, *refs):
    q_ref, rest_ref = refs[-2:]
    first, column = 0, 0
    for count in counts:
        terms = refs[first:first + count]
        span = terms[0].shape[-1]
        for i in range(4):
            part = silu(sum(t[0, i].astype(f32) for t in terms)).astype(bf16)
            if i == 0:
                q_ref[:, column:column + span] = part
            else:
                rest_ref[i - 1, :, column:column + span] = part
        first += count
        column += span


def activate(chunks, after):
    each, width = chunks[0][0].shape[2], sum(terms[0].shape[3] for terms in chunks)
    flat = [term for terms in chunks for term in terms]
    return pl.pallas_call(
        functools.partial(activate_kernel, [len(terms) for terms in chunks]),
        grid=(1,),
        in_specs=[pl.BlockSpec((1,) + t.shape[1:], lambda j: (0, 0, 0, 0)) for t in flat]
        + anywhere(after),
        out_specs=(
            pl.BlockSpec((each, width), lambda j: (0, 0)),
            pl.BlockSpec((3, each, width), lambda j: (0, 0, 0)),
        ),
        out_shape=(
            jax.ShapeDtypeStruct((each, width), bf16),
            jax.ShapeDtypeStruct((3, each, width), bf16),
        ),
        compiler_params=params(),
        cost_estimate=LIGHT,
        name="activate",
    )(*flat, *after)


def edge_kernel(base_ref, start_ref, end_ref, out_ref):
    row = lax.broadcasted_iota(jnp.int32, (DH, DH), 0)
    for b in range(start_ref.shape[0]):
        start, end = start_ref[b:b + 1, :], end_ref[b:b + 1, :]
        both = jnp.where(row == 0, start, end) - base_ref[0]
        out_ref[b * DH:(b + 1) * DH, :] = both.astype(f32).T[:, :2].astype(jnp.int32)


def edge_columns(base, start, end):
    count = start.shape[0]
    lines = pl.BlockSpec((count // DH, DH), lambda j, base: (0, 0))
    return pl.pallas_call(
        edge_kernel,
        grid_spec=pltpu.PrefetchScalarGridSpec(
            num_scalar_prefetch=1,
            grid=(1,),
            in_specs=[lines, lines],
            out_specs=pl.BlockSpec((count, 2), lambda j, base: (0, 0)),
        ),
        out_shape=jax.ShapeDtypeStruct((count, 2), jnp.int32),
        compiler_params=params(),
        cost_estimate=LIGHT,
        name="edges",
    )(base.reshape(1), start.reshape(-1, DH), end.reshape(-1, DH))


def attend_kernel(owners, sends, at_ref, *refs):
    queries, edges = refs[:owners], refs[owners:2 * owners]
    k_ref, v_ref = refs[2 * owners:2 * owners + 2]
    outs, mask_ref = refs[-1 - sends:-1], refs[-1]
    events = mask_ref.shape[1]
    each = outs[0].shape[1]

    @pl.when(pl.program_id(0) == 0)
    def _():
        zs, chunks, _, piece, _ = edges[0].shape
        at = lax.broadcasted_iota(jnp.int32, (piece, events), 1)
        first = 0
        for p in range(owners):
            for r in range(chunks):
                for z in range(zs):
                    edge = edges[p][z, r, 0]
                    seen = (at >= edge[:, :1]) & (at < edge[:, 1:])
                    mask_ref[first:first + piece, :] = jnp.where(seen, 1.0, 0.0).astype(bf16)
                    first += piece

    for h in range(k_ref.shape[1] // DH):
        at = slice(h * DH, (h + 1) * DH)
        query = jnp.concatenate([q[:, at] for q in queries])
        u = lax.dot_general(
            query, k_ref[:, at], (((1,), (1,)), ((), ())), preferred_element_type=f32
        ) * (0.5 * DH ** (-0.5))
        weights = (u + u * jnp.tanh(u)).astype(bf16) * mask_ref[...]
        term = jnp.dot(weights, v_ref[:, at], preferred_element_type=f32).astype(bf16)
        first = 0
        for out in outs:
            for p in range(out.shape[0]):
                out[p, :, at] = term[first:first + each]
                first += each


def edge_spec(edges, p):
    zs, chunks, _, piece, ends = edges.shape
    return pl.BlockSpec((zs, chunks, 1, piece, ends), lambda j, at: (0, 0, at[0] ^ p, 0, 0))


def attend(at, queries, k_cache, v_cache, edges, head_first, after):
    owners, (each, width) = len(queries), queries[0].shape
    rows, events, counts = owners * each, k_cache.shape[0], parts_of(owners)
    first = head_first * DH
    span = max(h for h in range(DH, 4 * DH, DH) if width % h == 0 and first % h == 0)
    cache = pl.BlockSpec((events, span), lambda j, at: (0, first // span + j))
    return pl.pallas_call(
        functools.partial(attend_kernel, owners, len(counts)),
        grid_spec=pltpu.PrefetchScalarGridSpec(
            num_scalar_prefetch=1,
            grid=(width // span,),
            in_specs=[pl.BlockSpec((each, span), lambda j, at: (0, j))] * owners
            + [edge_spec(edges, p) for p in range(owners)]
            + [cache, cache]
            + anywhere(after),
            out_specs=[pl.BlockSpec((n, each, span), lambda j, at: (0, 0, j)) for n in counts],
            scratch_shapes=[pltpu.VMEM((rows, events), bf16)],
        ),
        out_shape=[jax.ShapeDtypeStruct((n, each, width), bf16) for n in counts],
        compiler_params=params(),
        cost_estimate=LIGHT,
        name="attend",
    )(at, *queries, *[edges] * owners, far(k_cache), far(v_cache), *after)


def merge(means, squares, widths):
    width = sum(widths)
    mean = sum(m * (w / width) for m, w in zip(means, widths))
    square = sum(squares) + sum(w * (m - mean) * (m - mean) for m, w in zip(means, widths))
    return mean, square


def stat_columns(stats):
    stats = [s[...] for s in stats]
    stats = [s if s.shape[0] > 8 else jnp.concatenate([s] * (DH // 8)).T for s in stats]
    return [s[:, :1] for s in stats], [s[:, 4:5] for s in stats]


def finish_kernel(terms, widths, at_ref, edge_ref, q_ref, rest_ref, *refs):
    sums, others = refs[:terms], refs[terms:terms + len(widths)]
    att_ref, stat_ref = refs[-2:]
    rows, width = att_ref.shape
    zs, chunks = edge_ref.shape[:2]
    edge = jnp.concatenate(
        [edge_ref[z, r, 0] for r in range(chunks) for z in range(zs)]
    ).astype(f32)
    root = lax.rsqrt(edge[:, 1:] - edge[:, :1])
    total = jnp.zeros((rows, 1), f32)
    for first in range(0, width, DH):
        at = slice(first, first + DH)
        summed = sum(s[0, :, at].astype(f32) for s in sums)
        product = q_ref[:, at].astype(f32) * rest_ref[0, :, at].astype(f32)
        weight = silu(jnp.sum(product, axis=1, keepdims=True) * DH ** (-0.5))
        value = summed * root + weight * rest_ref[1, :, at].astype(f32)
        att_ref[:, at] = value
        total += jnp.sum(value, axis=1, keepdims=True)
    mean = total / width
    spread = jnp.zeros((rows, DH), f32)
    for first in range(0, width, DH):
        away = att_ref[:, first:first + DH] - mean
        spread += away * away
    square = jnp.sum(spread, axis=1, keepdims=True)
    if others:
        means, squares = stat_columns(others)
        mean, square = merge([mean] + means, [square] + squares, [width] + widths)
    lane = lax.broadcasted_iota(jnp.int32, (rows, DH), 1)
    stat = jnp.where(lane < 4, mean, square)
    stat_ref[...] = stat if stat_ref.shape == stat.shape else stat.T[:8]


def finish(at, edges, query, rest, sums, others, widths, after):
    rows, width = query.shape
    stat = (8, rows) if others and rows == DH else (rows, DH)
    return pl.pallas_call(
        functools.partial(finish_kernel, len(sums), widths),
        grid_spec=pltpu.PrefetchScalarGridSpec(
            num_scalar_prefetch=1,
            grid=(1,),
            in_specs=[
                edge_spec(edges, 0),
                pl.BlockSpec((rows, width), lambda j, at: (0, 0)),
                pl.BlockSpec((2, rows, width), lambda j, at: (0, 0, 0)),
            ]
            + [pl.BlockSpec((1, rows, width), lambda j, at: (0, 0, 0))] * len(sums)
            + [pl.BlockSpec((rows, DH), lambda j, at: (0, 0))] * len(others)
            + anywhere(after),
            out_specs=(
                pl.BlockSpec((rows, width), lambda j, at: (0, 0)),
                pl.BlockSpec(stat, lambda j, at: (0, 0)),
            ),
        ),
        out_shape=(
            jax.ShapeDtypeStruct((rows, width), f32),
            jax.ShapeDtypeStruct(stat, f32),
        ),
        compiler_params=params(),
        cost_estimate=LIGHT,
        name="finish",
    )(at, edges, query, rest, *sums, *others, *after)


def merge_kernel(width, *refs):
    (m, n), (s, t) = (
        [r[:4] if r.shape[0] == 8 else r[:, :4] for r in refs[:2]],
        [r[4:] if r.shape[0] == 8 else r[:, 4:8] for r in refs[:2]],
    )
    mean, square = merge([m, n], [s, t], [width] * 2)
    if refs[2].shape[0] == 8:
        refs[2][:4], refs[2][4:] = mean, square
    else:
        lane = lax.broadcasted_iota(jnp.int32, refs[2].shape, 1)
        refs[2][...] = jnp.where(lane < 4, mean[:, :1], square[:, :1])


def merge_stats(stats, width):
    return pl.pallas_call(
        functools.partial(merge_kernel, width),
        out_shape=jax.ShapeDtypeStruct(stats[0].shape, f32),
        compiler_params=params(),
        cost_estimate=LIGHT,
        name="merge",
    )(*stats)


def gate_kernel(count, parts, width, *refs):
    stats, atts, rests, outs = (
        refs[:count], refs[count:count + parts],
        refs[count + parts:count + 2 * parts], refs[count + 2 * parts:],
    )
    means, squares = stat_columns(stats)
    mean, square = merge(means, squares, [width] * count)
    scale = lax.rsqrt(square / (width * count) + EPSILON)
    rows, column = outs[0].shape[0], 0
    for att, rest in zip(atts, rests):
        span = att.shape[1]
        normed = (att[...] - mean) * scale
        gated = (normed * rest[0].astype(f32)).astype(bf16)
        for r, out in enumerate(outs):
            out[:, column:column + span] = gated[r * rows:(r + 1) * rows]
        column += span
    for out in outs:
        if out.shape[1] > column:
            out[:, column:] = jnp.zeros((rows, out.shape[1] - column), bf16)


def gate_rows(stats, stat_width, atts, rests, chunks):
    rows, width = atts[0].shape[0], sum(a.shape[1] for a in atts)
    widths = [width + DH * min(r, 1) for r in range(chunks)]
    return pl.pallas_call(
        functools.partial(gate_kernel, len(stats), len(atts), stat_width),
        grid=(1,),
        in_specs=[pl.BlockSpec(s.shape, lambda j: (0, 0)) for s in stats]
        + [pl.BlockSpec((rows, a.shape[1]), lambda j: (0, 0)) for a in atts]
        + [pl.BlockSpec((1, rows, r.shape[2]), lambda j: (2, 0, 0)) for r in rests],
        out_specs=[pl.BlockSpec((rows // chunks, w), lambda j: (0, 0)) for w in widths],
        out_shape=[jax.ShapeDtypeStruct((rows // chunks, w), bf16) for w in widths],
        compiler_params=params(),
        cost_estimate=LIGHT,
        name="gate",
    )(*stats, *atts, *rests)


def output_kernel(owners, slots, after, index_ref, *refs):
    rows, w_ref, outs, lhs_ref = refs[:owners], refs[owners], refs[owners + 1 + after:-1], refs[-1]
    piece = rows[0].shape[1]

    @pl.when(pl.program_id(0) == 0)
    def _():
        first = 0
        for slot in slots:
            for p in range(owners):
                lhs_ref[first:first + piece, :] = rows[p][index_ref[0] ^ slot]
                first += piece

    sums = jnp.dot(lhs_ref[...], w_ref[...], preferred_element_type=f32).astype(bf16)
    first = 0
    for out in outs:
        for k in range(out.shape[0]):
            for p in range(owners):
                out[k, p] = sums[first:first + piece]
                first += piece


def output(index, slots, counts, blocks, w_out, column, columns, after):
    owners, each, zs = len(blocks), blocks[0].shape[0], sum(counts)
    width, piece = w_out.shape[0], each // zs
    span = max(c for c in (512, 256, columns) if columns % c == 0 and column % c == 0)
    row_spec = pl.BlockSpec((zs, piece, width), lambda j, at: (0, 0, 0))
    return pl.pallas_call(
        functools.partial(output_kernel, owners, slots, len(after)),
        grid_spec=pltpu.PrefetchScalarGridSpec(
            num_scalar_prefetch=1,
            grid=(columns // span,),
            in_specs=[row_spec] * owners
            + [pl.BlockSpec((width, span), lambda j, at: (0, column // span + j))]
            + anywhere(after),
            out_specs=[
                pl.BlockSpec((n, owners, piece, span), lambda j, at: (0, 0, 0, j)) for n in counts
            ],
            scratch_shapes=[pltpu.VMEM((owners * each, width), bf16)],
        ),
        out_shape=[jax.ShapeDtypeStruct((n, owners, piece, columns), bf16) for n in counts],
        compiler_params=params(),
        cost_estimate=LIGHT,
        name="output",
    )(
        index.reshape(1).astype(jnp.int32),
        *[b.reshape(zs, piece, b.shape[1]) for b in blocks], far(w_out), *after,
    )


def close_kernel(counts, at_ref, t_ref, *refs):
    out_ref, mark_ref = refs[-2:]
    mark_ref[...] = jnp.zeros_like(mark_ref)
    first, column = 0, 0
    for count in counts:
        terms = refs[first:first + count]
        span = terms[0].shape[-1]
        at = slice(column, column + span)
        for p in range(out_ref.shape[0]):
            total = t_ref[p, :, at].astype(f32)
            for term in terms:
                total = total + term[0, p ^ at_ref[0]].astype(f32)
            out_ref[p, :, at] = total.astype(bf16)
        first += count
        column += span


def close(place, index, tokens, chunks, r, groups, out, after):
    _, owners, piece, _ = groups[0][0].shape
    width = tokens.shape[1]
    at = jnp.stack([place, index * chunks + r]).astype(jnp.int32)
    flat = [term for terms in groups for term in terms]
    into = [] if out is None else [out]
    return pl.pallas_call(
        functools.partial(close_kernel, [len(terms) for terms in groups]),
        grid_spec=pltpu.PrefetchScalarGridSpec(
            num_scalar_prefetch=1,
            grid=(1,),
            in_specs=[pl.BlockSpec((owners, piece, width), lambda j, at: (at[1], 0, 0))]
            + [pl.BlockSpec((1,) + t.shape[1:], lambda j, at: (0, 0, 0, 0)) for t in flat]
            + anywhere(into) + anywhere(after),
            out_specs=(
                pl.BlockSpec((owners, piece, width), lambda j, at: (r, 0, 0)),
                pl.BlockSpec((8, DH), lambda j, at: (0, 0)),
            ),
        ),
        out_shape=(
            jax.ShapeDtypeStruct((chunks * owners, piece, width), bf16),
            jax.ShapeDtypeStruct((8, DH), f32),
        ),
        input_output_aliases={} if out is None else {2 + len(flat): 0},
        compiler_params=params(),
        cost_estimate=LIGHT,
        name="close",
    )(at, far(tokens.reshape(-1, piece, width)), *flat, *into, *after)


def bits_of(axis):
    count = lax.axis_size(axis)
    assert count & (count - 1) == 0
    return count.bit_length() - 1


def reverse(index, bits):
    return sum((((index >> b) & 1) << (bits - 1 - b) for b in range(bits)), 0 * index)


def swap(x, axis, bit):
    return lax.ppermute(
        x, axis, [(i, i ^ (1 << bit)) for i in range(lax.axis_size(axis))]
    )


def scatter(keep, gots, axis, after=()):
    terms, sent = [keep, gots[0]], gots[-1]
    for b in range(1, bits_of(axis)):
        sent = fold([keep, gots[-1]] if b == 1 else terms, after)
        terms.append(swap(sent, axis, b))
    return terms, sent


def gather(x, axis, after=()):
    blocks = [x]
    for b in reversed(range(bits_of(axis))):
        blocks = blocks + [swap(block, axis, b) for block in blocks]
        if len(blocks) == 2:
            blocks[1] = tie(blocks[1], after)
    return blocks


def all_stats(stat, width, axis):
    count = lax.axis_size(axis)
    if count > 8 or count & (count - 1):
        every = lax.all_gather(stat, axis)
        return [every[i] for i in range(count)], width
    stats = [stat]
    for b in range(bits_of(axis)):
        if b:
            width, stats = 2 * width, [merge_stats(stats, width)]
        stats.append(swap(stats[0], axis, b))
    return stats, width


def head_chunks(heads):
    if heads % 8:
        return [1] * heads
    unit = heads // 8
    return [unit, 2 * unit, 2 * unit, 2 * unit, unit]


GROUPS = [[0, 1], [2], [3], [4]]
ORDER = [
    "P0", "P1", "F0", "P2", "F1", "P3", "F2", "A0", "F3", "P4", "A1", "F4", "T0", "G0", "A2",
    "T1", "A3", "G1", "T2", "E0", "G2", "T3", "G3", "E1", "E2", "E3",
]


def local(tokens, w_qkvu, k_cache, v_cache, w_out, vis_start, vis_end):
    cand, depth = tokens.shape
    owners, zs = lax.axis_size("hist"), lax.axis_size("head")
    index = lax.axis_index("head")
    place = reverse(lax.axis_index("hist"), bits_of("hist"))
    width = w_qkvu.shape[2]
    events = k_cache.shape[0]
    chunks = 2 if cand % (2 * owners * zs * 16) == 0 else 1
    piece = cand // (zs * chunks * owners)

    def arrange(x):
        x = x.reshape((zs, chunks, owners, piece) + x.shape[1:])
        if piece % 16 == 0:
            return x
        blocks = [lax.dynamic_index_in_dim(x, p ^ place, 2, False) for p in range(owners)]
        x = jnp.stack(blocks).swapaxes(1, 2)
        return x.reshape((1, 1, owners, zs * chunks * piece) + x.shape[4:])

    at = (place if piece % 16 == 0 else jnp.int32(0)).reshape(1)
    ordered = arrange(tokens)
    first_event = lax.axis_index("hist") * events
    edges = arrange(edge_columns(first_event, vis_start, vis_end))

    sizes = head_chunks(width // DH)
    firsts = [sum(sizes[:c]) for c in range(len(sizes))]
    groups, order = GROUPS, ORDER
    if len(sizes) != 5:
        groups = [[c] for c in range(len(sizes))]
        order = [step + str(c) for step in "PFATGE" for c in range(len(sizes))]
    last = len(groups) - 1
    heads = [sum(sizes[c] for c in group) for group in groups]
    chain, keeps, firsts_got, terms, sums = [], {}, {}, {}, {}
    halves, queries, parts, atts, stats = {}, {}, {}, {}, {}
    for step, c in [(name[0], int(name[1:])) for name in order]:
        after = chain[-1:]
        if step == "P":
            keep, *sends = project(at, ordered, w_qkvu, firsts[c], sizes[c], after)
            before = firsts_got[c - 1] if c >= 1 else []
            before = before + [terms[0][-1]] if c == 2 and 0 in terms else before
            firsts_got[c] = [swap(tie(send, before), "hist", 0) for send in reversed(sends)][::-1]
            keeps[c] = keep
            chain.append(keep)
        elif step == "F":
            terms[c], sent = scatter(keeps[c], firsts_got[c], "hist", after)
            chain.append(sent)
        elif step == "A":
            parts[c] = activate([terms[k] for k in groups[c]], after)
            queries[c] = gather(parts[c][0], "hist")
            chain.append(parts[c][0])
        elif step == "T":
            first = firsts[groups[c][0]]
            keep, *sends = attend(at, queries[c], k_cache, v_cache, edges, first, after)
            halves[c] = keep, [swap(send, "hist", 0) for send in sends]
            chain.append(keep)
        elif step == "G":
            sums[c], sent = scatter(*halves[c], "hist", after)
            chain.append(sent)
        else:
            others = [stats[k] for k in range(last)] if c == last else []
            widths = [size * DH for size in heads[:last]] if c == last else []
            atts[c], stats[c] = finish(at, edges, *parts[c], sums[c], others, widths, after)
            chain.append(atts[c])

    atts = [atts[c] for c in range(last + 1)]
    rests = [parts[c][1] for c in range(last + 1)]
    every, stat_width = all_stats(stats[last], width, "head")
    gated = gate_rows(every, stat_width, atts, rests, chunks)
    columns = w_out.shape[1]
    straight = piece % 16 == 0 and zs & (zs - 1) == 0
    out = None
    if not straight:
        for r, rows in enumerate(gated):
            whole = jnp.concatenate(gather(rows, "hist"))[:, :width]
            whole = jnp.dot(whole, w_out, preferred_element_type=f32).astype(bf16)
            whole = whole.reshape(owners, zs, piece, -1).swapaxes(0, 1)
            whole = lax.psum_scatter(whole, "head", scatter_dimension=0, tiled=True)
            out, _ = close(place, index, tokens, chunks, r, [[whole]], out, [])
        return out.reshape(cand // zs, -1)
    slots = [reverse(k, bits_of("head")) for k in range(zs)]
    unit = columns // 8
    spans = [[columns]] * chunks
    if unit % (2 * DH) == 0 and chunks == 2:
        spans = [[4 * unit, 4 * unit], [5 * unit, 3 * unit]]
    counts = [zs // 2] * 2 if zs > 1 else [1]
    plan = [(r, sum(row[:g]), span) for r, row in enumerate(spans) for g, span in enumerate(row)]
    chain, first_out, blocks, made, folded = [], [], {}, [], []

    def fold_next():
        own, arrived = made[len(folded)]
        terms, sent = scatter(own, arrived, "head", chain) if arrived else ([own], own)
        folded.append(terms)
        return [sent]

    for n, (r, column, span) in enumerate(plan):
        if r not in blocks:
            blocks[r] = gather(gated[r], "hist", first_out)
        own, *others = output(index, slots, counts, blocks[r], w_out, column, span, chain)
        before = made[n - 2][1] if n > 1 else []
        before = before + [folded[0][-1]] if folded else before
        made.append((own, [swap(tie(x, before), "head", 0) for x in others]))
        chain, first_out = [own], first_out or [own]
        if n == 2:
            chain = fold_next()
    done = 0
    for r, row in enumerate(spans):
        while len(folded) < min(len(plan), done + len(row) + 2):
            chain = fold_next()
        terms, done = folded[done:done + len(row)], done + len(row)
        out, mark = close(place, index, tokens, chunks, r, terms, out, chain)
        chain = [mark]
    return out.reshape(cand // zs, -1)


def solution(mesh):
    in_specs = (
        P("groups", "hist"),
        P("hist", None, "head"),
        P(("groups", "hist"), "head"),
        P(("groups", "hist"), "head"),
        P("head", "hist"),
        P("groups"),
        P("groups"),
    )
    out_specs = P(("groups", "head"), "hist")
    return jax.shard_map(local, mesh=mesh, in_specs=in_specs, out_specs=out_specs, check_vma=False)
```

```python
import functools

import jax
import jax.numpy as jnp
from jax import lax
from jax.experimental import pallas as pl
from jax.experimental.pallas import tpu as pltpu
from jax.sharding import PartitionSpec as P

DH = 128
EPSILON = 1e-05
VMEM_LIMIT = 28 * 1024 * 1024

bf16 = jnp.bfloat16
f32 = jnp.float32


def silu(v):
    u = 0.5 * v
    return u + u * jnp.tanh(u)


def params():
    return pltpu.CompilerParams(vmem_limit_bytes=VMEM_LIMIT)


LIGHT = pl.CostEstimate(flops=1000, bytes_accessed=1000, transcendentals=0)


def far(x):
    return pltpu.with_memory_space_constraint(x, pltpu.HBM)


def anywhere(arrays):
    return [pl.BlockSpec(memory_space=pl.ANY)] * len(arrays)


def project_kernel(parts, owners, after, at_ref, *refs):
    rows, weights = refs[:owners], refs[owners:owners + parts]
    outs, lhs_ref = refs[owners + parts + after:-parts - 1], refs[-parts - 1]
    wides = refs[-parts:]
    zs, chunks, _, piece, _ = rows[0].shape
    depth = weights[0].shape[0]

    @pl.when(pl.program_id(0) == 0)
    def _():
        first = 0
        for p in range(owners):
            for r in range(chunks):
                for z in range(zs):
                    lhs_ref[first:first + piece, :] = rows[p][z, r, 0]
                    first += piece

    res = None
    for k, wide in enumerate(wides):
        wide[...] = weights[k].reshape(depth * 4, DH)[...].astype(f32)
        rhs = jnp.concatenate(
            [wide[pl.ds(i, depth, stride=4), :].astype(bf16) for i in range(4)], axis=1
        )
        term = jnp.dot(lhs_ref[:, k * depth:(k + 1) * depth], rhs, preferred_element_type=f32)
        res = term if res is None else res + term
    res = res.astype(bf16)
    each, first = outs[0].shape[2], 0
    for out in outs:
        for p in range(out.shape[0]):
            for i in range(4):
                out[p, i] = res[first:first + each, i * DH:(i + 1) * DH]
            first += each


def parts_of(owners):
    half = owners // 2
    return [half, half // 2, half // 2] if half > 1 else [half, half]


def project(at, tokens, w, head_first, heads, after):
    zs, chunks, owners, piece, depth = tokens.shape
    each, counts = zs * chunks * piece, parts_of(owners)
    parts = 4 if depth % 512 == 0 else 1
    return pl.pallas_call(
        functools.partial(project_kernel, parts, owners, len(after)),
        grid_spec=pltpu.PrefetchScalarGridSpec(
            num_scalar_prefetch=1,
            grid=(heads,),
            in_specs=[
                pl.BlockSpec(
                    (zs, chunks, 1, piece, depth), lambda j, at, p=p: (0, 0, at[0] ^ p, 0, 0)
                )
                for p in range(owners)
            ]
            + [
                pl.BlockSpec((depth // parts, 4, DH), lambda j, at, k=k: (k, 0, head_first + j))
                for k in range(parts)
            ]
            + anywhere(after),
            out_specs=[
                pl.BlockSpec((n, 4, each, DH), lambda j, at: (0, 0, 0, j)) for n in counts
            ],
            scratch_shapes=[pltpu.VMEM((owners * each, depth), bf16)]
            + [pltpu.VMEM((depth // parts * 4, DH), f32) for _ in range(parts)],
        ),
        out_shape=[jax.ShapeDtypeStruct((n, 4, each, heads * DH), bf16) for n in counts],
        compiler_params=params(),
        cost_estimate=LIGHT,
        name="project",
    )(at, *[far(tokens)] * owners, *[far(w)] * parts, *after)


def tie_kernel(*refs):
    pass


def tie(x, after):
    if not after:
        return x
    return pl.pallas_call(
        tie_kernel,
        in_specs=anywhere([x, *after]),
        out_specs=pl.BlockSpec(memory_space=pl.ANY),
        out_shape=jax.ShapeDtypeStruct(x.shape, x.dtype),
        input_output_aliases={0: 0},
        compiler_params=params(),
        cost_estimate=LIGHT,
        name="tie",
    )(x, *after)


def fold_kernel(count, *refs):
    refs[-1][...] = sum(r[...].astype(f32) for r in refs[:count]).astype(bf16)


def fold(terms, after=()):
    half = terms[0].shape[0] // 2 if len(terms) == 2 else terms[-1].shape[0] // 2
    tail = terms[0].shape[1:]
    steps = 2 if tail[-1] % 256 == 0 else 1
    block = (half,) + tail[:-1] + (tail[-1] // steps,)
    middle = (0,) * (len(tail) - 1)
    firsts = [0 if t.shape[0] == half else 1 for t in terms]
    return pl.pallas_call(
        functools.partial(fold_kernel, len(terms)),
        grid=(steps,),
        in_specs=[pl.BlockSpec(block, lambda j, f=f: (f,) + middle + (j,)) for f in firsts]
        + anywhere(after),
        out_specs=pl.BlockSpec(block, lambda j: (0,) + middle + (j,)),
        out_shape=jax.ShapeDtypeStruct((half,) + tail, bf16),
        compiler_params=params(),
        cost_estimate=LIGHT,
        name="fold",
    )(*terms, *after)


def activate_kernel(counts, *refs):
    q_ref, rest_ref = refs[-2:]
    first, column = 0, 0
    for count in counts:
        terms = refs[first:first + count]
        span = terms[0].shape[-1]
        for i in range(4):
            part = silu(sum(t[0, i].astype(f32) for t in terms)).astype(bf16)
            if i == 0:
                q_ref[:, column:column + span] = part
            else:
                rest_ref[i - 1, :, column:column + span] = part
        first += count
        column += span


def activate(chunks, after):
    each, width = chunks[0][0].shape[2], sum(terms[0].shape[3] for terms in chunks)
    flat = [term for terms in chunks for term in terms]
    return pl.pallas_call(
        functools.partial(activate_kernel, [len(terms) for terms in chunks]),
        grid=(1,),
        in_specs=[pl.BlockSpec((1,) + t.shape[1:], lambda j: (0, 0, 0, 0)) for t in flat]
        + anywhere(after),
        out_specs=(
            pl.BlockSpec((each, width), lambda j: (0, 0)),
            pl.BlockSpec((3, each, width), lambda j: (0, 0, 0)),
        ),
        out_shape=(
            jax.ShapeDtypeStruct((each, width), bf16),
            jax.ShapeDtypeStruct((3, each, width), bf16),
        ),
        compiler_params=params(),
        cost_estimate=LIGHT,
        name="activate",
    )(*flat, *after)


def edge_kernel(base_ref, start_ref, end_ref, out_ref):
    row = lax.broadcasted_iota(jnp.int32, (DH, DH), 0)
    for b in range(start_ref.shape[0]):
        start, end = start_ref[b:b + 1, :], end_ref[b:b + 1, :]
        both = jnp.where(row == 0, start, end) - base_ref[0]
        out_ref[b * DH:(b + 1) * DH, :] = both.astype(f32).T[:, :2].astype(jnp.int32)


def edge_columns(base, start, end):
    count = start.shape[0]
    lines = pl.BlockSpec((count // DH, DH), lambda j, base: (0, 0))
    return pl.pallas_call(
        edge_kernel,
        grid_spec=pltpu.PrefetchScalarGridSpec(
            num_scalar_prefetch=1,
            grid=(1,),
            in_specs=[lines, lines],
            out_specs=pl.BlockSpec((count, 2), lambda j, base: (0, 0)),
        ),
        out_shape=jax.ShapeDtypeStruct((count, 2), jnp.int32),
        compiler_params=params(),
        cost_estimate=LIGHT,
        name="edges",
    )(base.reshape(1), start.reshape(-1, DH), end.reshape(-1, DH))


def attend_kernel(owners, sends, at_ref, *refs):
    queries, edges = refs[:owners], refs[owners:2 * owners]
    k_ref, v_ref = refs[2 * owners:2 * owners + 2]
    outs, mask_ref = refs[-1 - sends:-1], refs[-1]
    events = mask_ref.shape[1]
    each = outs[0].shape[1]

    @pl.when(pl.program_id(0) == 0)
    def _():
        zs, chunks, _, piece, _ = edges[0].shape
        at = lax.broadcasted_iota(jnp.int32, (piece, events), 1)
        first = 0
        for p in range(owners):
            for r in range(chunks):
                for z in range(zs):
                    edge = edges[p][z, r, 0]
                    seen = (at >= edge[:, :1]) & (at < edge[:, 1:])
                    mask_ref[first:first + piece, :] = jnp.where(seen, 1.0, 0.0).astype(bf16)
                    first += piece

    for h in range(k_ref.shape[1] // DH):
        at = slice(h * DH, (h + 1) * DH)
        query = jnp.concatenate([q[:, at] for q in queries])
        u = lax.dot_general(
            query, k_ref[:, at], (((1,), (1,)), ((), ())), preferred_element_type=f32
        ) * (0.5 * DH ** (-0.5))
        weights = (u + u * jnp.tanh(u)).astype(bf16) * mask_ref[...]
        term = jnp.dot(weights, v_ref[:, at], preferred_element_type=f32).astype(bf16)
        first = 0
        for out in outs:
            for p in range(out.shape[0]):
                out[p, :, at] = term[first:first + each]
                first += each


def edge_spec(edges, p):
    zs, chunks, _, piece, ends = edges.shape
    return pl.BlockSpec((zs, chunks, 1, piece, ends), lambda j, at: (0, 0, at[0] ^ p, 0, 0))


def attend(at, queries, k_cache, v_cache, edges, head_first, after):
    owners, (each, width) = len(queries), queries[0].shape
    rows, events, counts = owners * each, k_cache.shape[0], parts_of(owners)
    first = head_first * DH
    span = max(h for h in range(DH, 4 * DH, DH) if width % h == 0 and first % h == 0)
    cache = pl.BlockSpec((events, span), lambda j, at: (0, first // span + j))
    return pl.pallas_call(
        functools.partial(attend_kernel, owners, len(counts)),
        grid_spec=pltpu.PrefetchScalarGridSpec(
            num_scalar_prefetch=1,
            grid=(width // span,),
            in_specs=[pl.BlockSpec((each, span), lambda j, at: (0, j))] * owners
            + [edge_spec(edges, p) for p in range(owners)]
            + [cache, cache]
            + anywhere(after),
            out_specs=[pl.BlockSpec((n, each, span), lambda j, at: (0, 0, j)) for n in counts],
            scratch_shapes=[pltpu.VMEM((rows, events), bf16)],
        ),
        out_shape=[jax.ShapeDtypeStruct((n, each, width), bf16) for n in counts],
        compiler_params=params(),
        cost_estimate=LIGHT,
        name="attend",
    )(at, *queries, *[edges] * owners, far(k_cache), far(v_cache), *after)


def merge(means, squares, widths):
    width = sum(widths)
    mean = sum(m * (w / width) for m, w in zip(means, widths))
    square = sum(squares) + sum(w * (m - mean) * (m - mean) for m, w in zip(means, widths))
    return mean, square


def stat_columns(stats):
    stats = [s[...] for s in stats]
    stats = [s if s.shape[0] > 8 else jnp.concatenate([s] * (DH // 8)).T for s in stats]
    return [s[:, :1] for s in stats], [s[:, 4:5] for s in stats]


def finish_kernel(terms, widths, at_ref, edge_ref, q_ref, rest_ref, *refs):
    sums, others = refs[:terms], refs[terms:terms + len(widths)]
    att_ref, stat_ref = refs[-2:]
    rows, width = att_ref.shape
    zs, chunks = edge_ref.shape[:2]
    edge = jnp.concatenate(
        [edge_ref[z, r, 0] for r in range(chunks) for z in range(zs)]
    ).astype(f32)
    root = lax.rsqrt(edge[:, 1:] - edge[:, :1])
    total = jnp.zeros((rows, 1), f32)
    for first in range(0, width, DH):
        at = slice(first, first + DH)
        summed = sum(s[0, :, at].astype(f32) for s in sums)
        product = q_ref[:, at].astype(f32) * rest_ref[0, :, at].astype(f32)
        weight = silu(jnp.sum(product, axis=1, keepdims=True) * DH ** (-0.5))
        value = summed * root + weight * rest_ref[1, :, at].astype(f32)
        att_ref[:, at] = value
        total += jnp.sum(value, axis=1, keepdims=True)
    mean = total / width
    spread = jnp.zeros((rows, DH), f32)
    for first in range(0, width, DH):
        away = att_ref[:, first:first + DH] - mean
        spread += away * away
    square = jnp.sum(spread, axis=1, keepdims=True)
    if others:
        means, squares = stat_columns(others)
        mean, square = merge([mean] + means, [square] + squares, [width] + widths)
    lane = lax.broadcasted_iota(jnp.int32, (rows, DH), 1)
    stat = jnp.where(lane < 4, mean, square)
    stat_ref[...] = stat if stat_ref.shape == stat.shape else stat.T[:8]


def finish(at, edges, query, rest, sums, others, widths, after):
    rows, width = query.shape
    stat = (8, rows) if others and rows == DH else (rows, DH)
    return pl.pallas_call(
        functools.partial(finish_kernel, len(sums), widths),
        grid_spec=pltpu.PrefetchScalarGridSpec(
            num_scalar_prefetch=1,
            grid=(1,),
            in_specs=[
                edge_spec(edges, 0),
                pl.BlockSpec((rows, width), lambda j, at: (0, 0)),
                pl.BlockSpec((2, rows, width), lambda j, at: (0, 0, 0)),
            ]
            + [pl.BlockSpec((1, rows, width), lambda j, at: (0, 0, 0))] * len(sums)
            + [pl.BlockSpec((rows, DH), lambda j, at: (0, 0))] * len(others)
            + anywhere(after),
            out_specs=(
                pl.BlockSpec((rows, width), lambda j, at: (0, 0)),
                pl.BlockSpec(stat, lambda j, at: (0, 0)),
            ),
        ),
        out_shape=(
            jax.ShapeDtypeStruct((rows, width), f32),
            jax.ShapeDtypeStruct(stat, f32),
        ),
        compiler_params=params(),
        cost_estimate=LIGHT,
        name="finish",
    )(at, edges, query, rest, *sums, *others, *after)


def merge_kernel(width, *refs):
    (m, n), (s, t) = (
        [r[:4] if r.shape[0] == 8 else r[:, :4] for r in refs[:2]],
        [r[4:] if r.shape[0] == 8 else r[:, 4:8] for r in refs[:2]],
    )
    mean, square = merge([m, n], [s, t], [width] * 2)
    if refs[2].shape[0] == 8:
        refs[2][:4], refs[2][4:] = mean, square
    else:
        lane = lax.broadcasted_iota(jnp.int32, refs[2].shape, 1)
        refs[2][...] = jnp.where(lane < 4, mean[:, :1], square[:, :1])


def merge_stats(stats, width):
    return pl.pallas_call(
        functools.partial(merge_kernel, width),
        out_shape=jax.ShapeDtypeStruct(stats[0].shape, f32),
        compiler_params=params(),
        cost_estimate=LIGHT,
        name="merge",
    )(*stats)


def gate_kernel(count, parts, width, *refs):
    stats, atts, rests, outs = (
        refs[:count], refs[count:count + parts],
        refs[count + parts:count + 2 * parts], refs[count + 2 * parts:],
    )
    means, squares = stat_columns(stats)
    mean, square = merge(means, squares, [width] * count)
    scale = lax.rsqrt(square / (width * count) + EPSILON)
    rows, column = outs[0].shape[0], 0
    for att, rest in zip(atts, rests):
        span = att.shape[1]
        normed = (att[...] - mean) * scale
        gated = (normed * rest[0].astype(f32)).astype(bf16)
        for r, out in enumerate(outs):
            out[:, column:column + span] = gated[r * rows:(r + 1) * rows]
        column += span
    for out in outs:
        if out.shape[1] > column:
            out[:, column:] = jnp.zeros((rows, out.shape[1] - column), bf16)


def gate_rows(stats, stat_width, atts, rests, chunks):
    rows, width = atts[0].shape[0], sum(a.shape[1] for a in atts)
    widths = [width + DH * min(r, 1) for r in range(chunks)]
    return pl.pallas_call(
        functools.partial(gate_kernel, len(stats), len(atts), stat_width),
        grid=(1,),
        in_specs=[pl.BlockSpec(s.shape, lambda j: (0, 0)) for s in stats]
        + [pl.BlockSpec((rows, a.shape[1]), lambda j: (0, 0)) for a in atts]
        + [pl.BlockSpec((1, rows, r.shape[2]), lambda j: (2, 0, 0)) for r in rests],
        out_specs=[pl.BlockSpec((rows // chunks, w), lambda j: (0, 0)) for w in widths],
        out_shape=[jax.ShapeDtypeStruct((rows // chunks, w), bf16) for w in widths],
        compiler_params=params(),
        cost_estimate=LIGHT,
        name="gate",
    )(*stats, *atts, *rests)


def output_kernel(owners, slots, after, index_ref, *refs):
    rows, w_ref, outs, lhs_ref = refs[:owners], refs[owners], refs[owners + 1 + after:-1], refs[-1]
    piece = rows[0].shape[1]

    @pl.when(pl.program_id(0) == 0)
    def _():
        first = 0
        for slot in slots:
            for p in range(owners):
                lhs_ref[first:first + piece, :] = rows[p][index_ref[0] ^ slot]
                first += piece

    sums = jnp.dot(lhs_ref[...], w_ref[...], preferred_element_type=f32).astype(bf16)
    first = 0
    for out in outs:
        for k in range(out.shape[0]):
            for p in range(owners):
                out[k, p] = sums[first:first + piece]
                first += piece


def output(index, slots, counts, blocks, w_out, column, columns, after):
    owners, each, zs = len(blocks), blocks[0].shape[0], sum(counts)
    width, piece = w_out.shape[0], each // zs
    span = max(c for c in (512, 256, columns) if columns % c == 0 and column % c == 0)
    row_spec = pl.BlockSpec((zs, piece, width), lambda j, at: (0, 0, 0))
    return pl.pallas_call(
        functools.partial(output_kernel, owners, slots, len(after)),
        grid_spec=pltpu.PrefetchScalarGridSpec(
            num_scalar_prefetch=1,
            grid=(columns // span,),
            in_specs=[row_spec] * owners
            + [pl.BlockSpec((width, span), lambda j, at: (0, column // span + j))]
            + anywhere(after),
            out_specs=[
                pl.BlockSpec((n, owners, piece, span), lambda j, at: (0, 0, 0, j)) for n in counts
            ],
            scratch_shapes=[pltpu.VMEM((owners * each, width), bf16)],
        ),
        out_shape=[jax.ShapeDtypeStruct((n, owners, piece, columns), bf16) for n in counts],
        compiler_params=params(),
        cost_estimate=LIGHT,
        name="output",
    )(
        index.reshape(1).astype(jnp.int32),
        *[b.reshape(zs, piece, b.shape[1]) for b in blocks], far(w_out), *after,
    )


def close_kernel(counts, at_ref, t_ref, *refs):
    out_ref, mark_ref = refs[-2:]
    mark_ref[...] = jnp.zeros_like(mark_ref)
    first, column = 0, 0
    for count in counts:
        terms = refs[first:first + count]
        span = terms[0].shape[-1]
        at = slice(column, column + span)
        for p in range(out_ref.shape[0]):
            total = t_ref[p, :, at].astype(f32)
            for term in terms:
                total = total + term[0, p ^ at_ref[0]].astype(f32)
            out_ref[p, :, at] = total.astype(bf16)
        first += count
        column += span


def close(place, index, tokens, chunks, r, g, groups, out, after):
    _, owners, piece, _ = groups[0][0].shape
    span, width = sum(terms[0].shape[-1] for terms in groups), tokens.shape[1]
    at = jnp.stack([place, index * chunks + r]).astype(jnp.int32)
    flat = [term for terms in groups for term in terms]
    into = [] if out is None else [out]
    return pl.pallas_call(
        functools.partial(close_kernel, [len(terms) for terms in groups]),
        grid_spec=pltpu.PrefetchScalarGridSpec(
            num_scalar_prefetch=1,
            grid=(1,),
            in_specs=[pl.BlockSpec((owners, piece, span), lambda j, at: (at[1], 0, g))]
            + [pl.BlockSpec((1,) + t.shape[1:], lambda j, at: (0, 0, 0, 0)) for t in flat]
            + anywhere(into) + anywhere(after),
            out_specs=(
                pl.BlockSpec((owners, piece, span), lambda j, at: (r, 0, g)),
                pl.BlockSpec((8, DH), lambda j, at: (0, 0)),
            ),
        ),
        out_shape=(
            jax.ShapeDtypeStruct((chunks * owners, piece, width), bf16),
            jax.ShapeDtypeStruct((8, DH), f32),
        ),
        input_output_aliases={} if out is None else {2 + len(flat): 0},
        compiler_params=params(),
        cost_estimate=LIGHT,
        name="close",
    )(at, far(tokens.reshape(-1, piece, width)), *flat, *into, *after)


def bits_of(axis):
    count = lax.axis_size(axis)
    assert count & (count - 1) == 0
    return count.bit_length() - 1


def reverse(index, bits):
    return sum((((index >> b) & 1) << (bits - 1 - b) for b in range(bits)), 0 * index)


def swap(x, axis, bit):
    return lax.ppermute(
        x, axis, [(i, i ^ (1 << bit)) for i in range(lax.axis_size(axis))]
    )


def scatter(keep, gots, axis, after=()):
    terms, sent = [keep, gots[0]], gots[-1]
    for b in range(1, bits_of(axis)):
        sent = fold([keep, gots[-1]] if b == 1 else terms, after)
        terms.append(swap(sent, axis, b))
    return terms, sent


def gather(x, axis, after=()):
    blocks = [x]
    for b in reversed(range(bits_of(axis))):
        blocks = blocks + [swap(block, axis, b) for block in blocks]
        if len(blocks) == 2:
            blocks[1] = tie(blocks[1], after)
    return blocks


def all_stats(stat, width, axis):
    count = lax.axis_size(axis)
    if count > 8 or count & (count - 1):
        every = lax.all_gather(stat, axis)
        return [every[i] for i in range(count)], width
    stats = [stat]
    for b in range(bits_of(axis)):
        if b:
            width, stats = 2 * width, [merge_stats(stats, width)]
        stats.append(swap(stats[0], axis, b))
    return stats, width


def head_chunks(heads):
    if heads % 8:
        return [1] * heads
    unit = heads // 8
    return [unit, 2 * unit, 2 * unit, 2 * unit, unit]


GROUPS = [[0, 1], [2], [3], [4]]
ORDER = [
    "P0", "P1", "F0", "P2", "F1", "P3", "F2", "A0", "F3", "P4", "A1", "F4", "T0", "G0", "A2",
    "T1", "A3", "G1", "T2", "E0", "G2", "T3", "G3", "E1", "E2", "E3",
]


def local(tokens, w_qkvu, k_cache, v_cache, w_out, vis_start, vis_end):
    cand, depth = tokens.shape
    owners, zs = lax.axis_size("hist"), lax.axis_size("head")
    index = lax.axis_index("head")
    place = reverse(lax.axis_index("hist"), bits_of("hist"))
    width = w_qkvu.shape[2]
    events = k_cache.shape[0]
    chunks = 2 if cand % (2 * owners * zs * 16) == 0 else 1
    piece = cand // (zs * chunks * owners)

    def arrange(x):
        x = x.reshape((zs, chunks, owners, piece) + x.shape[1:])
        if piece % 16 == 0:
            return x
        blocks = [lax.dynamic_index_in_dim(x, p ^ place, 2, False) for p in range(owners)]
        x = jnp.stack(blocks).swapaxes(1, 2)
        return x.reshape((1, 1, owners, zs * chunks * piece) + x.shape[4:])

    at = (place if piece % 16 == 0 else jnp.int32(0)).reshape(1)
    ordered = arrange(tokens)
    first_event = lax.axis_index("hist") * events
    edges = arrange(edge_columns(first_event, vis_start, vis_end))

    sizes = head_chunks(width // DH)
    firsts = [sum(sizes[:c]) for c in range(len(sizes))]
    groups, order = GROUPS, ORDER
    if len(sizes) != 5:
        groups = [[c] for c in range(len(sizes))]
        order = [step + str(c) for step in "PFATGE" for c in range(len(sizes))]
    last = len(groups) - 1
    heads = [sum(sizes[c] for c in group) for group in groups]
    chain, keeps, firsts_got, terms, sums = [], {}, {}, {}, {}
    halves, queries, parts, atts, stats = {}, {}, {}, {}, {}
    for step, c in [(name[0], int(name[1:])) for name in order]:
        after = chain[-1:]
        if step == "P":
            keep, *sends = project(at, ordered, w_qkvu, firsts[c], sizes[c], after)
            before = firsts_got[c - 1] if c >= 1 else []
            before = before + [terms[0][-1]] if c == 2 and 0 in terms else before
            firsts_got[c] = [swap(tie(send, before), "hist", 0) for send in reversed(sends)][::-1]
            keeps[c] = keep
            chain.append(keep)
        elif step == "F":
            terms[c], sent = scatter(keeps[c], firsts_got[c], "hist", after)
            chain.append(sent)
        elif step == "A":
            parts[c] = activate([terms[k] for k in groups[c]], after)
            queries[c] = gather(parts[c][0], "hist")
            chain.append(parts[c][0])
        elif step == "T":
            first = firsts[groups[c][0]]
            keep, *sends = attend(at, queries[c], k_cache, v_cache, edges, first, after)
            halves[c] = keep, [swap(send, "hist", 0) for send in sends]
            chain.append(keep)
        elif step == "G":
            sums[c], sent = scatter(*halves[c], "hist", after)
            chain.append(sent)
        else:
            others = [stats[k] for k in range(last)] if c == last else []
            widths = [size * DH for size in heads[:last]] if c == last else []
            atts[c], stats[c] = finish(at, edges, *parts[c], sums[c], others, widths, after)
            chain.append(atts[c])

    atts = [atts[c] for c in range(last + 1)]
    rests = [parts[c][1] for c in range(last + 1)]
    every, stat_width = all_stats(stats[last], width, "head")
    gated = gate_rows(every, stat_width, atts, rests, chunks)
    columns = w_out.shape[1]
    straight = piece % 16 == 0 and zs & (zs - 1) == 0
    out = None
    if not straight:
        for r, rows in enumerate(gated):
            whole = jnp.concatenate(gather(rows, "hist"))[:, :width]
            whole = jnp.dot(whole, w_out, preferred_element_type=f32).astype(bf16)
            whole = whole.reshape(owners, zs, piece, -1).swapaxes(0, 1)
            whole = lax.psum_scatter(whole, "head", scatter_dimension=0, tiled=True)
            out, _ = close(place, index, tokens, chunks, r, 0, [[whole]], out, [])
        return out.reshape(cand // zs, -1)
    slots = [reverse(k, bits_of("head")) for k in range(zs)]
    groups = 2 if columns % 1024 == 0 else 1
    span = columns // groups
    counts = [zs // 2] * 2 if zs > 1 else [1]
    plan = [(r, g) for r in range(chunks) for g in range(groups)]
    chain, first_out, blocks, made, folded = [], [], {}, [], []

    def fold_next():
        own, arrived = made[len(folded)]
        terms, sent = scatter(own, arrived, "head", chain) if arrived else ([own], own)
        folded.append(terms)
        return [sent]

    for n, (r, g) in enumerate(plan):
        if r not in blocks:
            blocks[r] = gather(gated[r], "hist", first_out)
        own, *others = output(index, slots, counts, blocks[r], w_out, g * span, span, chain)
        before = made[n - 2][1] if n > 1 else []
        before = before + [folded[0][-1]] if folded else before
        made.append((own, [swap(tie(x, before), "head", 0) for x in others]))
        chain, first_out = [own], first_out or [own]
        if n == 2:
            chain = fold_next()
    closed = 0
    while closed < len(plan):
        if len(folded) < len(plan):
            chain = fold_next()
        if len(folded) > closed + 2 or len(folded) == len(plan):
            r, g = plan[closed]
            some = 1 if r < chunks - 1 else groups
            out, mark = close(
                place, index, tokens, chunks, r, g, folded[closed:closed + some], out, chain
            )
            chain, closed = [mark], closed + some
    return out.reshape(cand // zs, -1)


def solution(mesh):
    in_specs = (
        P("groups", "hist"),
        P("hist", None, "head"),
        P(("groups", "hist"), "head"),
        P(("groups", "hist"), "head"),
        P("head", "hist"),
        P("groups"),
        P("groups"),
    )
    out_specs = P(("groups", "head"), "hist")
    return jax.shard_map(local, mesh=mesh, in_specs=in_specs, out_specs=out_specs, check_vma=False)
```

```python
import functools

import jax
import jax.numpy as jnp
from jax import lax
from jax.experimental import pallas as pl
from jax.experimental.pallas import tpu as pltpu
from jax.sharding import PartitionSpec as P

DH = 128
EPSILON = 1e-05
VMEM_LIMIT = 20 * 1024 * 1024

bf16 = jnp.bfloat16
f32 = jnp.float32


def silu(v):
    u = 0.5 * v
    return u + u * jnp.tanh(u)


def params():
    return pltpu.CompilerParams(vmem_limit_bytes=VMEM_LIMIT)


LIGHT = pl.CostEstimate(flops=1000, bytes_accessed=1000, transcendentals=0)


def far(x):
    return pltpu.with_memory_space_constraint(x, pltpu.HBM)


def anywhere(arrays):
    return [pl.BlockSpec(memory_space=pl.ANY)] * len(arrays)


def project_kernel(parts, owners, after, at_ref, *refs):
    rows, weights = refs[:owners], refs[owners:owners + parts]
    outs, lhs_ref = refs[owners + parts + after:-parts - 1], refs[-parts - 1]
    wides = refs[-parts:]
    zs, chunks, _, piece, _ = rows[0].shape
    depth = weights[0].shape[0]

    @pl.when(pl.program_id(0) == 0)
    def _():
        first = 0
        for p in range(owners):
            for r in range(chunks):
                for z in range(zs):
                    lhs_ref[first:first + piece, :] = rows[p][z, r, 0]
                    first += piece

    res = None
    for k, wide in enumerate(wides):
        wide[...] = weights[k].reshape(depth * 4, DH)[...].astype(f32)
        rhs = jnp.concatenate(
            [wide[pl.ds(i, depth, stride=4), :].astype(bf16) for i in range(4)], axis=1
        )
        term = jnp.dot(lhs_ref[:, k * depth:(k + 1) * depth], rhs, preferred_element_type=f32)
        res = term if res is None else res + term
    res = res.astype(bf16)
    each, first = outs[0].shape[2], 0
    for out in outs:
        for p in range(out.shape[0]):
            for i in range(4):
                out[p, i] = res[first:first + each, i * DH:(i + 1) * DH]
            first += each


def parts_of(owners):
    half = owners // 2
    return [half, half // 2, half // 2] if half > 1 else [half, half]


def project(at, tokens, w, head_first, heads, after):
    zs, chunks, owners, piece, depth = tokens.shape
    each, counts = zs * chunks * piece, parts_of(owners)
    parts = 4 if depth % 512 == 0 else 1
    return pl.pallas_call(
        functools.partial(project_kernel, parts, owners, len(after)),
        grid_spec=pltpu.PrefetchScalarGridSpec(
            num_scalar_prefetch=1,
            grid=(heads,),
            in_specs=[
                pl.BlockSpec(
                    (zs, chunks, 1, piece, depth), lambda j, at, p=p: (0, 0, at[0] ^ p, 0, 0)
                )
                for p in range(owners)
            ]
            + [
                pl.BlockSpec((depth // parts, 4, DH), lambda j, at, k=k: (k, 0, head_first + j))
                for k in range(parts)
            ]
            + anywhere(after),
            out_specs=[
                pl.BlockSpec((n, 4, each, DH), lambda j, at: (0, 0, 0, j)) for n in counts
            ],
            scratch_shapes=[pltpu.VMEM((owners * each, depth), bf16)]
            + [pltpu.VMEM((depth // parts * 4, DH), f32) for _ in range(parts)],
        ),
        out_shape=[jax.ShapeDtypeStruct((n, 4, each, heads * DH), bf16) for n in counts],
        compiler_params=params(),
        cost_estimate=LIGHT,
        name="project",
    )(at, *[far(tokens)] * owners, *[far(w)] * parts, *after)


def tie_kernel(*refs):
    pass


def tie(x, after):
    if not after:
        return x
    return pl.pallas_call(
        tie_kernel,
        in_specs=anywhere([x, *after]),
        out_specs=pl.BlockSpec(memory_space=pl.ANY),
        out_shape=jax.ShapeDtypeStruct(x.shape, x.dtype),
        input_output_aliases={0: 0},
        compiler_params=params(),
        cost_estimate=LIGHT,
        name="tie",
    )(x, *after)


def fold_kernel(count, *refs):
    refs[-1][...] = sum(r[...].astype(f32) for r in refs[:count]).astype(bf16)


def fold(terms, after=()):
    half = terms[0].shape[0] // 2 if len(terms) == 2 else terms[-1].shape[0] // 2
    tail = terms[0].shape[1:]
    steps = 2 if tail[-1] % 256 == 0 else 1
    block = (half,) + tail[:-1] + (tail[-1] // steps,)
    middle = (0,) * (len(tail) - 1)
    firsts = [0 if t.shape[0] == half else 1 for t in terms]
    return pl.pallas_call(
        functools.partial(fold_kernel, len(terms)),
        grid=(steps,),
        in_specs=[pl.BlockSpec(block, lambda j, f=f: (f,) + middle + (j,)) for f in firsts]
        + anywhere(after),
        out_specs=pl.BlockSpec(block, lambda j: (0,) + middle + (j,)),
        out_shape=jax.ShapeDtypeStruct((half,) + tail, bf16),
        compiler_params=params(),
        cost_estimate=LIGHT,
        name="fold",
    )(*terms, *after)


def activate_kernel(counts, *refs):
    q_ref, rest_ref = refs[-2:]
    first, column = 0, 0
    for count in counts:
        terms = refs[first:first + count]
        span = terms[0].shape[-1]
        for i in range(4):
            part = silu(sum(t[0, i].astype(f32) for t in terms)).astype(bf16)
            if i == 0:
                q_ref[:, column:column + span] = part
            else:
                rest_ref[i - 1, :, column:column + span] = part
        first += count
        column += span


def activate(chunks, after):
    each, width = chunks[0][0].shape[2], sum(terms[0].shape[3] for terms in chunks)
    flat = [term for terms in chunks for term in terms]
    return pl.pallas_call(
        functools.partial(activate_kernel, [len(terms) for terms in chunks]),
        grid=(1,),
        in_specs=[pl.BlockSpec((1,) + t.shape[1:], lambda j: (0, 0, 0, 0)) for t in flat]
        + anywhere(after),
        out_specs=(
            pl.BlockSpec((each, width), lambda j: (0, 0)),
            pl.BlockSpec((3, each, width), lambda j: (0, 0, 0)),
        ),
        out_shape=(
            jax.ShapeDtypeStruct((each, width), bf16),
            jax.ShapeDtypeStruct((3, each, width), bf16),
        ),
        compiler_params=params(),
        cost_estimate=LIGHT,
        name="activate",
    )(*flat, *after)


def edge_kernel(base_ref, start_ref, end_ref, out_ref):
    row = lax.broadcasted_iota(jnp.int32, (DH, DH), 0)
    for b in range(start_ref.shape[0]):
        start, end = start_ref[b:b + 1, :], end_ref[b:b + 1, :]
        both = jnp.where(row == 0, start, end) - base_ref[0]
        out_ref[b * DH:(b + 1) * DH, :] = both.astype(f32).T[:, :2].astype(jnp.int32)


def edge_columns(base, start, end):
    count = start.shape[0]
    lines = pl.BlockSpec((count // DH, DH), lambda j, base: (0, 0))
    return pl.pallas_call(
        edge_kernel,
        grid_spec=pltpu.PrefetchScalarGridSpec(
            num_scalar_prefetch=1,
            grid=(1,),
            in_specs=[lines, lines],
            out_specs=pl.BlockSpec((count, 2), lambda j, base: (0, 0)),
        ),
        out_shape=jax.ShapeDtypeStruct((count, 2), jnp.int32),
        compiler_params=params(),
        cost_estimate=LIGHT,
        name="edges",
    )(base.reshape(1), start.reshape(-1, DH), end.reshape(-1, DH))


def attend_kernel(owners, sends, at_ref, *refs):
    queries, edges = refs[:owners], refs[owners:2 * owners]
    k_ref, v_ref = refs[2 * owners:2 * owners + 2]
    outs, mask_ref = refs[-1 - sends:-1], refs[-1]
    events = mask_ref.shape[1]
    each = outs[0].shape[1]

    @pl.when(pl.program_id(0) == 0)
    def _():
        zs, chunks, _, piece, _ = edges[0].shape
        at = lax.broadcasted_iota(jnp.int32, (piece, events), 1)
        first = 0
        for p in range(owners):
            for r in range(chunks):
                for z in range(zs):
                    edge = edges[p][z, r, 0]
                    seen = (at >= edge[:, :1]) & (at < edge[:, 1:])
                    mask_ref[first:first + piece, :] = jnp.where(seen, 1.0, 0.0).astype(bf16)
                    first += piece

    for h in range(k_ref.shape[1] // DH):
        at = slice(h * DH, (h + 1) * DH)
        query = jnp.concatenate([q[:, at] for q in queries])
        u = lax.dot_general(
            query, k_ref[:, at], (((1,), (1,)), ((), ())), preferred_element_type=f32
        ) * (0.5 * DH ** (-0.5))
        weights = (u + u * jnp.tanh(u)).astype(bf16) * mask_ref[...]
        term = jnp.dot(weights, v_ref[:, at], preferred_element_type=f32).astype(bf16)
        first = 0
        for out in outs:
            for p in range(out.shape[0]):
                out[p, :, at] = term[first:first + each]
                first += each


def edge_spec(edges, p):
    zs, chunks, _, piece, ends = edges.shape
    return pl.BlockSpec((zs, chunks, 1, piece, ends), lambda j, at: (0, 0, at[0] ^ p, 0, 0))


def attend(at, queries, k_cache, v_cache, edges, head_first, after):
    owners, (each, width) = len(queries), queries[0].shape
    rows, events, counts = owners * each, k_cache.shape[0], parts_of(owners)
    first = head_first * DH
    span = max(h for h in range(DH, 4 * DH, DH) if width % h == 0 and first % h == 0)
    cache = pl.BlockSpec((events, span), lambda j, at: (0, first // span + j))
    return pl.pallas_call(
        functools.partial(attend_kernel, owners, len(counts)),
        grid_spec=pltpu.PrefetchScalarGridSpec(
            num_scalar_prefetch=1,
            grid=(width // span,),
            in_specs=[pl.BlockSpec((each, span), lambda j, at: (0, j))] * owners
            + [edge_spec(edges, p) for p in range(owners)]
            + [cache, cache]
            + anywhere(after),
            out_specs=[pl.BlockSpec((n, each, span), lambda j, at: (0, 0, j)) for n in counts],
            scratch_shapes=[pltpu.VMEM((rows, events), bf16)],
        ),
        out_shape=[jax.ShapeDtypeStruct((n, each, width), bf16) for n in counts],
        compiler_params=params(),
        cost_estimate=LIGHT,
        name="attend",
    )(at, *queries, *[edges] * owners, far(k_cache), far(v_cache), *after)


def merge(means, squares, widths):
    width = sum(widths)
    mean = sum(m * (w / width) for m, w in zip(means, widths))
    square = sum(squares) + sum(w * (m - mean) * (m - mean) for m, w in zip(means, widths))
    return mean, square


def stat_columns(stats):
    stats = [s[...] for s in stats]
    stats = [s if s.shape[0] > 8 else jnp.concatenate([s] * (DH // 8)).T for s in stats]
    return [s[:, :1] for s in stats], [s[:, 4:5] for s in stats]


def finish_kernel(terms, widths, at_ref, edge_ref, q_ref, rest_ref, *refs):
    sums, others = refs[:terms], refs[terms:terms + len(widths)]
    att_ref, stat_ref = refs[-2:]
    rows, width = att_ref.shape
    zs, chunks = edge_ref.shape[:2]
    edge = jnp.concatenate(
        [edge_ref[z, r, 0] for r in range(chunks) for z in range(zs)]
    ).astype(f32)
    root = lax.rsqrt(edge[:, 1:] - edge[:, :1])
    total = jnp.zeros((rows, 1), f32)
    for first in range(0, width, DH):
        at = slice(first, first + DH)
        summed = sum(s[0, :, at].astype(f32) for s in sums)
        product = q_ref[:, at].astype(f32) * rest_ref[0, :, at].astype(f32)
        weight = silu(jnp.sum(product, axis=1, keepdims=True) * DH ** (-0.5))
        value = summed * root + weight * rest_ref[1, :, at].astype(f32)
        att_ref[:, at] = value
        total += jnp.sum(value, axis=1, keepdims=True)
    mean = total / width
    spread = jnp.zeros((rows, DH), f32)
    for first in range(0, width, DH):
        away = att_ref[:, first:first + DH] - mean
        spread += away * away
    square = jnp.sum(spread, axis=1, keepdims=True)
    if others:
        means, squares = stat_columns(others)
        mean, square = merge([mean] + means, [square] + squares, [width] + widths)
    lane = lax.broadcasted_iota(jnp.int32, (rows, DH), 1)
    stat = jnp.where(lane < 4, mean, square)
    stat_ref[...] = stat if stat_ref.shape == stat.shape else stat.T[:8]


def finish(at, edges, query, rest, sums, others, widths, after):
    rows, width = query.shape
    stat = (8, rows) if others and rows == DH else (rows, DH)
    return pl.pallas_call(
        functools.partial(finish_kernel, len(sums), widths),
        grid_spec=pltpu.PrefetchScalarGridSpec(
            num_scalar_prefetch=1,
            grid=(1,),
            in_specs=[
                edge_spec(edges, 0),
                pl.BlockSpec((rows, width), lambda j, at: (0, 0)),
                pl.BlockSpec((2, rows, width), lambda j, at: (0, 0, 0)),
            ]
            + [pl.BlockSpec((1, rows, width), lambda j, at: (0, 0, 0))] * len(sums)
            + [pl.BlockSpec((rows, DH), lambda j, at: (0, 0))] * len(others)
            + anywhere(after),
            out_specs=(
                pl.BlockSpec((rows, width), lambda j, at: (0, 0)),
                pl.BlockSpec(stat, lambda j, at: (0, 0)),
            ),
        ),
        out_shape=(
            jax.ShapeDtypeStruct((rows, width), f32),
            jax.ShapeDtypeStruct(stat, f32),
        ),
        compiler_params=params(),
        cost_estimate=LIGHT,
        name="finish",
    )(at, edges, query, rest, *sums, *others, *after)


def merge_kernel(width, *refs):
    (m, n), (s, t) = (
        [r[:4] if r.shape[0] == 8 else r[:, :4] for r in refs[:2]],
        [r[4:] if r.shape[0] == 8 else r[:, 4:8] for r in refs[:2]],
    )
    mean, square = merge([m, n], [s, t], [width] * 2)
    if refs[2].shape[0] == 8:
        refs[2][:4], refs[2][4:] = mean, square
    else:
        lane = lax.broadcasted_iota(jnp.int32, refs[2].shape, 1)
        refs[2][...] = jnp.where(lane < 4, mean[:, :1], square[:, :1])


def merge_stats(stats, width):
    return pl.pallas_call(
        functools.partial(merge_kernel, width),
        out_shape=jax.ShapeDtypeStruct(stats[0].shape, f32),
        compiler_params=params(),
        cost_estimate=LIGHT,
        name="merge",
    )(*stats)


def gate_kernel(count, parts, width, *refs):
    stats, atts, rests, outs = (
        refs[:count], refs[count:count + parts],
        refs[count + parts:count + 2 * parts], refs[count + 2 * parts:],
    )
    means, squares = stat_columns(stats)
    mean, square = merge(means, squares, [width] * count)
    scale = lax.rsqrt(square / (width * count) + EPSILON)
    rows, column = outs[0].shape[0], 0
    for att, rest in zip(atts, rests):
        span = att.shape[1]
        normed = (att[...] - mean) * scale
        gated = (normed * rest[0].astype(f32)).astype(bf16)
        for r, out in enumerate(outs):
            out[:, column:column + span] = gated[r * rows:(r + 1) * rows]
        column += span
    for out in outs:
        if out.shape[1] > column:
            out[:, column:] = jnp.zeros((rows, out.shape[1] - column), bf16)


def gate_rows(stats, stat_width, atts, rests, chunks):
    rows, width = atts[0].shape[0], sum(a.shape[1] for a in atts)
    widths = [width + DH * min(r, 1) for r in range(chunks)]
    return pl.pallas_call(
        functools.partial(gate_kernel, len(stats), len(atts), stat_width),
        grid=(1,),
        in_specs=[pl.BlockSpec(s.shape, lambda j: (0, 0)) for s in stats]
        + [pl.BlockSpec((rows, a.shape[1]), lambda j: (0, 0)) for a in atts]
        + [pl.BlockSpec((1, rows, r.shape[2]), lambda j: (2, 0, 0)) for r in rests],
        out_specs=[pl.BlockSpec((rows // chunks, w), lambda j: (0, 0)) for w in widths],
        out_shape=[jax.ShapeDtypeStruct((rows // chunks, w), bf16) for w in widths],
        compiler_params=params(),
        cost_estimate=LIGHT,
        name="gate",
    )(*stats, *atts, *rests)


def output_kernel(owners, slots, after, index_ref, *refs):
    rows, w_ref, outs, lhs_ref = refs[:owners], refs[owners], refs[owners + 1 + after:-1], refs[-1]
    piece = rows[0].shape[1]

    @pl.when(pl.program_id(0) == 0)
    def _():
        first = 0
        for slot in slots:
            for p in range(owners):
                lhs_ref[first:first + piece, :] = rows[p][index_ref[0] ^ slot]
                first += piece

    sums = jnp.dot(lhs_ref[...], w_ref[...], preferred_element_type=f32).astype(bf16)
    first = 0
    for out in outs:
        for k in range(out.shape[0]):
            for p in range(owners):
                out[k, p] = sums[first:first + piece]
                first += piece


def output(index, slots, counts, blocks, w_out, column, columns, after):
    owners, each, zs = len(blocks), blocks[0].shape[0], sum(counts)
    width, piece = w_out.shape[0], each // zs
    span = max(c for c in (512, 256, columns) if columns % c == 0 and column % c == 0)
    row_spec = pl.BlockSpec((zs, piece, width), lambda j, at: (0, 0, 0))
    return pl.pallas_call(
        functools.partial(output_kernel, owners, slots, len(after)),
        grid_spec=pltpu.PrefetchScalarGridSpec(
            num_scalar_prefetch=1,
            grid=(columns // span,),
            in_specs=[row_spec] * owners
            + [pl.BlockSpec((width, span), lambda j, at: (0, column // span + j))]
            + anywhere(after),
            out_specs=[
                pl.BlockSpec((n, owners, piece, span), lambda j, at: (0, 0, 0, j)) for n in counts
            ],
            scratch_shapes=[pltpu.VMEM((owners * each, width), bf16)],
        ),
        out_shape=[jax.ShapeDtypeStruct((n, owners, piece, columns), bf16) for n in counts],
        compiler_params=params(),
        cost_estimate=LIGHT,
        name="output",
    )(
        index.reshape(1).astype(jnp.int32),
        *[b.reshape(zs, piece, b.shape[1]) for b in blocks], far(w_out), *after,
    )


def close_kernel(counts, at_ref, t_ref, *refs):
    out_ref, mark_ref = refs[-2:]
    mark_ref[...] = jnp.zeros_like(mark_ref)
    first, column = 0, 0
    for count in counts:
        terms = refs[first:first + count]
        span = terms[0].shape[-1]
        at = slice(column, column + span)
        for p in range(out_ref.shape[0]):
            total = t_ref[p, :, at].astype(f32)
            for term in terms:
                total = total + term[0, p ^ at_ref[0]].astype(f32)
            out_ref[p, :, at] = total.astype(bf16)
        first += count
        column += span


def close(place, index, tokens, chunks, r, g, groups, out, after):
    _, owners, piece, _ = groups[0][0].shape
    span, width = sum(terms[0].shape[-1] for terms in groups), tokens.shape[1]
    at = jnp.stack([place, index * chunks + r]).astype(jnp.int32)
    flat = [term for terms in groups for term in terms]
    into = [] if out is None else [out]
    return pl.pallas_call(
        functools.partial(close_kernel, [len(terms) for terms in groups]),
        grid_spec=pltpu.PrefetchScalarGridSpec(
            num_scalar_prefetch=1,
            grid=(1,),
            in_specs=[pl.BlockSpec((owners, piece, span), lambda j, at: (at[1], 0, g))]
            + [pl.BlockSpec((1,) + t.shape[1:], lambda j, at: (0, 0, 0, 0)) for t in flat]
            + anywhere(into) + anywhere(after),
            out_specs=(
                pl.BlockSpec((owners, piece, span), lambda j, at: (r, 0, g)),
                pl.BlockSpec((8, DH), lambda j, at: (0, 0)),
            ),
        ),
        out_shape=(
            jax.ShapeDtypeStruct((chunks * owners, piece, width), bf16),
            jax.ShapeDtypeStruct((8, DH), f32),
        ),
        input_output_aliases={} if out is None else {2 + len(flat): 0},
        compiler_params=params(),
        cost_estimate=LIGHT,
        name="close",
    )(at, far(tokens.reshape(-1, piece, width)), *flat, *into, *after)


def bits_of(axis):
    count = lax.axis_size(axis)
    assert count & (count - 1) == 0
    return count.bit_length() - 1


def reverse(index, bits):
    return sum((((index >> b) & 1) << (bits - 1 - b) for b in range(bits)), 0 * index)


def swap(x, axis, bit):
    return lax.ppermute(
        x, axis, [(i, i ^ (1 << bit)) for i in range(lax.axis_size(axis))]
    )


def scatter(keep, gots, axis, after=()):
    terms, sent = [keep, gots[0]], gots[-1]
    for b in range(1, bits_of(axis)):
        sent = fold([keep, gots[-1]] if b == 1 else terms, after)
        terms.append(swap(sent, axis, b))
    return terms, sent


def gather(x, axis, after=()):
    blocks = [x]
    for b in reversed(range(bits_of(axis))):
        blocks = blocks + [swap(block, axis, b) for block in blocks]
        if len(blocks) == 2:
            blocks[1] = tie(blocks[1], after)
    return blocks


def all_stats(stat, width, axis):
    count = lax.axis_size(axis)
    if count > 8 or count & (count - 1):
        every = lax.all_gather(stat, axis)
        return [every[i] for i in range(count)], width
    stats = [stat]
    for b in range(bits_of(axis)):
        if b:
            width, stats = 2 * width, [merge_stats(stats, width)]
        stats.append(swap(stats[0], axis, b))
    return stats, width


def head_chunks(heads):
    if heads % 8:
        return [1] * heads
    unit = heads // 8
    return [unit, 2 * unit, 2 * unit, 2 * unit, unit]


GROUPS = [[0, 1], [2], [3], [4]]
ORDER = [
    "P0", "P1", "F0", "P2", "F1", "P3", "F2", "A0", "F3", "P4", "A1", "F4", "T0", "G0", "A2",
    "T1", "A3", "G1", "T2", "E0", "G2", "T3", "G3", "E1", "E2", "E3",
]


def local(tokens, w_qkvu, k_cache, v_cache, w_out, vis_start, vis_end):
    cand, depth = tokens.shape
    owners, zs = lax.axis_size("hist"), lax.axis_size("head")
    index = lax.axis_index("head")
    place = reverse(lax.axis_index("hist"), bits_of("hist"))
    width = w_qkvu.shape[2]
    events = k_cache.shape[0]
    chunks = 2 if cand % (2 * owners * zs * 16) == 0 else 1
    piece = cand // (zs * chunks * owners)

    def arrange(x):
        x = x.reshape((zs, chunks, owners, piece) + x.shape[1:])
        if piece % 16 == 0:
            return x
        blocks = [lax.dynamic_index_in_dim(x, p ^ place, 2, False) for p in range(owners)]
        x = jnp.stack(blocks).swapaxes(1, 2)
        return x.reshape((1, 1, owners, zs * chunks * piece) + x.shape[4:])

    at = (place if piece % 16 == 0 else jnp.int32(0)).reshape(1)
    ordered = arrange(tokens)
    first_event = lax.axis_index("hist") * events
    edges = arrange(edge_columns(first_event, vis_start, vis_end))

    sizes = head_chunks(width // DH)
    firsts = [sum(sizes[:c]) for c in range(len(sizes))]
    groups, order = GROUPS, ORDER
    if len(sizes) != 5:
        groups = [[c] for c in range(len(sizes))]
        order = [step + str(c) for step in "PFATGE" for c in range(len(sizes))]
    last = len(groups) - 1
    heads = [sum(sizes[c] for c in group) for group in groups]
    chain, keeps, firsts_got, terms, sums = [], {}, {}, {}, {}
    halves, queries, parts, atts, stats = {}, {}, {}, {}, {}
    for step, c in [(name[0], int(name[1:])) for name in order]:
        after = chain[-1:]
        if step == "P":
            keep, *sends = project(at, ordered, w_qkvu, firsts[c], sizes[c], after)
            before = firsts_got[c - 1] if c >= 1 else []
            before = before + [terms[0][-1]] if c == 2 and 0 in terms else before
            firsts_got[c] = [swap(tie(send, before), "hist", 0) for send in reversed(sends)][::-1]
            keeps[c] = keep
            chain.append(keep)
        elif step == "F":
            terms[c], sent = scatter(keeps[c], firsts_got[c], "hist", after)
            chain.append(sent)
        elif step == "A":
            parts[c] = activate([terms[k] for k in groups[c]], after)
            queries[c] = gather(parts[c][0], "hist")
            chain.append(parts[c][0])
        elif step == "T":
            first = firsts[groups[c][0]]
            keep, *sends = attend(at, queries[c], k_cache, v_cache, edges, first, after)
            halves[c] = keep, [swap(send, "hist", 0) for send in sends]
            chain.append(keep)
        elif step == "G":
            sums[c], sent = scatter(*halves[c], "hist", after)
            chain.append(sent)
        else:
            others = [stats[k] for k in range(last)] if c == last else []
            widths = [size * DH for size in heads[:last]] if c == last else []
            atts[c], stats[c] = finish(at, edges, *parts[c], sums[c], others, widths, after)
            chain.append(atts[c])

    atts = [atts[c] for c in range(last + 1)]
    rests = [parts[c][1] for c in range(last + 1)]
    every, stat_width = all_stats(stats[last], width, "head")
    gated = gate_rows(every, stat_width, atts, rests, chunks)
    columns = w_out.shape[1]
    straight = piece % 16 == 0 and zs & (zs - 1) == 0
    out = None
    if not straight:
        for r, rows in enumerate(gated):
            whole = jnp.concatenate(gather(rows, "hist"))[:, :width]
            whole = jnp.dot(whole, w_out, preferred_element_type=f32).astype(bf16)
            whole = whole.reshape(owners, zs, piece, -1).swapaxes(0, 1)
            whole = lax.psum_scatter(whole, "head", scatter_dimension=0, tiled=True)
            out, _ = close(place, index, tokens, chunks, r, 0, [[whole]], out, [])
        return out.reshape(cand // zs, -1)
    slots = [reverse(k, bits_of("head")) for k in range(zs)]
    groups = 2 if columns % 1024 == 0 else 1
    span = columns // groups
    counts = [zs // 2] * 2 if zs > 1 else [1]
    plan = [(r, g) for r in range(chunks) for g in range(groups)]
    chain, first_out, blocks, made, folded = [], [], {}, [], []

    def fold_next():
        own, arrived = made[len(folded)]
        terms, sent = scatter(own, arrived, "head", chain) if arrived else ([own], own)
        folded.append(terms)
        return [sent]

    for n, (r, g) in enumerate(plan):
        if r not in blocks:
            blocks[r] = gather(gated[r], "hist", first_out)
        own, *others = output(index, slots, counts, blocks[r], w_out, g * span, span, chain)
        before = made[n - 2][1] if n > 1 else []
        before = before + [folded[0][-1]] if folded else before
        made.append((own, [swap(tie(x, before), "head", 0) for x in others]))
        chain, first_out = [own], first_out or [own]
        if n == 2:
            chain = fold_next()
    closed = 0
    while closed < len(plan):
        if len(folded) < len(plan):
            chain = fold_next()
        if len(folded) > closed + 2 or len(folded) == len(plan):
            r, g = plan[closed]
            some = 1 if r < chunks - 1 else groups
            out, mark = close(
                place, index, tokens, chunks, r, g, folded[closed:closed + some], out, chain
            )
            chain, closed = [mark], closed + some
    return out.reshape(cand // zs, -1)


def solution(mesh):
    in_specs = (
        P("groups", "hist"),
        P("hist", None, "head"),
        P(("groups", "hist"), "head"),
        P(("groups", "hist"), "head"),
        P("head", "hist"),
        P("groups"),
        P("groups"),
    )
    out_specs = P(("groups", "head"), "hist")
    return jax.shard_map(local, mesh=mesh, in_specs=in_specs, out_specs=out_specs, check_vma=False)
```

```python
import functools

import jax
import jax.numpy as jnp
from jax import lax
from jax.experimental import pallas as pl
from jax.experimental.pallas import tpu as pltpu
from jax.sharding import PartitionSpec as P

DH = 128
EPSILON = 1e-05
VMEM_LIMIT = 28 * 1024 * 1024

bf16 = jnp.bfloat16
f32 = jnp.float32


def silu(v):
    u = 0.5 * v
    return u + u * jnp.tanh(u)


def params():
    return pltpu.CompilerParams(vmem_limit_bytes=VMEM_LIMIT)


LIGHT = pl.CostEstimate(flops=1000, bytes_accessed=1000, transcendentals=0)


def far(x):
    return pltpu.with_memory_space_constraint(x, pltpu.HBM)


def anywhere(arrays):
    return [pl.BlockSpec(memory_space=pl.ANY)] * len(arrays)


def project_kernel(parts, owners, after, at_ref, *refs):
    rows, weights = refs[:owners], refs[owners:owners + parts]
    outs, lhs_ref = refs[owners + parts + after:-parts - 1], refs[-parts - 1]
    wides = refs[-parts:]
    zs, chunks, _, piece, _ = rows[0].shape
    depth = weights[0].shape[0]

    @pl.when(pl.program_id(0) == 0)
    def _():
        first = 0
        for p in range(owners):
            for r in range(chunks):
                for z in range(zs):
                    lhs_ref[first:first + piece, :] = rows[p][z, r, 0]
                    first += piece

    res = None
    for k, wide in enumerate(wides):
        wide[...] = weights[k].reshape(depth * 4, DH)[...].astype(f32)
        rhs = jnp.concatenate(
            [wide[pl.ds(i, depth, stride=4), :].astype(bf16) for i in range(4)], axis=1
        )
        term = jnp.dot(lhs_ref[:, k * depth:(k + 1) * depth], rhs, preferred_element_type=f32)
        res = term if res is None else res + term
    res = res.astype(bf16)
    each, first = outs[0].shape[2], 0
    for out in outs:
        for p in range(out.shape[0]):
            for i in range(4):
                out[p, i] = res[first:first + each, i * DH:(i + 1) * DH]
            first += each


def parts_of(owners):
    half = owners // 2
    return [half, half // 2, half // 2] if half > 1 else [half, half]


def project(at, tokens, w, head_first, heads, after):
    zs, chunks, owners, piece, depth = tokens.shape
    each, counts = zs * chunks * piece, parts_of(owners)
    parts = 4 if depth % 512 == 0 else 1
    return pl.pallas_call(
        functools.partial(project_kernel, parts, owners, len(after)),
        grid_spec=pltpu.PrefetchScalarGridSpec(
            num_scalar_prefetch=1,
            grid=(heads,),
            in_specs=[
                pl.BlockSpec(
                    (zs, chunks, 1, piece, depth), lambda j, at, p=p: (0, 0, at[0] ^ p, 0, 0)
                )
                for p in range(owners)
            ]
            + [
                pl.BlockSpec((depth // parts, 4, DH), lambda j, at, k=k: (k, 0, head_first + j))
                for k in range(parts)
            ]
            + anywhere(after),
            out_specs=[
                pl.BlockSpec((n, 4, each, DH), lambda j, at: (0, 0, 0, j)) for n in counts
            ],
            scratch_shapes=[pltpu.VMEM((owners * each, depth), bf16)]
            + [pltpu.VMEM((depth // parts * 4, DH), f32) for _ in range(parts)],
        ),
        out_shape=[jax.ShapeDtypeStruct((n, 4, each, heads * DH), bf16) for n in counts],
        compiler_params=params(),
        cost_estimate=LIGHT,
        name="project",
    )(at, *[far(tokens)] * owners, *[far(w)] * parts, *after)


def tie_kernel(*refs):
    pass


def tie(x, after):
    if not after:
        return x
    return pl.pallas_call(
        tie_kernel,
        in_specs=anywhere([x, *after]),
        out_specs=pl.BlockSpec(memory_space=pl.ANY),
        out_shape=jax.ShapeDtypeStruct(x.shape, x.dtype),
        input_output_aliases={0: 0},
        compiler_params=params(),
        cost_estimate=LIGHT,
        name="tie",
    )(x, *after)


def fold_kernel(count, *refs):
    refs[-1][...] = sum(r[...].astype(f32) for r in refs[:count]).astype(bf16)


def fold(terms, after=()):
    half = terms[0].shape[0] // 2 if len(terms) == 2 else terms[-1].shape[0] // 2
    tail = terms[0].shape[1:]
    steps = 2 if tail[-1] % 256 == 0 else 1
    block = (half,) + tail[:-1] + (tail[-1] // steps,)
    middle = (0,) * (len(tail) - 1)
    firsts = [0 if t.shape[0] == half else 1 for t in terms]
    return pl.pallas_call(
        functools.partial(fold_kernel, len(terms)),
        grid=(steps,),
        in_specs=[pl.BlockSpec(block, lambda j, f=f: (f,) + middle + (j,)) for f in firsts]
        + anywhere(after),
        out_specs=pl.BlockSpec(block, lambda j: (0,) + middle + (j,)),
        out_shape=jax.ShapeDtypeStruct((half,) + tail, bf16),
        compiler_params=params(),
        cost_estimate=LIGHT,
        name="fold",
    )(*terms, *after)


def activate_kernel(counts, *refs):
    q_ref, rest_ref = refs[-2:]
    first, column = 0, 0
    for count in counts:
        terms = refs[first:first + count]
        span = terms[0].shape[-1]
        for i in range(4):
            part = silu(sum(t[0, i].astype(f32) for t in terms)).astype(bf16)
            if i == 0:
                q_ref[:, column:column + span] = part
            else:
                rest_ref[i - 1, :, column:column + span] = part
        first += count
        column += span


def activate(chunks, after):
    each, width = chunks[0][0].shape[2], sum(terms[0].shape[3] for terms in chunks)
    flat = [term for terms in chunks for term in terms]
    return pl.pallas_call(
        functools.partial(activate_kernel, [len(terms) for terms in chunks]),
        grid=(1,),
        in_specs=[pl.BlockSpec((1,) + t.shape[1:], lambda j: (0, 0, 0, 0)) for t in flat]
        + anywhere(after),
        out_specs=(
            pl.BlockSpec((each, width), lambda j: (0, 0)),
            pl.BlockSpec((3, each, width), lambda j: (0, 0, 0)),
        ),
        out_shape=(
            jax.ShapeDtypeStruct((each, width), bf16),
            jax.ShapeDtypeStruct((3, each, width), bf16),
        ),
        compiler_params=params(),
        cost_estimate=LIGHT,
        name="activate",
    )(*flat, *after)


def edge_kernel(base_ref, start_ref, end_ref, out_ref):
    row = lax.broadcasted_iota(jnp.int32, (DH, DH), 0)
    for b in range(start_ref.shape[0]):
        start, end = start_ref[b:b + 1, :], end_ref[b:b + 1, :]
        both = jnp.where(row == 0, start, end) - base_ref[0]
        out_ref[b * DH:(b + 1) * DH, :] = both.astype(f32).T[:, :2].astype(jnp.int32)


def edge_columns(base, start, end):
    count = start.shape[0]
    lines = pl.BlockSpec((count // DH, DH), lambda j, base: (0, 0))
    return pl.pallas_call(
        edge_kernel,
        grid_spec=pltpu.PrefetchScalarGridSpec(
            num_scalar_prefetch=1,
            grid=(1,),
            in_specs=[lines, lines],
            out_specs=pl.BlockSpec((count, 2), lambda j, base: (0, 0)),
        ),
        out_shape=jax.ShapeDtypeStruct((count, 2), jnp.int32),
        compiler_params=params(),
        cost_estimate=LIGHT,
        name="edges",
    )(base.reshape(1), start.reshape(-1, DH), end.reshape(-1, DH))


def attend_kernel(owners, sends, at_ref, *refs):
    queries, edges = refs[:owners], refs[owners:2 * owners]
    k_ref, v_ref = refs[2 * owners:2 * owners + 2]
    outs, mask_ref = refs[-1 - sends:-1], refs[-1]
    events = mask_ref.shape[1]
    each = outs[0].shape[1]

    @pl.when(pl.program_id(0) == 0)
    def _():
        zs, chunks, _, piece, _ = edges[0].shape
        at = lax.broadcasted_iota(jnp.int32, (piece, events), 1)
        first = 0
        for p in range(owners):
            for r in range(chunks):
                for z in range(zs):
                    edge = edges[p][z, r, 0]
                    seen = (at >= edge[:, :1]) & (at < edge[:, 1:])
                    mask_ref[first:first + piece, :] = jnp.where(seen, 1.0, 0.0).astype(bf16)
                    first += piece

    for h in range(k_ref.shape[1] // DH):
        at = slice(h * DH, (h + 1) * DH)
        query = jnp.concatenate([q[:, at] for q in queries])
        u = lax.dot_general(
            query, k_ref[:, at], (((1,), (1,)), ((), ())), preferred_element_type=f32
        ) * (0.5 * DH ** (-0.5))
        weights = (u + u * jnp.tanh(u)).astype(bf16) * mask_ref[...]
        term = jnp.dot(weights, v_ref[:, at], preferred_element_type=f32).astype(bf16)
        first = 0
        for out in outs:
            for p in range(out.shape[0]):
                out[p, :, at] = term[first:first + each]
                first += each


def edge_spec(edges, p):
    zs, chunks, _, piece, ends = edges.shape
    return pl.BlockSpec((zs, chunks, 1, piece, ends), lambda j, at: (0, 0, at[0] ^ p, 0, 0))


def attend(at, queries, k_cache, v_cache, edges, head_first, after):
    owners, (each, width) = len(queries), queries[0].shape
    rows, events, counts = owners * each, k_cache.shape[0], parts_of(owners)
    first = head_first * DH
    span = max(h for h in range(DH, 4 * DH, DH) if width % h == 0 and first % h == 0)
    cache = pl.BlockSpec((events, span), lambda j, at: (0, first // span + j))
    return pl.pallas_call(
        functools.partial(attend_kernel, owners, len(counts)),
        grid_spec=pltpu.PrefetchScalarGridSpec(
            num_scalar_prefetch=1,
            grid=(width // span,),
            in_specs=[pl.BlockSpec((each, span), lambda j, at: (0, j))] * owners
            + [edge_spec(edges, p) for p in range(owners)]
            + [cache, cache]
            + anywhere(after),
            out_specs=[pl.BlockSpec((n, each, span), lambda j, at: (0, 0, j)) for n in counts],
            scratch_shapes=[pltpu.VMEM((rows, events), bf16)],
        ),
        out_shape=[jax.ShapeDtypeStruct((n, each, width), bf16) for n in counts],
        compiler_params=params(),
        cost_estimate=LIGHT,
        name="attend",
    )(at, *queries, *[edges] * owners, far(k_cache), far(v_cache), *after)


def merge(means, squares, widths):
    width = sum(widths)
    mean = sum(m * (w / width) for m, w in zip(means, widths))
    square = sum(squares) + sum(w * (m - mean) * (m - mean) for m, w in zip(means, widths))
    return mean, square


def stat_columns(stats):
    stats = [s[...] for s in stats]
    stats = [s if s.shape[0] > 8 else jnp.concatenate([s] * (DH // 8)).T for s in stats]
    return [s[:, :1] for s in stats], [s[:, 4:5] for s in stats]


def finish_kernel(terms, widths, at_ref, edge_ref, q_ref, rest_ref, *refs):
    sums, others = refs[:terms], refs[terms:terms + len(widths)]
    att_ref, stat_ref = refs[-2:]
    rows, width = att_ref.shape
    zs, chunks = edge_ref.shape[:2]
    edge = jnp.concatenate(
        [edge_ref[z, r, 0] for r in range(chunks) for z in range(zs)]
    ).astype(f32)
    root = lax.rsqrt(edge[:, 1:] - edge[:, :1])
    total = jnp.zeros((rows, 1), f32)
    for first in range(0, width, DH):
        at = slice(first, first + DH)
        summed = sum(s[0, :, at].astype(f32) for s in sums)
        product = q_ref[:, at].astype(f32) * rest_ref[0, :, at].astype(f32)
        weight = silu(jnp.sum(product, axis=1, keepdims=True) * DH ** (-0.5))
        value = summed * root + weight * rest_ref[1, :, at].astype(f32)
        att_ref[:, at] = value
        total += jnp.sum(value, axis=1, keepdims=True)
    mean = total / width
    spread = jnp.zeros((rows, DH), f32)
    for first in range(0, width, DH):
        away = att_ref[:, first:first + DH] - mean
        spread += away * away
    square = jnp.sum(spread, axis=1, keepdims=True)
    if others:
        means, squares = stat_columns(others)
        mean, square = merge([mean] + means, [square] + squares, [width] + widths)
    lane = lax.broadcasted_iota(jnp.int32, (rows, DH), 1)
    stat = jnp.where(lane < 4, mean, square)
    stat_ref[...] = stat if stat_ref.shape == stat.shape else stat.T[:8]


def finish(at, edges, query, rest, sums, others, widths, after):
    rows, width = query.shape
    stat = (8, rows) if others and rows == DH else (rows, DH)
    return pl.pallas_call(
        functools.partial(finish_kernel, len(sums), widths),
        grid_spec=pltpu.PrefetchScalarGridSpec(
            num_scalar_prefetch=1,
            grid=(1,),
            in_specs=[
                edge_spec(edges, 0),
                pl.BlockSpec((rows, width), lambda j, at: (0, 0)),
                pl.BlockSpec((2, rows, width), lambda j, at: (0, 0, 0)),
            ]
            + [pl.BlockSpec((1, rows, width), lambda j, at: (0, 0, 0))] * len(sums)
            + [pl.BlockSpec((rows, DH), lambda j, at: (0, 0))] * len(others)
            + anywhere(after),
            out_specs=(
                pl.BlockSpec((rows, width), lambda j, at: (0, 0)),
                pl.BlockSpec(stat, lambda j, at: (0, 0)),
            ),
        ),
        out_shape=(
            jax.ShapeDtypeStruct((rows, width), f32),
            jax.ShapeDtypeStruct(stat, f32),
        ),
        compiler_params=params(),
        cost_estimate=LIGHT,
        name="finish",
    )(at, edges, query, rest, *sums, *others, *after)


def merge_kernel(width, *refs):
    (m, n), (s, t) = (
        [r[:4] if r.shape[0] == 8 else r[:, :4] for r in refs[:2]],
        [r[4:] if r.shape[0] == 8 else r[:, 4:8] for r in refs[:2]],
    )
    mean, square = merge([m, n], [s, t], [width] * 2)
    if refs[2].shape[0] == 8:
        refs[2][:4], refs[2][4:] = mean, square
    else:
        lane = lax.broadcasted_iota(jnp.int32, refs[2].shape, 1)
        refs[2][...] = jnp.where(lane < 4, mean[:, :1], square[:, :1])


def merge_stats(stats, width):
    return pl.pallas_call(
        functools.partial(merge_kernel, width),
        out_shape=jax.ShapeDtypeStruct(stats[0].shape, f32),
        compiler_params=params(),
        cost_estimate=LIGHT,
        name="merge",
    )(*stats)


def gate_kernel(count, parts, width, *refs):
    stats, atts, rests, outs = (
        refs[:count], refs[count:count + parts],
        refs[count + parts:count + 2 * parts], refs[count + 2 * parts:],
    )
    means, squares = stat_columns(stats)
    mean, square = merge(means, squares, [width] * count)
    scale = lax.rsqrt(square / (width * count) + EPSILON)
    rows, column = outs[0].shape[0], 0
    for att, rest in zip(atts, rests):
        span = att.shape[1]
        normed = (att[...] - mean) * scale
        gated = (normed * rest[0].astype(f32)).astype(bf16)
        for r, out in enumerate(outs):
            out[:, column:column + span] = gated[r * rows:(r + 1) * rows]
        column += span
    for out in outs:
        if out.shape[1] > column:
            out[:, column:] = jnp.zeros((rows, out.shape[1] - column), bf16)


def gate_rows(stats, stat_width, atts, rests, chunks):
    rows, width = atts[0].shape[0], sum(a.shape[1] for a in atts)
    widths = [width + DH * min(r, 1) for r in range(chunks)]
    return pl.pallas_call(
        functools.partial(gate_kernel, len(stats), len(atts), stat_width),
        grid=(1,),
        in_specs=[pl.BlockSpec(s.shape, lambda j: (0, 0)) for s in stats]
        + [pl.BlockSpec((rows, a.shape[1]), lambda j: (0, 0)) for a in atts]
        + [pl.BlockSpec((1, rows, r.shape[2]), lambda j: (2, 0, 0)) for r in rests],
        out_specs=[pl.BlockSpec((rows // chunks, w), lambda j: (0, 0)) for w in widths],
        out_shape=[jax.ShapeDtypeStruct((rows // chunks, w), bf16) for w in widths],
        compiler_params=params(),
        cost_estimate=LIGHT,
        name="gate",
    )(*stats, *atts, *rests)


def output_kernel(owners, slots, after, index_ref, *refs):
    rows, w_ref, outs, lhs_ref = refs[:owners], refs[owners], refs[owners + 1 + after:-1], refs[-1]
    piece = rows[0].shape[1]

    @pl.when(pl.program_id(0) == 0)
    def _():
        first = 0
        for slot in slots:
            for p in range(owners):
                lhs_ref[first:first + piece, :] = rows[p][index_ref[0] ^ slot]
                first += piece

    sums = jnp.dot(lhs_ref[...], w_ref[...], preferred_element_type=f32).astype(bf16)
    first = 0
    for out in outs:
        for k in range(out.shape[0]):
            for p in range(owners):
                out[k, p] = sums[first:first + piece]
                first += piece


def output(index, slots, counts, blocks, w_out, column, columns, after):
    owners, each, zs = len(blocks), blocks[0].shape[0], sum(counts)
    width, piece = w_out.shape[0], each // zs
    span = max(c for c in (512, 256, columns) if columns % c == 0 and column % c == 0)
    row_spec = pl.BlockSpec((zs, piece, width), lambda j, at: (0, 0, 0))
    return pl.pallas_call(
        functools.partial(output_kernel, owners, slots, len(after)),
        grid_spec=pltpu.PrefetchScalarGridSpec(
            num_scalar_prefetch=1,
            grid=(columns // span,),
            in_specs=[row_spec] * owners
            + [pl.BlockSpec((width, span), lambda j, at: (0, column // span + j))]
            + anywhere(after),
            out_specs=[
                pl.BlockSpec((n, owners, piece, span), lambda j, at: (0, 0, 0, j)) for n in counts
            ],
            scratch_shapes=[pltpu.VMEM((owners * each, width), bf16)],
        ),
        out_shape=[jax.ShapeDtypeStruct((n, owners, piece, columns), bf16) for n in counts],
        compiler_params=params(),
        cost_estimate=LIGHT,
        name="output",
    )(
        index.reshape(1).astype(jnp.int32),
        *[b.reshape(zs, piece, b.shape[1]) for b in blocks], far(w_out), *after,
    )


def close_kernel(counts, at_ref, t_ref, *refs):
    out_ref, mark_ref = refs[-2:]
    mark_ref[...] = jnp.zeros_like(mark_ref)
    first, column = 0, 0
    for count in counts:
        terms = refs[first:first + count]
        span = terms[0].shape[-1]
        at = slice(column, column + span)
        for p in range(out_ref.shape[0]):
            total = t_ref[p, :, at].astype(f32)
            for term in terms:
                total = total + term[0, p ^ at_ref[0]].astype(f32)
            out_ref[p, :, at] = total.astype(bf16)
        first += count
        column += span


def close(place, index, tokens, chunks, r, g, groups, out, after):
    _, owners, piece, _ = groups[0][0].shape
    span, width = sum(terms[0].shape[-1] for terms in groups), tokens.shape[1]
    at = jnp.stack([place, index * chunks + r]).astype(jnp.int32)
    flat = [term for terms in groups for term in terms]
    into = [] if out is None else [out]
    return pl.pallas_call(
        functools.partial(close_kernel, [len(terms) for terms in groups]),
        grid_spec=pltpu.PrefetchScalarGridSpec(
            num_scalar_prefetch=1,
            grid=(1,),
            in_specs=[pl.BlockSpec((owners, piece, span), lambda j, at: (at[1], 0, g))]
            + [pl.BlockSpec((1,) + t.shape[1:], lambda j, at: (0, 0, 0, 0)) for t in flat]
            + anywhere(into) + anywhere(after),
            out_specs=(
                pl.BlockSpec((owners, piece, span), lambda j, at: (r, 0, g)),
                pl.BlockSpec((8, DH), lambda j, at: (0, 0)),
            ),
        ),
        out_shape=(
            jax.ShapeDtypeStruct((chunks * owners, piece, width), bf16),
            jax.ShapeDtypeStruct((8, DH), f32),
        ),
        input_output_aliases={} if out is None else {2 + len(flat): 0},
        compiler_params=params(),
        cost_estimate=LIGHT,
        name="close",
    )(at, far(tokens.reshape(-1, piece, width)), *flat, *into, *after)


def bits_of(axis):
    count = lax.axis_size(axis)
    assert count & (count - 1) == 0
    return count.bit_length() - 1


def reverse(index, bits):
    return sum((((index >> b) & 1) << (bits - 1 - b) for b in range(bits)), 0 * index)


def swap(x, axis, bit):
    return lax.ppermute(
        x, axis, [(i, i ^ (1 << bit)) for i in range(lax.axis_size(axis))]
    )


def scatter(keep, gots, axis, after=()):
    terms, sent = [keep, gots[0]], gots[-1]
    for b in range(1, bits_of(axis)):
        sent = fold([keep, gots[-1]] if b == 1 else terms, after)
        terms.append(swap(sent, axis, b))
    return terms, sent


def gather(x, axis, after=()):
    blocks = [x]
    for b in reversed(range(bits_of(axis))):
        blocks = blocks + [swap(block, axis, b) for block in blocks]
        if len(blocks) == 2:
            blocks[1] = tie(blocks[1], after)
    return blocks


def all_stats(stat, width, axis):
    count = lax.axis_size(axis)
    if count > 8 or count & (count - 1):
        every = lax.all_gather(stat, axis)
        return [every[i] for i in range(count)], width
    stats = [stat]
    for b in range(bits_of(axis)):
        if b:
            width, stats = 2 * width, [merge_stats(stats, width)]
        stats.append(swap(stats[0], axis, b))
    return stats, width


def head_chunks(heads):
    if heads % 8:
        return [1] * heads
    unit = heads // 8
    return [unit, 2 * unit, 2 * unit, 2 * unit, unit]


GROUPS = [[0, 1], [2], [3], [4]]
ORDER = [
    "P0", "P1", "F0", "P2", "F1", "P3", "F2", "A0", "F3", "P4", "A1", "F4", "T0", "G0", "A2",
    "T1", "A3", "G1", "T2", "T3", "G2", "E0", "G3", "E1", "E2", "E3",
]


def local(tokens, w_qkvu, k_cache, v_cache, w_out, vis_start, vis_end):
    cand, depth = tokens.shape
    owners, zs = lax.axis_size("hist"), lax.axis_size("head")
    index = lax.axis_index("head")
    place = reverse(lax.axis_index("hist"), bits_of("hist"))
    width = w_qkvu.shape[2]
    events = k_cache.shape[0]
    chunks = 2 if cand % (2 * owners * zs * 16) == 0 else 1
    piece = cand // (zs * chunks * owners)

    def arrange(x):
        x = x.reshape((zs, chunks, owners, piece) + x.shape[1:])
        if piece % 16 == 0:
            return x
        blocks = [lax.dynamic_index_in_dim(x, p ^ place, 2, False) for p in range(owners)]
        x = jnp.stack(blocks).swapaxes(1, 2)
        return x.reshape((1, 1, owners, zs * chunks * piece) + x.shape[4:])

    at = (place if piece % 16 == 0 else jnp.int32(0)).reshape(1)
    ordered = arrange(tokens)
    first_event = lax.axis_index("hist") * events
    edges = arrange(edge_columns(first_event, vis_start, vis_end))

    sizes = head_chunks(width // DH)
    firsts = [sum(sizes[:c]) for c in range(len(sizes))]
    groups, order = GROUPS, ORDER
    if len(sizes) != 5:
        groups = [[c] for c in range(len(sizes))]
        order = [step + str(c) for step in "PFATGE" for c in range(len(sizes))]
    last = len(groups) - 1
    heads = [sum(sizes[c] for c in group) for group in groups]
    chain, keeps, firsts_got, terms, sums = [], {}, {}, {}, {}
    halves, queries, parts, atts, stats = {}, {}, {}, {}, {}
    for step, c in [(name[0], int(name[1:])) for name in order]:
        after = chain[-1:]
        if step == "P":
            keep, *sends = project(at, ordered, w_qkvu, firsts[c], sizes[c], after)
            before = firsts_got[c - 1] if c >= 1 else []
            before = before + [terms[0][-1]] if c == 2 and 0 in terms else before
            firsts_got[c] = [swap(tie(send, before), "hist", 0) for send in reversed(sends)][::-1]
            keeps[c] = keep
            chain.append(keep)
        elif step == "F":
            terms[c], sent = scatter(keeps[c], firsts_got[c], "hist", after)
            chain.append(sent)
        elif step == "A":
            parts[c] = activate([terms[k] for k in groups[c]], after)
            queries[c] = gather(parts[c][0], "hist")
            chain.append(parts[c][0])
        elif step == "T":
            first = firsts[groups[c][0]]
            keep, *sends = attend(at, queries[c], k_cache, v_cache, edges, first, after)
            before = queries[last][1:2] if c == last - 1 and last in queries else []
            halves[c] = keep, [swap(tie(send, before), "hist", 0) for send in sends]
            chain.append(keep)
        elif step == "G":
            sums[c], sent = scatter(*halves[c], "hist", after)
            chain.append(sent)
        else:
            others = [stats[k] for k in range(last)] if c == last else []
            widths = [size * DH for size in heads[:last]] if c == last else []
            atts[c], stats[c] = finish(at, edges, *parts[c], sums[c], others, widths, after)
            chain.append(atts[c])

    atts = [atts[c] for c in range(last + 1)]
    rests = [parts[c][1] for c in range(last + 1)]
    every, stat_width = all_stats(stats[last], width, "head")
    gated = gate_rows(every, stat_width, atts, rests, chunks)
    columns = w_out.shape[1]
    straight = piece % 16 == 0 and zs & (zs - 1) == 0
    out = None
    if not straight:
        for r, rows in enumerate(gated):
            whole = jnp.concatenate(gather(rows, "hist"))[:, :width]
            whole = jnp.dot(whole, w_out, preferred_element_type=f32).astype(bf16)
            whole = whole.reshape(owners, zs, piece, -1).swapaxes(0, 1)
            whole = lax.psum_scatter(whole, "head", scatter_dimension=0, tiled=True)
            out, _ = close(place, index, tokens, chunks, r, 0, [[whole]], out, [])
        return out.reshape(cand // zs, -1)
    slots = [reverse(k, bits_of("head")) for k in range(zs)]
    groups = 2 if columns % 1024 == 0 else 1
    span = columns // groups
    counts = [zs // 2] * 2 if zs > 1 else [1]
    plan = [(r, g) for r in range(chunks) for g in range(groups)]
    chain, first_out, blocks, made, folded = [], [], {}, [], []

    def fold_next():
        own, arrived = made[len(folded)]
        terms, sent = scatter(own, arrived, "head", chain) if arrived else ([own], own)
        folded.append(terms)
        return [sent]

    for n, (r, g) in enumerate(plan):
        if r not in blocks:
            blocks[r] = gather(gated[r], "hist", first_out)
        own, *others = output(index, slots, counts, blocks[r], w_out, g * span, span, chain)
        before = made[n - 2][1] if n > 1 else []
        before = before + [folded[0][-1]] if folded else before
        made.append((own, [swap(tie(x, before), "head", 0) for x in others]))
        chain, first_out = [own], first_out or [own]
        if n == 2:
            chain = fold_next()
    closed = 0
    while closed < len(plan):
        if len(folded) < len(plan):
            chain = fold_next()
        if len(folded) > closed + 2 or len(folded) == len(plan):
            r, g = plan[closed]
            some = 1 if r < chunks - 1 else groups
            out, mark = close(
                place, index, tokens, chunks, r, g, folded[closed:closed + some], out, chain
            )
            chain, closed = [mark], closed + some
    return out.reshape(cand // zs, -1)


def solution(mesh):
    in_specs = (
        P("groups", "hist"),
        P("hist", None, "head"),
        P(("groups", "hist"), "head"),
        P(("groups", "hist"), "head"),
        P("head", "hist"),
        P("groups"),
        P("groups"),
    )
    out_specs = P(("groups", "head"), "hist")
    return jax.shard_map(local, mesh=mesh, in_specs=in_specs, out_specs=out_specs, check_vma=False)
```

```python
import functools

import jax
import jax.numpy as jnp
from jax import lax
from jax.experimental import pallas as pl
from jax.experimental.pallas import tpu as pltpu
from jax.sharding import PartitionSpec as P

DH = 128
EPSILON = 1e-05
VMEM_LIMIT = 28 * 1024 * 1024

bf16 = jnp.bfloat16
f32 = jnp.float32


def silu(v):
    u = 0.5 * v
    return u + u * jnp.tanh(u)


def params():
    return pltpu.CompilerParams(vmem_limit_bytes=VMEM_LIMIT)


LIGHT = pl.CostEstimate(flops=1000, bytes_accessed=1000, transcendentals=0)


def far(x):
    return pltpu.with_memory_space_constraint(x, pltpu.HBM)


def anywhere(arrays):
    return [pl.BlockSpec(memory_space=pl.ANY)] * len(arrays)


def project_kernel(parts, owners, after, at_ref, *refs):
    rows, weights = refs[:owners], refs[owners:owners + parts]
    outs, lhs_ref = refs[owners + parts + after:-parts - 1], refs[-parts - 1]
    wides = refs[-parts:]
    zs, chunks, _, piece, _ = rows[0].shape
    depth = weights[0].shape[0]

    @pl.when(pl.program_id(0) == 0)
    def _():
        first = 0
        for p in range(owners):
            for r in range(chunks):
                for z in range(zs):
                    lhs_ref[first:first + piece, :] = rows[p][z, r, 0]
                    first += piece

    res = None
    for k, wide in enumerate(wides):
        wide[...] = weights[k].reshape(depth * 4, DH)[...].astype(f32)
        rhs = jnp.concatenate(
            [wide[pl.ds(i, depth, stride=4), :].astype(bf16) for i in range(4)], axis=1
        )
        term = jnp.dot(lhs_ref[:, k * depth:(k + 1) * depth], rhs, preferred_element_type=f32)
        res = term if res is None else res + term
    res = res.astype(bf16)
    each, first = outs[0].shape[2], 0
    for out in outs:
        for p in range(out.shape[0]):
            for i in range(4):
                out[p, i] = res[first:first + each, i * DH:(i + 1) * DH]
            first += each


def parts_of(owners):
    half = owners // 2
    return [half, half // 2, half // 2] if half > 1 else [half, half]


def project(at, tokens, w, head_first, heads, after):
    zs, chunks, owners, piece, depth = tokens.shape
    each, counts = zs * chunks * piece, parts_of(owners)
    parts = 4 if depth % 512 == 0 else 1
    return pl.pallas_call(
        functools.partial(project_kernel, parts, owners, len(after)),
        grid_spec=pltpu.PrefetchScalarGridSpec(
            num_scalar_prefetch=1,
            grid=(heads,),
            in_specs=[
                pl.BlockSpec(
                    (zs, chunks, 1, piece, depth), lambda j, at, p=p: (0, 0, at[0] ^ p, 0, 0)
                )
                for p in range(owners)
            ]
            + [
                pl.BlockSpec((depth // parts, 4, DH), lambda j, at, k=k: (k, 0, head_first + j))
                for k in range(parts)
            ]
            + anywhere(after),
            out_specs=[
                pl.BlockSpec((n, 4, each, DH), lambda j, at: (0, 0, 0, j)) for n in counts
            ],
            scratch_shapes=[pltpu.VMEM((owners * each, depth), bf16)]
            + [pltpu.VMEM((depth // parts * 4, DH), f32) for _ in range(parts)],
        ),
        out_shape=[jax.ShapeDtypeStruct((n, 4, each, heads * DH), bf16) for n in counts],
        compiler_params=params(),
        cost_estimate=LIGHT,
        name="project",
    )(at, *[far(tokens)] * owners, *[far(w)] * parts, *after)


def tie_kernel(*refs):
    pass


def tie(x, after):
    if not after:
        return x
    return pl.pallas_call(
        tie_kernel,
        in_specs=anywhere([x, *after]),
        out_specs=pl.BlockSpec(memory_space=pl.ANY),
        out_shape=jax.ShapeDtypeStruct(x.shape, x.dtype),
        input_output_aliases={0: 0},
        compiler_params=params(),
        cost_estimate=LIGHT,
        name="tie",
    )(x, *after)


def fold_kernel(count, *refs):
    refs[-1][...] = sum(r[...].astype(f32) for r in refs[:count]).astype(bf16)


def fold(terms, after=()):
    half = terms[0].shape[0] // 2 if len(terms) == 2 else terms[-1].shape[0] // 2
    tail = terms[0].shape[1:]
    steps = 2 if tail[-1] % 256 == 0 else 1
    block = (half,) + tail[:-1] + (tail[-1] // steps,)
    middle = (0,) * (len(tail) - 1)
    firsts = [0 if t.shape[0] == half else 1 for t in terms]
    return pl.pallas_call(
        functools.partial(fold_kernel, len(terms)),
        grid=(steps,),
        in_specs=[pl.BlockSpec(block, lambda j, f=f: (f,) + middle + (j,)) for f in firsts]
        + anywhere(after),
        out_specs=pl.BlockSpec(block, lambda j: (0,) + middle + (j,)),
        out_shape=jax.ShapeDtypeStruct((half,) + tail, bf16),
        compiler_params=params(),
        cost_estimate=LIGHT,
        name="fold",
    )(*terms, *after)


def activate_kernel(counts, *refs):
    q_ref, rest_ref = refs[-2:]
    first, column = 0, 0
    for count in counts:
        terms = refs[first:first + count]
        span = terms[0].shape[-1]
        for i in range(4):
            part = silu(sum(t[0, i].astype(f32) for t in terms)).astype(bf16)
            if i == 0:
                q_ref[:, column:column + span] = part
            else:
                rest_ref[i - 1, :, column:column + span] = part
        first += count
        column += span


def activate(chunks, after):
    each, width = chunks[0][0].shape[2], sum(terms[0].shape[3] for terms in chunks)
    flat = [term for terms in chunks for term in terms]
    return pl.pallas_call(
        functools.partial(activate_kernel, [len(terms) for terms in chunks]),
        grid=(1,),
        in_specs=[pl.BlockSpec((1,) + t.shape[1:], lambda j: (0, 0, 0, 0)) for t in flat]
        + anywhere(after),
        out_specs=(
            pl.BlockSpec((each, width), lambda j: (0, 0)),
            pl.BlockSpec((3, each, width), lambda j: (0, 0, 0)),
        ),
        out_shape=(
            jax.ShapeDtypeStruct((each, width), bf16),
            jax.ShapeDtypeStruct((3, each, width), bf16),
        ),
        compiler_params=params(),
        cost_estimate=LIGHT,
        name="activate",
    )(*flat, *after)


def edge_kernel(base_ref, start_ref, end_ref, out_ref):
    row = lax.broadcasted_iota(jnp.int32, (DH, DH), 0)
    for b in range(start_ref.shape[0]):
        start, end = start_ref[b:b + 1, :], end_ref[b:b + 1, :]
        both = jnp.where(row == 0, start, end) - base_ref[0]
        out_ref[b * DH:(b + 1) * DH, :] = both.astype(f32).T[:, :2].astype(jnp.int32)


def edge_columns(base, start, end):
    count = start.shape[0]
    lines = pl.BlockSpec((count // DH, DH), lambda j, base: (0, 0))
    return pl.pallas_call(
        edge_kernel,
        grid_spec=pltpu.PrefetchScalarGridSpec(
            num_scalar_prefetch=1,
            grid=(1,),
            in_specs=[lines, lines],
            out_specs=pl.BlockSpec((count, 2), lambda j, base: (0, 0)),
        ),
        out_shape=jax.ShapeDtypeStruct((count, 2), jnp.int32),
        compiler_params=params(),
        cost_estimate=LIGHT,
        name="edges",
    )(base.reshape(1), start.reshape(-1, DH), end.reshape(-1, DH))


def attend_kernel(owners, sends, at_ref, *refs):
    queries, edges = refs[:owners], refs[owners:2 * owners]
    k_ref, v_ref = refs[2 * owners:2 * owners + 2]
    outs, mask_ref = refs[-1 - sends:-1], refs[-1]
    events = mask_ref.shape[1]
    each = outs[0].shape[1]

    @pl.when(pl.program_id(0) == 0)
    def _():
        zs, chunks, _, piece, _ = edges[0].shape
        at = lax.broadcasted_iota(jnp.int32, (piece, events), 1)
        first = 0
        for p in range(owners):
            for r in range(chunks):
                for z in range(zs):
                    edge = edges[p][z, r, 0]
                    seen = (at >= edge[:, :1]) & (at < edge[:, 1:])
                    mask_ref[first:first + piece, :] = jnp.where(seen, 1.0, 0.0).astype(bf16)
                    first += piece

    for h in range(k_ref.shape[1] // DH):
        at = slice(h * DH, (h + 1) * DH)
        query = jnp.concatenate([q[:, at] for q in queries])
        u = lax.dot_general(
            query, k_ref[:, at], (((1,), (1,)), ((), ())), preferred_element_type=f32
        ) * (0.5 * DH ** (-0.5))
        weights = (u + u * jnp.tanh(u)).astype(bf16) * mask_ref[...]
        term = jnp.dot(weights, v_ref[:, at], preferred_element_type=f32).astype(bf16)
        first = 0
        for out in outs:
            for p in range(out.shape[0]):
                out[p, :, at] = term[first:first + each]
                first += each


def edge_spec(edges, p):
    zs, chunks, _, piece, ends = edges.shape
    return pl.BlockSpec((zs, chunks, 1, piece, ends), lambda j, at: (0, 0, at[0] ^ p, 0, 0))


def attend(at, queries, k_cache, v_cache, edges, head_first, after):
    owners, (each, width) = len(queries), queries[0].shape
    rows, events, counts = owners * each, k_cache.shape[0], parts_of(owners)
    first = head_first * DH
    span = max(h for h in range(DH, 4 * DH, DH) if width % h == 0 and first % h == 0)
    cache = pl.BlockSpec((events, span), lambda j, at: (0, first // span + j))
    return pl.pallas_call(
        functools.partial(attend_kernel, owners, len(counts)),
        grid_spec=pltpu.PrefetchScalarGridSpec(
            num_scalar_prefetch=1,
            grid=(width // span,),
            in_specs=[pl.BlockSpec((each, span), lambda j, at: (0, j))] * owners
            + [edge_spec(edges, p) for p in range(owners)]
            + [cache, cache]
            + anywhere(after),
            out_specs=[pl.BlockSpec((n, each, span), lambda j, at: (0, 0, j)) for n in counts],
            scratch_shapes=[pltpu.VMEM((rows, events), bf16)],
        ),
        out_shape=[jax.ShapeDtypeStruct((n, each, width), bf16) for n in counts],
        compiler_params=params(),
        cost_estimate=LIGHT,
        name="attend",
    )(at, *queries, *[edges] * owners, far(k_cache), far(v_cache), *after)


def merge(means, squares, widths):
    width = sum(widths)
    mean = sum(m * (w / width) for m, w in zip(means, widths))
    square = sum(squares) + sum(w * (m - mean) * (m - mean) for m, w in zip(means, widths))
    return mean, square


def stat_columns(stats):
    stats = [s[...] for s in stats]
    stats = [s if s.shape[0] > 8 else jnp.concatenate([s] * (DH // 8)).T for s in stats]
    return [s[:, :1] for s in stats], [s[:, 4:5] for s in stats]


def finish_kernel(terms, widths, at_ref, edge_ref, q_ref, rest_ref, *refs):
    sums, others = refs[:terms], refs[terms:terms + len(widths)]
    att_ref, stat_ref = refs[-2:]
    rows, width = att_ref.shape
    zs, chunks = edge_ref.shape[:2]
    edge = jnp.concatenate(
        [edge_ref[z, r, 0] for r in range(chunks) for z in range(zs)]
    ).astype(f32)
    root = lax.rsqrt(edge[:, 1:] - edge[:, :1])
    total = jnp.zeros((rows, 1), f32)
    for first in range(0, width, DH):
        at = slice(first, first + DH)
        summed = sum(s[0, :, at].astype(f32) for s in sums)
        product = q_ref[:, at].astype(f32) * rest_ref[0, :, at].astype(f32)
        weight = silu(jnp.sum(product, axis=1, keepdims=True) * DH ** (-0.5))
        value = summed * root + weight * rest_ref[1, :, at].astype(f32)
        att_ref[:, at] = value
        total += jnp.sum(value, axis=1, keepdims=True)
    mean = total / width
    spread = jnp.zeros((rows, DH), f32)
    for first in range(0, width, DH):
        away = att_ref[:, first:first + DH] - mean
        spread += away * away
    square = jnp.sum(spread, axis=1, keepdims=True)
    if others:
        means, squares = stat_columns(others)
        mean, square = merge([mean] + means, [square] + squares, [width] + widths)
    lane = lax.broadcasted_iota(jnp.int32, (rows, DH), 1)
    stat = jnp.where(lane < 4, mean, square)
    stat_ref[...] = stat if stat_ref.shape == stat.shape else stat.T[:8]


def finish(at, edges, query, rest, sums, others, widths, after):
    rows, width = query.shape
    stat = (8, rows) if others and rows == DH else (rows, DH)
    return pl.pallas_call(
        functools.partial(finish_kernel, len(sums), widths),
        grid_spec=pltpu.PrefetchScalarGridSpec(
            num_scalar_prefetch=1,
            grid=(1,),
            in_specs=[
                edge_spec(edges, 0),
                pl.BlockSpec((rows, width), lambda j, at: (0, 0)),
                pl.BlockSpec((2, rows, width), lambda j, at: (0, 0, 0)),
            ]
            + [pl.BlockSpec((1, rows, width), lambda j, at: (0, 0, 0))] * len(sums)
            + [pl.BlockSpec((rows, DH), lambda j, at: (0, 0))] * len(others)
            + anywhere(after),
            out_specs=(
                pl.BlockSpec((rows, width), lambda j, at: (0, 0)),
                pl.BlockSpec(stat, lambda j, at: (0, 0)),
            ),
        ),
        out_shape=(
            jax.ShapeDtypeStruct((rows, width), f32),
            jax.ShapeDtypeStruct(stat, f32),
        ),
        compiler_params=params(),
        cost_estimate=LIGHT,
        name="finish",
    )(at, edges, query, rest, *sums, *others, *after)


def merge_kernel(width, *refs):
    (m, n), (s, t) = (
        [r[:4] if r.shape[0] == 8 else r[:, :4] for r in refs[:2]],
        [r[4:] if r.shape[0] == 8 else r[:, 4:8] for r in refs[:2]],
    )
    mean, square = merge([m, n], [s, t], [width] * 2)
    if refs[2].shape[0] == 8:
        refs[2][:4], refs[2][4:] = mean, square
    else:
        lane = lax.broadcasted_iota(jnp.int32, refs[2].shape, 1)
        refs[2][...] = jnp.where(lane < 4, mean[:, :1], square[:, :1])


def merge_stats(stats, width):
    return pl.pallas_call(
        functools.partial(merge_kernel, width),
        out_shape=jax.ShapeDtypeStruct(stats[0].shape, f32),
        compiler_params=params(),
        cost_estimate=LIGHT,
        name="merge",
    )(*stats)


def gate_kernel(count, parts, width, *refs):
    stats, atts, rests, outs = (
        refs[:count], refs[count:count + parts],
        refs[count + parts:count + 2 * parts], refs[count + 2 * parts:],
    )
    means, squares = stat_columns(stats)
    mean, square = merge(means, squares, [width] * count)
    scale = lax.rsqrt(square / (width * count) + EPSILON)
    rows, column = outs[0].shape[0], 0
    for att, rest in zip(atts, rests):
        span = att.shape[1]
        normed = (att[...] - mean) * scale
        gated = (normed * rest[0].astype(f32)).astype(bf16)
        for r, out in enumerate(outs):
            out[:, column:column + span] = gated[r * rows:(r + 1) * rows]
        column += span
    for out in outs:
        if out.shape[1] > column:
            out[:, column:] = jnp.zeros((rows, out.shape[1] - column), bf16)


def gate_rows(stats, stat_width, atts, rests, chunks):
    rows, width = atts[0].shape[0], sum(a.shape[1] for a in atts)
    widths = [width + DH * min(r, 1) for r in range(chunks)]
    return pl.pallas_call(
        functools.partial(gate_kernel, len(stats), len(atts), stat_width),
        grid=(1,),
        in_specs=[pl.BlockSpec(s.shape, lambda j: (0, 0)) for s in stats]
        + [pl.BlockSpec((rows, a.shape[1]), lambda j: (0, 0)) for a in atts]
        + [pl.BlockSpec((1, rows, r.shape[2]), lambda j: (2, 0, 0)) for r in rests],
        out_specs=[pl.BlockSpec((rows // chunks, w), lambda j: (0, 0)) for w in widths],
        out_shape=[jax.ShapeDtypeStruct((rows // chunks, w), bf16) for w in widths],
        compiler_params=params(),
        cost_estimate=LIGHT,
        name="gate",
    )(*stats, *atts, *rests)


def output_kernel(owners, slots, after, index_ref, *refs):
    rows, w_ref, outs, lhs_ref = refs[:owners], refs[owners], refs[owners + 1 + after:-1], refs[-1]
    piece = rows[0].shape[1]

    @pl.when(pl.program_id(0) == 0)
    def _():
        first = 0
        for slot in slots:
            for p in range(owners):
                lhs_ref[first:first + piece, :] = rows[p][index_ref[0] ^ slot]
                first += piece

    sums = jnp.dot(lhs_ref[...], w_ref[...], preferred_element_type=f32).astype(bf16)
    first = 0
    for out in outs:
        for k in range(out.shape[0]):
            for p in range(owners):
                out[k, p] = sums[first:first + piece]
                first += piece


def output(index, slots, counts, blocks, w_out, column, columns, after):
    owners, each, zs = len(blocks), blocks[0].shape[0], sum(counts)
    width, piece = w_out.shape[0], each // zs
    span = max(c for c in (512, 256, columns) if columns % c == 0 and column % c == 0)
    row_spec = pl.BlockSpec((zs, piece, width), lambda j, at: (0, 0, 0))
    return pl.pallas_call(
        functools.partial(output_kernel, owners, slots, len(after)),
        grid_spec=pltpu.PrefetchScalarGridSpec(
            num_scalar_prefetch=1,
            grid=(columns // span,),
            in_specs=[row_spec] * owners
            + [pl.BlockSpec((width, span), lambda j, at: (0, column // span + j))]
            + anywhere(after),
            out_specs=[
                pl.BlockSpec((n, owners, piece, span), lambda j, at: (0, 0, 0, j)) for n in counts
            ],
            scratch_shapes=[pltpu.VMEM((owners * each, width), bf16)],
        ),
        out_shape=[jax.ShapeDtypeStruct((n, owners, piece, columns), bf16) for n in counts],
        compiler_params=params(),
        cost_estimate=LIGHT,
        name="output",
    )(
        index.reshape(1).astype(jnp.int32),
        *[b.reshape(zs, piece, b.shape[1]) for b in blocks], far(w_out), *after,
    )


def close_kernel(counts, at_ref, t_ref, *refs):
    out_ref, mark_ref = refs[-2:]
    mark_ref[...] = jnp.zeros_like(mark_ref)
    first, column = 0, 0
    for count in counts:
        terms = refs[first:first + count]
        span = terms[0].shape[-1]
        at = slice(column, column + span)
        for p in range(out_ref.shape[0]):
            total = t_ref[p, :, at].astype(f32)
            for term in terms:
                total = total + term[0, p ^ at_ref[0]].astype(f32)
            out_ref[p, :, at] = total.astype(bf16)
        first += count
        column += span


def close(place, index, tokens, chunks, r, g, groups, out, after):
    _, owners, piece, _ = groups[0][0].shape
    span, width = sum(terms[0].shape[-1] for terms in groups), tokens.shape[1]
    at = jnp.stack([place, index * chunks + r]).astype(jnp.int32)
    flat = [term for terms in groups for term in terms]
    into = [] if out is None else [out]
    return pl.pallas_call(
        functools.partial(close_kernel, [len(terms) for terms in groups]),
        grid_spec=pltpu.PrefetchScalarGridSpec(
            num_scalar_prefetch=1,
            grid=(1,),
            in_specs=[pl.BlockSpec((owners, piece, span), lambda j, at: (at[1], 0, g))]
            + [pl.BlockSpec((1,) + t.shape[1:], lambda j, at: (0, 0, 0, 0)) for t in flat]
            + anywhere(into) + anywhere(after),
            out_specs=(
                pl.BlockSpec((owners, piece, span), lambda j, at: (r, 0, g)),
                pl.BlockSpec((8, DH), lambda j, at: (0, 0)),
            ),
        ),
        out_shape=(
            jax.ShapeDtypeStruct((chunks * owners, piece, width), bf16),
            jax.ShapeDtypeStruct((8, DH), f32),
        ),
        input_output_aliases={} if out is None else {2 + len(flat): 0},
        compiler_params=params(),
        cost_estimate=LIGHT,
        name="close",
    )(at, far(tokens.reshape(-1, piece, width)), *flat, *into, *after)


def bits_of(axis):
    count = lax.axis_size(axis)
    assert count & (count - 1) == 0
    return count.bit_length() - 1


def reverse(index, bits):
    return sum((((index >> b) & 1) << (bits - 1 - b) for b in range(bits)), 0 * index)


def swap(x, axis, bit):
    return lax.ppermute(
        x, axis, [(i, i ^ (1 << bit)) for i in range(lax.axis_size(axis))]
    )


def scatter(keep, gots, axis, after=()):
    terms, sent = [keep, gots[0]], gots[-1]
    for b in range(1, bits_of(axis)):
        sent = fold([keep, gots[-1]] if b == 1 else terms, after)
        terms.append(swap(sent, axis, b))
    return terms, sent


def gather(x, axis, after=()):
    blocks = [x]
    for b in reversed(range(bits_of(axis))):
        blocks = blocks + [swap(block, axis, b) for block in blocks]
        if len(blocks) == 2:
            blocks[1] = tie(blocks[1], after)
    return blocks


def all_stats(stat, width, axis):
    count = lax.axis_size(axis)
    if count > 8 or count & (count - 1):
        every = lax.all_gather(stat, axis)
        return [every[i] for i in range(count)], width
    stats = [stat]
    for b in range(bits_of(axis)):
        if b:
            width, stats = 2 * width, [merge_stats(stats, width)]
        stats.append(swap(stats[0], axis, b))
    return stats, width


def head_chunks(heads):
    if heads % 8:
        return [1] * heads
    unit = heads // 8
    if unit % 2:
        return [unit, 2 * unit, 2 * unit, 2 * unit, unit]
    return [3 * unit // 2, 2 * unit, 2 * unit, 3 * unit // 2, unit]


GROUPS = [[0, 1], [2], [3], [4]]
ORDER = [
    "P0", "P1", "F0", "P2", "F1", "P3", "F2", "A0", "F3", "P4", "A1", "F4", "T0", "G0", "A2",
    "T1", "A3", "G1", "T2", "T3", "G2", "E0", "G3", "E1", "E2", "E3",
]


def local(tokens, w_qkvu, k_cache, v_cache, w_out, vis_start, vis_end):
    cand, depth = tokens.shape
    owners, zs = lax.axis_size("hist"), lax.axis_size("head")
    index = lax.axis_index("head")
    place = reverse(lax.axis_index("hist"), bits_of("hist"))
    width = w_qkvu.shape[2]
    events = k_cache.shape[0]
    chunks = 2 if cand % (2 * owners * zs * 16) == 0 else 1
    piece = cand // (zs * chunks * owners)

    def arrange(x):
        x = x.reshape((zs, chunks, owners, piece) + x.shape[1:])
        if piece % 16 == 0:
            return x
        blocks = [lax.dynamic_index_in_dim(x, p ^ place, 2, False) for p in range(owners)]
        x = jnp.stack(blocks).swapaxes(1, 2)
        return x.reshape((1, 1, owners, zs * chunks * piece) + x.shape[4:])

    at = (place if piece % 16 == 0 else jnp.int32(0)).reshape(1)
    ordered = arrange(tokens)
    first_event = lax.axis_index("hist") * events
    edges = arrange(edge_columns(first_event, vis_start, vis_end))

    sizes = head_chunks(width // DH)
    firsts = [sum(sizes[:c]) for c in range(len(sizes))]
    groups, order = GROUPS, ORDER
    if len(sizes) != 5:
        groups = [[c] for c in range(len(sizes))]
        order = [step + str(c) for step in "PFATGE" for c in range(len(sizes))]
    last = len(groups) - 1
    heads = [sum(sizes[c] for c in group) for group in groups]
    chain, keeps, firsts_got, terms, sums = [], {}, {}, {}, {}
    halves, queries, parts, atts, stats = {}, {}, {}, {}, {}
    for step, c in [(name[0], int(name[1:])) for name in order]:
        after = chain[-1:]
        if step == "P":
            keep, *sends = project(at, ordered, w_qkvu, firsts[c], sizes[c], after)
            before = firsts_got[c - 1] if c >= 1 else []
            before = before + [terms[0][-1]] if c == 2 and 0 in terms else before
            firsts_got[c] = [swap(tie(send, before), "hist", 0) for send in reversed(sends)][::-1]
            keeps[c] = keep
            chain.append(keep)
        elif step == "F":
            terms[c], sent = scatter(keeps[c], firsts_got[c], "hist", after)
            chain.append(sent)
        elif step == "A":
            parts[c] = activate([terms[k] for k in groups[c]], after)
            queries[c] = gather(parts[c][0], "hist")
            chain.append(parts[c][0])
        elif step == "T":
            first = firsts[groups[c][0]]
            keep, *sends = attend(at, queries[c], k_cache, v_cache, edges, first, after)
            before = queries[last][1:2] if c == last - 1 and last in queries else []
            halves[c] = keep, [swap(tie(send, before), "hist", 0) for send in sends]
            chain.append(keep)
        elif step == "G":
            sums[c], sent = scatter(*halves[c], "hist", after)
            chain.append(sent)
        else:
            others = [stats[k] for k in range(last)] if c == last else []
            widths = [size * DH for size in heads[:last]] if c == last else []
            atts[c], stats[c] = finish(at, edges, *parts[c], sums[c], others, widths, after)
            chain.append(atts[c])

    atts = [atts[c] for c in range(last + 1)]
    rests = [parts[c][1] for c in range(last + 1)]
    every, stat_width = all_stats(stats[last], width, "head")
    gated = gate_rows(every, stat_width, atts, rests, chunks)
    columns = w_out.shape[1]
    straight = piece % 16 == 0 and zs & (zs - 1) == 0
    out = None
    if not straight:
        for r, rows in enumerate(gated):
            whole = jnp.concatenate(gather(rows, "hist"))[:, :width]
            whole = jnp.dot(whole, w_out, preferred_element_type=f32).astype(bf16)
            whole = whole.reshape(owners, zs, piece, -1).swapaxes(0, 1)
            whole = lax.psum_scatter(whole, "head", scatter_dimension=0, tiled=True)
            out, _ = close(place, index, tokens, chunks, r, 0, [[whole]], out, [])
        return out.reshape(cand // zs, -1)
    slots = [reverse(k, bits_of("head")) for k in range(zs)]
    groups = 2 if columns % 1024 == 0 else 1
    span = columns // groups
    counts = [zs // 2] * 2 if zs > 1 else [1]
    plan = [(r, g) for r in range(chunks) for g in range(groups)]
    chain, first_out, blocks, made, folded = [], [], {}, [], []

    def fold_next():
        own, arrived = made[len(folded)]
        terms, sent = scatter(own, arrived, "head", chain) if arrived else ([own], own)
        folded.append(terms)
        return [sent]

    for n, (r, g) in enumerate(plan):
        if r not in blocks:
            blocks[r] = gather(gated[r], "hist", first_out)
        own, *others = output(index, slots, counts, blocks[r], w_out, g * span, span, chain)
        before = made[n - 2][1] if n > 1 else []
        before = before + [folded[0][-1]] if folded else before
        made.append((own, [swap(tie(x, before), "head", 0) for x in others]))
        chain, first_out = [own], first_out or [own]
        if n == 2:
            chain = fold_next()
    closed = 0
    while closed < len(plan):
        if len(folded) < len(plan):
            chain = fold_next()
        if len(folded) > closed + 2 or len(folded) == len(plan):
            r, g = plan[closed]
            some = 1 if r < chunks - 1 else groups
            out, mark = close(
                place, index, tokens, chunks, r, g, folded[closed:closed + some], out, chain
            )
            chain, closed = [mark], closed + some
    return out.reshape(cand // zs, -1)


def solution(mesh):
    in_specs = (
        P("groups", "hist"),
        P("hist", None, "head"),
        P(("groups", "hist"), "head"),
        P(("groups", "hist"), "head"),
        P("head", "hist"),
        P("groups"),
        P("groups"),
    )
    out_specs = P(("groups", "head"), "hist")
    return jax.shard_map(local, mesh=mesh, in_specs=in_specs, out_specs=out_specs, check_vma=False)
```

```python
import functools

import jax
import jax.numpy as jnp
from jax import lax
from jax.experimental import pallas as pl
from jax.experimental.pallas import tpu as pltpu
from jax.sharding import PartitionSpec as P

DH = 128
EPSILON = 1e-05
VMEM_LIMIT = 28 * 1024 * 1024

bf16 = jnp.bfloat16
f32 = jnp.float32


def silu(v):
    u = 0.5 * v
    return u + u * jnp.tanh(u)


def params():
    return pltpu.CompilerParams(vmem_limit_bytes=VMEM_LIMIT)


LIGHT = pl.CostEstimate(flops=1000, bytes_accessed=1000, transcendentals=0)


def far(x):
    return pltpu.with_memory_space_constraint(x, pltpu.HBM)


def anywhere(arrays):
    return [pl.BlockSpec(memory_space=pl.ANY)] * len(arrays)


def project_kernel(parts, owners, after, at_ref, *refs):
    rows, weights = refs[:owners], refs[owners:owners + parts]
    outs, lhs_ref = refs[owners + parts + after:-parts - 1], refs[-parts - 1]
    wides = refs[-parts:]
    zs, chunks, _, piece, _ = rows[0].shape
    depth = weights[0].shape[0]

    @pl.when(pl.program_id(0) == 0)
    def _():
        first = 0
        for p in range(owners):
            for r in range(chunks):
                for z in range(zs):
                    lhs_ref[first:first + piece, :] = rows[p][z, r, 0]
                    first += piece

    res = None
    for k, wide in enumerate(wides):
        wide[...] = weights[k].reshape(depth * 4, DH)[...].astype(f32)
        rhs = jnp.concatenate(
            [wide[pl.ds(i, depth, stride=4), :].astype(bf16) for i in range(4)], axis=1
        )
        term = jnp.dot(lhs_ref[:, k * depth:(k + 1) * depth], rhs, preferred_element_type=f32)
        res = term if res is None else res + term
    res = res.astype(bf16)
    each, first = outs[0].shape[2], 0
    for out in outs:
        for p in range(out.shape[0]):
            for i in range(4):
                out[p, i] = res[first:first + each, i * DH:(i + 1) * DH]
            first += each


def parts_of(owners):
    half = owners // 2
    return [half, half // 2, half // 2] if half > 1 else [half, half]


def project(at, tokens, w, head_first, heads, after):
    zs, chunks, owners, piece, depth = tokens.shape
    each, counts = zs * chunks * piece, parts_of(owners)
    parts = 4 if depth % 512 == 0 else 1
    return pl.pallas_call(
        functools.partial(project_kernel, parts, owners, len(after)),
        grid_spec=pltpu.PrefetchScalarGridSpec(
            num_scalar_prefetch=1,
            grid=(heads,),
            in_specs=[
                pl.BlockSpec(
                    (zs, chunks, 1, piece, depth), lambda j, at, p=p: (0, 0, at[0] ^ p, 0, 0)
                )
                for p in range(owners)
            ]
            + [
                pl.BlockSpec((depth // parts, 4, DH), lambda j, at, k=k: (k, 0, head_first + j))
                for k in range(parts)
            ]
            + anywhere(after),
            out_specs=[
                pl.BlockSpec((n, 4, each, DH), lambda j, at: (0, 0, 0, j)) for n in counts
            ],
            scratch_shapes=[pltpu.VMEM((owners * each, depth), bf16)]
            + [pltpu.VMEM((depth // parts * 4, DH), f32) for _ in range(parts)],
        ),
        out_shape=[jax.ShapeDtypeStruct((n, 4, each, heads * DH), bf16) for n in counts],
        compiler_params=params(),
        cost_estimate=LIGHT,
        name="project",
    )(at, *[far(tokens)] * owners, *[far(w)] * parts, *after)


def tie_kernel(*refs):
    pass


def tie(x, after):
    if not after:
        return x
    return pl.pallas_call(
        tie_kernel,
        in_specs=anywhere([x, *after]),
        out_specs=pl.BlockSpec(memory_space=pl.ANY),
        out_shape=jax.ShapeDtypeStruct(x.shape, x.dtype),
        input_output_aliases={0: 0},
        compiler_params=params(),
        cost_estimate=LIGHT,
        name="tie",
    )(x, *after)


def fold_kernel(count, *refs):
    refs[-1][...] = sum(r[...].astype(f32) for r in refs[:count]).astype(bf16)


def fold(terms, after=()):
    half = terms[0].shape[0] // 2 if len(terms) == 2 else terms[-1].shape[0] // 2
    tail = terms[0].shape[1:]
    steps = 2 if tail[-1] % 256 == 0 else 1
    block = (half,) + tail[:-1] + (tail[-1] // steps,)
    middle = (0,) * (len(tail) - 1)
    firsts = [0 if t.shape[0] == half else 1 for t in terms]
    return pl.pallas_call(
        functools.partial(fold_kernel, len(terms)),
        grid=(steps,),
        in_specs=[pl.BlockSpec(block, lambda j, f=f: (f,) + middle + (j,)) for f in firsts]
        + anywhere(after),
        out_specs=pl.BlockSpec(block, lambda j: (0,) + middle + (j,)),
        out_shape=jax.ShapeDtypeStruct((half,) + tail, bf16),
        compiler_params=params(),
        cost_estimate=LIGHT,
        name="fold",
    )(*terms, *after)


def activate_kernel(counts, *refs):
    q_ref, rest_ref = refs[-2:]
    first, column = 0, 0
    for count in counts:
        terms = refs[first:first + count]
        span = terms[0].shape[-1]
        for i in range(4):
            part = silu(sum(t[0, i].astype(f32) for t in terms)).astype(bf16)
            if i == 0:
                q_ref[:, column:column + span] = part
            else:
                rest_ref[i - 1, :, column:column + span] = part
        first += count
        column += span


def activate(chunks, after):
    each, width = chunks[0][0].shape[2], sum(terms[0].shape[3] for terms in chunks)
    flat = [term for terms in chunks for term in terms]
    return pl.pallas_call(
        functools.partial(activate_kernel, [len(terms) for terms in chunks]),
        grid=(1,),
        in_specs=[pl.BlockSpec((1,) + t.shape[1:], lambda j: (0, 0, 0, 0)) for t in flat]
        + anywhere(after),
        out_specs=(
            pl.BlockSpec((each, width), lambda j: (0, 0)),
            pl.BlockSpec((3, each, width), lambda j: (0, 0, 0)),
        ),
        out_shape=(
            jax.ShapeDtypeStruct((each, width), bf16),
            jax.ShapeDtypeStruct((3, each, width), bf16),
        ),
        compiler_params=params(),
        cost_estimate=LIGHT,
        name="activate",
    )(*flat, *after)


def edge_kernel(base_ref, start_ref, end_ref, out_ref):
    row = lax.broadcasted_iota(jnp.int32, (DH, DH), 0)
    for b in range(start_ref.shape[0]):
        start, end = start_ref[b:b + 1, :], end_ref[b:b + 1, :]
        both = jnp.where(row == 0, start, end) - base_ref[0]
        out_ref[b * DH:(b + 1) * DH, :] = both.astype(f32).T[:, :2].astype(jnp.int32)


def edge_columns(base, start, end):
    count = start.shape[0]
    lines = pl.BlockSpec((count // DH, DH), lambda j, base: (0, 0))
    return pl.pallas_call(
        edge_kernel,
        grid_spec=pltpu.PrefetchScalarGridSpec(
            num_scalar_prefetch=1,
            grid=(1,),
            in_specs=[lines, lines],
            out_specs=pl.BlockSpec((count, 2), lambda j, base: (0, 0)),
        ),
        out_shape=jax.ShapeDtypeStruct((count, 2), jnp.int32),
        compiler_params=params(),
        cost_estimate=LIGHT,
        name="edges",
    )(base.reshape(1), start.reshape(-1, DH), end.reshape(-1, DH))


def attend_kernel(owners, sends, at_ref, *refs):
    queries, edges = refs[:owners], refs[owners:2 * owners]
    k_ref, v_ref = refs[2 * owners:2 * owners + 2]
    outs, mask_ref = refs[-1 - sends:-1], refs[-1]
    events = mask_ref.shape[1]
    each = outs[0].shape[1]

    @pl.when(pl.program_id(0) == 0)
    def _():
        zs, chunks, _, piece, _ = edges[0].shape
        at = lax.broadcasted_iota(jnp.int32, (piece, events), 1)
        first = 0
        for p in range(owners):
            for r in range(chunks):
                for z in range(zs):
                    edge = edges[p][z, r, 0]
                    seen = (at >= edge[:, :1]) & (at < edge[:, 1:])
                    mask_ref[first:first + piece, :] = jnp.where(seen, 1.0, 0.0).astype(bf16)
                    first += piece

    for h in range(k_ref.shape[1] // DH):
        at = slice(h * DH, (h + 1) * DH)
        query = jnp.concatenate([q[:, at] for q in queries])
        u = lax.dot_general(
            query, k_ref[:, at], (((1,), (1,)), ((), ())), preferred_element_type=f32
        ) * (0.5 * DH ** (-0.5))
        weights = (u + u * jnp.tanh(u)).astype(bf16) * mask_ref[...]
        term = jnp.dot(weights, v_ref[:, at], preferred_element_type=f32).astype(bf16)
        first = 0
        for out in outs:
            for p in range(out.shape[0]):
                out[p, :, at] = term[first:first + each]
                first += each


def edge_spec(edges, p):
    zs, chunks, _, piece, ends = edges.shape
    return pl.BlockSpec((zs, chunks, 1, piece, ends), lambda j, at: (0, 0, at[0] ^ p, 0, 0))


def attend(at, queries, k_cache, v_cache, edges, head_first, after):
    owners, (each, width) = len(queries), queries[0].shape
    rows, events, counts = owners * each, k_cache.shape[0], parts_of(owners)
    first = head_first * DH
    span = max(h for h in range(DH, 4 * DH, DH) if width % h == 0 and first % h == 0)
    cache = pl.BlockSpec((events, span), lambda j, at: (0, first // span + j))
    return pl.pallas_call(
        functools.partial(attend_kernel, owners, len(counts)),
        grid_spec=pltpu.PrefetchScalarGridSpec(
            num_scalar_prefetch=1,
            grid=(width // span,),
            in_specs=[pl.BlockSpec((each, span), lambda j, at: (0, j))] * owners
            + [edge_spec(edges, p) for p in range(owners)]
            + [cache, cache]
            + anywhere(after),
            out_specs=[pl.BlockSpec((n, each, span), lambda j, at: (0, 0, j)) for n in counts],
            scratch_shapes=[pltpu.VMEM((rows, events), bf16)],
        ),
        out_shape=[jax.ShapeDtypeStruct((n, each, width), bf16) for n in counts],
        compiler_params=params(),
        cost_estimate=LIGHT,
        name="attend",
    )(at, *queries, *[edges] * owners, far(k_cache), far(v_cache), *after)


def merge(means, squares, widths):
    width = sum(widths)
    mean = sum(m * (w / width) for m, w in zip(means, widths))
    square = sum(squares) + sum(w * (m - mean) * (m - mean) for m, w in zip(means, widths))
    return mean, square


def stat_columns(stats):
    stats = [s[...] for s in stats]
    stats = [s if s.shape[0] > 8 else jnp.concatenate([s] * (DH // 8)).T for s in stats]
    return [s[:, :1] for s in stats], [s[:, 4:5] for s in stats]


def finish_kernel(terms, widths, at_ref, edge_ref, q_ref, rest_ref, *refs):
    sums, others = refs[:terms], refs[terms:terms + len(widths)]
    att_ref, stat_ref = refs[-2:]
    rows, width = att_ref.shape
    zs, chunks = edge_ref.shape[:2]
    edge = jnp.concatenate(
        [edge_ref[z, r, 0] for r in range(chunks) for z in range(zs)]
    ).astype(f32)
    root = lax.rsqrt(edge[:, 1:] - edge[:, :1])
    total = jnp.zeros((rows, 1), f32)
    for first in range(0, width, DH):
        at = slice(first, first + DH)
        summed = sum(s[0, :, at].astype(f32) for s in sums)
        product = q_ref[:, at].astype(f32) * rest_ref[0, :, at].astype(f32)
        weight = silu(jnp.sum(product, axis=1, keepdims=True) * DH ** (-0.5))
        value = summed * root + weight * rest_ref[1, :, at].astype(f32)
        att_ref[:, at] = value
        total += jnp.sum(value, axis=1, keepdims=True)
    mean = total / width
    spread = jnp.zeros((rows, DH), f32)
    for first in range(0, width, DH):
        away = att_ref[:, first:first + DH] - mean
        spread += away * away
    square = jnp.sum(spread, axis=1, keepdims=True)
    if others:
        means, squares = stat_columns(others)
        mean, square = merge([mean] + means, [square] + squares, [width] + widths)
    lane = lax.broadcasted_iota(jnp.int32, (rows, DH), 1)
    stat = jnp.where(lane < 4, mean, square)
    stat_ref[...] = stat if stat_ref.shape == stat.shape else stat.T[:8]


def finish(at, edges, query, rest, sums, others, widths, after):
    rows, width = query.shape
    stat = (8, rows) if others and rows == DH else (rows, DH)
    return pl.pallas_call(
        functools.partial(finish_kernel, len(sums), widths),
        grid_spec=pltpu.PrefetchScalarGridSpec(
            num_scalar_prefetch=1,
            grid=(1,),
            in_specs=[
                edge_spec(edges, 0),
                pl.BlockSpec((rows, width), lambda j, at: (0, 0)),
                pl.BlockSpec((2, rows, width), lambda j, at: (0, 0, 0)),
            ]
            + [pl.BlockSpec((1, rows, width), lambda j, at: (0, 0, 0))] * len(sums)
            + [pl.BlockSpec((rows, DH), lambda j, at: (0, 0))] * len(others)
            + anywhere(after),
            out_specs=(
                pl.BlockSpec((rows, width), lambda j, at: (0, 0)),
                pl.BlockSpec(stat, lambda j, at: (0, 0)),
            ),
        ),
        out_shape=(
            jax.ShapeDtypeStruct((rows, width), f32),
            jax.ShapeDtypeStruct(stat, f32),
        ),
        compiler_params=params(),
        cost_estimate=LIGHT,
        name="finish",
    )(at, edges, query, rest, *sums, *others, *after)


def merge_kernel(width, *refs):
    (m, n), (s, t) = (
        [r[:4] if r.shape[0] == 8 else r[:, :4] for r in refs[:2]],
        [r[4:] if r.shape[0] == 8 else r[:, 4:8] for r in refs[:2]],
    )
    mean, square = merge([m, n], [s, t], [width] * 2)
    if refs[2].shape[0] == 8:
        refs[2][:4], refs[2][4:] = mean, square
    else:
        lane = lax.broadcasted_iota(jnp.int32, refs[2].shape, 1)
        refs[2][...] = jnp.where(lane < 4, mean[:, :1], square[:, :1])


def merge_stats(stats, width):
    return pl.pallas_call(
        functools.partial(merge_kernel, width),
        out_shape=jax.ShapeDtypeStruct(stats[0].shape, f32),
        compiler_params=params(),
        cost_estimate=LIGHT,
        name="merge",
    )(*stats)


def gate_kernel(count, parts, width, *refs):
    stats, atts, rests, outs = (
        refs[:count], refs[count:count + parts],
        refs[count + parts:count + 2 * parts], refs[count + 2 * parts:],
    )
    means, squares = stat_columns(stats)
    mean, square = merge(means, squares, [width] * count)
    scale = lax.rsqrt(square / (width * count) + EPSILON)
    rows, column = outs[0].shape[0], 0
    for att, rest in zip(atts, rests):
        span = att.shape[1]
        normed = (att[...] - mean) * scale
        gated = (normed * rest[0].astype(f32)).astype(bf16)
        for r, out in enumerate(outs):
            out[:, column:column + span] = gated[r * rows:(r + 1) * rows]
        column += span
    for out in outs:
        if out.shape[1] > column:
            out[:, column:] = jnp.zeros((rows, out.shape[1] - column), bf16)


def gate_rows(stats, stat_width, atts, rests, chunks):
    rows, width = atts[0].shape[0], sum(a.shape[1] for a in atts)
    widths = [width + DH * min(r, 1) for r in range(chunks)]
    return pl.pallas_call(
        functools.partial(gate_kernel, len(stats), len(atts), stat_width),
        grid=(1,),
        in_specs=[pl.BlockSpec(s.shape, lambda j: (0, 0)) for s in stats]
        + [pl.BlockSpec((rows, a.shape[1]), lambda j: (0, 0)) for a in atts]
        + [pl.BlockSpec((1, rows, r.shape[2]), lambda j: (2, 0, 0)) for r in rests],
        out_specs=[pl.BlockSpec((rows // chunks, w), lambda j: (0, 0)) for w in widths],
        out_shape=[jax.ShapeDtypeStruct((rows // chunks, w), bf16) for w in widths],
        compiler_params=params(),
        cost_estimate=LIGHT,
        name="gate",
    )(*stats, *atts, *rests)


def output_kernel(owners, slots, after, index_ref, *refs):
    rows, w_ref, outs, lhs_ref = refs[:owners], refs[owners], refs[owners + 1 + after:-1], refs[-1]
    piece = rows[0].shape[1]

    @pl.when(pl.program_id(0) == 0)
    def _():
        first = 0
        for slot in slots:
            for p in range(owners):
                lhs_ref[first:first + piece, :] = rows[p][index_ref[0] ^ slot]
                first += piece

    sums = jnp.dot(lhs_ref[...], w_ref[...], preferred_element_type=f32).astype(bf16)
    first = 0
    for out in outs:
        for k in range(out.shape[0]):
            for p in range(owners):
                out[k, p] = sums[first:first + piece]
                first += piece


def output(index, slots, counts, blocks, w_out, column, columns, after):
    owners, each, zs = len(blocks), blocks[0].shape[0], sum(counts)
    width, piece = w_out.shape[0], each // zs
    span = max(c for c in (512, 256, columns) if columns % c == 0 and column % c == 0)
    row_spec = pl.BlockSpec((zs, piece, width), lambda j, at: (0, 0, 0))
    return pl.pallas_call(
        functools.partial(output_kernel, owners, slots, len(after)),
        grid_spec=pltpu.PrefetchScalarGridSpec(
            num_scalar_prefetch=1,
            grid=(columns // span,),
            in_specs=[row_spec] * owners
            + [pl.BlockSpec((width, span), lambda j, at: (0, column // span + j))]
            + anywhere(after),
            out_specs=[
                pl.BlockSpec((n, owners, piece, span), lambda j, at: (0, 0, 0, j)) for n in counts
            ],
            scratch_shapes=[pltpu.VMEM((owners * each, width), bf16)],
        ),
        out_shape=[jax.ShapeDtypeStruct((n, owners, piece, columns), bf16) for n in counts],
        compiler_params=params(),
        cost_estimate=LIGHT,
        name="output",
    )(
        index.reshape(1).astype(jnp.int32),
        *[b.reshape(zs, piece, b.shape[1]) for b in blocks], far(w_out), *after,
    )


def close_kernel(counts, at_ref, t_ref, *refs):
    out_ref, mark_ref = refs[-2:]
    mark_ref[...] = jnp.zeros_like(mark_ref)
    first, column = 0, 0
    for count in counts:
        terms = refs[first:first + count]
        span = terms[0].shape[-1]
        at = slice(column, column + span)
        for p in range(out_ref.shape[0]):
            total = t_ref[p, :, at].astype(f32)
            for term in terms:
                total = total + term[0, p ^ at_ref[0]].astype(f32)
            out_ref[p, :, at] = total.astype(bf16)
        first += count
        column += span


def close(place, index, tokens, chunks, r, g, groups, out, after):
    _, owners, piece, _ = groups[0][0].shape
    span, width = sum(terms[0].shape[-1] for terms in groups), tokens.shape[1]
    at = jnp.stack([place, index * chunks + r]).astype(jnp.int32)
    flat = [term for terms in groups for term in terms]
    into = [] if out is None else [out]
    return pl.pallas_call(
        functools.partial(close_kernel, [len(terms) for terms in groups]),
        grid_spec=pltpu.PrefetchScalarGridSpec(
            num_scalar_prefetch=1,
            grid=(1,),
            in_specs=[pl.BlockSpec((owners, piece, span), lambda j, at: (at[1], 0, g))]
            + [pl.BlockSpec((1,) + t.shape[1:], lambda j, at: (0, 0, 0, 0)) for t in flat]
            + anywhere(into) + anywhere(after),
            out_specs=(
                pl.BlockSpec((owners, piece, span), lambda j, at: (r, 0, g)),
                pl.BlockSpec((8, DH), lambda j, at: (0, 0)),
            ),
        ),
        out_shape=(
            jax.ShapeDtypeStruct((chunks * owners, piece, width), bf16),
            jax.ShapeDtypeStruct((8, DH), f32),
        ),
        input_output_aliases={} if out is None else {2 + len(flat): 0},
        compiler_params=params(),
        cost_estimate=LIGHT,
        name="close",
    )(at, far(tokens.reshape(-1, piece, width)), *flat, *into, *after)


def bits_of(axis):
    count = lax.axis_size(axis)
    assert count & (count - 1) == 0
    return count.bit_length() - 1


def reverse(index, bits):
    return sum((((index >> b) & 1) << (bits - 1 - b) for b in range(bits)), 0 * index)


def swap(x, axis, bit):
    return lax.ppermute(
        x, axis, [(i, i ^ (1 << bit)) for i in range(lax.axis_size(axis))]
    )


def scatter(keep, gots, axis, after=()):
    terms, sent = [keep, gots[0]], gots[-1]
    for b in range(1, bits_of(axis)):
        sent = fold([keep, gots[-1]] if b == 1 else terms, after)
        terms.append(swap(sent, axis, b))
    return terms, sent


def gather(x, axis, after=()):
    blocks = [x]
    for b in reversed(range(bits_of(axis))):
        blocks = blocks + [swap(block, axis, b) for block in blocks]
        if len(blocks) == 2:
            blocks[1] = tie(blocks[1], after)
    return blocks


def all_stats(stat, width, axis):
    count = lax.axis_size(axis)
    if count > 8 or count & (count - 1):
        every = lax.all_gather(stat, axis)
        return [every[i] for i in range(count)], width
    stats = [stat]
    for b in range(bits_of(axis)):
        if b:
            width, stats = 2 * width, [merge_stats(stats, width)]
        stats.append(swap(stats[0], axis, b))
    return stats, width


def head_chunks(heads):
    if heads % 8:
        return [1] * heads
    unit = heads // 8
    return [unit, 2 * unit, 2 * unit, 2 * unit, unit]


GROUPS = [[0, 1], [2], [3], [4]]
ORDER = [
    "P0", "P1", "F0", "P2", "F1", "P3", "F2", "A0", "F3", "P4", "A1", "F4", "T0", "G0", "A2",
    "T1", "A3", "G1", "T2", "T3", "G2", "G3", "E0", "E1", "E2", "E3",
]


def local(tokens, w_qkvu, k_cache, v_cache, w_out, vis_start, vis_end):
    cand, depth = tokens.shape
    owners, zs = lax.axis_size("hist"), lax.axis_size("head")
    index = lax.axis_index("head")
    place = reverse(lax.axis_index("hist"), bits_of("hist"))
    width = w_qkvu.shape[2]
    events = k_cache.shape[0]
    chunks = 2 if cand % (2 * owners * zs * 16) == 0 else 1
    piece = cand // (zs * chunks * owners)

    def arrange(x):
        x = x.reshape((zs, chunks, owners, piece) + x.shape[1:])
        if piece % 16 == 0:
            return x
        blocks = [lax.dynamic_index_in_dim(x, p ^ place, 2, False) for p in range(owners)]
        x = jnp.stack(blocks).swapaxes(1, 2)
        return x.reshape((1, 1, owners, zs * chunks * piece) + x.shape[4:])

    at = (place if piece % 16 == 0 else jnp.int32(0)).reshape(1)
    ordered = arrange(tokens)
    first_event = lax.axis_index("hist") * events
    edges = arrange(edge_columns(first_event, vis_start, vis_end))

    sizes = head_chunks(width // DH)
    firsts = [sum(sizes[:c]) for c in range(len(sizes))]
    groups, order = GROUPS, ORDER
    if len(sizes) != 5:
        groups = [[c] for c in range(len(sizes))]
        order = [step + str(c) for step in "PFATGE" for c in range(len(sizes))]
    last = len(groups) - 1
    heads = [sum(sizes[c] for c in group) for group in groups]
    chain, keeps, firsts_got, terms, sums = [], {}, {}, {}, {}
    halves, queries, parts, atts, stats = {}, {}, {}, {}, {}
    for step, c in [(name[0], int(name[1:])) for name in order]:
        after = chain[-1:]
        if step == "P":
            keep, *sends = project(at, ordered, w_qkvu, firsts[c], sizes[c], after)
            before = firsts_got[c - 1] if c >= 1 else []
            before = before + [terms[0][-1]] if c == 2 and 0 in terms else before
            firsts_got[c] = [swap(tie(send, before), "hist", 0) for send in reversed(sends)][::-1]
            keeps[c] = keep
            chain.append(keep)
        elif step == "F":
            terms[c], sent = scatter(keeps[c], firsts_got[c], "hist", after)
            chain.append(sent)
        elif step == "A":
            parts[c] = activate([terms[k] for k in groups[c]], after)
            queries[c] = gather(parts[c][0], "hist")
            chain.append(parts[c][0])
        elif step == "T":
            first = firsts[groups[c][0]]
            keep, *sends = attend(at, queries[c], k_cache, v_cache, edges, first, after)
            before = queries[last][1:2] if c == last - 1 and last in queries else []
            halves[c] = keep, [swap(tie(send, before), "hist", 0) for send in sends]
            chain.append(keep)
        elif step == "G":
            sums[c], sent = scatter(*halves[c], "hist", after)
            chain.append(sent)
        else:
            others = [stats[k] for k in range(last)] if c == last else []
            widths = [size * DH for size in heads[:last]] if c == last else []
            atts[c], stats[c] = finish(at, edges, *parts[c], sums[c], others, widths, after)
            chain.append(atts[c])

    atts = [atts[c] for c in range(last + 1)]
    rests = [parts[c][1] for c in range(last + 1)]
    every, stat_width = all_stats(stats[last], width, "head")
    gated = gate_rows(every, stat_width, atts, rests, chunks)
    columns = w_out.shape[1]
    straight = piece % 16 == 0 and zs & (zs - 1) == 0
    out = None
    if not straight:
        for r, rows in enumerate(gated):
            whole = jnp.concatenate(gather(rows, "hist"))[:, :width]
            whole = jnp.dot(whole, w_out, preferred_element_type=f32).astype(bf16)
            whole = whole.reshape(owners, zs, piece, -1).swapaxes(0, 1)
            whole = lax.psum_scatter(whole, "head", scatter_dimension=0, tiled=True)
            out, _ = close(place, index, tokens, chunks, r, 0, [[whole]], out, [])
        return out.reshape(cand // zs, -1)
    slots = [reverse(k, bits_of("head")) for k in range(zs)]
    groups = 2 if columns % 1024 == 0 else 1
    span = columns // groups
    counts = [zs // 2] * 2 if zs > 1 else [1]
    plan = [(r, g) for r in range(chunks) for g in range(groups)]
    chain, first_out, blocks, made, folded = [], [], {}, [], []

    def fold_next():
        own, arrived = made[len(folded)]
        terms, sent = scatter(own, arrived, "head", chain) if arrived else ([own], own)
        folded.append(terms)
        return [sent]

    for n, (r, g) in enumerate(plan):
        if r not in blocks:
            blocks[r] = gather(gated[r], "hist", first_out)
        own, *others = output(index, slots, counts, blocks[r], w_out, g * span, span, chain)
        before = made[n - 2][1] if n > 1 else []
        before = before + [folded[0][-1]] if folded else before
        made.append((own, [swap(tie(x, before), "head", 0) for x in others]))
        chain, first_out = [own], first_out or [own]
        if n == 2:
            chain = fold_next()
    closed = 0
    while closed < len(plan):
        if len(folded) < len(plan):
            chain = fold_next()
        if len(folded) > closed + 2 or len(folded) == len(plan):
            r, g = plan[closed]
            some = 1 if r < chunks - 1 else groups
            out, mark = close(
                place, index, tokens, chunks, r, g, folded[closed:closed + some], out, chain
            )
            chain, closed = [mark], closed + some
    return out.reshape(cand // zs, -1)


def solution(mesh):
    in_specs = (
        P("groups", "hist"),
        P("hist", None, "head"),
        P(("groups", "hist"), "head"),
        P(("groups", "hist"), "head"),
        P("head", "hist"),
        P("groups"),
        P("groups"),
    )
    out_specs = P(("groups", "head"), "hist")
    return jax.shard_map(local, mesh=mesh, in_specs=in_specs, out_specs=out_specs, check_vma=False)
```
